32 devices in a mesh: dp: 8 (over y, x, core), tensor: 4 (over z).
Axes of the slice: x: 2, y: 2, z: 4, core: 2. Of those that a mesh axis runs over, the one named last changes fastest.
Arguments:
- patches: bfloat16 [32, 256, 768], P('dp', None, 'tensor'), may hold values from -6 to 6
- ctx_idx: int32 [32, 128], P('dp'), may hold values from 0 to 255, as said below
- tgt_idx: int32 [32, 64], P('dp'), may hold values from 0 to 255, as said below
- owner: int32 [19], replicated, may hold values from 0 to 22, as said below
- weights: float32 [4, 24, 384, 384], P('tensor', 'dp'), may hold values from -0.3125 to 0.3125
- stats_left: float32 [4, 24, 384, 384], P('tensor', 'dp')
- stats_right: float32 [4, 24, 384, 384], P('tensor', 'dp')
- root_left: float32 [4, 24, 384, 384], P('tensor', 'dp')
- root_right: float32 [4, 24, 384, 384], P('tensor', 'dp')
- teacher_slot_blocks: float32 [4, 24, 384, 384], P('tensor', 'dp'), may hold values from -0.3125 to 0.3125
- embed: float32 [768, 768], P('tensor', 'dp'), may hold values from -0.21875 to 0.21875
- embed_m: float32 [768, 768], P('tensor', 'dp')
- embed_v: float32 [768, 768], P('tensor', 'dp')
- teacher_embed: float32 [768, 768], P('tensor', 'dp'), may hold values from -0.21875 to 0.21875
- enc_vectors: float32 [7, 768], replicated
- enc_m: float32 [7, 768], replicated
- enc_v: float32 [7, 768], replicated
- pred_vectors: float32 [11, 384], replicated
- pred_m: float32 [11, 384], replicated
- pred_v: float32 [11, 384], replicated
- teacher_vectors: float32 [7, 768], replicated
Outputs:
- loss: float32 [], replicated
- block_grads: float32 [4, 24, 384, 384], P('tensor', 'dp')
- new_weights: float32 [4, 24, 384, 384], P('tensor', 'dp')
- new_left: float32 [4, 24, 384, 384], P('tensor', 'dp')
- new_right: float32 [4, 24, 384, 384], P('tensor', 'dp')
- new_teacher_blocks: float32 [4, 24, 384, 384], P('tensor', 'dp')
- new_embed: float32 [768, 768], P('tensor', 'dp')
- new_embed_m: float32 [768, 768], P('tensor', 'dp')
- new_embed_v: float32 [768, 768], P('tensor', 'dp')
- new_teacher_embed: float32 [768, 768], P('tensor', 'dp')
- new_enc_vectors: float32 [7, 768], replicated
- new_enc_m: float32 [7, 768], replicated
- new_enc_v: float32 [7, 768], replicated
- new_pred_vectors: float32 [11, 384], replicated
- new_pred_m: float32 [11, 384], replicated
- new_pred_v: float32 [11, 384], replicated
- new_teacher_vectors: float32 [7, 768], replicated
The draws below stay inside these ranges and needn't reach their ends.
Inputs may be any that keep to these rules, and one draw needn't show every extreme that they name: `ctx_idx`: within an image the 128 context patches and the 64 target patches are all distinct, and the two sets share none. `tgt_idx`: see ctx_idx. `owner`: the 19 slots are distinct; slot s lies on index s // 3 of dp. The filled slots are, for k below 19, local slot k // 8 of index k % 8; which block takes which of them is drawn.
All inputs are finite; a program needn't handle non-finite values.
Results may differ from the reference program's by a relative error of at most 0.012.
The reference program's roundings to bfloat16 on the way count: a program that leaves them out, or rounds other values in their place, can miss the bound.
Values may be sent and summed in bfloat16 or wider, within the bound.
A program may use at most 192 MiB of HBM per device.

```python
import math
import jax
import jax.numpy as jnp
from jax import lax

D = 768
HD = 64
PREDICT_WIDTH = 384
PHD = 32
PIX = 768
SIDE = 16
CTX = 128
TGT = 64
LAYERS = 1
PLAYERS = 2
STEP = 10
NPATCH = 256
SHAMPOO_SIDE = 384
NB = 19
SLOT_DEV = 3
SLOT_TOTAL = 24
IMAGES = 32
N_DP = 8
N_TENSOR = 4


def grad_unit():
    return 1.0 / (D * math.sqrt(IMAGES * TGT))


def patch_orders(key):
    keys = jax.random.split(jax.random.fold_in(key, 7), IMAGES)
    return jax.vmap(lambda single: jax.random.permutation(single, NPATCH))(keys).astype(jnp.int32)


def draw_ctx_idx(key, part):
    return patch_orders(key)[:, :CTX]


def draw_tgt_idx(key, part):
    return patch_orders(key)[:, CTX:CTX + TGT]


def draw_owner(key, part):
    order = jax.random.permutation(jax.random.fold_in(key, 11), NB).astype(jnp.int32)
    return (order % N_DP * SLOT_DEV + order // N_DP).astype(jnp.int32)


def level_draw(key, power):
    base = 0.0526 * SHAMPOO_SIDE * (32.0 * grad_unit()) ** 2
    scale_factor = jnp.exp(jax.random.uniform(key, (N_TENSOR, SLOT_TOTAL, 1, 1), jnp.float32, 0.0, math.log(4.0)))
    return (base * scale_factor) ** power


def definite_draw(key, level):
    random_noise = jax.random.normal(key, (N_TENSOR, SLOT_TOTAL, SHAMPOO_SIDE, SHAMPOO_SIDE), jnp.float32)
    symmetric = (random_noise + jnp.swapaxes(random_noise, 2, 3)) * (0.2 / math.sqrt(SHAMPOO_SIDE))
    return level * (jnp.eye(SHAMPOO_SIDE, dtype=jnp.float32) + symmetric)


def draw_stats_left(key, part):
    return definite_draw(jax.random.fold_in(key, 22), level_draw(jax.random.fold_in(key, 21), 1.0))


def draw_stats_right(key, part):
    return definite_draw(jax.random.fold_in(key, 24), level_draw(jax.random.fold_in(key, 23), 1.0))


def draw_root_left(key, part):
    return definite_draw(jax.random.fold_in(key, 26), level_draw(jax.random.fold_in(key, 25), -0.25))


def draw_root_right(key, part):
    return definite_draw(jax.random.fold_in(key, 28), level_draw(jax.random.fold_in(key, 27), -0.25))


def first_moment(key, shape):
    return 0.11 * grad_unit() * jax.random.normal(key, shape, jnp.float32)


def second_moment(key, shape):
    scale_factor = jnp.exp(jax.random.uniform(key, shape, jnp.float32, 0.0, math.log(4.0)))
    return 0.001 * grad_unit() ** 2 * scale_factor


def draw_embed_m(key, part):
    return first_moment(jax.random.fold_in(key, 41), (PIX, D))


def draw_embed_v(key, part):
    return second_moment(jax.random.fold_in(key, 42), (PIX, D))


def draw_enc_m(key, part):
    return first_moment(jax.random.fold_in(key, 43), (4 * LAYERS + 3, D))


def draw_enc_v(key, part):
    return second_moment(jax.random.fold_in(key, 44), (4 * LAYERS + 3, D))


def draw_pred_m(key, part):
    return first_moment(jax.random.fold_in(key, 45), (4 * PLAYERS + 3, PREDICT_WIDTH))


def draw_pred_v(key, part):
    return second_moment(jax.random.fold_in(key, 46), (4 * PLAYERS + 3, PREDICT_WIDTH))


def vector_draw(key, count_rows, columns):
    gains = jax.random.uniform(jax.random.fold_in(key, 1), (count_rows, columns), jnp.float32, 0.5, 1.5)
    shifts = 0.3 * jax.random.normal(jax.random.fold_in(key, 2), (count_rows, columns), jnp.float32)
    row_number = jnp.arange(count_rows)
    is_gain = ((row_number % 2 == 0) & (row_number < count_rows - 1))[:, None]
    return jnp.where(is_gain, gains, shifts)


def draw_enc_vectors(key, part):
    return vector_draw(jax.random.fold_in(key, 31), 4 * LAYERS + 3, D)


def draw_pred_vectors(key, part):
    return vector_draw(jax.random.fold_in(key, 32), 4 * PLAYERS + 3, PREDICT_WIDTH)


def draw_teacher_vectors(key, part):
    return vector_draw(jax.random.fold_in(key, 33), 4 * LAYERS + 3, D)


def block_scale(own_key, shape, pieces, smallest, high):
    loudness = 1.0
    for dim, parts in pieces:
        heights = jax.random.uniform(jax.random.fold_in(jax.random.fold_in(own_key, 6), dim), (parts,), jnp.float32, smallest / len(pieces), high / len(pieces))
        loudness = loudness * jnp.repeat(jnp.exp(heights), shape[dim] // parts).reshape((-1,) + (1,) * (len(shape) - 1 - dim))
    return loudness


def centred(stream_key, extent, width, reach, cuts=(), kind=jnp.bfloat16):
    factor_of = block_scale(stream_key, extent, cuts, -0.22, 0.18) if cuts else 1.0
    values = jax.random.normal(stream_key, extent, jnp.float32) * width * factor_of
    return jnp.minimum(jnp.maximum(values, -reach), reach).astype(kind)


def setup_inputs(seed: int = 0) -> dict:
    key_of = jax.random.split(jax.random.key(seed), 22)
    return {
        "patches": centred(key_of[0], (IMAGES, NPATCH, PIX), 1.0, 6.0, ((0, 8), (2, 4))),
        "ctx_idx": draw_ctx_idx(jax.random.fold_in(key_of[21], 71), 0),
        "tgt_idx": draw_tgt_idx(jax.random.fold_in(key_of[21], 71), 0),
        "owner": draw_owner(jax.random.fold_in(key_of[21], 71), 0),
        "weights": centred(key_of[4], (N_TENSOR, SLOT_TOTAL, SHAMPOO_SIDE, SHAMPOO_SIDE), PREDICT_WIDTH ** -0.5, 0.3125, ((0, 4), (1, 8)), jnp.float32),
        "stats_left": draw_stats_left(jax.random.fold_in(key_of[21], 71), 0),
        "stats_right": draw_stats_right(jax.random.fold_in(key_of[21], 71), 0),
        "root_left": draw_root_left(jax.random.fold_in(key_of[21], 71), 0),
        "root_right": draw_root_right(jax.random.fold_in(key_of[21], 71), 0),
        "teacher_slot_blocks": centred(key_of[9], (N_TENSOR, SLOT_TOTAL, SHAMPOO_SIDE, SHAMPOO_SIDE), PREDICT_WIDTH ** -0.5, 0.3125, ((0, 4), (1, 8)), jnp.float32),
        "embed": centred(key_of[10], (PIX, D), PIX ** -0.5, 0.21875, ((0, 4), (1, 8)), jnp.float32),
        "embed_m": draw_embed_m(jax.random.fold_in(key_of[21], 71), 0),
        "embed_v": draw_embed_v(jax.random.fold_in(key_of[21], 71), 0),
        "teacher_embed": centred(key_of[13], (PIX, D), PIX ** -0.5, 0.21875, ((0, 4), (1, 8)), jnp.float32),
        "enc_vectors": draw_enc_vectors(jax.random.fold_in(key_of[21], 71), 0),
        "enc_m": draw_enc_m(jax.random.fold_in(key_of[21], 71), 0),
        "enc_v": draw_enc_v(jax.random.fold_in(key_of[21], 71), 0),
        "pred_vectors": draw_pred_vectors(jax.random.fold_in(key_of[21], 71), 0),
        "pred_m": draw_pred_m(jax.random.fold_in(key_of[21], 71), 0),
        "pred_v": draw_pred_v(jax.random.fold_in(key_of[21], 71), 0),
        "teacher_vectors": draw_teacher_vectors(jax.random.fold_in(key_of[21], 71), 0),
    }


exact = lax.Precision.HIGHEST
batch_images = 16

@jax.custom_vjp
def low(v):
    return lax.optimization_barrier(v.astype(jnp.bfloat16)).astype(jnp.float32)

@jax.custom_vjp
def low_back(v):
    return v

def low_keep(v):
    return (low(v), None)

def low_pass(kept, grad):
    return (grad,)

def back_keep(v):
    return (v, None)

def back_low(kept, grad):
    return (low(grad),)
low.defvjp(low_keep, low_pass)
low_back.defvjp(back_keep, back_low)

def einsum_high(form, first, second):
    return jnp.einsum(form, first, second, precision=exact, preferred_element_type=jnp.float32)

def layer_norm(values, gain_row, shift_row):
    centre = values - lax.optimization_barrier(jnp.mean(values, -1, keepdims=True))
    return centre * lax.rsqrt(lax.optimization_barrier(jnp.mean(centre * centre, -1, keepdims=True)) + 1e-06) * gain_row + shift_row

def sincos(cell_index, columns):
    quarter = columns // 4
    frequency = 1.0 / 10000.0 ** (jnp.arange(quarter).astype(jnp.float32) / quarter)
    col_angle = (cell_index % SIDE).astype(jnp.float32)[..., None] * frequency
    row_angle = (cell_index // SIDE).astype(jnp.float32)[..., None] * frequency
    return jnp.concatenate([jnp.sin(col_angle), jnp.cos(col_angle), jnp.sin(row_angle), jnp.cos(row_angle)], -1)

def tile(blocks, first_block, per_side):
    edge_size = blocks.shape[-1]
    picked = blocks[first_block:first_block + per_side * per_side]
    return picked.reshape(per_side, per_side, edge_size, edge_size).transpose(0, 2, 1, 3).reshape(per_side * edge_size, per_side * edge_size)

def encoder_mats(blocks):
    per_side = D // SHAMPOO_SIDE
    count_per = per_side * per_side
    result = []
    for depth in range(LAYERS):
        first_block = 3 * count_per * depth
        result.append([(tile(rank_blocks, first_block, per_side), tile(rank_blocks, first_block + count_per, per_side), tile(rank_blocks, first_block + 2 * count_per, per_side)) for rank_blocks in blocks])
    return result

def predictor_mats(blocks):
    base_block = 3 * (D // SHAMPOO_SIDE) ** 2 * LAYERS
    result = []
    for depth in range(PLAYERS):
        first_block = base_block + 3 * depth
        result.append([(rank_blocks[first_block], rank_blocks[first_block + 1], rank_blocks[first_block + 2]) for rank_blocks in blocks])
    quarter_width = D // N_TENSOR
    in_rows = jnp.concatenate([rank_blocks[-1][:, :quarter_width].T for rank_blocks in blocks], 0)
    out_cols = jnp.concatenate([rank_blocks[-1][:, quarter_width:] for rank_blocks in blocks], 1)
    return (result, in_rows, out_cols)

def sublayers(resid, rank_mats, vector_rows, head_size):
    normed = low(layer_norm(resid, vector_rows[0], vector_rows[1]))
    mixed = 0.0
    for attn_w, up_w, down_t in rank_mats:
        columns = attn_w.shape[1] // 4
        weight_low = low(attn_w)
        qkv_rows = low_back(low(einsum_high('gsd,dc->gsc', normed, weight_low[:, :3 * columns])))
        shaped = resid.shape[:2] + (columns // head_size, head_size)
        queries = qkv_rows[..., :columns].reshape(shaped)
        keys_all = qkv_rows[..., columns:2 * columns].reshape(shaped)
        values_all = qkv_rows[..., 2 * columns:3 * columns].reshape(shaped)
        scores = low_back(einsum_high('gqhe,gkhe->ghqk', queries, keys_all) / math.sqrt(head_size))
        softened = low(jax.nn.softmax(scores, -1))
        attended = low_back(low(einsum_high('ghqk,gkhe->gqhe', softened, values_all))).reshape(resid.shape[:2] + (columns,))
        mixed = mixed + einsum_high('gsc,dc->gsd', attended, weight_low[:, 3 * columns:])
    resid = resid + low_back(mixed)
    normed = low(layer_norm(resid, vector_rows[2], vector_rows[3]))
    mixed = 0.0
    for attn_w, up_w, down_t in rank_mats:
        hidden = low_back(einsum_high('gsd,dc->gsc', normed, low(up_w)))
        active = low(jax.nn.gelu(hidden, approximate=False))
        mixed = mixed + einsum_high('gsc,dc->gsd', active, low(down_t))
    return resid + low_back(mixed)

def teacher_target(teacher, tembed, tvectors, patch, target_idx):
    encoder = encoder_mats(teacher)
    resid = einsum_high('gsp,pd->gsd', patch, low(tembed)) + tvectors[4 * LAYERS + 2] + sincos(jnp.arange(NPATCH), D)
    for depth in range(LAYERS):
        resid = sublayers(resid, encoder[depth], tvectors[4 * depth:4 * depth + 4], HD)
    final = layer_norm(layer_norm(resid, tvectors[4 * LAYERS], tvectors[4 * LAYERS + 1]), 1.0, 0.0)
    return jnp.take_along_axis(low(final), target_idx[:, :, None], 1)

def student_loss(params, patch, context, target_idx, target):
    blocks, embed, enc_vectors, pred_vectors = params
    encoder = encoder_mats(blocks)
    predictor, in_rows, out_cols = predictor_mats(blocks)
    picked = jnp.take_along_axis(patch, context[:, :, None], 1)
    resid = low_back(einsum_high('gsp,pd->gsd', picked, low(embed))) + enc_vectors[4 * LAYERS + 2] + sincos(context, D)
    for depth in range(LAYERS):
        resid = sublayers(resid, encoder[depth], enc_vectors[4 * depth:4 * depth + 4], HD)
    encoded = low_back(low(layer_norm(resid, enc_vectors[4 * LAYERS], enc_vectors[4 * LAYERS + 1])))
    projected = low_back(einsum_high('gsd,dp->gsp', encoded, low(in_rows)))
    group_size = context.shape[0]
    tokens = jnp.concatenate([projected, jnp.zeros((group_size, TGT, PREDICT_WIDTH), jnp.float32)], 1)
    tokens = tokens + sincos(jnp.concatenate([context, target_idx], 1), PREDICT_WIDTH)
    tokens = tokens.at[:, CTX:].add(pred_vectors[4 * PLAYERS + 2])
    for depth in range(PLAYERS):
        tokens = sublayers(tokens, predictor[depth], pred_vectors[4 * depth:4 * depth + 4], PHD)
    final = low(layer_norm(tokens, pred_vectors[4 * PLAYERS], pred_vectors[4 * PLAYERS + 1]))[:, CTX:]
    predicted = low_back(einsum_high('gsp,pd->gsd', final, low(out_cols)))
    residual_gap = predicted - target
    magnitude = jnp.abs(residual_gap)
    terms = jnp.where(magnitude < 1.0, 0.5 * residual_gap * residual_gap, magnitude - 0.5)
    return jnp.sum(terms) / (IMAGES * TGT * D)

def adamw(master, moment, second, gradient, step_rate, weight_decay):
    moment = 0.9 * moment + 0.1 * gradient
    second = 0.999 * second + 0.001 * gradient * gradient
    unbiased_first = moment / (1.0 - 0.9 ** STEP)
    unbiased_second = second / (1.0 - 0.999 ** STEP)
    return (master - step_rate * (unbiased_first / (jnp.sqrt(unbiased_second) + 1e-08) + weight_decay * master), moment, second)

def reference(patches, ctx_idx, tgt_idx, owner, weights, stats_left, stats_right, root_left, root_right, teacher_slot_blocks, embed, embed_m, embed_v, teacher_embed, enc_vectors, enc_m, enc_v, pred_vectors, pred_m, pred_v, teacher_vectors):
    student = weights[:, owner]
    teacher = teacher_slot_blocks[:, owner[:3 * (D // SHAMPOO_SIDE) ** 2 * LAYERS]]
    params = (student, embed, enc_vectors, pred_vectors)
    steps_count = IMAGES // batch_images

    def one_group(carry, data):
        patch, context, target_idx = data
        patch = patch.astype(jnp.float32)
        target = teacher_target(teacher, teacher_embed, teacher_vectors, patch, target_idx)
        loss_part, backward = jax.vjp(lambda inner: student_loss(inner, patch, context, target_idx, target), params)
        grads_part = backward(jnp.ones_like(loss_part))[0]
        return (jax.tree.map(jnp.add, carry, (grads_part, loss_part)), None)
    start = jax.tree.map(jnp.zeros_like, (params, jnp.zeros((), jnp.float32)))
    data = (patches.reshape(steps_count, batch_images, NPATCH, PIX), ctx_idx.reshape(steps_count, batch_images, CTX), tgt_idx.reshape(steps_count, batch_images, TGT))
    (grads, loss), _ = lax.scan(one_group, start, data)
    grad_blocks, grad_embed, grad_enc, grad_pred = grads
    slot_grads = jnp.zeros_like(weights).at[:, owner].set(grad_blocks)
    new_left = 0.95 * stats_left + 0.05 * einsum_high('tsij,tskj->tsik', slot_grads, slot_grads)
    new_right = 0.95 * stats_right + 0.05 * einsum_high('tsji,tsjk->tsik', slot_grads, slot_grads)
    direction = einsum_high('tsij,tsjk->tsik', einsum_high('tsij,tsjk->tsik', root_left, slot_grads), root_right)
    direction = direction * lax.rsqrt(lax.optimization_barrier(jnp.mean(direction * direction, axis=(2, 3), keepdims=True)) + 1e-06)
    new_weights = weights - 0.05 * (direction + 0.05 * weights)
    new_teacher_blocks = 0.7 * teacher_slot_blocks + 0.3 * new_weights
    new_embed, new_embed_m, new_embed_v = adamw(embed, embed_m, embed_v, grad_embed, 0.05, 0.05)
    new_enc, new_enc_m, new_enc_v = adamw(enc_vectors, enc_m, enc_v, grad_enc, 0.5, 0.0)
    new_pred, new_pred_m, new_pred_v = adamw(pred_vectors, pred_m, pred_v, grad_pred, 0.5, 0.0)
    new_teacher_embed = 0.7 * teacher_embed + 0.3 * new_embed
    new_teacher_vectors = 0.7 * teacher_vectors + 0.3 * new_enc
    return (loss, slot_grads, new_weights, new_left, new_right, new_teacher_blocks, new_embed, new_embed_m, new_embed_v, new_teacher_embed, new_enc, new_enc_m, new_enc_v, new_pred, new_pred_m, new_pred_v, new_teacher_vectors)
```

```python
import math

import jax
import jax.numpy as jnp
from jax import lax
from jax.sharding import PartitionSpec as P

HD = 64
PHD = 32
SIDE = 16
STEP = 10

AXES = ("dp", "tensor")
exact = lax.Precision.HIGHEST
f32 = jnp.float32
bf16 = jnp.bfloat16


def dot32(form, first, second):
    return jnp.einsum(form, first, second, preferred_element_type=f32)


def gelu_exact(values):
    return jax.nn.gelu(values, approximate=False)


def layer_norm(values, gain_row, shift_row):
    centre = values - jnp.mean(values, -1, keepdims=True)
    return (
        centre * lax.rsqrt(jnp.mean(centre * centre, -1, keepdims=True) + 1e-06) * gain_row
        + shift_row
    )


def norm_backward(grad, values, gain_row):
    centre = values - jnp.mean(values, -1, keepdims=True)
    scale = lax.rsqrt(jnp.mean(centre * centre, -1, keepdims=True) + 1e-06)
    unit = centre * scale
    weighted = grad * gain_row
    inner = (
        weighted
        - jnp.mean(weighted, -1, keepdims=True)
        - unit * jnp.mean(weighted * unit, -1, keepdims=True)
    )
    return (inner * scale, jnp.sum(grad * unit, 0), jnp.sum(grad, 0))


def sincos(cell_index, columns):
    quarter = columns // 4
    frequency = 1.0 / 10000.0 ** (jnp.arange(quarter).astype(f32) / quarter)
    col_angle = (cell_index % SIDE).astype(f32)[..., None] * frequency
    row_angle = (cell_index // SIDE).astype(f32)[..., None] * frequency
    return jnp.concatenate(
        [jnp.sin(col_angle), jnp.cos(col_angle), jnp.sin(row_angle), jnp.cos(row_angle)], -1
    )


def heads(rows, count, length, head_size):
    groups = rows.shape[0]
    columns = rows.shape[2] // 3
    shaped = rows.reshape(groups, count, length, 3, columns // head_size, head_size)
    shaped = shaped.transpose(3, 0, 1, 4, 2, 5)
    return (shaped[0], shaped[1], shaped[2])


def flat(pieces):
    groups, count, head_count, length, head_size = pieces.shape
    return pieces.transpose(0, 1, 3, 2, 4).reshape(groups, count * length, head_count * head_size)


def attend_forward(resid, attn_w, gain_row, shift_row, head_size, count, bias):
    normed = layer_norm(resid, gain_row, shift_row).astype(bf16)
    columns = attn_w.shape[2] // 4
    length = resid.shape[0] // count
    rows = dot32("nd,tdc->tnc", normed, attn_w[:, :, : 3 * columns]).astype(bf16)
    queries, keys_all, values_all = heads(rows, count, length, head_size)
    scores = dot32("tghqe,tghke->tghqk", queries, keys_all) / math.sqrt(head_size) + bias
    expo = jnp.exp(scores - jnp.max(scores, -1, keepdims=True))
    soft = expo / jnp.sum(expo, -1, keepdims=True)
    attended = flat(dot32("tghqk,tghke->tghqe", soft.astype(bf16), values_all).astype(bf16))
    mixed = dot32("tnc,tdc->nd", attended, attn_w[:, :, 3 * columns :])
    return (resid + mixed, (normed, queries, keys_all, values_all, soft, attended))


def attend_backward(grad_out, resid, attn_w, gain_row, kept, head_size, count):
    normed, queries, keys_all, values_all, soft, attended = kept
    columns = attn_w.shape[2] // 4
    root = math.sqrt(head_size)
    low = grad_out.astype(bf16)
    grad_out_w = dot32("nd,tnc->tdc", low, attended)
    grad_att = dot32("nd,tdc->tnc", low, attn_w[:, :, 3 * columns :]).astype(bf16)
    groups, _, head_count, length, _ = queries.shape
    grad_heads = grad_att.reshape(groups, count, length, head_count, head_size).transpose(
        0, 1, 3, 2, 4
    )
    grad_values = dot32("tghqk,tghqe->tghke", soft.astype(bf16), grad_heads).astype(bf16)
    grad_soft = dot32("tghqe,tghke->tghqk", grad_heads, values_all)
    grad_scores = (soft * (grad_soft - jnp.sum(grad_soft * soft, -1, keepdims=True))).astype(bf16)
    grad_queries = (dot32("tghqk,tghke->tghqe", grad_scores, keys_all) / root).astype(bf16)
    grad_keys = (dot32("tghqk,tghqe->tghke", grad_scores, queries) / root).astype(bf16)
    grad_rows = jnp.concatenate([flat(grad_queries), flat(grad_keys), flat(grad_values)], 2)
    grad_in_w = dot32("nd,tnc->tdc", normed, grad_rows)
    grad_normed = dot32("tnc,tdc->nd", grad_rows, attn_w[:, :, : 3 * columns])
    grad_resid, grad_gain, grad_shift = norm_backward(grad_normed, resid, gain_row)
    return (
        grad_out + grad_resid,
        jnp.concatenate([grad_in_w, grad_out_w], 2),
        grad_gain,
        grad_shift,
    )


def feed_forward(resid, up_w, down_t, gain_row, shift_row):
    normed = layer_norm(resid, gain_row, shift_row).astype(bf16)
    hidden = dot32("nd,tdc->tnc", normed, up_w)
    active = gelu_exact(hidden).astype(bf16)
    return (resid + dot32("tnc,tdc->nd", active, down_t), (normed, hidden))


def feed_backward(grad_out, resid, up_w, down_t, gain_row, kept):
    normed, hidden = kept
    low = grad_out.astype(bf16)
    active, gelu_back = jax.vjp(gelu_exact, hidden)
    grad_down = dot32("nd,tnc->tdc", low, active.astype(bf16))
    grad_hidden = gelu_back(dot32("nd,tdc->tnc", low, down_t))[0].astype(bf16)
    grad_up = dot32("nd,tnc->tdc", normed, grad_hidden)
    grad_normed = dot32("tnc,tdc->nd", grad_hidden, up_w)
    grad_resid, grad_gain, grad_shift = norm_backward(grad_normed, resid, gain_row)
    return (grad_out + grad_resid, grad_up, grad_down, grad_gain, grad_shift)


def adamw(master, moment, second, gradient, step_rate, weight_decay):
    moment = 0.9 * moment + 0.1 * gradient
    second = 0.999 * second + 0.001 * gradient * gradient
    unbiased_first = moment / (1.0 - 0.9**STEP)
    unbiased_second = second / (1.0 - 0.999**STEP)
    return (
        master
        - step_rate
        * (unbiased_first / (jnp.sqrt(unbiased_second) + 1e-08) + weight_decay * master),
        moment,
        second,
    )


class Routes:
    def __init__(self, nd, nt):
        self.nd, self.nt, self.half = nd, nt, nt // 2
        self.low_bits = [1 << s for s in range(1, nd.bit_length() - 1)]
        self.stages = len(self.low_bits)

    def order(self, core):
        return self.low_bits if core == 0 else self.low_bits[::-1]

    def pairs(self, target, keep):
        found = []
        for d in range(self.nd):
            for z in range(self.nt):
                if keep(d, z):
                    d2, z2 = target(d, z)
                    found.append((d * self.nt + z, d2 * self.nt + z2))
        return found

    def stage(self, number, values, role):
        def target(d, z):
            if number == self.stages:
                return d ^ 1, z
            return d ^ self.order(d & 1)[number], z

        return lax.ppermute(
            values,
            AXES,
            self.pairs(target, lambda d, z: role is None or z // self.half == role),
        )

    def across(self, r, values, from_role=None, to_role=None):
        def keep(d, z):
            return (from_role is None or z // self.half == from_role) and (
                to_role is None or (z ^ r) // self.half == to_role
            )

        return lax.ppermute(values, AXES, self.pairs(lambda d, z: (d, z ^ r), keep))

    def holders(self, d):
        place = jnp.arange(self.nd, dtype=jnp.int32)
        held = d ^ (place >> self.stages)
        core = held & 1
        for s in range(self.stages):
            bit = (place >> s) & 1
            held = held ^ (bit * jnp.where(core == 0, self.order(0)[s], self.order(1)[s]))
        return held

    def spread(self, stack, role):
        for number in range(self.stages + 1):
            stack = jnp.concatenate([stack, self.stage(number, stack, role)], 1)
        return stack

    def reduce(self, grads, role, is_role):
        current = grads
        for number in reversed(range(self.stages + 1)):
            middle = current.shape[1] // 2
            got = self.stage(number, current[:, middle:].astype(bf16), role)
            current = current[:, :middle].astype(f32) + got.astype(f32)
        total = jnp.where(is_role, current[0], 0.0)
        for r in range(1, self.nt):
            got = self.across(r, current[r].astype(bf16), from_role=role)
            total = total + got.astype(f32)
        return total

    def total(self, values):
        for bit in [1] + self.low_bits:
            values = values + lax.ppermute(
                values, AXES, self.pairs(lambda d, z, b=bit: (d ^ b, z), lambda d, z: True)
            )
        r = 1
        while r < self.nt:
            values = values + self.across(r, values)
            r *= 2
        return values


def shards(
    patches,
    ctx_idx,
    tgt_idx,
    owner,
    weights,
    stats_left,
    stats_right,
    root_left,
    root_right,
    teacher_slot_blocks,
    embed,
    embed_m,
    embed_v,
    teacher_embed,
    enc_vectors,
    enc_m,
    enc_v,
    pred_vectors,
    pred_m,
    pred_v,
    teacher_vectors,
):
    nt = lax.axis_size("tensor")
    nd = lax.axis_size("dp")
    routes = Routes(nd, nt)
    half = nt // 2
    d = lax.axis_index("dp")
    z = lax.axis_index("tensor")
    role = z // half
    student_role = role == 0
    images, npatches, pix_part = patches.shape
    slots = weights.shape[1]
    edge = weights.shape[-1]
    slot_count = slots * nd
    block_count = owner.shape[0]
    width = enc_vectors.shape[1]
    narrow = pred_vectors.shape[1]
    players = (pred_vectors.shape[0] - 3) // 4
    side = width // edge
    per_mat = side * side
    teach_count = 3 * per_mat
    quarter = width // nt
    context_len = ctx_idx.shape[1]
    target_len = tgt_idx.shape[1]
    seq_len = context_len + target_len
    share = images // half
    rows_part = edge // nd

    both = jnp.stack([weights[0], teacher_slot_blocks[0]]).astype(bf16)
    both = both.reshape(2, slots, nd, rows_part, edge)
    both = lax.all_to_all(both, "dp", split_axis=2, concat_axis=0, tiled=False)
    by_slot = both.transpose(1, 0, 2, 3, 4).reshape(2, slot_count, rows_part, edge)
    mine = by_slot[0][owner]
    teach = by_slot[1][owner[:teach_count]]

    chunk = rows_part
    wide_t = jnp.stack([embed, teacher_embed]).astype(bf16).transpose(0, 2, 1)
    high = d // (nd // 2)
    first = lax.dynamic_slice_in_dim(wide_t, high * chunk, chunk, 1)
    second = lax.dynamic_slice_in_dim(wide_t, (1 - high) * chunk, chunk, 1)

    def swap_pairs(flip, inverse):
        found = []
        for a in range(nd):
            h = a // (nd // 2)
            b = 2 * (a % (nd // 2)) + (h if not flip else 1 - h)
            found.append((b, a) if inverse else (a, b))
        return found

    got_first = lax.ppermute(first, "dp", swap_pairs(False, False))
    got_second = lax.ppermute(second, "dp", swap_pairs(True, False))
    odd = d % 2
    low_half = jnp.where(odd == 0, got_first, got_second)
    high_half = jnp.where(odd == 0, got_second, got_first)
    emb_rows = jnp.concatenate([low_half, high_half], 1)

    def square(blocks, number):
        picked = blocks[number * per_mat : (number + 1) * per_mat]
        return (
            picked.reshape(side, side, rows_part, edge)
            .transpose(0, 2, 1, 3)
            .reshape(side * rows_part, side * edge)
        )

    def gather_encoder(of_student, of_teacher):
        own = jnp.where(student_role, of_student, of_teacher)
        other = jnp.where(student_role, of_teacher, of_student)
        parts = [own]
        for r in range(1, nt):
            parts.append(routes.across(r, own if r < half else other))
        return routes.spread(jnp.stack(parts), None)

    attn_emb = gather_encoder(
        jnp.concatenate([square(mine, 0), emb_rows[0]], 1),
        jnp.concatenate([square(teach, 0), emb_rows[1]], 1),
    )
    attn_w = attn_emb[:, :, :width]
    emb_t = attn_emb[:, :, width:]
    up_w = gather_encoder(square(mine, 1), square(teach, 1))
    down_t = gather_encoder(square(mine, 2), square(teach, 2))
    pred_own = mine[teach_count:].transpose(1, 0, 2).reshape(rows_part, -1)
    pred_parts = [pred_own]
    for r in range(1, nt):
        pred_parts.append(routes.across(r, pred_own, to_role=1))
    pred_all = routes.spread(jnp.stack(pred_parts), 1)

    def pred_mat(number):
        return pred_all[:, :, number * edge : (number + 1) * edge]

    holder = routes.holders(d)
    inside = jnp.arange(rows_part, dtype=jnp.int32)
    feat = (
        jnp.arange(side, dtype=jnp.int32)[None, :, None] * edge
        + holder[:, None, None] * rows_part
        + inside[None, None, :]
    ).reshape(-1)
    feat_p = (holder[:, None] * rows_part + inside[None, :]).reshape(-1)
    one_hot = (feat[:, None] == jnp.arange(width)[None, :]).astype(f32)
    one_hot_p = (feat_p[:, None] == jnp.arange(narrow)[None, :]).astype(f32)

    def to_local(rows, hot):
        return jnp.einsum("nf,lf->nl", rows, hot, precision=exact, preferred_element_type=f32)

    def to_global(rows, hot):
        return jnp.einsum("nl,lf->nf", rows, hot, precision=exact, preferred_element_type=f32)

    vec = to_local(jnp.where(student_role, enc_vectors, teacher_vectors), one_hot)
    pvec = to_local(pred_vectors, one_hot_p)
    group_feat = (
        (z ^ jnp.arange(nt, dtype=jnp.int32))[:, None] * quarter
        + jnp.arange(quarter, dtype=jnp.int32)[None, :]
    ).reshape(-1)
    swap = (feat[:, None] == group_feat[None, :]).astype(bf16)

    part = z % half
    picked = jnp.take_along_axis(patches, ctx_idx[:, :, None], 1)

    def rows_for(target_z):
        where = (target_z % half) * share
        ctx_rows = lax.dynamic_slice_in_dim(picked, where, share, 0).reshape(-1, pix_part)
        all_rows = lax.dynamic_slice_in_dim(patches, where, share, 0).reshape(-1, pix_part)
        padded = jnp.pad(ctx_rows, ((0, all_rows.shape[0] - ctx_rows.shape[0]), (0, 0)))
        return jnp.where(target_z // half == 0, padded, all_rows)

    patch_rows = jnp.stack(
        [rows_for(z)] + [routes.across(r, rows_for(z ^ r)) for r in range(1, nt)]
    )
    my_ctx = lax.dynamic_slice_in_dim(ctx_idx, part * share, share, 0)
    my_tgt = lax.dynamic_slice_in_dim(tgt_idx, part * share, share, 0)
    full_rows = share * npatches
    ctx_rows = share * context_len
    ctx_places = jnp.pad(my_ctx.reshape(-1), (0, full_rows - ctx_rows))
    places = jnp.where(student_role, ctx_places, jnp.arange(full_rows) % npatches)
    table = to_local(sincos(jnp.arange(npatches), width), one_hot)
    table_p = to_local(sincos(jnp.arange(npatches), narrow), one_hot_p)
    count = full_rows // npatches
    span = jnp.arange(npatches) // context_len
    bias = jnp.where(student_role & (span[:, None] != span[None, :]), -1e30, 0.0).astype(f32)

    resid = dot32("rnp,rdp->nd", patch_rows, emb_t) + vec[6] + table[places]
    middle, kept_attn = attend_forward(resid, attn_w, vec[0], vec[1], HD, count, bias)
    output, kept_feed = feed_forward(middle, up_w, down_t, vec[2], vec[3])
    final = layer_norm(output, vec[4], vec[5])
    encoded = final[:ctx_rows].astype(bf16)
    target = layer_norm(final, 1.0, 0.0).astype(bf16).reshape(share, npatches, width)
    target = jnp.take_along_axis(target, my_tgt[:, :, None], 1).reshape(-1, width)
    target = jnp.dot(target, swap, preferred_element_type=f32)

    enc_feat = routes.across(half, encoded, from_role=0)
    enc_feat = jnp.dot(enc_feat, swap, preferred_element_type=f32).astype(bf16)
    enc_feat = enc_feat.reshape(ctx_rows, nt, quarter)
    inout = pred_mat(3 * players)
    in_w = inout[:, :, :quarter]
    out_w = inout[:, :, quarter:]
    projected = dot32("ntc,tpc->np", enc_feat, in_w).reshape(share, context_len, narrow)
    tokens = jnp.concatenate(
        [projected, jnp.broadcast_to(pvec[4 * players + 2], (share, target_len, narrow))], 1
    )
    tokens = (tokens + table_p[jnp.concatenate([my_ctx, my_tgt], 1)]).reshape(-1, narrow)
    zero = jnp.zeros((), f32)
    pred_kept = []
    for depth in range(players):
        mats = [pred_mat(3 * depth + i) for i in range(3)]
        rows = pvec[4 * depth : 4 * depth + 4]
        mid, kept_a = attend_forward(tokens, mats[0], rows[0], rows[1], PHD, share, zero)
        out, kept_f = feed_forward(mid, mats[1], mats[2], rows[2], rows[3])
        pred_kept.append((tokens, kept_a, mid, kept_f))
        tokens = out
    gain_last, shift_last = pvec[4 * players], pvec[4 * players + 1]
    normed = layer_norm(tokens, gain_last, shift_last).astype(bf16)
    normed_tgt = normed.reshape(share, seq_len, narrow)[:, context_len:].reshape(-1, narrow)
    predicted = dot32("np,tpc->ntc", normed_tgt, out_w).reshape(-1, width)
    denominator = images * nd * target_len * width
    gap = predicted - target
    magnitude = jnp.abs(gap)
    loss_part = jnp.sum(jnp.where(magnitude < 1.0, 0.5 * gap * gap, magnitude - 0.5)) / denominator
    grad_pred = (jnp.clip(gap, -1.0, 1.0) / denominator).astype(bf16).reshape(-1, nt, quarter)
    grad_out_w = dot32("np,ntc->tpc", normed_tgt, grad_pred)
    grad_tgt = dot32("ntc,tpc->np", grad_pred, out_w).reshape(share, target_len, narrow)
    grad_last = jnp.pad(grad_tgt, ((0, 0), (context_len, 0), (0, 0))).reshape(-1, narrow)
    grad_tokens, gain_g, shift_g = norm_backward(grad_last, tokens, gain_last)
    pred_vec_grads = {4 * players: gain_g, 4 * players + 1: shift_g}
    pred_mat_grads = {}
    for depth in reversed(range(players)):
        mats = [pred_mat(3 * depth + i) for i in range(3)]
        rows = pvec[4 * depth : 4 * depth + 4]
        before, kept_a, mid, kept_f = pred_kept[depth]
        grad_tokens, up_g, down_g, gain_two, shift_two = feed_backward(
            grad_tokens, mid, mats[1], mats[2], rows[2], kept_f
        )
        grad_tokens, attn_g, gain_one, shift_one = attend_backward(
            grad_tokens, before, mats[0], rows[0], kept_a, PHD, share
        )
        for i, value in enumerate([attn_g, up_g, down_g]):
            pred_mat_grads[3 * depth + i] = value
        for i, value in enumerate([gain_one, shift_one, gain_two, shift_two]):
            pred_vec_grads[4 * depth + i] = value
    grad_seq = grad_tokens.reshape(share, seq_len, narrow)
    pred_vec_grads[4 * players + 2] = jnp.sum(grad_seq[:, context_len:], (0, 1))
    grad_proj = grad_seq[:, :context_len].reshape(-1, narrow).astype(bf16)
    grad_in_w = dot32("np,ntc->tpc", grad_proj, enc_feat)
    pred_mat_grads[3 * players] = jnp.concatenate([grad_in_w, grad_out_w], 2)
    grad_enc = dot32("np,tpc->ntc", grad_proj, in_w).astype(bf16).reshape(-1, width)
    grad_enc = jnp.einsum("nf,lf->nl", grad_enc, swap, preferred_element_type=f32).astype(bf16)
    grad_enc = routes.across(half, grad_enc, from_role=1).astype(f32)
    pred_grads = jnp.concatenate([pred_mat_grads[i] for i in range(3 * players + 1)], 2)
    pred_sum = routes.reduce(pred_grads, 1, role == 1)

    def student_part(values, axis):
        return lax.slice_in_dim(values, 0, values.shape[axis] // count, axis=axis)

    grad_resid, gain_g, shift_g = norm_backward(grad_enc, output[:ctx_rows], vec[4])
    enc_vec_grads = {4: gain_g, 5: shift_g}
    grad_resid, up_g, down_g, gain_two, shift_two = feed_backward(
        grad_resid,
        middle[:ctx_rows],
        up_w,
        down_t,
        vec[2],
        (kept_feed[0][:ctx_rows], student_part(kept_feed[1], 1)),
    )
    kept = (kept_attn[0][:ctx_rows],) + tuple(student_part(v, 1) for v in kept_attn[1:])
    grad_resid, attn_g, gain_one, shift_one = attend_backward(
        grad_resid, resid[:ctx_rows], attn_w, vec[0], kept, HD, 1
    )
    for i, value in enumerate([gain_one, shift_one, gain_two, shift_two]):
        enc_vec_grads[i] = value
    enc_vec_grads[6] = jnp.sum(grad_resid, 0)
    emb_g = dot32("nd,rnp->rdp", grad_resid.astype(bf16), patch_rows[:, :ctx_rows])
    down_sum = routes.reduce(down_g, 0, student_role)
    up_sum = routes.reduce(up_g, 0, student_role)
    attn_emb_sum = routes.reduce(jnp.concatenate([attn_g, emb_g], 2), 0, student_role)
    attn_sum, emb_sum = attn_emb_sum[:, :width], attn_emb_sum[:, width:]

    enc_rows = to_global(jnp.stack([enc_vec_grads[i] for i in range(7)]), one_hot)
    pred_rows = to_global(
        jnp.stack([pred_vec_grads[i] for i in range(4 * players + 3)]), one_hot_p
    )
    enc_rows = jnp.where(student_role, enc_rows, 0.0)
    pred_rows = jnp.where(role == 1, pred_rows, 0.0)
    loss_row = jnp.where(role == 1, loss_part, 0.0)
    packed = jnp.concatenate([enc_rows.reshape(-1), pred_rows.reshape(-1), loss_row[None]])
    packed = jnp.pad(packed, (0, -packed.shape[0] % 1024)).reshape(-1, 128)
    packed = routes.total(packed).reshape(-1)
    enc_total = packed[: enc_rows.size].reshape(enc_rows.shape)
    pred_total = packed[enc_rows.size : enc_rows.size + pred_rows.size].reshape(pred_rows.shape)
    loss_total = packed[enc_rows.size + pred_rows.size]

    def unsquare(rows):
        return (
            rows.reshape(side, rows_part, side, edge)
            .transpose(0, 2, 1, 3)
            .reshape(per_mat, rows_part, edge)
        )

    by_block = jnp.concatenate(
        [
            unsquare(attn_sum),
            unsquare(up_sum),
            unsquare(down_sum),
            pred_sum.reshape(rows_part, -1, edge).transpose(1, 0, 2),
            jnp.zeros((1, rows_part, edge), f32),
        ],
        0,
    ).astype(bf16)
    slot_of = (
        jnp.full((slot_count,), block_count, jnp.int32)
        .at[owner]
        .set(jnp.arange(block_count, dtype=jnp.int32))
    )
    slot_rows = by_block[slot_of].reshape(nd, slots, rows_part, edge)
    slot_rows = lax.all_to_all(slot_rows, "dp", split_axis=0, concat_axis=1, tiled=False)
    low_grads = slot_rows.reshape(slots, edge, edge)
    slot_grads = low_grads.astype(f32)[None]

    emb_halves = emb_sum.reshape(side, chunk, pix_part)
    send_first = lax.dynamic_index_in_dim(emb_halves, odd, 0, keepdims=False)
    send_second = lax.dynamic_index_in_dim(emb_halves, 1 - odd, 0, keepdims=False)
    back_first = lax.ppermute(send_first, "dp", swap_pairs(False, True))
    back_second = lax.ppermute(send_second, "dp", swap_pairs(True, True))
    embed_grad = jnp.concatenate(
        [
            jnp.where(high == 0, back_first, back_second),
            jnp.where(high == 0, back_second, back_first),
        ],
        0,
    ).T

    new_left = 0.95 * stats_left + 0.05 * dot32("sij,skj->sik", low_grads, low_grads)[None]
    new_right = 0.95 * stats_right + 0.05 * dot32("sji,sjk->sik", low_grads, low_grads)[None]
    left_side = jnp.einsum(
        "tsij,tsjk->tsik", root_left, slot_grads, precision=exact, preferred_element_type=f32
    )
    direction = jnp.einsum(
        "tsij,tsjk->tsik", left_side, root_right, precision=exact, preferred_element_type=f32
    )
    direction = direction * lax.rsqrt(
        jnp.mean(direction * direction, axis=(2, 3), keepdims=True) + 1e-06
    )
    new_weights = weights - 0.05 * (direction + 0.05 * weights)
    new_teacher_blocks = 0.7 * teacher_slot_blocks + 0.3 * new_weights
    new_embed, new_embed_m, new_embed_v = adamw(embed, embed_m, embed_v, embed_grad, 0.05, 0.05)
    new_enc, new_enc_m, new_enc_v = adamw(enc_vectors, enc_m, enc_v, enc_total, 0.5, 0.0)
    new_pred, new_pred_m, new_pred_v = adamw(pred_vectors, pred_m, pred_v, pred_total, 0.5, 0.0)
    new_teacher_embed = 0.7 * teacher_embed + 0.3 * new_embed
    new_teacher_vectors = 0.7 * teacher_vectors + 0.3 * new_enc
    return (
        loss_total,
        slot_grads,
        new_weights,
        new_left,
        new_right,
        new_teacher_blocks,
        new_embed,
        new_embed_m,
        new_embed_v,
        new_teacher_embed,
        new_enc,
        new_enc_m,
        new_enc_v,
        new_pred,
        new_pred_m,
        new_pred_v,
        new_teacher_vectors,
    )


def solution(mesh):
    blocks = P("tensor", "dp", None, None)
    table = P("tensor", "dp")
    in_specs = (
        (P("dp", None, "tensor"), P("dp", None), P("dp", None), P())
        + (blocks,) * 6
        + (table,) * 4
        + (P(),) * 7
    )
    out_specs = (P(),) + (blocks,) * 5 + (table,) * 4 + (P(),) * 7
    return jax.shard_map(shards, mesh=mesh, in_specs=in_specs, out_specs=out_specs, check_vma=False)
```

```python
import functools
import math

import jax
import jax.numpy as jnp
from jax import lax
from jax.experimental import pallas as pl
from jax.experimental.pallas import tpu as pltpu
from jax.sharding import PartitionSpec as P

HD = 64
PHD = 32
SIDE = 16
STEP = 10
KERNEL_BYTES = 60 * 1024 * 1024

AXES = ("dp", "tensor")
exact = lax.Precision.HIGHEST
f32 = jnp.float32
bf16 = jnp.bfloat16
VMEM = pltpu.VMEM


def nn(first, second):
    return lax.dot_general(first, second, (((1,), (0,)), ((), ())), preferred_element_type=f32)


def nt_(first, second):
    return lax.dot_general(first, second, (((1,), (1,)), ((), ())), preferred_element_type=f32)


def tn(first, second):
    return lax.dot_general(first, second, (((0,), (0,)), ((), ())), preferred_element_type=f32)


def norm_parts(values):
    centre = values - jnp.mean(values, -1, keepdims=True)
    scale = lax.rsqrt(jnp.mean(centre * centre, -1, keepdims=True) + 1e-06)
    return centre * scale, scale


def layer_norm(values, gain_row, shift_row):
    return norm_parts(values)[0] * gain_row + shift_row


def norm_backward(grad, values, gain_row):
    unit, scale = norm_parts(values)
    weighted = grad * gain_row
    inner = (
        weighted
        - jnp.mean(weighted, -1, keepdims=True)
        - unit * jnp.mean(weighted * unit, -1, keepdims=True)
    )
    return (
        inner * scale,
        jnp.sum(grad * unit, 0, keepdims=True),
        jnp.sum(grad, 0, keepdims=True),
    )


def gelu_parts(values):
    below = 0.5 * (1.0 + lax.erf(values * math.sqrt(0.5)))
    density = jnp.exp(-0.5 * values * values) * (1.0 / math.sqrt(2.0 * math.pi))
    return values * below, below + values * density


def softened(queries, keys, head_size, allowed):
    scores = nt_(queries, keys) * (1.0 / math.sqrt(head_size))
    if allowed is not None:
        scores = jnp.where(allowed, scores, -1e30)
    expo = jnp.exp(scores - jnp.max(scores, -1, keepdims=True))
    return expo * (1.0 / jnp.sum(expo, -1, keepdims=True))


def attend(rows, head_size, length, allowed):
    columns = rows.shape[1] // 3
    images = []
    for at in range(0, rows.shape[0], length):
        outs = []
        for h in range(0, columns, head_size):
            q, k, v = (
                rows[at : at + length, j * columns + h : j * columns + h + head_size]
                for j in range(3)
            )
            soft = softened(q, k, head_size, allowed)
            outs.append(nn(soft.astype(bf16), v).astype(bf16))
        images.append(jnp.concatenate(outs, 1))
    return jnp.concatenate(images, 0) if len(images) > 1 else images[0]


def attend_back(rows, grad, head_size, length, allowed):
    columns = rows.shape[1] // 3
    factor = 1.0 / math.sqrt(head_size)
    images = []
    for at in range(0, rows.shape[0], length):
        outs = [[], [], []]
        for h in range(0, columns, head_size):
            q, k, v = (
                rows[at : at + length, j * columns + h : j * columns + h + head_size]
                for j in range(3)
            )
            g = grad[at : at + length, h : h + head_size]
            soft = softened(q, k, head_size, allowed)
            outs[2].append(tn(soft.astype(bf16), g).astype(bf16))
            ds = nt_(g, v)
            ds = (soft * (ds - jnp.sum(ds * soft, -1, keepdims=True))).astype(bf16)
            outs[0].append((nn(ds, k) * factor).astype(bf16))
            outs[1].append((tn(ds, q) * factor).astype(bf16))
        images.append(jnp.concatenate(outs[0] + outs[1] + outs[2], 1))
    return jnp.concatenate(images, 0) if len(images) > 1 else images[0]


def same_image(role, length, context):
    row = lax.broadcasted_iota(jnp.int32, (length, length), 0) // context
    column = lax.broadcasted_iota(jnp.int32, (length, length), 1) // context
    return (row == column) | (role != 0)


def encoder_attend_kernel(
    edge, unit, context, head_size, kept, role_ref, patch_ref, base_ref, emb_ref, w_ref, vec_ref,
    mid_ref, resid_ref, normed_ref, rows_ref, att_ref, x_ref, h_ref,
):
    step = pl.program_id(0)
    groups = pl.num_programs(0) // 2
    side = 2
    wide = side * edge
    pix = patch_ref.shape[2]
    columns = wide // 4

    @pl.when(step == 0)
    def _():
        x_ref[...] = base_ref[...]

    @pl.when(step < groups)
    def _():
        for r in range(side):
            x_ref[:, r * edge : (r + 1) * edge] += nt_(
                patch_ref[0], emb_ref[0, :, r * pix : (r + 1) * pix]
            )

    @pl.when(step == groups - 1)
    def _():
        values = x_ref[...]
        resid_ref[...] = values[:kept]
        low = layer_norm(values, vec_ref[0:1], vec_ref[1:2]).astype(bf16)
        h_ref[...] = low
        normed_ref[...] = low[:kept]

    @pl.when(step >= groups)
    def _():
        rows = sum(
            nn(h_ref[:, r * edge : (r + 1) * edge], w_ref[0, :, r * wide : r * wide + 3 * columns])
            for r in range(side)
        ).astype(bf16)
        rows_ref[0] = rows[:kept]
        att = attend(rows, head_size, unit, same_image(role_ref[0], unit, context))
        att_ref[0] = att[:kept]
        for r in range(side):
            x_ref[:, r * edge : (r + 1) * edge] += nt_(
                att, w_ref[0, :, r * wide + 3 * columns : (r + 1) * wide]
            )

    @pl.when(step == 2 * groups - 1)
    def _():
        mid_ref[...] = x_ref[...]


def encoder_feed_kernel(
    edge, kept, mid_ref, up_ref, down_ref, vec_ref, pick_ref, swap_ref,
    out_ref, normed_ref, hidden_ref, feat_ref, target_ref, x_ref, h_ref,
):
    step = pl.program_id(0)
    groups = pl.num_programs(0)
    side = 2
    wide = side * edge

    @pl.when(step == 0)
    def _():
        values = mid_ref[...]
        x_ref[...] = values
        low = layer_norm(values, vec_ref[2:3], vec_ref[3:4]).astype(bf16)
        h_ref[...] = low
        normed_ref[...] = low[:kept]

    hidden = sum(
        nn(h_ref[:, r * edge : (r + 1) * edge], up_ref[0, :, r * wide : (r + 1) * wide])
        for r in range(side)
    )
    hidden_ref[0] = hidden[:kept]
    active = gelu_parts(hidden)[0].astype(bf16)
    for r in range(side):
        x_ref[:, r * edge : (r + 1) * edge] += nt_(
            active, down_ref[0, :, r * wide : (r + 1) * wide]
        )

    @pl.when(step == groups - 1)
    def _():
        values = x_ref[...]
        out_ref[...] = values[:kept]
        final = layer_norm(values, vec_ref[4:5], vec_ref[5:6])
        encoded = final[:kept].astype(bf16)
        target = norm_parts(final)[0].astype(bf16)
        picked = nn(pick_ref[...], target).astype(bf16)
        for t in range(swap_ref.shape[0]):
            feat_ref[t] = nn(encoded, swap_ref[t]).astype(bf16)
            target_ref[t] = nn(picked, swap_ref[t]).astype(bf16)


def put_halves(keep_ref, send_ref, t, columns, value):
    middle = value.shape[0] // 2
    low = value.astype(bf16)
    keep_ref[t, :, columns] = low[:middle]
    send_ref[t, :, columns] = low[middle:]


def predictor_kernel(
    share, context, players, head_size, denominator,
    feat_ref, target_ref, base_ref, w_ref, vec_ref, swap_ref,
    keep_ref, send_ref, vec_grad_ref, loss_ref, back_ref,
    x_ref, mid_ref, h_ref, h2_ref, rows_ref, att_ref, hidden_ref, acc_ref, d_ref, low_ref, f_ref,
):
    groups = w_ref.shape[0]
    edge = w_ref.shape[1]
    length = base_ref.shape[0] // share
    quarter = feat_ref.shape[2]
    columns = edge // 4
    last = 3 * players * edge
    in_cols = slice(last, last + quarter)
    out_cols = slice(last + quarter, last + 2 * quarter)

    def span(number):
        return slice(number * edge, (number + 1) * edge)

    vec_grad_ref[...] = jnp.zeros_like(vec_grad_ref)

    projected = sum(nt_(feat_ref[t], w_ref[t, :, in_cols]) for t in range(groups))
    x_ref[0] = base_ref[...]
    for i in range(share):
        x_ref[0, i * length : i * length + context] += projected[i * context : (i + 1) * context]

    for j in range(players):
        values = x_ref[j]
        h_ref[j] = layer_norm(values, vec_ref[4 * j : 4 * j + 1], vec_ref[4 * j + 1 : 4 * j + 2]).astype(bf16)
        mid_ref[j] = values

        @pl.loop(0, groups)
        def _(t, j=j):
            rows = nn(h_ref[j], w_ref[t, :, 3 * j * edge : 3 * j * edge + 3 * columns]).astype(bf16)
            rows_ref[j, t] = rows
            att = attend(rows, head_size, length, None)
            att_ref[j, t] = att
            mid_ref[j] += nt_(att, w_ref[t, :, 3 * j * edge + 3 * columns : (3 * j + 1) * edge])

        values = mid_ref[j]
        h2_ref[j] = layer_norm(values, vec_ref[4 * j + 2 : 4 * j + 3], vec_ref[4 * j + 3 : 4 * j + 4]).astype(bf16)
        x_ref[j + 1] = values

        @pl.loop(0, groups)
        def _(t, j=j):
            hidden = nn(h2_ref[j], w_ref[t, :, span(3 * j + 1)])
            hidden_ref[j, t] = hidden
            x_ref[j + 1] += nt_(gelu_parts(hidden)[0].astype(bf16), w_ref[t, :, span(3 * j + 2)])

    final_gain = vec_ref[4 * players : 4 * players + 1]
    final = layer_norm(x_ref[players], final_gain, vec_ref[4 * players + 1 : 4 * players + 2]).astype(bf16)
    f_ref[...] = jnp.concatenate(
        [final[i * length + context : (i + 1) * length] for i in range(share)], 0
    )
    total = jnp.zeros((1, 1), f32)
    grad_f = jnp.zeros(f_ref.shape, f32)
    for t in range(groups):
        out_w = w_ref[t, :, out_cols]
        gap = nn(f_ref[...], out_w) - target_ref[t].astype(f32)
        size = jnp.abs(gap)
        terms = jnp.where(size < 1.0, 0.5 * gap * gap, size - 0.5)
        total += jnp.sum(jnp.sum(terms, 1, keepdims=True), 0, keepdims=True)
        grad_pred = (jnp.clip(gap, -1.0, 1.0) * (1.0 / denominator)).astype(bf16)
        put_halves(keep_ref, send_ref, t, out_cols, tn(f_ref[...], grad_pred))
        grad_f += nt_(grad_pred, out_w)
    loss_ref[...] = jnp.broadcast_to(total * (1.0 / denominator), loss_ref.shape)
    d_ref[...] = jnp.zeros_like(d_ref)
    tail = length - context
    for i in range(share):
        d_ref[i * length + context : (i + 1) * length] = grad_f[i * tail : (i + 1) * tail]
    grad, gain_g, shift_g = norm_backward(d_ref[...], x_ref[players], final_gain)
    d_ref[...] = grad
    vec_grad_ref[4 * players : 4 * players + 1] = gain_g
    vec_grad_ref[4 * players + 1 : 4 * players + 2] = shift_g

    for j in reversed(range(players)):
        low_ref[...] = d_ref[...].astype(bf16)
        acc_ref[...] = jnp.zeros_like(acc_ref)

        @pl.loop(0, groups)
        def _(t, j=j):
            active, slope = gelu_parts(hidden_ref[j, t])
            low = low_ref[...]
            put_halves(keep_ref, send_ref, t, span(3 * j + 2), tn(low, active.astype(bf16)))
            grad_hidden = (nn(low, w_ref[t, :, span(3 * j + 2)]) * slope).astype(bf16)
            put_halves(keep_ref, send_ref, t, span(3 * j + 1), tn(h2_ref[j], grad_hidden))
            acc_ref[...] += nt_(grad_hidden, w_ref[t, :, span(3 * j + 1)])

        grad, gain_g, shift_g = norm_backward(acc_ref[...], mid_ref[j], vec_ref[4 * j + 2 : 4 * j + 3])
        vec_grad_ref[4 * j + 2 : 4 * j + 3] = gain_g
        vec_grad_ref[4 * j + 3 : 4 * j + 4] = shift_g
        grad = d_ref[...] + grad
        d_ref[...] = grad
        low_ref[...] = grad.astype(bf16)
        acc_ref[...] = jnp.zeros_like(acc_ref)

        @pl.loop(0, groups)
        def _(t, j=j):
            low = low_ref[...]
            attn_w = w_ref[t, :, span(3 * j)]
            grad_att = nn(low, attn_w[:, 3 * columns :]).astype(bf16)
            grad_rows = attend_back(rows_ref[j, t], grad_att, head_size, length, None)
            grad_w = jnp.concatenate([tn(h_ref[j], grad_rows), tn(low, att_ref[j, t])], 1)
            put_halves(keep_ref, send_ref, t, span(3 * j), grad_w)
            acc_ref[...] += nt_(grad_rows, attn_w[:, : 3 * columns])

        grad, gain_g, shift_g = norm_backward(acc_ref[...], x_ref[j], vec_ref[4 * j : 4 * j + 1])
        vec_grad_ref[4 * j : 4 * j + 1] = gain_g
        vec_grad_ref[4 * j + 1 : 4 * j + 2] = shift_g
        d_ref[...] += grad

    mask_grad = jnp.zeros((1, edge), f32)
    for i in range(share):
        mask_grad += jnp.sum(d_ref[i * length + context : (i + 1) * length], 0, keepdims=True)
    vec_grad_ref[4 * players + 2 : 4 * players + 3] = mask_grad
    low = jnp.concatenate(
        [d_ref[i * length : i * length + context] for i in range(share)], 0
    ).astype(bf16)
    back = jnp.zeros((low.shape[0], swap_ref.shape[1]), f32)
    for t in range(groups):
        put_halves(keep_ref, send_ref, t, in_cols, tn(low, feat_ref[t]))
        back += nt_(nn(low, w_ref[t, :, in_cols]).astype(bf16), swap_ref[t])
    back_ref[...] = back.astype(bf16)


def encoder_feed_back_kernel(
    edge, back_ref, out_ref, mid_ref, normed_ref, hidden_ref, up_ref, down_ref, vec_ref,
    up_keep, up_send, down_keep, down_send, grad_ref, vec_grad_ref, d_ref, low_ref, acc_ref,
):
    step = pl.program_id(0)
    groups = pl.num_programs(0)
    wide = 2 * edge

    @pl.when(step == 0)
    def _():
        grad, gain_g, shift_g = norm_backward(back_ref[...].astype(f32), out_ref[...], vec_ref[4:5])
        d_ref[...] = grad
        low_ref[...] = grad.astype(bf16)
        acc_ref[...] = jnp.zeros_like(acc_ref)
        vec_grad_ref[...] = jnp.zeros_like(vec_grad_ref)
        vec_grad_ref[4:5] = gain_g
        vec_grad_ref[5:6] = shift_g

    active, slope = gelu_parts(hidden_ref[0])
    active = active.astype(bf16)
    grad_hidden = sum(
        nn(low_ref[:, r * edge : (r + 1) * edge], down_ref[0, :, r * wide : (r + 1) * wide])
        for r in range(2)
    )
    grad_hidden = (grad_hidden * slope).astype(bf16)
    for r in range(2):
        mine = slice(r * edge, (r + 1) * edge)
        columns = slice(r * wide, (r + 1) * wide)
        put_halves(down_keep, down_send, 0, columns, tn(low_ref[:, mine], active))
        put_halves(up_keep, up_send, 0, columns, tn(normed_ref[:, mine], grad_hidden))
        acc_ref[:, mine] += nt_(grad_hidden, up_ref[0, :, columns])

    @pl.when(step == groups - 1)
    def _():
        grad, gain_g, shift_g = norm_backward(acc_ref[...], mid_ref[...], vec_ref[2:3])
        grad_ref[...] = d_ref[...] + grad
        vec_grad_ref[2:3] = gain_g
        vec_grad_ref[3:4] = shift_g


def encoder_attend_back_kernel(
    edge, unit, context, head_size,
    role_ref, grad_ref, resid_ref, normed_ref, rows_ref, att_ref, w_ref, patch_ref, vec_ref,
    keep_ref, send_ref, vec_grad_ref, low_ref, acc_ref,
):
    step = pl.program_id(0)
    groups = pl.num_programs(0) // 2
    wide = 2 * edge
    columns = wide // 4
    pix = patch_ref.shape[2]

    @pl.when(step == 0)
    def _():
        low_ref[...] = grad_ref[...].astype(bf16)
        acc_ref[...] = jnp.zeros_like(acc_ref)

    @pl.when(step < groups)
    def _():
        grad_att = sum(
            nn(
                low_ref[:, r * edge : (r + 1) * edge],
                w_ref[0, :, r * wide + 3 * columns : (r + 1) * wide],
            )
            for r in range(2)
        ).astype(bf16)
        allowed = same_image(role_ref[0], unit, context)
        grad_rows = attend_back(rows_ref[0], grad_att, head_size, unit, allowed)
        for r in range(2):
            mine = slice(r * edge, (r + 1) * edge)
            grad_w = jnp.concatenate(
                [tn(normed_ref[:, mine], grad_rows), tn(low_ref[:, mine], att_ref[0])], 1
            )
            put_halves(keep_ref, send_ref, step, slice(r * wide, (r + 1) * wide), grad_w)
            acc_ref[:, mine] += nt_(grad_rows, w_ref[0, :, r * wide : r * wide + 3 * columns])

    @pl.when(step == groups - 1)
    def _():
        grad, gain_g, shift_g = norm_backward(acc_ref[...], resid_ref[...], vec_ref[0:1])
        grad = grad_ref[...] + grad
        low_ref[...] = grad.astype(bf16)
        vec_grad_ref[...] = jnp.zeros_like(vec_grad_ref)
        vec_grad_ref[0:1] = gain_g
        vec_grad_ref[1:2] = shift_g
        vec_grad_ref[6:7] = jnp.sum(grad, 0, keepdims=True)

    @pl.when(step >= groups)
    def _():
        grad_w = jnp.concatenate(
            [tn(low_ref[:, r * edge : (r + 1) * edge], patch_ref[0]) for r in range(2)], 1
        )
        put_halves(keep_ref, send_ref, step - groups, slice(2 * wide, 2 * wide + 2 * pix), grad_w)


def split(values):
    high = values.astype(bf16)
    return high, (values - high.astype(f32)).astype(bf16)


def shampoo_kernel(
    grad_ref, weight_ref, left_ref, right_ref, root_left_ref, root_right_ref, teacher_ref,
    grad_out, weight_out, left_out, right_out, teacher_out,
):
    low = grad_ref[0]
    grad_out[0, 0] = low.astype(f32)
    left_out[0, 0] = 0.95 * left_ref[0, 0] + 0.05 * nt_(low, low)
    right_out[0, 0] = 0.95 * right_ref[0, 0] + 0.05 * tn(low, low)
    high, rest = split(root_left_ref[0, 0])
    side = nn(high, low) + nn(rest, low)
    high, rest = split(side)
    root_high, root_rest = split(root_right_ref[0, 0])
    step = nn(high, root_high) + nn(high, root_rest) + nn(rest, root_high)
    mean = jnp.mean(jnp.mean(step * step, 1, keepdims=True), 0, keepdims=True)
    step = step * lax.rsqrt(mean + 1e-06)
    weight = weight_ref[0, 0]
    new = weight - 0.05 * (step + 0.05 * weight)
    weight_out[0, 0] = new
    teacher_out[0, 0] = 0.7 * teacher_ref[0, 0] + 0.3 * new


def whole(shape):
    return pl.BlockSpec(shape, lambda *_: (0,) * len(shape))


def by_group(shape):
    return pl.BlockSpec((1,) + shape, lambda t: (t, 0, 0))


def compiled():
    return pltpu.CompilerParams(
        dimension_semantics=("arbitrary",), vmem_limit_bytes=KERNEL_BYTES
    )


def cost(flops, moved):
    return pl.CostEstimate(flops=int(flops), bytes_accessed=int(moved), transcendentals=0)


def sincos(cell_index, columns):
    quarter = columns // 4
    frequency = 1.0 / 10000.0 ** (jnp.arange(quarter).astype(f32) / quarter)
    col_angle = (cell_index % SIDE).astype(f32)[..., None] * frequency
    row_angle = (cell_index // SIDE).astype(f32)[..., None] * frequency
    return jnp.concatenate(
        [jnp.sin(col_angle), jnp.cos(col_angle), jnp.sin(row_angle), jnp.cos(row_angle)], -1
    )


def adamw(master, moment, second, gradient, step_rate, weight_decay):
    moment = 0.9 * moment + 0.1 * gradient
    second = 0.999 * second + 0.001 * gradient * gradient
    unbiased_first = moment / (1.0 - 0.9**STEP)
    unbiased_second = second / (1.0 - 0.999**STEP)
    return (
        master
        - step_rate
        * (unbiased_first / (jnp.sqrt(unbiased_second) + 1e-08) + weight_decay * master),
        moment,
        second,
    )


class Routes:
    def __init__(self, nd, nt):
        self.nd, self.nt, self.half = nd, nt, nt // 2
        self.low_bits = [1 << s for s in range(1, nd.bit_length() - 1)]
        self.stages = len(self.low_bits)

    def order(self, core):
        return self.low_bits if core == 0 else self.low_bits[::-1]

    def pairs(self, target, keep):
        found = []
        for d in range(self.nd):
            for z in range(self.nt):
                if keep(d, z):
                    d2, z2 = target(d, z)
                    found.append((d * self.nt + z, d2 * self.nt + z2))
        return found

    def stage(self, number, values, role):
        def target(d, z):
            if number == self.stages:
                return d ^ 1, z
            return d ^ self.order(d & 1)[number], z

        return lax.ppermute(
            values,
            AXES,
            self.pairs(target, lambda d, z: role is None or z // self.half == role),
        )

    def across(self, r, values, from_role=None, to_role=None):
        def keep(d, z):
            return (from_role is None or z // self.half == from_role) and (
                to_role is None or (z ^ r) // self.half == to_role
            )

        return lax.ppermute(values, AXES, self.pairs(lambda d, z: (d, z ^ r), keep))

    def holders(self, d):
        place = jnp.arange(self.nd, dtype=jnp.int32)
        held = d ^ (place >> self.stages)
        core = held & 1
        for s in range(self.stages):
            bit = (place >> s) & 1
            held = held ^ (bit * jnp.where(core == 0, self.order(0)[s], self.order(1)[s]))
        return held

    def spread(self, stack, role):
        for number in range(self.stages + 1):
            stack = jnp.concatenate([stack, self.stage(number, stack, role)], 1)
        return stack

    def reduce(self, keep, send, role, is_role):
        for number in reversed(range(self.stages + 1)):
            got = self.stage(number, send, role)
            keep = (keep.astype(f32) + got.astype(f32)).astype(bf16)
            if number:
                middle = keep.shape[1] // 2
                keep, send = keep[:, :middle], keep[:, middle:]
        total = jnp.where(is_role, keep[0].astype(f32), 0.0)
        for r in range(1, self.nt):
            total = total + self.across(r, keep[r], from_role=role).astype(f32)
        return total

    def total(self, values):
        for bit in [1] + self.low_bits:
            values = values + lax.ppermute(
                values, AXES, self.pairs(lambda d, z, b=bit: (d ^ b, z), lambda d, z: True)
            )
        r = 1
        while r < self.nt:
            values = values + self.across(r, values)
            r *= 2
        return values


def shards(
    patches,
    ctx_idx,
    tgt_idx,
    owner,
    weights,
    stats_left,
    stats_right,
    root_left,
    root_right,
    teacher_slot_blocks,
    embed,
    embed_m,
    embed_v,
    teacher_embed,
    enc_vectors,
    enc_m,
    enc_v,
    pred_vectors,
    pred_m,
    pred_v,
    teacher_vectors,
):
    nt = lax.axis_size("tensor")
    nd = lax.axis_size("dp")
    routes = Routes(nd, nt)
    half = nt // 2
    d = lax.axis_index("dp")
    z = lax.axis_index("tensor")
    role = z // half
    student_role = role == 0
    images, npatches, pix_part = patches.shape
    slots = weights.shape[1]
    edge = weights.shape[-1]
    slot_count = slots * nd
    block_count = owner.shape[0]
    width = enc_vectors.shape[1]
    narrow = pred_vectors.shape[1]
    players = (pred_vectors.shape[0] - 3) // 4
    side = width // edge
    teach_count = 3 * side * side
    quarter = width // nt
    context_len = ctx_idx.shape[1]
    target_len = tgt_idx.shape[1]
    seq_len = context_len + target_len
    share = images // half
    rows_part = edge // nd

    both = jnp.stack([weights[0], teacher_slot_blocks[0]]).astype(bf16)
    both = both.reshape(2, slots, nd, rows_part, edge)
    both = lax.all_to_all(both, "dp", split_axis=2, concat_axis=0, tiled=False)
    by_slot = both.transpose(1, 0, 2, 3, 4).reshape(2, slot_count, rows_part, edge)
    mine = by_slot[0][owner].transpose(1, 0, 2).reshape(rows_part, -1)
    teach = by_slot[1][owner[:teach_count]].transpose(1, 0, 2).reshape(rows_part, -1)

    chunk = rows_part
    wide_t = jnp.stack([embed, teacher_embed]).astype(bf16).transpose(0, 2, 1)
    high = d // (nd // 2)
    first = lax.dynamic_slice_in_dim(wide_t, high * chunk, chunk, 1)
    second = lax.dynamic_slice_in_dim(wide_t, (1 - high) * chunk, chunk, 1)

    def swap_pairs(flip, inverse):
        found = []
        for a in range(nd):
            h = a // (nd // 2)
            b = 2 * (a % (nd // 2)) + (h if not flip else 1 - h)
            found.append((b, a) if inverse else (a, b))
        return found

    got_first = lax.ppermute(first, "dp", swap_pairs(False, False))
    got_second = lax.ppermute(second, "dp", swap_pairs(True, False))
    odd = d % 2
    emb_rows = jnp.concatenate(
        [
            jnp.where(odd == 0, got_first, got_second),
            jnp.where(odd == 0, got_second, got_first),
        ],
        2,
    )

    def gather_encoder(of_student, of_teacher):
        own = jnp.where(student_role, of_student, of_teacher)
        other = jnp.where(student_role, of_teacher, of_student)
        parts = [own]
        for r in range(1, nt):
            parts.append(routes.across(r, own if r < half else other))
        return routes.spread(jnp.stack(parts), None)

    mat = side * width
    attn_emb = gather_encoder(
        jnp.concatenate([mine[:, :mat], emb_rows[0]], 1),
        jnp.concatenate([teach[:, :mat], emb_rows[1]], 1),
    )
    up_w = gather_encoder(mine[:, mat : 2 * mat], teach[:, mat : 2 * mat])
    down_t = gather_encoder(mine[:, 2 * mat : 3 * mat], teach[:, 2 * mat :])
    pred_own = mine[:, 3 * mat :]
    pred_parts = [pred_own]
    for r in range(1, nt):
        pred_parts.append(routes.across(r, pred_own, to_role=1))
    pred_all = routes.spread(jnp.stack(pred_parts), 1)

    holder = routes.holders(d)
    inside = jnp.arange(rows_part, dtype=jnp.int32)
    feat_p = (holder[:, None] * rows_part + inside[None, :]).reshape(-1)
    feat = jnp.concatenate([r * edge + feat_p for r in range(side)])
    one_hot = (feat[:, None] == jnp.arange(width)[None, :]).astype(f32)
    one_hot_p = (feat_p[:, None] == jnp.arange(narrow)[None, :]).astype(f32)

    def to_local(rows, hot):
        return jnp.einsum("nf,lf->nl", rows, hot, precision=exact, preferred_element_type=f32)

    def to_global(rows, hot):
        return jnp.einsum("nl,lf->nf", rows, hot, precision=exact, preferred_element_type=f32)

    vec = to_local(jnp.where(student_role, enc_vectors, teacher_vectors), one_hot)
    vec = jnp.pad(vec, ((0, 1), (0, 0)))
    pvec = to_local(pred_vectors, one_hot_p)
    pvec = jnp.pad(pvec, ((0, 16 - pvec.shape[0]), (0, 0)))
    pred_z = half + z % half
    group_feat = (pred_z ^ jnp.arange(nt, dtype=jnp.int32))[:, None] * quarter + jnp.arange(
        quarter, dtype=jnp.int32
    )
    swap = (feat[None, :, None] == group_feat[:, None, :]).astype(bf16)

    part = z % half
    picked = jnp.take_along_axis(patches, ctx_idx[:, :, None], 1)

    def rows_for(target_z):
        where = (target_z % half) * share
        ctx_rows = lax.dynamic_slice_in_dim(picked, where, share, 0).reshape(-1, pix_part)
        all_rows = lax.dynamic_slice_in_dim(patches, where, share, 0).reshape(-1, pix_part)
        padded = jnp.pad(ctx_rows, ((0, all_rows.shape[0] - ctx_rows.shape[0]), (0, 0)))
        return jnp.where(target_z // half == 0, padded, all_rows)

    patch_rows = jnp.stack(
        [rows_for(z)] + [routes.across(r, rows_for(z ^ r)) for r in range(1, nt)]
    )
    my_ctx = lax.dynamic_slice_in_dim(ctx_idx, part * share, share, 0)
    my_tgt = lax.dynamic_slice_in_dim(tgt_idx, part * share, share, 0)
    full_rows = share * npatches
    ctx_rows = share * context_len
    tgt_rows = share * target_len
    ctx_places = jnp.pad(my_ctx.reshape(-1), (0, full_rows - ctx_rows))
    places = jnp.where(student_role, ctx_places, jnp.arange(full_rows) % npatches)
    table = to_local(sincos(jnp.arange(npatches), width), one_hot)
    table_p = to_local(sincos(jnp.arange(npatches), narrow), one_hot_p)
    base = table[places] + vec[6]
    tgt_places = (my_tgt + npatches * jnp.arange(share, dtype=jnp.int32)[:, None]).reshape(-1)
    pick = (tgt_places[:, None] == jnp.arange(full_rows)[None, :]).astype(bf16)
    role_word = role.astype(jnp.int32).reshape(1)

    attn_cols = side * width
    columns = width // nt
    resid, normed_a, rows_a, att_a, middle = [None] * 5
    middle, resid, normed_a, rows_a, att_a = pl.pallas_call(
        functools.partial(encoder_attend_kernel, edge, npatches, context_len, HD, ctx_rows),
        grid=(2 * nt,),
        in_specs=[
            pl.BlockSpec(memory_space=pltpu.SMEM),
            pl.BlockSpec((1, full_rows, pix_part), lambda i: (jnp.minimum(i, nt - 1), 0, 0)),
            whole((full_rows, width)),
            pl.BlockSpec(
                (1, edge, side * pix_part),
                lambda i: (jnp.minimum(i, nt - 1), 0, attn_cols // (side * pix_part)),
            ),
            pl.BlockSpec((1, edge, attn_cols), lambda i: (jnp.maximum(i - nt, 0), 0, 0)),
            whole((8, width)),
        ],
        out_specs=[
            whole((full_rows, width)),
            whole((ctx_rows, width)),
            whole((ctx_rows, width)),
            pl.BlockSpec((1, ctx_rows, 3 * columns), lambda i: (jnp.maximum(i - nt, 0), 0, 0)),
            pl.BlockSpec((1, ctx_rows, columns), lambda i: (jnp.maximum(i - nt, 0), 0, 0)),
        ],
        out_shape=[
            jax.ShapeDtypeStruct((full_rows, width), f32),
            jax.ShapeDtypeStruct((ctx_rows, width), f32),
            jax.ShapeDtypeStruct((ctx_rows, width), bf16),
            jax.ShapeDtypeStruct((nt, ctx_rows, 3 * columns), bf16),
            jax.ShapeDtypeStruct((nt, ctx_rows, columns), bf16),
        ],
        scratch_shapes=[VMEM((full_rows, width), f32), VMEM((full_rows, width), bf16)],
        compiler_params=compiled(),
        cost_estimate=cost(6e9, 12e6),
        name="encoder_attend",
    )(role_word, patch_rows, base, attn_emb, attn_emb, vec)
    output, normed_f, hidden, enc_feat, target = pl.pallas_call(
        functools.partial(encoder_feed_kernel, edge, ctx_rows),
        grid=(nt,),
        in_specs=[
            whole((full_rows, width)),
            by_group((edge, mat)),
            by_group((edge, mat)),
            whole((8, width)),
            whole((tgt_rows, full_rows)),
            whole((nt, width, quarter)),
        ],
        out_specs=[
            whole((ctx_rows, width)),
            whole((ctx_rows, width)),
            by_group((ctx_rows, width)),
            whole((nt, ctx_rows, quarter)),
            whole((nt, tgt_rows, quarter)),
        ],
        out_shape=[
            jax.ShapeDtypeStruct((ctx_rows, width), f32),
            jax.ShapeDtypeStruct((ctx_rows, width), bf16),
            jax.ShapeDtypeStruct((nt, ctx_rows, width), f32),
            jax.ShapeDtypeStruct((nt, ctx_rows, quarter), bf16),
            jax.ShapeDtypeStruct((nt, tgt_rows, quarter), bf16),
        ],
        scratch_shapes=[VMEM((full_rows, width), f32), VMEM((full_rows, width), bf16)],
        compiler_params=compiled(),
        cost_estimate=cost(8e9, 14e6),
        name="encoder_feed",
    )(middle, up_w, down_t, vec, pick, swap)

    feat_in = routes.across(half, enc_feat, from_role=0)
    tokens_at = table_p[jnp.concatenate([my_ctx, my_tgt], 1)]
    mask_rows = jnp.arange(seq_len)[None, :, None] >= context_len
    tokens_at = jnp.where(mask_rows, tokens_at + pvec[4 * players + 2], tokens_at)
    tokens_at = tokens_at.reshape(-1, narrow)
    token_rows = share * seq_len
    pred_cols = (3 * players + 1) * edge
    denominator = images * nd * target_len * width
    pred_columns = narrow // nt
    in_vmem = pl.BlockSpec(memory_space=VMEM)
    pred_keep, pred_send, pred_vec_g, loss_tile, back = pl.pallas_call(
        functools.partial(predictor_kernel, share, context_len, players, PHD, denominator),
        in_specs=[in_vmem] * 6,
        out_specs=[in_vmem] * 5,
        out_shape=[
            jax.ShapeDtypeStruct((nt, edge // 2, pred_cols), bf16),
            jax.ShapeDtypeStruct((nt, edge // 2, pred_cols), bf16),
            jax.ShapeDtypeStruct((16, narrow), f32),
            jax.ShapeDtypeStruct((8, 128), f32),
            jax.ShapeDtypeStruct((ctx_rows, width), bf16),
        ],
        scratch_shapes=[
            VMEM((players + 1, token_rows, narrow), f32),
            VMEM((players, token_rows, narrow), f32),
            VMEM((players, token_rows, narrow), bf16),
            VMEM((players, token_rows, narrow), bf16),
            VMEM((players, nt, token_rows, 3 * pred_columns), bf16),
            VMEM((players, nt, token_rows, pred_columns), bf16),
            VMEM((players, nt, token_rows, edge), f32),
            VMEM((token_rows, narrow), f32),
            VMEM((token_rows, narrow), f32),
            VMEM((token_rows, narrow), bf16),
            VMEM((tgt_rows, narrow), bf16),
        ],
        compiler_params=pltpu.CompilerParams(vmem_limit_bytes=KERNEL_BYTES),
        cost_estimate=cost(16e9, 30e6),
        name="predictor",
    )(feat_in, target, tokens_at, pred_all, pvec, swap)
    back = routes.across(half, back, from_role=1)

    half_shape = jax.ShapeDtypeStruct((nt, edge // 2, mat), bf16)
    up_keep, up_send, down_keep, down_send, grad_mid, vec_g1 = pl.pallas_call(
        functools.partial(encoder_feed_back_kernel, edge),
        grid=(nt,),
        in_specs=[
            whole((ctx_rows, width)),
            whole((ctx_rows, width)),
            whole((ctx_rows, width)),
            whole((ctx_rows, width)),
            by_group((ctx_rows, width)),
            by_group((edge, mat)),
            by_group((edge, mat)),
            whole((8, width)),
        ],
        out_specs=[by_group((edge // 2, mat))] * 4 + [whole((ctx_rows, width)), whole((8, width))],
        out_shape=[half_shape] * 4
        + [
            jax.ShapeDtypeStruct((ctx_rows, width), f32),
            jax.ShapeDtypeStruct((8, width), f32),
        ],
        scratch_shapes=[
            VMEM((ctx_rows, width), f32),
            VMEM((ctx_rows, width), bf16),
            VMEM((ctx_rows, width), f32),
        ],
        compiler_params=compiled(),
        cost_estimate=cost(8e9, 25e6),
        name="encoder_feed_back",
    )(back, output, middle, normed_f, hidden, up_w, down_t, vec)
    all_cols = attn_cols + side * pix_part
    attn_keep, attn_send, vec_g2 = pl.pallas_call(
        functools.partial(encoder_attend_back_kernel, edge, npatches, context_len, HD),
        grid=(2 * nt,),
        in_specs=[
            pl.BlockSpec(memory_space=pltpu.SMEM),
            whole((ctx_rows, width)),
            whole((ctx_rows, width)),
            whole((ctx_rows, width)),
            pl.BlockSpec((1, ctx_rows, 3 * columns), lambda i: (jnp.minimum(i, nt - 1), 0, 0)),
            pl.BlockSpec((1, ctx_rows, columns), lambda i: (jnp.minimum(i, nt - 1), 0, 0)),
            pl.BlockSpec((1, edge, attn_cols), lambda i: (jnp.minimum(i, nt - 1), 0, 0)),
            pl.BlockSpec((1, ctx_rows, pix_part), lambda i: (jnp.maximum(i - nt, 0), 0, 0)),
            whole((8, width)),
        ],
        out_specs=[
            whole((nt, edge // 2, all_cols)),
            whole((nt, edge // 2, all_cols)),
            whole((8, width)),
        ],
        out_shape=[
            jax.ShapeDtypeStruct((nt, edge // 2, all_cols), bf16),
            jax.ShapeDtypeStruct((nt, edge // 2, all_cols), bf16),
            jax.ShapeDtypeStruct((8, width), f32),
        ],
        scratch_shapes=[VMEM((ctx_rows, width), bf16), VMEM((ctx_rows, width), f32)],
        compiler_params=compiled(),
        cost_estimate=cost(6e9, 20e6),
        name="encoder_attend_back",
    )(role_word, grad_mid, resid, normed_a, rows_a, att_a, attn_emb, patch_rows, vec)

    pred_sum = routes.reduce(pred_keep, pred_send, 1, role == 1)
    down_sum = routes.reduce(down_keep, down_send, 0, student_role)
    up_sum = routes.reduce(up_keep, up_send, 0, student_role)
    attn_emb_sum = routes.reduce(attn_keep, attn_send, 0, student_role)

    enc_rows = to_global(vec_g1[:7] + vec_g2[:7], one_hot)
    pred_rows = to_global(pred_vec_g[: 4 * players + 3], one_hot_p)
    enc_rows = jnp.where(student_role, enc_rows, 0.0)
    pred_rows = jnp.where(role == 1, pred_rows, 0.0)
    loss_row = jnp.where(role == 1, loss_tile[0, 0], 0.0)
    packed = jnp.concatenate([enc_rows.reshape(-1), pred_rows.reshape(-1), loss_row[None]])
    packed = jnp.pad(packed, (0, -packed.shape[0] % 1024)).reshape(-1, 128)
    packed = routes.total(packed).reshape(-1)
    enc_total = packed[: enc_rows.size].reshape(enc_rows.shape)
    pred_total = packed[enc_rows.size : enc_rows.size + pred_rows.size].reshape(pred_rows.shape)
    loss_total = packed[enc_rows.size + pred_rows.size]

    by_block = jnp.concatenate(
        [
            attn_emb_sum[:, :mat],
            up_sum,
            down_sum,
            pred_sum,
            jnp.zeros((rows_part, edge), f32),
        ],
        1,
    ).astype(bf16)
    by_block = by_block.reshape(rows_part, block_count + 1, edge).transpose(1, 0, 2)
    slot_of = (
        jnp.full((slot_count,), block_count, jnp.int32)
        .at[owner]
        .set(jnp.arange(block_count, dtype=jnp.int32))
    )
    slot_rows = by_block[slot_of].reshape(nd, slots, rows_part, edge)
    slot_rows = lax.all_to_all(slot_rows, "dp", split_axis=0, concat_axis=1, tiled=False)
    low_grads = slot_rows.reshape(slots, edge, edge)

    emb_sum = attn_emb_sum[:, mat:]
    emb_halves = jnp.stack([emb_sum[:, :pix_part], emb_sum[:, pix_part:]])
    send_first = lax.dynamic_index_in_dim(emb_halves, odd, 0, keepdims=False)
    send_second = lax.dynamic_index_in_dim(emb_halves, 1 - odd, 0, keepdims=False)
    back_first = lax.ppermute(send_first, "dp", swap_pairs(False, True))
    back_second = lax.ppermute(send_second, "dp", swap_pairs(True, True))
    embed_grad = jnp.concatenate(
        [
            jnp.where(high == 0, back_first, back_second),
            jnp.where(high == 0, back_second, back_first),
        ],
        0,
    ).T

    slot_spec = pl.BlockSpec((1, 1, edge, edge), lambda s: (0, s, 0, 0))
    slot_shape = jax.ShapeDtypeStruct(weights.shape, f32)
    slot_grads, new_weights, new_left, new_right, new_teacher_blocks = pl.pallas_call(
        shampoo_kernel,
        grid=(slots,),
        in_specs=[pl.BlockSpec((1, edge, edge), lambda s: (s, 0, 0))] + [slot_spec] * 6,
        out_specs=[slot_spec] * 5,
        out_shape=[slot_shape] * 5,
        compiler_params=compiled(),
        cost_estimate=cost(3e9, 22e6),
        name="shampoo",
    )(low_grads, weights, stats_left, stats_right, root_left, root_right, teacher_slot_blocks)
    new_embed, new_embed_m, new_embed_v = adamw(embed, embed_m, embed_v, embed_grad, 0.05, 0.05)
    new_enc, new_enc_m, new_enc_v = adamw(enc_vectors, enc_m, enc_v, enc_total, 0.5, 0.0)
    new_pred, new_pred_m, new_pred_v = adamw(pred_vectors, pred_m, pred_v, pred_total, 0.5, 0.0)
    new_teacher_embed = 0.7 * teacher_embed + 0.3 * new_embed
    new_teacher_vectors = 0.7 * teacher_vectors + 0.3 * new_enc
    return (
        loss_total,
        slot_grads,
        new_weights,
        new_left,
        new_right,
        new_teacher_blocks,
        new_embed,
        new_embed_m,
        new_embed_v,
        new_teacher_embed,
        new_enc,
        new_enc_m,
        new_enc_v,
        new_pred,
        new_pred_m,
        new_pred_v,
        new_teacher_vectors,
    )


def solution(mesh):
    blocks = P("tensor", "dp", None, None)
    table = P("tensor", "dp")
    in_specs = (
        (P("dp", None, "tensor"), P("dp", None), P("dp", None), P())
        + (blocks,) * 6
        + (table,) * 4
        + (P(),) * 7
    )
    out_specs = (P(),) + (blocks,) * 5 + (table,) * 4 + (P(),) * 7
    return jax.shard_map(shards, mesh=mesh, in_specs=in_specs, out_specs=out_specs, check_vma=False)
```

```python
import functools
import math

import jax
import jax.numpy as jnp
from jax import lax
from jax.experimental import pallas as pl
from jax.experimental.pallas import tpu as pltpu
from jax.sharding import PartitionSpec as P

HD = 64
PHD = 32
SIDE = 16
STEP = 10
KERNEL_BYTES = 60 * 1024 * 1024

AXES = ("dp", "tensor")
exact = lax.Precision.HIGHEST
f32 = jnp.float32
bf16 = jnp.bfloat16
VMEM = pltpu.VMEM


def nn(first, second):
    return lax.dot_general(first, second, (((1,), (0,)), ((), ())), preferred_element_type=f32)


def nt_(first, second):
    return lax.dot_general(first, second, (((1,), (1,)), ((), ())), preferred_element_type=f32)


def tn(first, second):
    return lax.dot_general(first, second, (((0,), (0,)), ((), ())), preferred_element_type=f32)


def norm_parts(values):
    centre = values - jnp.mean(values, -1, keepdims=True)
    scale = lax.rsqrt(jnp.mean(centre * centre, -1, keepdims=True) + 1e-06)
    return centre * scale, scale


def layer_norm(values, gain_row, shift_row):
    return norm_parts(values)[0] * gain_row + shift_row


def norm_backward(grad, values, gain_row):
    unit, scale = norm_parts(values)
    weighted = grad * gain_row
    inner = (
        weighted
        - jnp.mean(weighted, -1, keepdims=True)
        - unit * jnp.mean(weighted * unit, -1, keepdims=True)
    )
    return (
        inner * scale,
        jnp.sum(grad * unit, 0, keepdims=True),
        jnp.sum(grad, 0, keepdims=True),
    )


def gelu_parts(values):
    below = 0.5 * (1.0 + lax.erf(values * math.sqrt(0.5)))
    density = jnp.exp(-0.5 * values * values) * (1.0 / math.sqrt(2.0 * math.pi))
    return values * below, below + values * density


def softened(queries, keys, head_size, allowed):
    scores = nt_(queries, keys) * (1.0 / math.sqrt(head_size))
    if allowed is not None:
        scores = jnp.where(allowed, scores, -1e30)
    expo = jnp.exp(scores - jnp.max(scores, -1, keepdims=True))
    return expo * (1.0 / jnp.sum(expo, -1, keepdims=True))


def attend(rows, head_size, length, allowed):
    columns = rows.shape[1] // 3
    images = []
    for at in range(0, rows.shape[0], length):
        outs = []
        for h in range(0, columns, head_size):
            q, k, v = (
                rows[at : at + length, j * columns + h : j * columns + h + head_size]
                for j in range(3)
            )
            soft = softened(q, k, head_size, allowed)
            outs.append(nn(soft.astype(bf16), v).astype(bf16))
        images.append(jnp.concatenate(outs, 1))
    return jnp.concatenate(images, 0) if len(images) > 1 else images[0]


def attend_back(rows, grad, head_size, length, allowed):
    columns = rows.shape[1] // 3
    factor = 1.0 / math.sqrt(head_size)
    images = []
    for at in range(0, rows.shape[0], length):
        outs = [[], [], []]
        for h in range(0, columns, head_size):
            q, k, v = (
                rows[at : at + length, j * columns + h : j * columns + h + head_size]
                for j in range(3)
            )
            g = grad[at : at + length, h : h + head_size]
            soft = softened(q, k, head_size, allowed)
            outs[2].append(tn(soft.astype(bf16), g).astype(bf16))
            ds = nt_(g, v)
            ds = (soft * (ds - jnp.sum(ds * soft, -1, keepdims=True))).astype(bf16)
            outs[0].append((nn(ds, k) * factor).astype(bf16))
            outs[1].append((tn(ds, q) * factor).astype(bf16))
        images.append(jnp.concatenate(outs[0] + outs[1] + outs[2], 1))
    return jnp.concatenate(images, 0) if len(images) > 1 else images[0]


def same_image(role, length, context):
    row = lax.broadcasted_iota(jnp.int32, (length, length), 0) // context
    column = lax.broadcasted_iota(jnp.int32, (length, length), 1) // context
    return (row == column) | (role != 0)


def encoder_attend_kernel(
    edge, unit, context, head_size, kept,
    role_ref, patch_ref, base_ref, emb_ref, order_ref, w_ref, vec_ref,
    mid_ref, resid_ref, normed_ref, rows_ref, att_ref, x_ref, h_ref,
):
    step = pl.program_id(0)
    groups = pl.num_programs(0) // 2
    side = 2
    wide = side * edge
    pix = patch_ref.shape[2]
    columns = wide // 4

    @pl.when(step == 0)
    def _():
        x_ref[...] = base_ref[...]

    @pl.when(step < groups)
    def _():
        ordered = sum(
            nn(order_ref[:, m * edge : (m + 1) * edge], emb_ref[0, :, m * pix : (m + 1) * pix])
            for m in range(side)
        ).astype(bf16)
        x_ref[...] += nt_(patch_ref[0], ordered)

    @pl.when(step == groups - 1)
    def _():
        values = x_ref[...]
        resid_ref[...] = values[:kept]
        low = layer_norm(values, vec_ref[0:1], vec_ref[1:2]).astype(bf16)
        h_ref[...] = low
        normed_ref[...] = low[:kept]

    @pl.when(step >= groups)
    def _():
        rows = sum(
            nn(h_ref[:, r * edge : (r + 1) * edge], w_ref[0, :, r * wide : r * wide + 3 * columns])
            for r in range(side)
        ).astype(bf16)
        rows_ref[0] = rows[:kept]
        att = attend(rows, head_size, unit, same_image(role_ref[0], unit, context))
        att_ref[0] = att[:kept]
        for r in range(side):
            x_ref[:, r * edge : (r + 1) * edge] += nt_(
                att, w_ref[0, :, r * wide + 3 * columns : (r + 1) * wide]
            )

    @pl.when(step == 2 * groups - 1)
    def _():
        mid_ref[...] = x_ref[...]


def encoder_feed_kernel(
    edge, kept, mid_ref, up_ref, down_ref, vec_ref, pick_ref, swap_ref,
    out_ref, normed_ref, hidden_ref, feat_ref, target_ref, x_ref, h_ref,
):
    step = pl.program_id(0)
    groups = pl.num_programs(0)
    side = 2
    wide = side * edge

    @pl.when(step == 0)
    def _():
        values = mid_ref[...]
        x_ref[...] = values
        low = layer_norm(values, vec_ref[2:3], vec_ref[3:4]).astype(bf16)
        h_ref[...] = low
        normed_ref[...] = low[:kept]

    hidden = sum(
        nn(h_ref[:, r * edge : (r + 1) * edge], up_ref[0, :, r * wide : (r + 1) * wide])
        for r in range(side)
    )
    hidden_ref[0] = hidden[:kept]
    active = gelu_parts(hidden)[0].astype(bf16)
    for r in range(side):
        x_ref[:, r * edge : (r + 1) * edge] += nt_(
            active, down_ref[0, :, r * wide : (r + 1) * wide]
        )

    @pl.when(step == groups - 1)
    def _():
        values = x_ref[...]
        out_ref[...] = values[:kept]
        final = layer_norm(values, vec_ref[4:5], vec_ref[5:6])
        encoded = final[:kept].astype(bf16)
        target = norm_parts(final)[0].astype(bf16)
        picked = nn(pick_ref[...], target).astype(bf16)
        for t in range(swap_ref.shape[0]):
            feat_ref[t] = nn(encoded, swap_ref[t]).astype(bf16)
            target_ref[t] = nn(picked, swap_ref[t]).astype(bf16)


def put(grad_ref, t, columns, value):
    grad_ref[t, :, columns] = value.astype(bf16)


def predictor_kernel(
    share, context, players, head_size, denominator,
    feat_ref, target_ref, base_ref, w_ref, vec_ref, swap_ref,
    grad_ref, vec_grad_ref, loss_ref, back_ref,
    x_ref, mid_ref, h_ref, h2_ref, rows_ref, att_ref, hidden_ref, acc_ref, d_ref, low_ref, f_ref,
):
    groups = w_ref.shape[0]
    edge = w_ref.shape[1]
    length = base_ref.shape[0] // share
    quarter = feat_ref.shape[2]
    columns = edge // 4
    last = 3 * players * edge
    in_cols = slice(last, last + quarter)
    out_cols = slice(last + quarter, last + 2 * quarter)

    def span(number):
        return slice(number * edge, (number + 1) * edge)

    vec_grad_ref[...] = jnp.zeros_like(vec_grad_ref)

    projected = sum(nt_(feat_ref[t], w_ref[t, :, in_cols]) for t in range(groups))
    x_ref[0] = base_ref[...]
    for i in range(share):
        x_ref[0, i * length : i * length + context] += projected[i * context : (i + 1) * context]

    for j in range(players):
        values = x_ref[j]
        h_ref[j] = layer_norm(values, vec_ref[4 * j : 4 * j + 1], vec_ref[4 * j + 1 : 4 * j + 2]).astype(bf16)
        mid_ref[j] = values

        @pl.loop(0, groups)
        def _(t, j=j):
            rows = nn(h_ref[j], w_ref[t, :, 3 * j * edge : 3 * j * edge + 3 * columns]).astype(bf16)
            rows_ref[j, t] = rows
            att = attend(rows, head_size, length, None)
            att_ref[j, t] = att
            mid_ref[j] += nt_(att, w_ref[t, :, 3 * j * edge + 3 * columns : (3 * j + 1) * edge])

        values = mid_ref[j]
        h2_ref[j] = layer_norm(values, vec_ref[4 * j + 2 : 4 * j + 3], vec_ref[4 * j + 3 : 4 * j + 4]).astype(bf16)
        x_ref[j + 1] = values

        @pl.loop(0, groups)
        def _(t, j=j):
            hidden = nn(h2_ref[j], w_ref[t, :, span(3 * j + 1)])
            hidden_ref[j, t] = hidden
            x_ref[j + 1] += nt_(gelu_parts(hidden)[0].astype(bf16), w_ref[t, :, span(3 * j + 2)])

    final_gain = vec_ref[4 * players : 4 * players + 1]
    final = layer_norm(x_ref[players], final_gain, vec_ref[4 * players + 1 : 4 * players + 2]).astype(bf16)
    f_ref[...] = jnp.concatenate(
        [final[i * length + context : (i + 1) * length] for i in range(share)], 0
    )
    total = jnp.zeros((1, 1), f32)
    grad_f = jnp.zeros(f_ref.shape, f32)
    for t in range(groups):
        out_w = w_ref[t, :, out_cols]
        gap = nn(f_ref[...], out_w) - target_ref[t].astype(f32)
        size = jnp.abs(gap)
        terms = jnp.where(size < 1.0, 0.5 * gap * gap, size - 0.5)
        total += jnp.sum(jnp.sum(terms, 1, keepdims=True), 0, keepdims=True)
        grad_pred = (jnp.clip(gap, -1.0, 1.0) * (1.0 / denominator)).astype(bf16)
        put(grad_ref, t, out_cols, tn(f_ref[...], grad_pred))
        grad_f += nt_(grad_pred, out_w)
    loss_ref[...] = jnp.broadcast_to(total * (1.0 / denominator), loss_ref.shape)
    d_ref[...] = jnp.zeros_like(d_ref)
    tail = length - context
    for i in range(share):
        d_ref[i * length + context : (i + 1) * length] = grad_f[i * tail : (i + 1) * tail]
    grad, gain_g, shift_g = norm_backward(d_ref[...], x_ref[players], final_gain)
    d_ref[...] = grad
    vec_grad_ref[4 * players : 4 * players + 1] = gain_g
    vec_grad_ref[4 * players + 1 : 4 * players + 2] = shift_g

    for j in reversed(range(players)):
        low_ref[...] = d_ref[...].astype(bf16)
        acc_ref[...] = jnp.zeros_like(acc_ref)

        @pl.loop(0, groups)
        def _(t, j=j):
            active, slope = gelu_parts(hidden_ref[j, t])
            low = low_ref[...]
            put(grad_ref, t, span(3 * j + 2), tn(low, active.astype(bf16)))
            grad_hidden = (nn(low, w_ref[t, :, span(3 * j + 2)]) * slope).astype(bf16)
            put(grad_ref, t, span(3 * j + 1), tn(h2_ref[j], grad_hidden))
            acc_ref[...] += nt_(grad_hidden, w_ref[t, :, span(3 * j + 1)])

        grad, gain_g, shift_g = norm_backward(acc_ref[...], mid_ref[j], vec_ref[4 * j + 2 : 4 * j + 3])
        vec_grad_ref[4 * j + 2 : 4 * j + 3] = gain_g
        vec_grad_ref[4 * j + 3 : 4 * j + 4] = shift_g
        grad = d_ref[...] + grad
        d_ref[...] = grad
        low_ref[...] = grad.astype(bf16)
        acc_ref[...] = jnp.zeros_like(acc_ref)

        @pl.loop(0, groups)
        def _(t, j=j):
            low = low_ref[...]
            attn_w = w_ref[t, :, span(3 * j)]
            grad_att = nn(low, attn_w[:, 3 * columns :]).astype(bf16)
            grad_rows = attend_back(rows_ref[j, t], grad_att, head_size, length, None)
            grad_w = jnp.concatenate([tn(h_ref[j], grad_rows), tn(low, att_ref[j, t])], 1)
            put(grad_ref, t, span(3 * j), grad_w)
            acc_ref[...] += nt_(grad_rows, attn_w[:, : 3 * columns])

        grad, gain_g, shift_g = norm_backward(acc_ref[...], x_ref[j], vec_ref[4 * j : 4 * j + 1])
        vec_grad_ref[4 * j : 4 * j + 1] = gain_g
        vec_grad_ref[4 * j + 1 : 4 * j + 2] = shift_g
        d_ref[...] += grad

    mask_grad = jnp.zeros((1, edge), f32)
    for i in range(share):
        mask_grad += jnp.sum(d_ref[i * length + context : (i + 1) * length], 0, keepdims=True)
    vec_grad_ref[4 * players + 2 : 4 * players + 3] = mask_grad
    low = jnp.concatenate(
        [d_ref[i * length : i * length + context] for i in range(share)], 0
    ).astype(bf16)
    back = jnp.zeros((low.shape[0], swap_ref.shape[1]), f32)
    for t in range(groups):
        put(grad_ref, t, in_cols, tn(low, feat_ref[t]))
        back += nt_(nn(low, w_ref[t, :, in_cols]).astype(bf16), swap_ref[t])
    back_ref[...] = back.astype(bf16)


def encoder_feed_back_kernel(
    edge, back_ref, out_ref, mid_ref, normed_ref, hidden_ref, up_ref, down_ref, vec_ref,
    up_grad, down_grad, grad_ref, vec_grad_ref, d_ref, low_ref, acc_ref,
):
    step = pl.program_id(0)
    groups = pl.num_programs(0)
    wide = 2 * edge

    @pl.when(step == 0)
    def _():
        grad, gain_g, shift_g = norm_backward(back_ref[...].astype(f32), out_ref[...], vec_ref[4:5])
        d_ref[...] = grad
        low_ref[...] = grad.astype(bf16)
        acc_ref[...] = jnp.zeros_like(acc_ref)
        vec_grad_ref[...] = jnp.zeros_like(vec_grad_ref)
        vec_grad_ref[4:5] = gain_g
        vec_grad_ref[5:6] = shift_g

    active, slope = gelu_parts(hidden_ref[0])
    active = active.astype(bf16)
    grad_hidden = sum(
        nn(low_ref[:, r * edge : (r + 1) * edge], down_ref[0, :, r * wide : (r + 1) * wide])
        for r in range(2)
    )
    grad_hidden = (grad_hidden * slope).astype(bf16)
    for r in range(2):
        mine = slice(r * edge, (r + 1) * edge)
        columns = slice(r * wide, (r + 1) * wide)
        put(down_grad, 0, columns, tn(low_ref[:, mine], active))
        put(up_grad, 0, columns, tn(normed_ref[:, mine], grad_hidden))
        acc_ref[:, mine] += nt_(grad_hidden, up_ref[0, :, columns])

    @pl.when(step == groups - 1)
    def _():
        grad, gain_g, shift_g = norm_backward(acc_ref[...], mid_ref[...], vec_ref[2:3])
        grad_ref[...] = d_ref[...] + grad
        vec_grad_ref[2:3] = gain_g
        vec_grad_ref[3:4] = shift_g


def encoder_attend_back_kernel(
    edge, unit, context, head_size,
    role_ref, mid_grad_ref, resid_ref, normed_ref, rows_ref, att_ref, w_ref, patch_ref, order_ref,
    vec_ref, grad_ref, vec_grad_ref, low_ref, acc_ref,
):
    step = pl.program_id(0)
    groups = pl.num_programs(0) // 2
    wide = 2 * edge
    columns = wide // 4
    pix = patch_ref.shape[2]

    @pl.when(step == 0)
    def _():
        low_ref[...] = mid_grad_ref[...].astype(bf16)
        acc_ref[...] = jnp.zeros_like(acc_ref)

    @pl.when(step < groups)
    def _():
        grad_att = sum(
            nn(
                low_ref[:, r * edge : (r + 1) * edge],
                w_ref[0, :, r * wide + 3 * columns : (r + 1) * wide],
            )
            for r in range(2)
        ).astype(bf16)
        allowed = same_image(role_ref[0], unit, context)
        grad_rows = attend_back(rows_ref[0], grad_att, head_size, unit, allowed)
        for r in range(2):
            mine = slice(r * edge, (r + 1) * edge)
            grad_w = jnp.concatenate(
                [tn(normed_ref[:, mine], grad_rows), tn(low_ref[:, mine], att_ref[0])], 1
            )
            put(grad_ref, step, slice(r * wide, (r + 1) * wide), grad_w)
            acc_ref[:, mine] += nt_(grad_rows, w_ref[0, :, r * wide : r * wide + 3 * columns])

    @pl.when(step == groups - 1)
    def _():
        grad, gain_g, shift_g = norm_backward(acc_ref[...], resid_ref[...], vec_ref[0:1])
        grad = mid_grad_ref[...] + grad
        low_ref[...] = nn(grad.astype(bf16), order_ref[...]).astype(bf16)
        vec_grad_ref[...] = jnp.zeros_like(vec_grad_ref)
        vec_grad_ref[0:1] = gain_g
        vec_grad_ref[1:2] = shift_g
        vec_grad_ref[6:7] = jnp.sum(grad, 0, keepdims=True)

    @pl.when(step >= groups)
    def _():
        grad_w = jnp.concatenate(
            [tn(low_ref[:, r * edge : (r + 1) * edge], patch_ref[0]) for r in range(2)], 1
        )
        put(grad_ref, step - groups, slice(2 * wide, 2 * wide + 2 * pix), grad_w)


def split(values):
    high = values.astype(bf16)
    return high, (values - high.astype(f32)).astype(bf16)


def shampoo_kernel(
    grad_ref, weight_ref, left_ref, right_ref, root_left_ref, root_right_ref, teacher_ref,
    grad_out, weight_out, left_out, right_out, teacher_out,
):
    low = grad_ref[0]
    grad_out[0, 0] = low.astype(f32)
    left_out[0, 0] = 0.95 * left_ref[0, 0] + 0.05 * nt_(low, low)
    right_out[0, 0] = 0.95 * right_ref[0, 0] + 0.05 * tn(low, low)
    high, rest = split(root_left_ref[0, 0])
    side = nn(high, low) + nn(rest, low)
    high, rest = split(side)
    root_high, root_rest = split(root_right_ref[0, 0])
    step = nn(high, root_high) + nn(high, root_rest) + nn(rest, root_high)
    mean = jnp.mean(jnp.mean(step * step, 1, keepdims=True), 0, keepdims=True)
    step = step * lax.rsqrt(mean + 1e-06)
    weight = weight_ref[0, 0]
    new = weight - 0.05 * (step + 0.05 * weight)
    weight_out[0, 0] = new
    teacher_out[0, 0] = 0.7 * teacher_ref[0, 0] + 0.3 * new


MESH = pl.DeviceIdType.MESH


def flip(place, bits):
    bit = 1
    while bit <= bits:
        if bits & bit:
            place = place + bit * (1 - 2 * lax.rem(lax.div(place, bit), 2))
        bit *= 2
    return place


def remote(source, target, send_sem, recv_sem, device):
    return pltpu.make_async_remote_copy(
        src_ref=source, dst_ref=target, send_sem=send_sem, recv_sem=recv_sem,
        device_id=device, device_id_type=MESH,
    )


def greet(routes, d, z):
    barrier = pltpu.get_barrier_semaphore()
    peers = [(d, flip(z, r)) for r in range(1, routes.nt)]
    peers += [routes.partner(s, d, z) for s in range(routes.stages + 1)]
    for peer in peers:
        pl.semaphore_signal(barrier, inc=1, device_id=peer, device_id_type=MESH)
    pl.semaphore_wait(barrier, len(peers))


def gather_kernel(
    routes, widths, few_rows, own_ref, other_ref, pred_ref, patch_ref,
    attn_ref, up_ref, down_ref, players_ref, rows_ref,
    z_send, z_recv, local_sem, patch_send, patch_recv, stage_send, stage_recv,
):
    d, z = lax.axis_index("dp"), lax.axis_index("tensor")
    nt, stages = routes.nt, routes.stages
    role = lax.rem(z, 2)
    mats = [attn_ref, up_ref, down_ref, players_ref]
    starts = [sum(widths[:m]) for m in range(3)]
    last = 3

    def source(m, r):
        if m == last:
            return pred_ref
        ref = own_ref if r % 2 == 0 else other_ref
        return ref.at[:, pl.ds(starts[m], widths[m])]

    def across(m, r):
        return remote(
            source(m, r), mats[m].at[r, 0], z_send.at[m, r], z_recv.at[m, r], (d, flip(z, r))
        )

    def local(m):
        return pltpu.make_async_copy(source(m, 0), mats[m].at[0, 0], local_sem.at[m])

    def patch(r, rows):
        return remote(
            patch_ref.at[r, pl.ds(0, rows)], rows_ref.at[r, pl.ds(0, rows)],
            patch_send.at[r], patch_recv.at[r], (d, flip(z, r)),
        )

    def stage(m, r, s):
        size = 1 << s
        return remote(
            mats[m].at[r, pl.ds(0, size)], mats[m].at[r, pl.ds(size, size)],
            stage_send.at[m, r, s], stage_recv.at[m, r, s], routes.partner(s, d, z),
        )

    def when(m, r):
        return role == 1 if m == last else None

    def guarded(condition, body):
        if condition is None:
            body()
        else:
            pl.when(condition)(body)

    greet(routes, d, z)
    all_rows = patch_ref.shape[1]
    own_patch = pltpu.make_async_copy(patch_ref.at[0], rows_ref.at[0], local_sem.at[last + 1])
    for m in range(4):
        guarded(when(m, 0), lambda m=m: local(m).start())
        for r in range(1, nt):
            to_role = lax.rem(flip(z, r), 2)
            if m == last:
                pl.when(to_role == 1)(lambda m=m, r=r: across(m, r).start())
            else:
                across(m, r).start()
        if m == 0:
            own_patch.start()
            for r in range(1, nt):
                to_role = lax.rem(flip(z, r), 2)
                pl.when(to_role == 0)(lambda r=r: patch(r, few_rows).start())
                pl.when(to_role == 1)(lambda r=r: patch(r, all_rows).start())

    items = [(m, r) for m in range(4) for r in range(nt)]

    def advance(m, r, s):
        if s == 0:
            if r == 0:
                local(m).wait()
            else:
                across(m, r).wait_recv()
        else:
            stage(m, r, s - 1).wait_recv()
        stage(m, r, s).start()

    for n in range(len(items) + stages):
        for s in reversed(range(stages + 1)):
            if 0 <= n - s < len(items):
                m, r = items[n - s]
                guarded(when(m, r), lambda m=m, r=r, s=s: advance(m, r, s))

    own_patch.wait()
    for r in range(1, nt):
        to_role = lax.rem(flip(z, r), 2)
        pl.when(role == 0)(lambda r=r: patch(r, few_rows).wait_recv())
        pl.when(role == 1)(lambda r=r: patch(r, all_rows).wait_recv())
        pl.when(to_role == 0)(lambda r=r: patch(r, few_rows).wait_send())
        pl.when(to_role == 1)(lambda r=r: patch(r, all_rows).wait_send())
    for m, r in items:

        def finish(m=m, r=r):
            stage(m, r, stages).wait_recv()
            for s in range(stages + 1):
                stage(m, r, s).wait_send()

        guarded(when(m, r), finish)
        if r:
            to_role = lax.rem(flip(z, r), 2)
            if m == last:
                pl.when(to_role == 1)(lambda m=m, r=r: across(m, r).wait_send())
            else:
                across(m, r).wait_send()


def reduce_kernel(
    routes, attn_cols, down_ref, up_ref, attn_ref, pred_ref, block_ref, emb_ref,
    core0, core1, core2, later0, later1, later2, enc_in, pred_in, load,
    load_sem, core_send, core_recv, stage_send, stage_recv, z_send, z_recv,
):
    d, z = lax.axis_index("dp"), lax.axis_index("tensor")
    nt, stages = routes.nt, routes.stages
    middle = routes.nd // 2
    role = lax.rem(z, 2)
    cores = [core0, core1, core2]
    laters = [later0, later1, later2]
    greet(routes, d, z)

    def run(kind, sources, incoming, starts):
        items = [(j, r) for j in range(len(sources)) for r in reversed(range(nt))]

        def part(j, r, first):
            ref, start, width = sources[j]
            return ref.at[r, pl.ds(first, middle), :, pl.ds(start, width)]

        def to_core(j, r):
            return remote(
                part(j, r, middle), cores[j].at[r, :, :, pl.ds(0, sources[j][2])],
                core_send.at[j, r], core_recv.at[j, r], routes.partner(stages, d, z),
            )

        def own(i):
            j, r = items[i]
            return pltpu.make_async_copy(
                part(j, r, 0), load.at[i % 2, :, :, pl.ds(0, sources[j][2])], load_sem.at[i % 2]
            )

        def stage(j, r, s):
            size = 1 << s
            return remote(
                cores[j].at[r, pl.ds(size, size), :, pl.ds(0, sources[j][2])],
                laters[j].at[r, pl.ds(size - 1, size), :, pl.ds(0, sources[j][2])],
                stage_send.at[j, r, s], stage_recv.at[j, r, s], routes.partner(s, d, z),
            )

        def across(j, r):
            return remote(
                cores[j].at[r, 0, :, pl.ds(0, sources[j][2])],
                incoming.at[r, :, pl.ds(starts[j], sources[j][2])],
                z_send.at[kind, j, r], z_recv.at[kind, j, r], (d, flip(z, r)),
            )

        def add(i, q):
            j, r = items[i]
            width = sources[j][2]
            if q == 0:
                own(i).wait()
                to_core(j, r).wait_recv()

                @pl.loop(0, middle)
                def _(k):
                    total = cores[j][r, k, :, 0:width].astype(f32)
                    total += load[i % 2, k, :, 0:width].astype(f32)
                    cores[j][r, k, :, 0:width] = total.astype(bf16)

                if i + 2 < len(items):
                    own(i + 2).start()
            else:
                s = stages - q
                stage(j, r, s).wait_recv()

                @pl.loop(0, 1 << s)
                def _(k):
                    total = cores[j][r, k, :, 0:width].astype(f32)
                    total += laters[j][r, k + ((1 << s) - 1), :, 0:width].astype(f32)
                    cores[j][r, k, :, 0:width] = total.astype(bf16)

            if q < stages:
                stage(j, r, stages - q - 1).start()
            elif r:
                across(j, r).start()

        for i in range(min(2, len(items))):
            own(i).start()
        for j, r in items:
            to_core(j, r).start()
        for n in range(len(items) + stages):
            for q in reversed(range(stages + 1)):
                if 0 <= n - q < len(items):
                    add(n - q, q)
        for j, r in items:
            to_core(j, r).wait_send()
            for s in range(stages):
                stage(j, r, s).wait_send()
            if r:
                across(j, r).wait_send()

    wide = down_ref.shape[3]
    all_cols = attn_ref.shape[3]
    pred_cols = pred_ref.shape[3]
    encoder = [(down_ref, 0, wide), (up_ref, 0, wide), (attn_ref, 0, all_cols)]
    encoder_at = [0, wide, 2 * wide]
    players = [(pred_ref, 0, wide), (pred_ref, wide, pred_cols - wide)]
    players_at = [0, wide]

    @pl.when(role == 0)
    def _():
        run(0, encoder, enc_in, encoder_at)

    @pl.when(role == 1)
    def _():
        run(1, players, pred_in, players_at)

    def collect(kind, sources, incoming, starts, put):
        for j, (_, _, width) in enumerate(sources):
            place = incoming.at[:, :, pl.ds(starts[j], width)]

            def arrive(r, j=j, width=width):
                pltpu.make_async_remote_copy(
                    src_ref=cores[j].at[r, 0, :, pl.ds(0, width)],
                    dst_ref=incoming.at[r, :, pl.ds(starts[j], width)],
                    send_sem=z_send.at[kind, j, r], recv_sem=z_recv.at[kind, j, r],
                    device_id=(d, flip(z, r)), device_id_type=MESH,
                ).wait_recv()

            del place

            @pl.when(role == kind)
            def _(j=j, width=width, arrive=arrive):
                total = cores[j][0, 0, :, 0:width].astype(f32)
                for r in range(2, nt, 2):
                    arrive(r)
                    total += incoming[r, :, starts[j] : starts[j] + width].astype(f32)
                put(j, total)

            @pl.when(role != kind)
            def _(j=j, width=width, arrive=arrive):
                total = None
                for r in range(1, nt, 2):
                    arrive(r)
                    got = incoming[r, :, starts[j] : starts[j] + width].astype(f32)
                    total = got if total is None else total + got
                put(j, total)

    def put_encoder(j, total):
        if j == 2:
            block_ref[:, 0:attn_cols] = total[:, :attn_cols].astype(bf16)
            emb_ref[...] = total[:, attn_cols:]
        else:
            first = attn_cols + (1 - j) * wide
            block_ref[:, first : first + wide] = total.astype(bf16)

    def put_players(j, total):
        first = attn_cols + 2 * wide + players_at[j]
        block_ref[:, first : first + total.shape[1]] = total.astype(bf16)

    collect(1, players, pred_in, players_at, put_players)
    collect(0, encoder, enc_in, encoder_at, put_encoder)
    end = attn_cols + 2 * wide + pred_cols
    block_ref[:, end:] = jnp.zeros((block_ref.shape[0], block_ref.shape[1] - end), bf16)


def whole(shape):
    return pl.BlockSpec(shape, lambda *_: (0,) * len(shape))


def by_group(shape):
    return pl.BlockSpec((1,) + shape, lambda t: (t, 0, 0))


def compiled():
    return pltpu.CompilerParams(
        dimension_semantics=("arbitrary",), vmem_limit_bytes=KERNEL_BYTES
    )


def cost(flops, moved):
    return pl.CostEstimate(flops=int(flops), bytes_accessed=int(moved), transcendentals=0)


def sincos(cell_index, columns):
    quarter = columns // 4
    frequency = 1.0 / 10000.0 ** (jnp.arange(quarter).astype(f32) / quarter)
    col_angle = (cell_index % SIDE).astype(f32)[..., None] * frequency
    row_angle = (cell_index // SIDE).astype(f32)[..., None] * frequency
    return jnp.concatenate(
        [jnp.sin(col_angle), jnp.cos(col_angle), jnp.sin(row_angle), jnp.cos(row_angle)], -1
    )


def adamw(master, moment, second, gradient, step_rate, weight_decay):
    moment = 0.9 * moment + 0.1 * gradient
    second = 0.999 * second + 0.001 * gradient * gradient
    unbiased_first = moment / (1.0 - 0.9**STEP)
    unbiased_second = second / (1.0 - 0.999**STEP)
    return (
        master
        - step_rate
        * (unbiased_first / (jnp.sqrt(unbiased_second) + 1e-08) + weight_decay * master),
        moment,
        second,
    )


class Routes:
    def __init__(self, nd, nt):
        self.nd, self.nt = nd, nt
        self.low_bits = [1 << s for s in range(1, nd.bit_length() - 1)]
        self.stages = len(self.low_bits)

    def order(self, core):
        return self.low_bits if core == 0 else self.low_bits[::-1]

    def pairs(self, target, keep):
        found = []
        for d in range(self.nd):
            for z in range(self.nt):
                if keep(d, z):
                    d2, z2 = target(d, z)
                    found.append((d * self.nt + z, d2 * self.nt + z2))
        return found

    def partner(self, number, d, z):
        if number == self.stages:
            return flip(d, 1), z
        core = lax.rem(d, 2)
        ends = flip(d, self.order(0)[number]), flip(d, self.order(1)[number])
        return ends[0] + core * (ends[1] - ends[0]), z

    def across(self, r, values, from_role=None):
        def keep(d, z):
            return from_role is None or z % 2 == from_role

        return lax.ppermute(values, AXES, self.pairs(lambda d, z: (d, z ^ r), keep))

    def holders(self, d):
        place = jnp.arange(self.nd, dtype=jnp.int32)
        held = d ^ (place >> self.stages)
        core = held & 1
        for s in range(self.stages):
            bit = (place >> s) & 1
            held = held ^ (bit * jnp.where(core == 0, self.order(0)[s], self.order(1)[s]))
        return held

    def total(self, values):
        for bit in [1] + self.low_bits:
            values = values + lax.ppermute(
                values, AXES, self.pairs(lambda d, z, b=bit: (d ^ b, z), lambda d, z: True)
            )
        r = 1
        while r < self.nt:
            values = values + self.across(r, values)
            r *= 2
        return values


def shards(
    patches,
    ctx_idx,
    tgt_idx,
    owner,
    weights,
    stats_left,
    stats_right,
    root_left,
    root_right,
    teacher_slot_blocks,
    embed,
    embed_m,
    embed_v,
    teacher_embed,
    enc_vectors,
    enc_m,
    enc_v,
    pred_vectors,
    pred_m,
    pred_v,
    teacher_vectors,
):
    nt = lax.axis_size("tensor")
    nd = lax.axis_size("dp")
    routes = Routes(nd, nt)
    half = nt // 2
    d = lax.axis_index("dp")
    z = lax.axis_index("tensor")
    role = z % 2
    student_role = role == 0
    images, npatches, pix_part = patches.shape
    slots = weights.shape[1]
    edge = weights.shape[-1]
    slot_count = slots * nd
    block_count = owner.shape[0]
    width = enc_vectors.shape[1]
    narrow = pred_vectors.shape[1]
    players = (pred_vectors.shape[0] - 3) // 4
    side = width // edge
    teach_count = 3 * side * side
    quarter = width // nt
    context_len = ctx_idx.shape[1]
    target_len = tgt_idx.shape[1]
    seq_len = context_len + target_len
    share = images // half
    rows_part = edge // nd

    both = jnp.stack([weights[0], teacher_slot_blocks[0]]).astype(bf16)
    both = both.reshape(2, slots, nd, rows_part, edge)
    both = lax.all_to_all(both, "dp", split_axis=2, concat_axis=0, tiled=False)
    by_slot = both.transpose(1, 0, 2, 3, 4).reshape(2, slot_count, rows_part, edge)
    mine = by_slot[0][owner].transpose(1, 0, 2).reshape(rows_part, -1)
    teach = by_slot[1][owner[:teach_count]].transpose(1, 0, 2).reshape(rows_part, -1)

    mat = side * width

    def embed_rows(values):
        turned = values.astype(bf16).T.reshape(side, rows_part, pix_part)
        return turned.transpose(1, 0, 2).reshape(rows_part, -1)

    of_student = jnp.concatenate(
        [mine[:, :mat], embed_rows(embed), mine[:, mat : 3 * mat]], 1
    )
    of_teacher = jnp.concatenate([teach[:, :mat], embed_rows(teacher_embed), teach[:, mat:]], 1)
    own = jnp.where(student_role, of_student, of_teacher)
    other = jnp.where(student_role, of_teacher, of_student)
    pred_own = mine[:, 3 * mat :]

    holder = routes.holders(d)
    inside = jnp.arange(rows_part, dtype=jnp.int32)
    feat_p = (holder[:, None] * rows_part + inside[None, :]).reshape(-1)
    feat = jnp.concatenate([r * edge + feat_p for r in range(side)])
    one_hot = (feat[:, None] == jnp.arange(width)[None, :]).astype(f32)
    one_hot_p = (feat_p[:, None] == jnp.arange(narrow)[None, :]).astype(f32)

    def to_local(rows, hot):
        return jnp.einsum("nf,lf->nl", rows, hot, precision=exact, preferred_element_type=f32)

    def to_global(rows, hot):
        return jnp.einsum("nl,lf->nf", rows, hot, precision=exact, preferred_element_type=f32)

    vec = to_local(jnp.where(student_role, enc_vectors, teacher_vectors), one_hot)
    vec = jnp.pad(vec, ((0, 1), (0, 0)))
    pvec = to_local(pred_vectors, one_hot_p)
    pvec = jnp.pad(pvec, ((0, 16 - pvec.shape[0]), (0, 0)))
    pred_z = z - role + 1
    group_feat = (pred_z ^ jnp.arange(nt, dtype=jnp.int32))[:, None] * quarter + jnp.arange(
        quarter, dtype=jnp.int32
    )
    emb_feat = jnp.concatenate(
        [holder[:, None] * 2 * rows_part + m * rows_part + inside[None, :] for m in range(2)]
    ).reshape(-1)
    order = (feat[:, None] == emb_feat[None, :]).astype(bf16)
    swap = (feat[None, :, None] == group_feat[:, None, :]).astype(bf16)

    part = z // 2
    hot = (ctx_idx[:, :, None] == jnp.arange(npatches)[None, None, :]).astype(bf16)
    picked = jnp.einsum("gcn,gnp->gcp", hot, patches, preferred_element_type=f32).astype(bf16)

    def rows_for(target_z):
        where = (target_z // 2) * share
        ctx = lax.dynamic_slice_in_dim(picked, where, share, 0).reshape(-1, pix_part)
        every = lax.dynamic_slice_in_dim(patches, where, share, 0).reshape(-1, pix_part)
        padded = jnp.pad(ctx, ((0, every.shape[0] - ctx.shape[0]), (0, 0)))
        return jnp.where(target_z % 2 == 0, padded, every)

    patch_out = jnp.stack([rows_for(z ^ r) for r in range(nt)])
    my_ctx = lax.dynamic_slice_in_dim(ctx_idx, part * share, share, 0)
    my_tgt = lax.dynamic_slice_in_dim(tgt_idx, part * share, share, 0)
    full_rows = share * npatches
    ctx_rows = share * context_len
    tgt_rows = share * target_len
    ctx_places = jnp.pad(my_ctx.reshape(-1), (0, full_rows - ctx_rows))
    places = jnp.where(student_role, ctx_places, jnp.arange(full_rows) % npatches)
    table = to_local(sincos(jnp.arange(npatches), width), one_hot)
    table_p = to_local(sincos(jnp.arange(npatches), narrow), one_hot_p)
    base = table[places] + vec[6]
    tgt_places = (my_tgt + npatches * jnp.arange(share, dtype=jnp.int32)[:, None]).reshape(-1)
    pick = (tgt_places[:, None] == jnp.arange(full_rows)[None, :]).astype(bf16)
    widths = [mat + side * pix_part, mat, mat, mine.shape[1] - 3 * mat]
    any_space = pl.BlockSpec(memory_space=pl.ANY)
    dma = pltpu.SemaphoreType.DMA
    attn_emb, up_w, down_t, pred_all, patch_rows = pl.pallas_call(
        functools.partial(gather_kernel, routes, widths, ctx_rows),
        in_specs=[any_space] * 4,
        out_specs=[any_space] * 5,
        out_shape=[jax.ShapeDtypeStruct((nt, nd, rows_part, c), bf16) for c in widths]
        + [jax.ShapeDtypeStruct((nt, full_rows, pix_part), bf16)],
        scratch_shapes=[
            dma((4, nt)),
            dma((4, nt)),
            dma((5,)),
            dma((nt,)),
            dma((nt,)),
            dma((4, nt, routes.stages + 1)),
            dma((4, nt, routes.stages + 1)),
        ],
        compiler_params=pltpu.CompilerParams(collective_id=0, has_side_effects=True),
        cost_estimate=cost(0, 50e6),
        name="gather_weights",
    )(own, other, pred_own, patch_out)
    attn_emb, up_w, down_t, pred_all = (
        value.reshape(nt, edge, -1) for value in (attn_emb, up_w, down_t, pred_all)
    )
    role_word = role.astype(jnp.int32).reshape(1)

    attn_cols = side * width
    columns = width // nt
    middle, resid, normed_a, rows_a, att_a = pl.pallas_call(
        functools.partial(encoder_attend_kernel, edge, npatches, context_len, HD, ctx_rows),
        grid=(2 * nt,),
        in_specs=[
            pl.BlockSpec(memory_space=pltpu.SMEM),
            pl.BlockSpec((1, full_rows, pix_part), lambda i: (jnp.minimum(i, nt - 1), 0, 0)),
            whole((full_rows, width)),
            pl.BlockSpec(
                (1, edge, side * pix_part),
                lambda i: (jnp.minimum(i, nt - 1), 0, attn_cols // (side * pix_part)),
            ),
            whole((width, width)),
            pl.BlockSpec((1, edge, attn_cols), lambda i: (jnp.maximum(i - nt, 0), 0, 0)),
            whole((8, width)),
        ],
        out_specs=[
            whole((full_rows, width)),
            whole((ctx_rows, width)),
            whole((ctx_rows, width)),
            pl.BlockSpec((1, ctx_rows, 3 * columns), lambda i: (jnp.maximum(i - nt, 0), 0, 0)),
            pl.BlockSpec((1, ctx_rows, columns), lambda i: (jnp.maximum(i - nt, 0), 0, 0)),
        ],
        out_shape=[
            jax.ShapeDtypeStruct((full_rows, width), f32),
            jax.ShapeDtypeStruct((ctx_rows, width), f32),
            jax.ShapeDtypeStruct((ctx_rows, width), bf16),
            jax.ShapeDtypeStruct((nt, ctx_rows, 3 * columns), bf16),
            jax.ShapeDtypeStruct((nt, ctx_rows, columns), bf16),
        ],
        scratch_shapes=[VMEM((full_rows, width), f32), VMEM((full_rows, width), bf16)],
        compiler_params=compiled(),
        cost_estimate=cost(6e9, 12e6),
        name="encoder_attend",
    )(role_word, patch_rows, base, attn_emb, order, attn_emb, vec)
    output, normed_f, hidden, enc_feat, target = pl.pallas_call(
        functools.partial(encoder_feed_kernel, edge, ctx_rows),
        grid=(nt,),
        in_specs=[
            whole((full_rows, width)),
            by_group((edge, mat)),
            by_group((edge, mat)),
            whole((8, width)),
            whole((tgt_rows, full_rows)),
            whole((nt, width, quarter)),
        ],
        out_specs=[
            whole((ctx_rows, width)),
            whole((ctx_rows, width)),
            by_group((ctx_rows, width)),
            whole((nt, ctx_rows, quarter)),
            whole((nt, tgt_rows, quarter)),
        ],
        out_shape=[
            jax.ShapeDtypeStruct((ctx_rows, width), f32),
            jax.ShapeDtypeStruct((ctx_rows, width), bf16),
            jax.ShapeDtypeStruct((nt, ctx_rows, width), f32),
            jax.ShapeDtypeStruct((nt, ctx_rows, quarter), bf16),
            jax.ShapeDtypeStruct((nt, tgt_rows, quarter), bf16),
        ],
        scratch_shapes=[VMEM((full_rows, width), f32), VMEM((full_rows, width), bf16)],
        compiler_params=compiled(),
        cost_estimate=cost(8e9, 14e6),
        name="encoder_feed",
    )(middle, up_w, down_t, vec, pick, swap)

    feat_in = routes.across(1, enc_feat, from_role=0)
    tokens_at = table_p[jnp.concatenate([my_ctx, my_tgt], 1)]
    mask_rows = jnp.arange(seq_len)[None, :, None] >= context_len
    tokens_at = jnp.where(mask_rows, tokens_at + pvec[4 * players + 2], tokens_at)
    tokens_at = tokens_at.reshape(-1, narrow)
    token_rows = share * seq_len
    pred_cols = (3 * players + 1) * edge
    denominator = images * nd * target_len * width
    pred_columns = narrow // nt
    in_vmem = pl.BlockSpec(memory_space=VMEM)
    pred_grads, pred_vec_g, loss_tile, back = pl.pallas_call(
        functools.partial(predictor_kernel, share, context_len, players, PHD, denominator),
        in_specs=[in_vmem] * 6,
        out_specs=[in_vmem] * 4,
        out_shape=[
            jax.ShapeDtypeStruct((nt, edge, pred_cols), bf16),
            jax.ShapeDtypeStruct((16, narrow), f32),
            jax.ShapeDtypeStruct((8, 128), f32),
            jax.ShapeDtypeStruct((ctx_rows, width), bf16),
        ],
        scratch_shapes=[
            VMEM((players + 1, token_rows, narrow), f32),
            VMEM((players, token_rows, narrow), f32),
            VMEM((players, token_rows, narrow), bf16),
            VMEM((players, token_rows, narrow), bf16),
            VMEM((players, nt, token_rows, 3 * pred_columns), bf16),
            VMEM((players, nt, token_rows, pred_columns), bf16),
            VMEM((players, nt, token_rows, edge), f32),
            VMEM((token_rows, narrow), f32),
            VMEM((token_rows, narrow), f32),
            VMEM((token_rows, narrow), bf16),
            VMEM((tgt_rows, narrow), bf16),
        ],
        compiler_params=pltpu.CompilerParams(vmem_limit_bytes=KERNEL_BYTES),
        cost_estimate=cost(16e9, 30e6),
        name="predictor",
    )(feat_in, target, tokens_at, pred_all, pvec, swap)
    back = routes.across(1, back, from_role=1)

    grad_shape = jax.ShapeDtypeStruct((nt, edge, mat), bf16)
    up_g, down_g, grad_mid, vec_g1 = pl.pallas_call(
        functools.partial(encoder_feed_back_kernel, edge),
        grid=(nt,),
        in_specs=[
            whole((ctx_rows, width)),
            whole((ctx_rows, width)),
            whole((ctx_rows, width)),
            whole((ctx_rows, width)),
            by_group((ctx_rows, width)),
            by_group((edge, mat)),
            by_group((edge, mat)),
            whole((8, width)),
        ],
        out_specs=[by_group((edge, mat))] * 2 + [whole((ctx_rows, width)), whole((8, width))],
        out_shape=[grad_shape] * 2
        + [
            jax.ShapeDtypeStruct((ctx_rows, width), f32),
            jax.ShapeDtypeStruct((8, width), f32),
        ],
        scratch_shapes=[
            VMEM((ctx_rows, width), f32),
            VMEM((ctx_rows, width), bf16),
            VMEM((ctx_rows, width), f32),
        ],
        compiler_params=compiled(),
        cost_estimate=cost(8e9, 25e6),
        name="encoder_feed_back",
    )(back, output, middle, normed_f, hidden, up_w, down_t, vec)
    all_cols = attn_cols + side * pix_part
    attn_g, vec_g2 = pl.pallas_call(
        functools.partial(encoder_attend_back_kernel, edge, npatches, context_len, HD),
        grid=(2 * nt,),
        in_specs=[
            pl.BlockSpec(memory_space=pltpu.SMEM),
            whole((ctx_rows, width)),
            whole((ctx_rows, width)),
            whole((ctx_rows, width)),
            pl.BlockSpec((1, ctx_rows, 3 * columns), lambda i: (jnp.minimum(i, nt - 1), 0, 0)),
            pl.BlockSpec((1, ctx_rows, columns), lambda i: (jnp.minimum(i, nt - 1), 0, 0)),
            pl.BlockSpec((1, edge, attn_cols), lambda i: (jnp.minimum(i, nt - 1), 0, 0)),
            pl.BlockSpec((1, ctx_rows, pix_part), lambda i: (jnp.maximum(i - nt, 0), 0, 0)),
            whole((width, width)),
            whole((8, width)),
        ],
        out_specs=[
            whole((nt, edge, all_cols)),
            whole((8, width)),
        ],
        out_shape=[
            jax.ShapeDtypeStruct((nt, edge, all_cols), bf16),
            jax.ShapeDtypeStruct((8, width), f32),
        ],
        scratch_shapes=[VMEM((ctx_rows, width), bf16), VMEM((ctx_rows, width), f32)],
        compiler_params=compiled(),
        cost_estimate=cost(6e9, 20e6),
        name="encoder_attend_back",
    )(role_word, grad_mid, resid, normed_a, rows_a, att_a, attn_emb, patch_rows, order, vec)

    places = [g.reshape(nt, nd, rows_part, -1) for g in (down_g, up_g, attn_g, pred_grads)]
    middle_size = nd // 2
    by_block, emb_sum = pl.pallas_call(
        functools.partial(reduce_kernel, routes, attn_cols),
        in_specs=[any_space] * 4,
        out_specs=[in_vmem] * 2,
        out_shape=[
            jax.ShapeDtypeStruct((rows_part, (block_count + 1) * edge), bf16),
            jax.ShapeDtypeStruct((rows_part, side * pix_part), f32),
        ],
        scratch_shapes=[
            VMEM((nt, middle_size, rows_part, mat), bf16),
            VMEM((nt, middle_size, rows_part, mat), bf16),
            VMEM((nt, middle_size, rows_part, all_cols), bf16),
            VMEM((nt, middle_size - 1, rows_part, mat), bf16),
            VMEM((nt, middle_size - 1, rows_part, mat), bf16),
            VMEM((nt, middle_size - 1, rows_part, all_cols), bf16),
            VMEM((nt, rows_part, 2 * mat + all_cols), bf16),
            VMEM((nt, rows_part, pred_cols), bf16),
            VMEM((2, middle_size, rows_part, all_cols), bf16),
            dma((2,)),
            dma((3, nt)),
            dma((3, nt)),
            dma((3, nt, routes.stages)),
            dma((3, nt, routes.stages)),
            dma((2, 3, nt)),
            dma((2, 3, nt)),
        ],
        compiler_params=pltpu.CompilerParams(
            collective_id=1, has_side_effects=True, vmem_limit_bytes=KERNEL_BYTES
        ),
        cost_estimate=cost(0, 60e6),
        name="reduce_gradients",
    )(*places)

    enc_rows = to_global(vec_g1[:7] + vec_g2[:7], one_hot)
    pred_rows = to_global(pred_vec_g[: 4 * players + 3], one_hot_p)
    enc_rows = jnp.where(student_role, enc_rows, 0.0)
    pred_rows = jnp.where(role == 1, pred_rows, 0.0)
    loss_row = jnp.where(role == 1, loss_tile[0, 0], 0.0)
    packed = jnp.concatenate([enc_rows.reshape(-1), pred_rows.reshape(-1), loss_row[None]])
    packed = jnp.pad(packed, (0, -packed.shape[0] % 1024)).reshape(-1, 128)
    packed = routes.total(packed).reshape(-1)
    enc_total = packed[: enc_rows.size].reshape(enc_rows.shape)
    pred_total = packed[enc_rows.size : enc_rows.size + pred_rows.size].reshape(pred_rows.shape)
    loss_total = packed[enc_rows.size + pred_rows.size]

    by_block = by_block.reshape(rows_part, block_count + 1, edge).transpose(1, 0, 2)
    slot_of = (
        jnp.full((slot_count,), block_count, jnp.int32)
        .at[owner]
        .set(jnp.arange(block_count, dtype=jnp.int32))
    )
    slot_rows = by_block[slot_of].reshape(nd, slots, rows_part, edge)
    slot_rows = lax.all_to_all(slot_rows, "dp", split_axis=0, concat_axis=1, tiled=False)
    low_grads = slot_rows.reshape(slots, edge, edge)

    embed_grad = emb_sum.reshape(rows_part, side, pix_part).transpose(1, 0, 2)
    embed_grad = embed_grad.reshape(-1, pix_part).T

    slot_spec = pl.BlockSpec((1, 1, edge, edge), lambda s: (0, s, 0, 0))
    slot_shape = jax.ShapeDtypeStruct(weights.shape, f32)
    slot_grads, new_weights, new_left, new_right, new_teacher_blocks = pl.pallas_call(
        shampoo_kernel,
        grid=(slots,),
        in_specs=[pl.BlockSpec((1, edge, edge), lambda s: (s, 0, 0))] + [slot_spec] * 6,
        out_specs=[slot_spec] * 5,
        out_shape=[slot_shape] * 5,
        compiler_params=compiled(),
        cost_estimate=cost(3e9, 22e6),
        name="shampoo",
    )(low_grads, weights, stats_left, stats_right, root_left, root_right, teacher_slot_blocks)
    new_embed, new_embed_m, new_embed_v = adamw(embed, embed_m, embed_v, embed_grad, 0.05, 0.05)
    new_enc, new_enc_m, new_enc_v = adamw(enc_vectors, enc_m, enc_v, enc_total, 0.5, 0.0)
    new_pred, new_pred_m, new_pred_v = adamw(pred_vectors, pred_m, pred_v, pred_total, 0.5, 0.0)
    new_teacher_embed = 0.7 * teacher_embed + 0.3 * new_embed
    new_teacher_vectors = 0.7 * teacher_vectors + 0.3 * new_enc
    return (
        loss_total,
        slot_grads,
        new_weights,
        new_left,
        new_right,
        new_teacher_blocks,
        new_embed,
        new_embed_m,
        new_embed_v,
        new_teacher_embed,
        new_enc,
        new_enc_m,
        new_enc_v,
        new_pred,
        new_pred_m,
        new_pred_v,
        new_teacher_vectors,
    )


def solution(mesh):
    blocks = P("tensor", "dp", None, None)
    table = P("tensor", "dp")
    in_specs = (
        (P("dp", None, "tensor"), P("dp", None), P("dp", None), P())
        + (blocks,) * 6
        + (table,) * 4
        + (P(),) * 7
    )
    out_specs = (P(),) + (blocks,) * 5 + (table,) * 4 + (P(),) * 7
    return jax.shard_map(shards, mesh=mesh, in_specs=in_specs, out_specs=out_specs, check_vma=False)
```

```python
import functools
import math

import jax
import jax.numpy as jnp
from jax import lax
from jax.experimental import pallas as pl
from jax.experimental.pallas import tpu as pltpu
from jax.sharding import PartitionSpec as P

HD = 64
PHD = 32
SIDE = 16
STEP = 10
KERNEL_BYTES = 60 * 1024 * 1024

AXES = ("dp", "tensor")
exact = lax.Precision.HIGHEST
f32 = jnp.float32
bf16 = jnp.bfloat16
VMEM = pltpu.VMEM


def nn(first, second):
    return lax.dot_general(first, second, (((1,), (0,)), ((), ())), preferred_element_type=f32)


def nt_(first, second):
    return lax.dot_general(first, second, (((1,), (1,)), ((), ())), preferred_element_type=f32)


def tn(first, second):
    return lax.dot_general(first, second, (((0,), (0,)), ((), ())), preferred_element_type=f32)


def norm_parts(values):
    centre = values - jnp.mean(values, -1, keepdims=True)
    scale = lax.rsqrt(jnp.mean(centre * centre, -1, keepdims=True) + 1e-06)
    return centre * scale, scale


def layer_norm(values, gain_row, shift_row):
    return norm_parts(values)[0] * gain_row + shift_row


def norm_backward(grad, values, gain_row):
    unit, scale = norm_parts(values)
    weighted = grad * gain_row
    inner = (
        weighted
        - jnp.mean(weighted, -1, keepdims=True)
        - unit * jnp.mean(weighted * unit, -1, keepdims=True)
    )
    return (
        inner * scale,
        jnp.sum(grad * unit, 0, keepdims=True),
        jnp.sum(grad, 0, keepdims=True),
    )


def gelu_parts(values):
    below = 0.5 * (1.0 + lax.erf(values * math.sqrt(0.5)))
    density = jnp.exp(-0.5 * values * values) * (1.0 / math.sqrt(2.0 * math.pi))
    return values * below, below + values * density


def softened(queries, keys, head_size, allowed):
    scores = nt_(queries, keys) * (1.0 / math.sqrt(head_size))
    if allowed is not None:
        scores = jnp.where(allowed, scores, -1e30)
    expo = jnp.exp(scores - jnp.max(scores, -1, keepdims=True))
    return expo * (1.0 / jnp.sum(expo, -1, keepdims=True))


def attend(rows, head_size, length, allowed):
    columns = rows.shape[1] // 3
    images = []
    for at in range(0, rows.shape[0], length):
        outs = []
        for h in range(0, columns, head_size):
            q, k, v = (
                rows[at : at + length, j * columns + h : j * columns + h + head_size]
                for j in range(3)
            )
            soft = softened(q, k, head_size, allowed)
            outs.append(nn(soft.astype(bf16), v).astype(bf16))
        images.append(jnp.concatenate(outs, 1))
    return jnp.concatenate(images, 0) if len(images) > 1 else images[0]


def attend_back(rows, grad, head_size, length, allowed):
    columns = rows.shape[1] // 3
    factor = 1.0 / math.sqrt(head_size)
    images = []
    for at in range(0, rows.shape[0], length):
        outs = [[], [], []]
        for h in range(0, columns, head_size):
            q, k, v = (
                rows[at : at + length, j * columns + h : j * columns + h + head_size]
                for j in range(3)
            )
            g = grad[at : at + length, h : h + head_size]
            soft = softened(q, k, head_size, allowed)
            outs[2].append(tn(soft.astype(bf16), g).astype(bf16))
            ds = nt_(g, v)
            ds = (soft * (ds - jnp.sum(ds * soft, -1, keepdims=True))).astype(bf16)
            outs[0].append((nn(ds, k) * factor).astype(bf16))
            outs[1].append((tn(ds, q) * factor).astype(bf16))
        images.append(jnp.concatenate(outs[0] + outs[1] + outs[2], 1))
    return jnp.concatenate(images, 0) if len(images) > 1 else images[0]


def same_image(role, length, context):
    row = lax.broadcasted_iota(jnp.int32, (length, length), 0) // context
    column = lax.broadcasted_iota(jnp.int32, (length, length), 1) // context
    return (row == column) | (role != 0)


def encoder_attend_kernel(
    edge, unit, context, head_size, kept,
    role_ref, patch_ref, base_ref, emb_ref, order_ref, w_ref, vec_ref,
    mid_ref, resid_ref, normed_ref, rows_ref, att_ref, x_ref, h_ref,
):
    step = pl.program_id(0)
    groups = pl.num_programs(0) // 2
    side = 2
    wide = side * edge
    pix = patch_ref.shape[2]
    columns = wide // 4

    @pl.when(step == 0)
    def _():
        x_ref[...] = base_ref[...]

    @pl.when(step < groups)
    def _():
        ordered = sum(
            nn(order_ref[:, m * edge : (m + 1) * edge], emb_ref[0, :, m * pix : (m + 1) * pix])
            for m in range(side)
        ).astype(bf16)
        x_ref[...] += nt_(patch_ref[0], ordered)

    @pl.when(step == groups - 1)
    def _():
        values = x_ref[...]
        resid_ref[...] = values[:kept]
        low = layer_norm(values, vec_ref[0:1], vec_ref[1:2]).astype(bf16)
        h_ref[...] = low
        normed_ref[...] = low[:kept]

    @pl.when(step >= groups)
    def _():
        rows = sum(
            nn(h_ref[:, r * edge : (r + 1) * edge], w_ref[0, :, r * wide : r * wide + 3 * columns])
            for r in range(side)
        ).astype(bf16)
        rows_ref[0] = rows[:kept]
        att = attend(rows, head_size, unit, same_image(role_ref[0], unit, context))
        att_ref[0] = att[:kept]
        for r in range(side):
            x_ref[:, r * edge : (r + 1) * edge] += nt_(
                att, w_ref[0, :, r * wide + 3 * columns : (r + 1) * wide]
            )

    @pl.when(step == 2 * groups - 1)
    def _():
        mid_ref[...] = x_ref[...]


def encoder_feed_kernel(
    edge, kept, mid_ref, up_ref, down_ref, vec_ref, pick_ref, swap_ref,
    out_ref, normed_ref, hidden_ref, feat_ref, target_ref, x_ref, h_ref,
):
    step = pl.program_id(0)
    groups = pl.num_programs(0)
    side = 2
    wide = side * edge

    @pl.when(step == 0)
    def _():
        values = mid_ref[...]
        x_ref[...] = values
        low = layer_norm(values, vec_ref[2:3], vec_ref[3:4]).astype(bf16)
        h_ref[...] = low
        normed_ref[...] = low[:kept]

    hidden = sum(
        nn(h_ref[:, r * edge : (r + 1) * edge], up_ref[0, :, r * wide : (r + 1) * wide])
        for r in range(side)
    )
    hidden_ref[0] = hidden[:kept]
    active = gelu_parts(hidden)[0].astype(bf16)
    for r in range(side):
        x_ref[:, r * edge : (r + 1) * edge] += nt_(
            active, down_ref[0, :, r * wide : (r + 1) * wide]
        )

    @pl.when(step == groups - 1)
    def _():
        values = x_ref[...]
        out_ref[...] = values[:kept]
        final = layer_norm(values, vec_ref[4:5], vec_ref[5:6])
        encoded = final[:kept].astype(bf16)
        target = norm_parts(final)[0].astype(bf16)
        picked = nn(pick_ref[...], target).astype(bf16)
        for t in range(swap_ref.shape[0]):
            feat_ref[t] = nn(encoded, swap_ref[t]).astype(bf16)
            target_ref[t] = nn(picked, swap_ref[t]).astype(bf16)


def put(grad_ref, t, columns, value):
    grad_ref[t, :, columns] = value.astype(bf16)


def predictor_kernel(
    share, context, players, head_size, denominator,
    feat_ref, target_ref, base_ref, w_ref, vec_ref, swap_ref,
    grad_ref, vec_grad_ref, loss_ref, back_ref,
    x_ref, mid_ref, h_ref, h2_ref, rows_ref, att_ref, hidden_ref, acc_ref, d_ref, low_ref, f_ref,
):
    groups = w_ref.shape[0]
    edge = w_ref.shape[1]
    length = base_ref.shape[0] // share
    quarter = feat_ref.shape[2]
    columns = edge // 4
    last = 3 * players * edge
    in_cols = slice(last, last + quarter)
    out_cols = slice(last + quarter, last + 2 * quarter)

    def span(number):
        return slice(number * edge, (number + 1) * edge)

    vec_grad_ref[...] = jnp.zeros_like(vec_grad_ref)

    projected = sum(nt_(feat_ref[t], w_ref[t, :, in_cols]) for t in range(groups))
    x_ref[0] = base_ref[...]
    for i in range(share):
        x_ref[0, i * length : i * length + context] += projected[i * context : (i + 1) * context]

    for j in range(players):
        values = x_ref[j]
        h_ref[j] = layer_norm(values, vec_ref[4 * j : 4 * j + 1], vec_ref[4 * j + 1 : 4 * j + 2]).astype(bf16)
        mid_ref[j] = values

        @pl.loop(0, groups)
        def _(t, j=j):
            rows = nn(h_ref[j], w_ref[t, :, 3 * j * edge : 3 * j * edge + 3 * columns]).astype(bf16)
            rows_ref[j, t] = rows
            att = attend(rows, head_size, length, None)
            att_ref[j, t] = att
            mid_ref[j] += nt_(att, w_ref[t, :, 3 * j * edge + 3 * columns : (3 * j + 1) * edge])

        values = mid_ref[j]
        h2_ref[j] = layer_norm(values, vec_ref[4 * j + 2 : 4 * j + 3], vec_ref[4 * j + 3 : 4 * j + 4]).astype(bf16)
        x_ref[j + 1] = values

        @pl.loop(0, groups)
        def _(t, j=j):
            hidden = nn(h2_ref[j], w_ref[t, :, span(3 * j + 1)])
            hidden_ref[j, t] = hidden
            x_ref[j + 1] += nt_(gelu_parts(hidden)[0].astype(bf16), w_ref[t, :, span(3 * j + 2)])

    final_gain = vec_ref[4 * players : 4 * players + 1]
    final = layer_norm(x_ref[players], final_gain, vec_ref[4 * players + 1 : 4 * players + 2]).astype(bf16)
    f_ref[...] = jnp.concatenate(
        [final[i * length + context : (i + 1) * length] for i in range(share)], 0
    )
    total = jnp.zeros((1, 1), f32)
    grad_f = jnp.zeros(f_ref.shape, f32)
    for t in range(groups):
        out_w = w_ref[t, :, out_cols]
        gap = nn(f_ref[...], out_w) - target_ref[t].astype(f32)
        size = jnp.abs(gap)
        terms = jnp.where(size < 1.0, 0.5 * gap * gap, size - 0.5)
        total += jnp.sum(jnp.sum(terms, 1, keepdims=True), 0, keepdims=True)
        grad_pred = (jnp.clip(gap, -1.0, 1.0) * (1.0 / denominator)).astype(bf16)
        put(grad_ref, t, out_cols, tn(f_ref[...], grad_pred))
        grad_f += nt_(grad_pred, out_w)
    loss_ref[...] = jnp.broadcast_to(total * (1.0 / denominator), loss_ref.shape)
    d_ref[...] = jnp.zeros_like(d_ref)
    tail = length - context
    for i in range(share):
        d_ref[i * length + context : (i + 1) * length] = grad_f[i * tail : (i + 1) * tail]
    grad, gain_g, shift_g = norm_backward(d_ref[...], x_ref[players], final_gain)
    d_ref[...] = grad
    vec_grad_ref[4 * players : 4 * players + 1] = gain_g
    vec_grad_ref[4 * players + 1 : 4 * players + 2] = shift_g

    for j in reversed(range(players)):
        low_ref[...] = d_ref[...].astype(bf16)
        acc_ref[...] = jnp.zeros_like(acc_ref)

        @pl.loop(0, groups)
        def _(t, j=j):
            active, slope = gelu_parts(hidden_ref[j, t])
            low = low_ref[...]
            put(grad_ref, t, span(3 * j + 2), tn(low, active.astype(bf16)))
            grad_hidden = (nn(low, w_ref[t, :, span(3 * j + 2)]) * slope).astype(bf16)
            put(grad_ref, t, span(3 * j + 1), tn(h2_ref[j], grad_hidden))
            acc_ref[...] += nt_(grad_hidden, w_ref[t, :, span(3 * j + 1)])

        grad, gain_g, shift_g = norm_backward(acc_ref[...], mid_ref[j], vec_ref[4 * j + 2 : 4 * j + 3])
        vec_grad_ref[4 * j + 2 : 4 * j + 3] = gain_g
        vec_grad_ref[4 * j + 3 : 4 * j + 4] = shift_g
        grad = d_ref[...] + grad
        d_ref[...] = grad
        low_ref[...] = grad.astype(bf16)
        acc_ref[...] = jnp.zeros_like(acc_ref)

        @pl.loop(0, groups)
        def _(t, j=j):
            low = low_ref[...]
            attn_w = w_ref[t, :, span(3 * j)]
            grad_att = nn(low, attn_w[:, 3 * columns :]).astype(bf16)
            grad_rows = attend_back(rows_ref[j, t], grad_att, head_size, length, None)
            grad_w = jnp.concatenate([tn(h_ref[j], grad_rows), tn(low, att_ref[j, t])], 1)
            put(grad_ref, t, span(3 * j), grad_w)
            acc_ref[...] += nt_(grad_rows, attn_w[:, : 3 * columns])

        grad, gain_g, shift_g = norm_backward(acc_ref[...], x_ref[j], vec_ref[4 * j : 4 * j + 1])
        vec_grad_ref[4 * j : 4 * j + 1] = gain_g
        vec_grad_ref[4 * j + 1 : 4 * j + 2] = shift_g
        d_ref[...] += grad

    mask_grad = jnp.zeros((1, edge), f32)
    for i in range(share):
        mask_grad += jnp.sum(d_ref[i * length + context : (i + 1) * length], 0, keepdims=True)
    vec_grad_ref[4 * players + 2 : 4 * players + 3] = mask_grad
    low = jnp.concatenate(
        [d_ref[i * length : i * length + context] for i in range(share)], 0
    ).astype(bf16)
    back = jnp.zeros((low.shape[0], swap_ref.shape[1]), f32)
    for t in range(groups):
        put(grad_ref, t, in_cols, tn(low, feat_ref[t]))
        back += nt_(nn(low, w_ref[t, :, in_cols]).astype(bf16), swap_ref[t])
    back_ref[...] = back.astype(bf16)


def encoder_feed_back_kernel(
    edge, back_ref, out_ref, mid_ref, normed_ref, hidden_ref, up_ref, down_ref, vec_ref,
    up_grad, down_grad, grad_ref, vec_grad_ref, d_ref, low_ref, acc_ref,
):
    step = pl.program_id(0)
    groups = pl.num_programs(0)
    wide = 2 * edge

    @pl.when(step == 0)
    def _():
        grad, gain_g, shift_g = norm_backward(back_ref[...].astype(f32), out_ref[...], vec_ref[4:5])
        d_ref[...] = grad
        low_ref[...] = grad.astype(bf16)
        acc_ref[...] = jnp.zeros_like(acc_ref)
        vec_grad_ref[...] = jnp.zeros_like(vec_grad_ref)
        vec_grad_ref[4:5] = gain_g
        vec_grad_ref[5:6] = shift_g

    active, slope = gelu_parts(hidden_ref[0])
    active = active.astype(bf16)
    grad_hidden = sum(
        nn(low_ref[:, r * edge : (r + 1) * edge], down_ref[0, :, r * wide : (r + 1) * wide])
        for r in range(2)
    )
    grad_hidden = (grad_hidden * slope).astype(bf16)
    for r in range(2):
        mine = slice(r * edge, (r + 1) * edge)
        columns = slice(r * wide, (r + 1) * wide)
        put(down_grad, 0, columns, tn(low_ref[:, mine], active))
        put(up_grad, 0, columns, tn(normed_ref[:, mine], grad_hidden))
        acc_ref[:, mine] += nt_(grad_hidden, up_ref[0, :, columns])

    @pl.when(step == groups - 1)
    def _():
        grad, gain_g, shift_g = norm_backward(acc_ref[...], mid_ref[...], vec_ref[2:3])
        grad_ref[...] = d_ref[...] + grad
        vec_grad_ref[2:3] = gain_g
        vec_grad_ref[3:4] = shift_g


def encoder_attend_back_kernel(
    edge, unit, context, head_size,
    role_ref, mid_grad_ref, resid_ref, normed_ref, rows_ref, att_ref, w_ref, patch_ref, order_ref,
    vec_ref, grad_ref, vec_grad_ref, low_ref, acc_ref,
):
    step = pl.program_id(0)
    groups = pl.num_programs(0) // 2
    wide = 2 * edge
    columns = wide // 4
    pix = patch_ref.shape[2]

    @pl.when(step == 0)
    def _():
        low_ref[...] = mid_grad_ref[...].astype(bf16)
        acc_ref[...] = jnp.zeros_like(acc_ref)

    @pl.when(step < groups)
    def _():
        grad_att = sum(
            nn(
                low_ref[:, r * edge : (r + 1) * edge],
                w_ref[0, :, r * wide + 3 * columns : (r + 1) * wide],
            )
            for r in range(2)
        ).astype(bf16)
        allowed = same_image(role_ref[0], unit, context)
        grad_rows = attend_back(rows_ref[0], grad_att, head_size, unit, allowed)
        for r in range(2):
            mine = slice(r * edge, (r + 1) * edge)
            grad_w = jnp.concatenate(
                [tn(normed_ref[:, mine], grad_rows), tn(low_ref[:, mine], att_ref[0])], 1
            )
            put(grad_ref, step, slice(r * wide, (r + 1) * wide), grad_w)
            acc_ref[:, mine] += nt_(grad_rows, w_ref[0, :, r * wide : r * wide + 3 * columns])

    @pl.when(step == groups - 1)
    def _():
        grad, gain_g, shift_g = norm_backward(acc_ref[...], resid_ref[...], vec_ref[0:1])
        grad = mid_grad_ref[...] + grad
        low_ref[...] = nn(grad.astype(bf16), order_ref[...]).astype(bf16)
        vec_grad_ref[...] = jnp.zeros_like(vec_grad_ref)
        vec_grad_ref[0:1] = gain_g
        vec_grad_ref[1:2] = shift_g
        vec_grad_ref[6:7] = jnp.sum(grad, 0, keepdims=True)

    @pl.when(step >= groups)
    def _():
        grad_w = jnp.concatenate(
            [tn(low_ref[:, r * edge : (r + 1) * edge], patch_ref[0]) for r in range(2)], 1
        )
        put(grad_ref, step - groups, slice(2 * wide, 2 * wide + 2 * pix), grad_w)


def split(values):
    high = values.astype(bf16)
    return high, (values - high.astype(f32)).astype(bf16)


def shampoo_kernel(
    grad_ref, weight_ref, left_ref, right_ref, root_left_ref, root_right_ref, teacher_ref,
    grad_out, weight_out, left_out, right_out, teacher_out,
):
    low = grad_ref[0]
    grad_out[0, 0] = low.astype(f32)
    left_out[0, 0] = 0.95 * left_ref[0, 0] + 0.05 * nt_(low, low)
    right_out[0, 0] = 0.95 * right_ref[0, 0] + 0.05 * tn(low, low)
    high, rest = split(root_left_ref[0, 0])
    side = nn(high, low) + nn(rest, low)
    high, rest = split(side)
    root_high, root_rest = split(root_right_ref[0, 0])
    step = nn(high, root_high) + nn(high, root_rest) + nn(rest, root_high)
    mean = jnp.mean(jnp.mean(step * step, 1, keepdims=True), 0, keepdims=True)
    step = step * lax.rsqrt(mean + 1e-06)
    weight = weight_ref[0, 0]
    new = weight - 0.05 * (step + 0.05 * weight)
    weight_out[0, 0] = new
    teacher_out[0, 0] = 0.7 * teacher_ref[0, 0] + 0.3 * new


MESH = pl.DeviceIdType.MESH


def flip(place, bits):
    bit = 1
    while bit <= bits:
        if bits & bit:
            place = place + bit * (1 - 2 * lax.rem(lax.div(place, bit), 2))
        bit *= 2
    return place


def remote(source, target, send_sem, recv_sem, device):
    return pltpu.make_async_remote_copy(
        src_ref=source, dst_ref=target, send_sem=send_sem, recv_sem=recv_sem,
        device_id=device, device_id_type=MESH,
    )


def greet(routes, d, z):
    barrier = pltpu.get_barrier_semaphore()
    peers = [(d, flip(z, r)) for r in range(1, routes.nt)]
    peers += [routes.partner(s, d, z) for s in range(routes.stages + 1)]
    for peer in peers:
        pl.semaphore_signal(barrier, inc=1, device_id=peer, device_id_type=MESH)
    pl.semaphore_wait(barrier, len(peers))


def guarded(condition, body):
    if condition is None:
        body()
    else:
        pl.when(condition)(body)


class Gather:
    ahead = 2

    def __init__(self, routes, widths, few_rows, sources, mats, sems):
        self.routes, self.widths, self.few_rows = routes, widths, few_rows
        self.own, self.other, self.pred, self.patch_in, self.rows = sources
        self.mats = mats
        self.sems = sems
        self.d, self.z = lax.axis_index("dp"), lax.axis_index("tensor")
        self.role = lax.rem(self.z, 2)
        self.last = len(widths) - 1
        self.items = [(m, r) for m in range(len(widths)) for r in range(routes.nt)]
        self.span = len(self.items) + self.ahead * routes.stages

    def peer(self, r):
        return self.d, flip(self.z, r)

    def peer_role(self, r):
        return lax.rem(flip(self.z, r), 2)

    def source(self, m, r):
        if m == self.last:
            return self.pred
        ref = self.own if r % 2 == 0 else self.other
        return ref.at[:, pl.ds(sum(self.widths[:m]), self.widths[m])]

    def across(self, m, r):
        send, recv = self.sems[0], self.sems[1]
        return remote(
            self.source(m, r), self.mats[m].at[r, 0], send.at[m, r], recv.at[m, r], self.peer(r)
        )

    def local(self, m):
        return pltpu.make_async_copy(self.source(m, 0), self.mats[m].at[0, 0], self.sems[2].at[m])

    def patch(self, r, rows):
        return remote(
            self.patch_in.at[r, pl.ds(0, rows)], self.rows.at[r, pl.ds(0, rows)],
            self.sems[3].at[r], self.sems[4].at[r], self.peer(r),
        )

    def own_patch(self):
        return pltpu.make_async_copy(
            self.patch_in.at[0], self.rows.at[0], self.sems[2].at[self.last + 1]
        )

    def stage(self, m, r, s):
        size = 1 << s
        return remote(
            self.mats[m].at[r, pl.ds(0, size)], self.mats[m].at[r, pl.ds(size, size)],
            self.sems[5].at[m, r, s], self.sems[6].at[m, r, s],
            self.routes.partner(s, self.d, self.z),
        )

    def mine(self, m):
        return self.role == 1 if m == self.last else None

    def theirs(self, m, r):
        return self.peer_role(r) == 1 if m == self.last else None

    def start(self):
        greet(self.routes, self.d, self.z)
        for m in range(len(self.widths)):
            guarded(self.mine(m), lambda m=m: self.local(m).start())
            for r in range(1, self.routes.nt):
                guarded(self.theirs(m, r), lambda m=m, r=r: self.across(m, r).start())
            if m == 0:
                self.own_patch().start()
                for r in range(1, self.routes.nt):
                    for role, rows in ((0, self.few_rows), (1, self.patch_in.shape[1])):
                        pl.when(self.peer_role(r) == role)(
                            lambda r=r, rows=rows: self.patch(r, rows).start()
                        )

    def advance(self, m, r, s):
        if s:
            self.stage(m, r, s - 1).wait_recv()
        elif r:
            self.across(m, r).wait_recv()
        else:
            self.local(m).wait()
        self.stage(m, r, s).start()

    def step(self, n):
        for s in reversed(range(self.routes.stages + 1)):
            if 0 <= n - self.ahead * s < len(self.items):
                m, r = self.items[n - self.ahead * s]
                guarded(self.mine(m), lambda m=m, r=r, s=s: self.advance(m, r, s))

    def arrive(self, m, r):
        self.stage(m, r, self.routes.stages).wait_recv()

    def wait_patches(self):
        self.own_patch().wait()
        for r in range(1, self.routes.nt):
            for role, rows in ((0, self.few_rows), (1, self.patch_in.shape[1])):
                pl.when(self.role == role)(lambda r=r, rows=rows: self.patch(r, rows).wait_recv())

    def finish(self):
        for r in range(1, self.routes.nt):
            for role, rows in ((0, self.few_rows), (1, self.patch_in.shape[1])):
                pl.when(self.peer_role(r) == role)(
                    lambda r=r, rows=rows: self.patch(r, rows).wait_send()
                )
        for m, r in self.items:

            def sent(m=m, r=r):
                for s in range(self.routes.stages + 1):
                    self.stage(m, r, s).wait_send()

            guarded(self.mine(m), sent)
            if r:
                guarded(self.theirs(m, r), lambda m=m, r=r: self.across(m, r).wait_send())


def gather_kernel(
    routes, widths, few_rows, own_ref, other_ref, pred_ref, patch_ref,
    attn_ref, up_ref, down_ref, players_ref, rows_ref, *sems,
):
    gather = Gather(
        routes, widths, few_rows, (own_ref, other_ref, pred_ref, patch_ref, rows_ref),
        (attn_ref, up_ref, down_ref, players_ref), sems,
    )
    gather.start()
    for n in range(gather.span):
        gather.step(n)
    for m, r in gather.items:
        guarded(gather.mine(m), lambda m=m, r=r: gather.arrive(m, r))
    gather.wait_patches()
    gather.finish()


def forward_kernel(
    routes, widths, unit, context, head_size,
    own_ref, other_ref, pred_ref, patch_ref, base_ref, order_ref, vec_ref, pick_ref, swap_ref,
    attn_out, up_out, down_out, players_out, rows_out, mid_out, resid_out, normed_out, qkv_out,
    att_out, out_out, normed2_out, hidden_out, feat_out, target_out,
    attn_ref, up_ref, down_ref, players_ref, rows_ref, x_ref, h_ref, sent_ref, feat_ref,
    back_sem, feat_send, feat_recv, *sems,
):
    nt, nd = routes.nt, routes.nd
    mats = (attn_ref, up_ref, down_ref, players_ref)
    outs = (attn_out, up_out, down_out, players_out)
    kept = resid_out.shape[0]
    gather = Gather(
        routes, widths, kept, (own_ref, other_ref, pred_ref, patch_ref, rows_ref), mats, sems
    )
    role = gather.role
    edge = nd * attn_ref.shape[2]
    side = 2
    wide = side * edge
    pix = rows_ref.shape[2]
    columns = wide // 4

    def matrix(ref, t, first, width):
        return ref[t, :, :, first : first + width].reshape(edge, width)

    def to_hbm(m, r):
        return pltpu.make_async_copy(mats[m].at[r], outs[m].at[r], back_sem.at[m, r])

    def feat_copy():
        return remote(sent_ref, feat_ref, feat_send, feat_recv, gather.peer(1))

    def embed():
        gather.wait_patches()
        x_ref[...] = base_ref[...]

        @pl.loop(0, nt)
        def _(t):
            ordered = sum(
                nn(
                    order_ref[:, m * edge : (m + 1) * edge],
                    matrix(attn_ref, t, side * wide + m * pix, pix),
                )
                for m in range(side)
            ).astype(bf16)
            x_ref[...] += nt_(rows_ref[t], ordered)

        values = x_ref[...]
        resid_out[...] = values[:kept]
        low = layer_norm(values, vec_ref[0:1], vec_ref[1:2]).astype(bf16)
        h_ref[...] = low
        normed_out[...] = low[:kept]

    def attention(t):
        rows = sum(
            nn(h_ref[:, r * edge : (r + 1) * edge], matrix(attn_ref, t, r * wide, 3 * columns))
            for r in range(side)
        ).astype(bf16)
        qkv_out[t] = rows[:kept]
        att = attend(rows, head_size, unit, same_image(role, unit, context))
        att_out[t] = att[:kept]
        for r in range(side):
            x_ref[:, r * edge : (r + 1) * edge] += nt_(
                att, matrix(attn_ref, t, r * wide + 3 * columns, columns)
            )

    def middle():
        values = x_ref[...]
        mid_out[...] = values[:kept]
        low = layer_norm(values, vec_ref[2:3], vec_ref[3:4]).astype(bf16)
        h_ref[...] = low
        normed2_out[...] = low[:kept]

    def feed(t):
        hidden = sum(
            nn(h_ref[:, r * edge : (r + 1) * edge], matrix(up_ref, t, r * wide, wide))
            for r in range(side)
        )
        hidden_out[t] = hidden[:kept]
        active = gelu_parts(hidden)[0].astype(bf16)
        for r in range(side):
            x_ref[:, r * edge : (r + 1) * edge] += nt_(
                active, matrix(down_ref, t, r * wide, wide)
            )

    def last():
        values = x_ref[...]
        out_out[...] = values[:kept]
        final = layer_norm(values, vec_ref[4:5], vec_ref[5:6])

        @pl.when(role == 0)
        def _():
            encoded = final[:kept].astype(bf16)
            for t in range(nt):
                sent_ref[t] = nn(encoded, swap_ref[t]).astype(bf16)
            feat_copy().start()

        @pl.when(role == 1)
        def _():
            target = norm_parts(final)[0].astype(bf16)
            picked = nn(pick_ref[...], target).astype(bf16)
            for t in range(nt):
                target_out[t] = nn(picked, swap_ref[t]).astype(bf16)

        @pl.when(role == 0)
        def _():
            target_out[...] = jnp.zeros_like(target_out)

    lag = gather.ahead * (routes.stages + 1)
    attn_at = nt - 1 + lag
    feed_at = 3 * nt - 1 + lag
    steps = len(gather.items) + lag
    gather.start()

    @pl.loop(0, steps)
    def _(n):
        for k in range(steps):

            @pl.when(n == k)
            def _(k=k):
                gather.step(k)
                if k >= lag:
                    m, r = gather.items[k - lag]

                    def here(m=m, r=r):
                        gather.arrive(m, r)
                        to_hbm(m, r).start()

                    guarded(gather.mine(m), here)

        pl.when(n == attn_at)(embed)

        @pl.when((n > attn_at) & (n <= attn_at + nt))
        def _():
            attention(n - attn_at - 1)

        pl.when(n == feed_at)(middle)

        @pl.when((n >= feed_at) & (n < feed_at + nt))
        def _():
            feed(n - feed_at)

        pl.when(n == feed_at + nt - 1)(last)

    rows_out[...] = rows_ref[:, :kept]

    @pl.when(role == 0)
    def _():
        feat_copy().wait_send()
        feat_out[...] = jnp.zeros_like(feat_out)

    @pl.when(role == 1)
    def _():
        feat_copy().wait_recv()
        feat_out[...] = feat_ref[...]

    gather.finish()
    for m, r in gather.items:
        guarded(gather.mine(m), lambda m=m, r=r: to_hbm(m, r).wait())


def reduce_kernel(
    routes, attn_cols, down_ref, up_ref, attn_ref, pred_ref, block_ref, emb_ref,
    core0, core1, core2, later0, later1, later2, enc_in, pred_in, load,
    load_sem, core_send, core_recv, stage_send, stage_recv, z_send, z_recv,
):
    d, z = lax.axis_index("dp"), lax.axis_index("tensor")
    nt, stages = routes.nt, routes.stages
    middle = routes.nd // 2
    role = lax.rem(z, 2)
    cores = [core0, core1, core2]
    laters = [later0, later1, later2]
    greet(routes, d, z)

    def run(kind, sources, incoming, starts):
        items = [(j, r) for j in range(len(sources)) for r in reversed(range(nt))]

        def part(j, r, first):
            ref, start, width = sources[j]
            return ref.at[r, pl.ds(first, middle), :, pl.ds(start, width)]

        def to_core(j, r):
            return remote(
                part(j, r, middle), cores[j].at[r, :, :, pl.ds(0, sources[j][2])],
                core_send.at[j, r], core_recv.at[j, r], routes.partner(stages, d, z),
            )

        def own(i):
            j, r = items[i]
            return pltpu.make_async_copy(
                part(j, r, 0), load.at[i % 2, :, :, pl.ds(0, sources[j][2])], load_sem.at[i % 2]
            )

        def stage(j, r, s):
            size = 1 << s
            return remote(
                cores[j].at[r, pl.ds(size, size), :, pl.ds(0, sources[j][2])],
                laters[j].at[r, pl.ds(size - 1, size), :, pl.ds(0, sources[j][2])],
                stage_send.at[j, r, s], stage_recv.at[j, r, s], routes.partner(s, d, z),
            )

        def across(j, r):
            return remote(
                cores[j].at[r, 0, :, pl.ds(0, sources[j][2])],
                incoming.at[r, :, pl.ds(starts[j], sources[j][2])],
                z_send.at[kind, j, r], z_recv.at[kind, j, r], (d, flip(z, r)),
            )

        def add(i, q):
            j, r = items[i]
            width = sources[j][2]
            if q == 0:
                own(i).wait()
                to_core(j, r).wait_recv()

                @pl.loop(0, middle)
                def _(k):
                    total = cores[j][r, k, :, 0:width].astype(f32)
                    total += load[i % 2, k, :, 0:width].astype(f32)
                    cores[j][r, k, :, 0:width] = total.astype(bf16)

                if i + 2 < len(items):
                    own(i + 2).start()
            else:
                s = stages - q
                stage(j, r, s).wait_recv()

                @pl.loop(0, 1 << s)
                def _(k):
                    total = cores[j][r, k, :, 0:width].astype(f32)
                    total += laters[j][r, k + ((1 << s) - 1), :, 0:width].astype(f32)
                    cores[j][r, k, :, 0:width] = total.astype(bf16)

            if q < stages:
                stage(j, r, stages - q - 1).start()
            elif r:
                across(j, r).start()

        for i in range(min(2, len(items))):
            own(i).start()
        for j, r in items:
            to_core(j, r).start()
        for n in range(len(items) + stages):
            for q in reversed(range(stages + 1)):
                if 0 <= n - q < len(items):
                    add(n - q, q)
        for j, r in items:
            to_core(j, r).wait_send()
            for s in range(stages):
                stage(j, r, s).wait_send()
            if r:
                across(j, r).wait_send()

    wide = down_ref.shape[3]
    all_cols = attn_ref.shape[3]
    pred_cols = pred_ref.shape[3]
    encoder = [(down_ref, 0, wide), (up_ref, 0, wide), (attn_ref, 0, all_cols)]
    encoder_at = [0, wide, 2 * wide]
    players = [(pred_ref, 0, wide), (pred_ref, wide, pred_cols - wide)]
    players_at = [0, wide]

    @pl.when(role == 0)
    def _():
        run(0, encoder, enc_in, encoder_at)

    @pl.when(role == 1)
    def _():
        run(1, players, pred_in, players_at)

    def collect(kind, sources, incoming, starts, put):
        for j, (_, _, width) in enumerate(sources):
            place = incoming.at[:, :, pl.ds(starts[j], width)]

            def arrive(r, j=j, width=width):
                pltpu.make_async_remote_copy(
                    src_ref=cores[j].at[r, 0, :, pl.ds(0, width)],
                    dst_ref=incoming.at[r, :, pl.ds(starts[j], width)],
                    send_sem=z_send.at[kind, j, r], recv_sem=z_recv.at[kind, j, r],
                    device_id=(d, flip(z, r)), device_id_type=MESH,
                ).wait_recv()

            del place

            @pl.when(role == kind)
            def _(j=j, width=width, arrive=arrive):
                total = cores[j][0, 0, :, 0:width].astype(f32)
                for r in range(2, nt, 2):
                    arrive(r)
                    total += incoming[r, :, starts[j] : starts[j] + width].astype(f32)
                put(j, total)

            @pl.when(role != kind)
            def _(j=j, width=width, arrive=arrive):
                total = None
                for r in range(1, nt, 2):
                    arrive(r)
                    got = incoming[r, :, starts[j] : starts[j] + width].astype(f32)
                    total = got if total is None else total + got
                put(j, total)

    def put_encoder(j, total):
        if j == 2:
            block_ref[:, 0:attn_cols] = total[:, :attn_cols].astype(bf16)
            emb_ref[...] = total[:, attn_cols:]
        else:
            first = attn_cols + (1 - j) * wide
            block_ref[:, first : first + wide] = total.astype(bf16)

    def put_players(j, total):
        first = attn_cols + 2 * wide + players_at[j]
        block_ref[:, first : first + total.shape[1]] = total.astype(bf16)

    collect(1, players, pred_in, players_at, put_players)
    collect(0, encoder, enc_in, encoder_at, put_encoder)
    end = attn_cols + 2 * wide + pred_cols
    block_ref[:, end:] = jnp.zeros((block_ref.shape[0], block_ref.shape[1] - end), bf16)


def whole(shape):
    return pl.BlockSpec(shape, lambda *_: (0,) * len(shape))


def by_group(shape):
    return pl.BlockSpec((1,) + shape, lambda t: (t, 0, 0))


def compiled():
    return pltpu.CompilerParams(
        dimension_semantics=("arbitrary",), vmem_limit_bytes=KERNEL_BYTES
    )


def cost(flops, moved):
    return pl.CostEstimate(flops=int(flops), bytes_accessed=int(moved), transcendentals=0)


def sincos(cell_index, columns):
    quarter = columns // 4
    frequency = 1.0 / 10000.0 ** (jnp.arange(quarter).astype(f32) / quarter)
    col_angle = (cell_index % SIDE).astype(f32)[..., None] * frequency
    row_angle = (cell_index // SIDE).astype(f32)[..., None] * frequency
    return jnp.concatenate(
        [jnp.sin(col_angle), jnp.cos(col_angle), jnp.sin(row_angle), jnp.cos(row_angle)], -1
    )


def adamw(master, moment, second, gradient, step_rate, weight_decay):
    moment = 0.9 * moment + 0.1 * gradient
    second = 0.999 * second + 0.001 * gradient * gradient
    unbiased_first = moment / (1.0 - 0.9**STEP)
    unbiased_second = second / (1.0 - 0.999**STEP)
    return (
        master
        - step_rate
        * (unbiased_first / (jnp.sqrt(unbiased_second) + 1e-08) + weight_decay * master),
        moment,
        second,
    )


class Routes:
    def __init__(self, nd, nt):
        self.nd, self.nt = nd, nt
        self.low_bits = [1 << s for s in range(1, nd.bit_length() - 1)]
        self.stages = len(self.low_bits)

    def order(self, core):
        return self.low_bits if core == 0 else self.low_bits[::-1]

    def pairs(self, target, keep):
        found = []
        for d in range(self.nd):
            for z in range(self.nt):
                if keep(d, z):
                    d2, z2 = target(d, z)
                    found.append((d * self.nt + z, d2 * self.nt + z2))
        return found

    def partner(self, number, d, z):
        if number == self.stages:
            return flip(d, 1), z
        core = lax.rem(d, 2)
        ends = flip(d, self.order(0)[number]), flip(d, self.order(1)[number])
        return ends[0] + core * (ends[1] - ends[0]), z

    def across(self, r, values, from_role=None):
        def keep(d, z):
            return from_role is None or z % 2 == from_role

        return lax.ppermute(values, AXES, self.pairs(lambda d, z: (d, z ^ r), keep))

    def holders(self, d):
        place = jnp.arange(self.nd, dtype=jnp.int32)
        held = d ^ (place >> self.stages)
        core = held & 1
        for s in range(self.stages):
            bit = (place >> s) & 1
            held = held ^ (bit * jnp.where(core == 0, self.order(0)[s], self.order(1)[s]))
        return held

    def total(self, values):
        for bit in [1] + self.low_bits:
            values = values + lax.ppermute(
                values, AXES, self.pairs(lambda d, z, b=bit: (d ^ b, z), lambda d, z: True)
            )
        r = 1
        while r < self.nt:
            values = values + self.across(r, values)
            r *= 2
        return values


def shards(
    patches,
    ctx_idx,
    tgt_idx,
    owner,
    weights,
    stats_left,
    stats_right,
    root_left,
    root_right,
    teacher_slot_blocks,
    embed,
    embed_m,
    embed_v,
    teacher_embed,
    enc_vectors,
    enc_m,
    enc_v,
    pred_vectors,
    pred_m,
    pred_v,
    teacher_vectors,
):
    nt = lax.axis_size("tensor")
    nd = lax.axis_size("dp")
    routes = Routes(nd, nt)
    half = nt // 2
    d = lax.axis_index("dp")
    z = lax.axis_index("tensor")
    role = z % 2
    student_role = role == 0
    images, npatches, pix_part = patches.shape
    slots = weights.shape[1]
    edge = weights.shape[-1]
    slot_count = slots * nd
    block_count = owner.shape[0]
    width = enc_vectors.shape[1]
    narrow = pred_vectors.shape[1]
    players = (pred_vectors.shape[0] - 3) // 4
    side = width // edge
    teach_count = 3 * side * side
    quarter = width // nt
    context_len = ctx_idx.shape[1]
    target_len = tgt_idx.shape[1]
    seq_len = context_len + target_len
    share = images // half
    rows_part = edge // nd

    both = jnp.stack([weights[0], teacher_slot_blocks[0]]).astype(bf16)
    both = both.reshape(2, slots, nd, rows_part, edge)
    both = lax.all_to_all(both, "dp", split_axis=2, concat_axis=0, tiled=False)
    by_slot = both.transpose(1, 0, 2, 3, 4).reshape(2, slot_count, rows_part, edge)
    mine = by_slot[0][owner].transpose(1, 0, 2).reshape(rows_part, -1)
    teach = by_slot[1][owner[:teach_count]].transpose(1, 0, 2).reshape(rows_part, -1)

    mat = side * width

    def embed_rows(values):
        turned = values.astype(bf16).T.reshape(side, rows_part, pix_part)
        return turned.transpose(1, 0, 2).reshape(rows_part, -1)

    of_student = jnp.concatenate(
        [mine[:, :mat], embed_rows(embed), mine[:, mat : 3 * mat]], 1
    )
    of_teacher = jnp.concatenate([teach[:, :mat], embed_rows(teacher_embed), teach[:, mat:]], 1)
    own = jnp.where(student_role, of_student, of_teacher)
    other = jnp.where(student_role, of_teacher, of_student)
    pred_own = mine[:, 3 * mat :]

    holder = routes.holders(d)
    inside = jnp.arange(rows_part, dtype=jnp.int32)
    feat_p = (holder[:, None] * rows_part + inside[None, :]).reshape(-1)
    feat = jnp.concatenate([r * edge + feat_p for r in range(side)])
    one_hot = (feat[:, None] == jnp.arange(width)[None, :]).astype(f32)
    one_hot_p = (feat_p[:, None] == jnp.arange(narrow)[None, :]).astype(f32)

    def to_local(rows, hot):
        return jnp.einsum("nf,lf->nl", rows, hot, precision=exact, preferred_element_type=f32)

    def to_global(rows, hot):
        return jnp.einsum("nl,lf->nf", rows, hot, precision=exact, preferred_element_type=f32)

    vec = to_local(jnp.where(student_role, enc_vectors, teacher_vectors), one_hot)
    vec = jnp.pad(vec, ((0, 1), (0, 0)))
    pvec = to_local(pred_vectors, one_hot_p)
    pvec = jnp.pad(pvec, ((0, 16 - pvec.shape[0]), (0, 0)))
    pred_z = z - role + 1
    group_feat = (pred_z ^ jnp.arange(nt, dtype=jnp.int32))[:, None] * quarter + jnp.arange(
        quarter, dtype=jnp.int32
    )
    emb_feat = jnp.concatenate(
        [holder[:, None] * 2 * rows_part + m * rows_part + inside[None, :] for m in range(2)]
    ).reshape(-1)
    order = (feat[:, None] == emb_feat[None, :]).astype(bf16)
    swap = (feat[None, :, None] == group_feat[:, None, :]).astype(bf16)

    part = z // 2
    hot = (ctx_idx[:, :, None] == jnp.arange(npatches)[None, None, :]).astype(bf16)
    picked = jnp.einsum("gcn,gnp->gcp", hot, patches, preferred_element_type=f32).astype(bf16)

    def rows_for(target_z):
        where = (target_z // 2) * share
        ctx = lax.dynamic_slice_in_dim(picked, where, share, 0).reshape(-1, pix_part)
        every = lax.dynamic_slice_in_dim(patches, where, share, 0).reshape(-1, pix_part)
        padded = jnp.pad(ctx, ((0, every.shape[0] - ctx.shape[0]), (0, 0)))
        return jnp.where(target_z % 2 == 0, padded, every)

    patch_out = jnp.stack([rows_for(z ^ r) for r in range(nt)])
    my_ctx = lax.dynamic_slice_in_dim(ctx_idx, part * share, share, 0)
    my_tgt = lax.dynamic_slice_in_dim(tgt_idx, part * share, share, 0)
    full_rows = share * npatches
    ctx_rows = share * context_len
    tgt_rows = share * target_len
    ctx_places = jnp.pad(my_ctx.reshape(-1), (0, full_rows - ctx_rows))
    places = jnp.where(student_role, ctx_places, jnp.arange(full_rows) % npatches)
    table = to_local(sincos(jnp.arange(npatches), width), one_hot)
    table_p = to_local(sincos(jnp.arange(npatches), narrow), one_hot_p)
    base = table[places] + vec[6]
    tgt_places = (my_tgt + npatches * jnp.arange(share, dtype=jnp.int32)[:, None]).reshape(-1)
    pick = (tgt_places[:, None] == jnp.arange(full_rows)[None, :]).astype(bf16)
    widths = [mat + side * pix_part, mat, mat, mine.shape[1] - 3 * mat]
    any_space = pl.BlockSpec(memory_space=pl.ANY)
    dma = pltpu.SemaphoreType.DMA
    attn_cols = side * width
    columns = width // nt
    mat_shapes = [jax.ShapeDtypeStruct((nt, nd, rows_part, c), bf16) for c in widths]
    gather_sems = [
        dma((4, nt)),
        dma((4, nt)),
        dma((5,)),
        dma((nt,)),
        dma((nt,)),
        dma((4, nt, routes.stages + 1)),
        dma((4, nt, routes.stages + 1)),
    ]
    in_vmem = pl.BlockSpec(memory_space=VMEM)
    role_word = role.astype(jnp.int32).reshape(1)
    if rows_part % 16 == 0:
        results = pl.pallas_call(
            functools.partial(forward_kernel, routes, widths, npatches, context_len, HD),
            in_specs=[any_space] * 4 + [in_vmem] * 5,
            out_specs=[any_space] * 4 + [in_vmem] * 11,
            out_shape=mat_shapes
            + [
                jax.ShapeDtypeStruct((nt, ctx_rows, pix_part), bf16),
                jax.ShapeDtypeStruct((ctx_rows, width), f32),
                jax.ShapeDtypeStruct((ctx_rows, width), f32),
                jax.ShapeDtypeStruct((ctx_rows, width), bf16),
                jax.ShapeDtypeStruct((nt, ctx_rows, 3 * columns), bf16),
                jax.ShapeDtypeStruct((nt, ctx_rows, columns), bf16),
                jax.ShapeDtypeStruct((ctx_rows, width), f32),
                jax.ShapeDtypeStruct((ctx_rows, width), bf16),
                jax.ShapeDtypeStruct((nt, ctx_rows, width), f32),
                jax.ShapeDtypeStruct((nt, ctx_rows, quarter), bf16),
                jax.ShapeDtypeStruct((nt, tgt_rows, quarter), bf16),
            ],
            scratch_shapes=[VMEM(shape.shape, bf16) for shape in mat_shapes]
            + [
                VMEM((nt, full_rows, pix_part), bf16),
                VMEM((full_rows, width), f32),
                VMEM((full_rows, width), bf16),
                VMEM((nt, ctx_rows, quarter), bf16),
                VMEM((nt, ctx_rows, quarter), bf16),
                dma((4, nt)),
                dma(()),
                dma(()),
            ]
            + gather_sems,
            compiler_params=pltpu.CompilerParams(
                collective_id=0, has_side_effects=True, vmem_limit_bytes=KERNEL_BYTES
            ),
            cost_estimate=cost(14e9, 60e6),
            name="gather_and_encode",
        )(own, other, pred_own, patch_out, base, order, vec, pick, swap)
        gathered, results = results[:4], results[4:]
        patch_rows, middle, resid, normed_a, rows_a, att_a = results[:6]
        output, normed_f, hidden, feat_in, target = results[6:]
        attn_emb, up_w, down_t, pred_all = (g.reshape(nt, edge, -1) for g in gathered)
    else:
        attn_emb, up_w, down_t, pred_all, patch_rows = pl.pallas_call(
            functools.partial(gather_kernel, routes, widths, ctx_rows),
            in_specs=[any_space] * 4,
            out_specs=[any_space] * 5,
            out_shape=mat_shapes
            + [jax.ShapeDtypeStruct((nt, full_rows, pix_part), bf16)],
            scratch_shapes=gather_sems,
            compiler_params=pltpu.CompilerParams(collective_id=0, has_side_effects=True),
            cost_estimate=cost(0, 50e6),
            name="gather_weights",
        )(own, other, pred_own, patch_out)
        attn_emb, up_w, down_t, pred_all = (
            value.reshape(nt, edge, -1) for value in (attn_emb, up_w, down_t, pred_all)
        )
        middle, resid, normed_a, rows_a, att_a = pl.pallas_call(
            functools.partial(encoder_attend_kernel, edge, npatches, context_len, HD, ctx_rows),
            grid=(2 * nt,),
            in_specs=[
                pl.BlockSpec(memory_space=pltpu.SMEM),
                pl.BlockSpec((1, full_rows, pix_part), lambda i: (jnp.minimum(i, nt - 1), 0, 0)),
                whole((full_rows, width)),
                pl.BlockSpec(
                    (1, edge, side * pix_part),
                    lambda i: (jnp.minimum(i, nt - 1), 0, attn_cols // (side * pix_part)),
                ),
                whole((width, width)),
                pl.BlockSpec((1, edge, attn_cols), lambda i: (jnp.maximum(i - nt, 0), 0, 0)),
                whole((8, width)),
            ],
            out_specs=[
                whole((full_rows, width)),
                whole((ctx_rows, width)),
                whole((ctx_rows, width)),
                pl.BlockSpec((1, ctx_rows, 3 * columns), lambda i: (jnp.maximum(i - nt, 0), 0, 0)),
                pl.BlockSpec((1, ctx_rows, columns), lambda i: (jnp.maximum(i - nt, 0), 0, 0)),
            ],
            out_shape=[
                jax.ShapeDtypeStruct((full_rows, width), f32),
                jax.ShapeDtypeStruct((ctx_rows, width), f32),
                jax.ShapeDtypeStruct((ctx_rows, width), bf16),
                jax.ShapeDtypeStruct((nt, ctx_rows, 3 * columns), bf16),
                jax.ShapeDtypeStruct((nt, ctx_rows, columns), bf16),
            ],
            scratch_shapes=[VMEM((full_rows, width), f32), VMEM((full_rows, width), bf16)],
            compiler_params=compiled(),
            cost_estimate=cost(6e9, 12e6),
            name="encoder_attend",
        )(role_word, patch_rows, base, attn_emb, order, attn_emb, vec)
        output, normed_f, hidden, enc_feat, target = pl.pallas_call(
            functools.partial(encoder_feed_kernel, edge, ctx_rows),
            grid=(nt,),
            in_specs=[
                whole((full_rows, width)),
                by_group((edge, mat)),
                by_group((edge, mat)),
                whole((8, width)),
                whole((tgt_rows, full_rows)),
                whole((nt, width, quarter)),
            ],
            out_specs=[
                whole((ctx_rows, width)),
                whole((ctx_rows, width)),
                by_group((ctx_rows, width)),
                whole((nt, ctx_rows, quarter)),
                whole((nt, tgt_rows, quarter)),
            ],
            out_shape=[
                jax.ShapeDtypeStruct((ctx_rows, width), f32),
                jax.ShapeDtypeStruct((ctx_rows, width), bf16),
                jax.ShapeDtypeStruct((nt, ctx_rows, width), f32),
                jax.ShapeDtypeStruct((nt, ctx_rows, quarter), bf16),
                jax.ShapeDtypeStruct((nt, tgt_rows, quarter), bf16),
            ],
            scratch_shapes=[VMEM((full_rows, width), f32), VMEM((full_rows, width), bf16)],
            compiler_params=compiled(),
            cost_estimate=cost(8e9, 14e6),
            name="encoder_feed",
        )(middle, up_w, down_t, vec, pick, swap)

        feat_in = routes.across(1, enc_feat, from_role=0)

    tokens_at = table_p[jnp.concatenate([my_ctx, my_tgt], 1)]
    mask_rows = jnp.arange(seq_len)[None, :, None] >= context_len
    tokens_at = jnp.where(mask_rows, tokens_at + pvec[4 * players + 2], tokens_at)
    tokens_at = tokens_at.reshape(-1, narrow)
    token_rows = share * seq_len
    pred_cols = (3 * players + 1) * edge
    denominator = images * nd * target_len * width
    pred_columns = narrow // nt
    pred_grads, pred_vec_g, loss_tile, back = pl.pallas_call(
        functools.partial(predictor_kernel, share, context_len, players, PHD, denominator),
        in_specs=[in_vmem] * 6,
        out_specs=[in_vmem] * 4,
        out_shape=[
            jax.ShapeDtypeStruct((nt, edge, pred_cols), bf16),
            jax.ShapeDtypeStruct((16, narrow), f32),
            jax.ShapeDtypeStruct((8, 128), f32),
            jax.ShapeDtypeStruct((ctx_rows, width), bf16),
        ],
        scratch_shapes=[
            VMEM((players + 1, token_rows, narrow), f32),
            VMEM((players, token_rows, narrow), f32),
            VMEM((players, token_rows, narrow), bf16),
            VMEM((players, token_rows, narrow), bf16),
            VMEM((players, nt, token_rows, 3 * pred_columns), bf16),
            VMEM((players, nt, token_rows, pred_columns), bf16),
            VMEM((players, nt, token_rows, edge), f32),
            VMEM((token_rows, narrow), f32),
            VMEM((token_rows, narrow), f32),
            VMEM((token_rows, narrow), bf16),
            VMEM((tgt_rows, narrow), bf16),
        ],
        compiler_params=pltpu.CompilerParams(vmem_limit_bytes=KERNEL_BYTES),
        cost_estimate=cost(16e9, 30e6),
        name="predictor",
    )(feat_in, target, tokens_at, pred_all, pvec, swap)
    back = routes.across(1, back, from_role=1)

    grad_shape = jax.ShapeDtypeStruct((nt, edge, mat), bf16)
    up_g, down_g, grad_mid, vec_g1 = pl.pallas_call(
        functools.partial(encoder_feed_back_kernel, edge),
        grid=(nt,),
        in_specs=[
            whole((ctx_rows, width)),
            whole((ctx_rows, width)),
            whole((ctx_rows, width)),
            whole((ctx_rows, width)),
            by_group((ctx_rows, width)),
            by_group((edge, mat)),
            by_group((edge, mat)),
            whole((8, width)),
        ],
        out_specs=[by_group((edge, mat))] * 2 + [whole((ctx_rows, width)), whole((8, width))],
        out_shape=[grad_shape] * 2
        + [
            jax.ShapeDtypeStruct((ctx_rows, width), f32),
            jax.ShapeDtypeStruct((8, width), f32),
        ],
        scratch_shapes=[
            VMEM((ctx_rows, width), f32),
            VMEM((ctx_rows, width), bf16),
            VMEM((ctx_rows, width), f32),
        ],
        compiler_params=compiled(),
        cost_estimate=cost(8e9, 25e6),
        name="encoder_feed_back",
    )(back, output, middle, normed_f, hidden, up_w, down_t, vec)
    all_cols = attn_cols + side * pix_part
    attn_g, vec_g2 = pl.pallas_call(
        functools.partial(encoder_attend_back_kernel, edge, npatches, context_len, HD),
        grid=(2 * nt,),
        in_specs=[
            pl.BlockSpec(memory_space=pltpu.SMEM),
            whole((ctx_rows, width)),
            whole((ctx_rows, width)),
            whole((ctx_rows, width)),
            pl.BlockSpec((1, ctx_rows, 3 * columns), lambda i: (jnp.minimum(i, nt - 1), 0, 0)),
            pl.BlockSpec((1, ctx_rows, columns), lambda i: (jnp.minimum(i, nt - 1), 0, 0)),
            pl.BlockSpec((1, edge, attn_cols), lambda i: (jnp.minimum(i, nt - 1), 0, 0)),
            pl.BlockSpec((1, ctx_rows, pix_part), lambda i: (jnp.maximum(i - nt, 0), 0, 0)),
            whole((width, width)),
            whole((8, width)),
        ],
        out_specs=[
            whole((nt, edge, all_cols)),
            whole((8, width)),
        ],
        out_shape=[
            jax.ShapeDtypeStruct((nt, edge, all_cols), bf16),
            jax.ShapeDtypeStruct((8, width), f32),
        ],
        scratch_shapes=[VMEM((ctx_rows, width), bf16), VMEM((ctx_rows, width), f32)],
        compiler_params=compiled(),
        cost_estimate=cost(6e9, 20e6),
        name="encoder_attend_back",
    )(role_word, grad_mid, resid, normed_a, rows_a, att_a, attn_emb, patch_rows, order, vec)

    places = [g.reshape(nt, nd, rows_part, -1) for g in (down_g, up_g, attn_g, pred_grads)]
    middle_size = nd // 2
    by_block, emb_sum = pl.pallas_call(
        functools.partial(reduce_kernel, routes, attn_cols),
        in_specs=[any_space] * 4,
        out_specs=[in_vmem] * 2,
        out_shape=[
            jax.ShapeDtypeStruct((rows_part, (block_count + 1) * edge), bf16),
            jax.ShapeDtypeStruct((rows_part, side * pix_part), f32),
        ],
        scratch_shapes=[
            VMEM((nt, middle_size, rows_part, mat), bf16),
            VMEM((nt, middle_size, rows_part, mat), bf16),
            VMEM((nt, middle_size, rows_part, all_cols), bf16),
            VMEM((nt, middle_size - 1, rows_part, mat), bf16),
            VMEM((nt, middle_size - 1, rows_part, mat), bf16),
            VMEM((nt, middle_size - 1, rows_part, all_cols), bf16),
            VMEM((nt, rows_part, 2 * mat + all_cols), bf16),
            VMEM((nt, rows_part, pred_cols), bf16),
            VMEM((2, middle_size, rows_part, all_cols), bf16),
            dma((2,)),
            dma((3, nt)),
            dma((3, nt)),
            dma((3, nt, routes.stages)),
            dma((3, nt, routes.stages)),
            dma((2, 3, nt)),
            dma((2, 3, nt)),
        ],
        compiler_params=pltpu.CompilerParams(
            collective_id=1, has_side_effects=True, vmem_limit_bytes=KERNEL_BYTES
        ),
        cost_estimate=cost(0, 60e6),
        name="reduce_gradients",
    )(*places)

    enc_rows = to_global(vec_g1[:7] + vec_g2[:7], one_hot)
    pred_rows = to_global(pred_vec_g[: 4 * players + 3], one_hot_p)
    enc_rows = jnp.where(student_role, enc_rows, 0.0)
    pred_rows = jnp.where(role == 1, pred_rows, 0.0)
    loss_row = jnp.where(role == 1, loss_tile[0, 0], 0.0)
    packed = jnp.concatenate([enc_rows.reshape(-1), pred_rows.reshape(-1), loss_row[None]])
    packed = jnp.pad(packed, (0, -packed.shape[0] % 1024)).reshape(-1, 128)
    packed = routes.total(packed).reshape(-1)
    enc_total = packed[: enc_rows.size].reshape(enc_rows.shape)
    pred_total = packed[enc_rows.size : enc_rows.size + pred_rows.size].reshape(pred_rows.shape)
    loss_total = packed[enc_rows.size + pred_rows.size]

    by_block = by_block.reshape(rows_part, block_count + 1, edge).transpose(1, 0, 2)
    slot_of = (
        jnp.full((slot_count,), block_count, jnp.int32)
        .at[owner]
        .set(jnp.arange(block_count, dtype=jnp.int32))
    )
    slot_rows = by_block[slot_of].reshape(nd, slots, rows_part, edge)
    slot_rows = lax.all_to_all(slot_rows, "dp", split_axis=0, concat_axis=1, tiled=False)
    low_grads = slot_rows.reshape(slots, edge, edge)

    embed_grad = emb_sum.reshape(rows_part, side, pix_part).transpose(1, 0, 2)
    embed_grad = embed_grad.reshape(-1, pix_part).T

    slot_spec = pl.BlockSpec((1, 1, edge, edge), lambda s: (0, s, 0, 0))
    slot_shape = jax.ShapeDtypeStruct(weights.shape, f32)
    slot_grads, new_weights, new_left, new_right, new_teacher_blocks = pl.pallas_call(
        shampoo_kernel,
        grid=(slots,),
        in_specs=[pl.BlockSpec((1, edge, edge), lambda s: (s, 0, 0))] + [slot_spec] * 6,
        out_specs=[slot_spec] * 5,
        out_shape=[slot_shape] * 5,
        compiler_params=compiled(),
        cost_estimate=cost(3e9, 22e6),
        name="shampoo",
    )(low_grads, weights, stats_left, stats_right, root_left, root_right, teacher_slot_blocks)
    new_embed, new_embed_m, new_embed_v = adamw(embed, embed_m, embed_v, embed_grad, 0.05, 0.05)
    new_enc, new_enc_m, new_enc_v = adamw(enc_vectors, enc_m, enc_v, enc_total, 0.5, 0.0)
    new_pred, new_pred_m, new_pred_v = adamw(pred_vectors, pred_m, pred_v, pred_total, 0.5, 0.0)
    new_teacher_embed = 0.7 * teacher_embed + 0.3 * new_embed
    new_teacher_vectors = 0.7 * teacher_vectors + 0.3 * new_enc
    return (
        loss_total,
        slot_grads,
        new_weights,
        new_left,
        new_right,
        new_teacher_blocks,
        new_embed,
        new_embed_m,
        new_embed_v,
        new_teacher_embed,
        new_enc,
        new_enc_m,
        new_enc_v,
        new_pred,
        new_pred_m,
        new_pred_v,
        new_teacher_vectors,
    )


def solution(mesh):
    blocks = P("tensor", "dp", None, None)
    table = P("tensor", "dp")
    in_specs = (
        (P("dp", None, "tensor"), P("dp", None), P("dp", None), P())
        + (blocks,) * 6
        + (table,) * 4
        + (P(),) * 7
    )
    out_specs = (P(),) + (blocks,) * 5 + (table,) * 4 + (P(),) * 7
    return jax.shard_map(shards, mesh=mesh, in_specs=in_specs, out_specs=out_specs, check_vma=False)
```

```python
import functools
import math

import jax
import jax.numpy as jnp
from jax import lax
from jax.experimental import pallas as pl
from jax.experimental.pallas import tpu as pltpu
from jax.sharding import PartitionSpec as P

HD = 64
PHD = 32
SIDE = 16
STEP = 10
KERNEL_BYTES = 60 * 1024 * 1024

AXES = ("dp", "tensor")
exact = lax.Precision.HIGHEST
f32 = jnp.float32
bf16 = jnp.bfloat16
VMEM = pltpu.VMEM


def nn(first, second):
    return lax.dot_general(first, second, (((1,), (0,)), ((), ())), preferred_element_type=f32)


def nt_(first, second):
    return lax.dot_general(first, second, (((1,), (1,)), ((), ())), preferred_element_type=f32)


def tn(first, second):
    return lax.dot_general(first, second, (((0,), (0,)), ((), ())), preferred_element_type=f32)


def norm_parts(values):
    centre = values - jnp.mean(values, -1, keepdims=True)
    scale = lax.rsqrt(jnp.mean(centre * centre, -1, keepdims=True) + 1e-06)
    return centre * scale, scale


def layer_norm(values, gain_row, shift_row):
    return norm_parts(values)[0] * gain_row + shift_row


def norm_backward(grad, values, gain_row):
    unit, scale = norm_parts(values)
    weighted = grad * gain_row
    inner = (
        weighted
        - jnp.mean(weighted, -1, keepdims=True)
        - unit * jnp.mean(weighted * unit, -1, keepdims=True)
    )
    return (
        inner * scale,
        jnp.sum(grad * unit, 0, keepdims=True),
        jnp.sum(grad, 0, keepdims=True),
    )


def gelu_parts(values):
    below = 0.5 * (1.0 + lax.erf(values * math.sqrt(0.5)))
    density = jnp.exp(-0.5 * values * values) * (1.0 / math.sqrt(2.0 * math.pi))
    return values * below, below + values * density


def softened(queries, keys, head_size, allowed):
    scores = nt_(queries, keys) * (1.0 / math.sqrt(head_size))
    if allowed is not None:
        scores = jnp.where(allowed, scores, -1e30)
    expo = jnp.exp(scores - jnp.max(scores, -1, keepdims=True))
    return expo * (1.0 / jnp.sum(expo, -1, keepdims=True))


def attend(rows, head_size, length, allowed):
    columns = rows.shape[1] // 3
    images = []
    for at in range(0, rows.shape[0], length):
        outs = []
        for h in range(0, columns, head_size):
            q, k, v = (
                rows[at : at + length, j * columns + h : j * columns + h + head_size]
                for j in range(3)
            )
            soft = softened(q, k, head_size, allowed)
            outs.append(nn(soft.astype(bf16), v).astype(bf16))
        images.append(jnp.concatenate(outs, 1))
    return jnp.concatenate(images, 0) if len(images) > 1 else images[0]


def attend_back(rows, grad, head_size, length, allowed):
    columns = rows.shape[1] // 3
    factor = 1.0 / math.sqrt(head_size)
    images = []
    for at in range(0, rows.shape[0], length):
        outs = [[], [], []]
        for h in range(0, columns, head_size):
            q, k, v = (
                rows[at : at + length, j * columns + h : j * columns + h + head_size]
                for j in range(3)
            )
            g = grad[at : at + length, h : h + head_size]
            soft = softened(q, k, head_size, allowed)
            outs[2].append(tn(soft.astype(bf16), g).astype(bf16))
            ds = nt_(g, v)
            ds = (soft * (ds - jnp.sum(ds * soft, -1, keepdims=True))).astype(bf16)
            outs[0].append((nn(ds, k) * factor).astype(bf16))
            outs[1].append((tn(ds, q) * factor).astype(bf16))
        images.append(jnp.concatenate(outs[0] + outs[1] + outs[2], 1))
    return jnp.concatenate(images, 0) if len(images) > 1 else images[0]


def same_image(role, length, context):
    row = lax.broadcasted_iota(jnp.int32, (length, length), 0) // context
    column = lax.broadcasted_iota(jnp.int32, (length, length), 1) // context
    return (row == column) | (role != 0)


def encoder_attend_kernel(
    edge, unit, context, head_size, kept,
    role_ref, patch_ref, base_ref, emb_ref, order_ref, w_ref, vec_ref,
    mid_ref, resid_ref, normed_ref, rows_ref, att_ref, x_ref, h_ref,
):
    step = pl.program_id(0)
    groups = pl.num_programs(0) // 2
    side = 2
    wide = side * edge
    pix = patch_ref.shape[2]
    columns = wide // 4

    @pl.when(step == 0)
    def _():
        x_ref[...] = base_ref[...]

    @pl.when(step < groups)
    def _():
        ordered = sum(
            nn(order_ref[:, m * edge : (m + 1) * edge], emb_ref[0, :, m * pix : (m + 1) * pix])
            for m in range(side)
        ).astype(bf16)
        x_ref[...] += nt_(patch_ref[0], ordered)

    @pl.when(step == groups - 1)
    def _():
        values = x_ref[...]
        resid_ref[...] = values[:kept]
        low = layer_norm(values, vec_ref[0:1], vec_ref[1:2]).astype(bf16)
        h_ref[...] = low
        normed_ref[...] = low[:kept]

    @pl.when(step >= groups)
    def _():
        rows = sum(
            nn(h_ref[:, r * edge : (r + 1) * edge], w_ref[0, :, r * wide : r * wide + 3 * columns])
            for r in range(side)
        ).astype(bf16)
        rows_ref[0] = rows[:kept]
        att = attend(rows, head_size, unit, same_image(role_ref[0], unit, context))
        att_ref[0] = att[:kept]
        for r in range(side):
            x_ref[:, r * edge : (r + 1) * edge] += nt_(
                att, w_ref[0, :, r * wide + 3 * columns : (r + 1) * wide]
            )

    @pl.when(step == 2 * groups - 1)
    def _():
        mid_ref[...] = x_ref[...]


def encoder_feed_kernel(
    edge, kept, mid_ref, up_ref, down_ref, vec_ref, pick_ref, swap_ref,
    out_ref, normed_ref, hidden_ref, feat_ref, target_ref, x_ref, h_ref,
):
    step = pl.program_id(0)
    groups = pl.num_programs(0)
    side = 2
    wide = side * edge

    @pl.when(step == 0)
    def _():
        values = mid_ref[...]
        x_ref[...] = values
        low = layer_norm(values, vec_ref[2:3], vec_ref[3:4]).astype(bf16)
        h_ref[...] = low
        normed_ref[...] = low[:kept]

    hidden = sum(
        nn(h_ref[:, r * edge : (r + 1) * edge], up_ref[0, :, r * wide : (r + 1) * wide])
        for r in range(side)
    )
    hidden_ref[0] = hidden[:kept]
    active = gelu_parts(hidden)[0].astype(bf16)
    for r in range(side):
        x_ref[:, r * edge : (r + 1) * edge] += nt_(
            active, down_ref[0, :, r * wide : (r + 1) * wide]
        )

    @pl.when(step == groups - 1)
    def _():
        values = x_ref[...]
        out_ref[...] = values[:kept]
        final = layer_norm(values, vec_ref[4:5], vec_ref[5:6])
        encoded = final[:kept].astype(bf16)
        target = norm_parts(final)[0].astype(bf16)
        picked = nn(pick_ref[...], target).astype(bf16)
        for t in range(swap_ref.shape[0]):
            feat_ref[t] = nn(encoded, swap_ref[t]).astype(bf16)
            target_ref[t] = nn(picked, swap_ref[t]).astype(bf16)


def put(grad_ref, t, columns, value):
    grad_ref[t, :, columns] = value.astype(bf16)


def predictor_kernel(
    share, context, players, head_size, denominator,
    feat_ref, target_ref, base_ref, w_ref, vec_ref, swap_ref,
    grad_ref, vec_grad_ref, loss_ref, back_ref,
    x_ref, mid_ref, h_ref, h2_ref, rows_ref, att_ref, hidden_ref, acc_ref, d_ref, low_ref, f_ref,
):
    groups = w_ref.shape[0]
    edge = w_ref.shape[1]
    length = base_ref.shape[0] // share
    quarter = feat_ref.shape[2]
    columns = edge // 4
    last = 3 * players * edge
    in_cols = slice(last, last + quarter)
    out_cols = slice(last + quarter, last + 2 * quarter)

    def span(number):
        return slice(number * edge, (number + 1) * edge)

    vec_grad_ref[...] = jnp.zeros_like(vec_grad_ref)

    projected = sum(nt_(feat_ref[t], w_ref[t, :, in_cols]) for t in range(groups))
    x_ref[0] = base_ref[...]
    for i in range(share):
        x_ref[0, i * length : i * length + context] += projected[i * context : (i + 1) * context]

    for j in range(players):
        values = x_ref[j]
        h_ref[j] = layer_norm(values, vec_ref[4 * j : 4 * j + 1], vec_ref[4 * j + 1 : 4 * j + 2]).astype(bf16)
        mid_ref[j] = values

        @pl.loop(0, groups)
        def _(t, j=j):
            rows = nn(h_ref[j], w_ref[t, :, 3 * j * edge : 3 * j * edge + 3 * columns]).astype(bf16)
            rows_ref[j, t] = rows
            att = attend(rows, head_size, length, None)
            att_ref[j, t] = att
            mid_ref[j] += nt_(att, w_ref[t, :, 3 * j * edge + 3 * columns : (3 * j + 1) * edge])

        values = mid_ref[j]
        h2_ref[j] = layer_norm(values, vec_ref[4 * j + 2 : 4 * j + 3], vec_ref[4 * j + 3 : 4 * j + 4]).astype(bf16)
        x_ref[j + 1] = values

        @pl.loop(0, groups)
        def _(t, j=j):
            hidden = nn(h2_ref[j], w_ref[t, :, span(3 * j + 1)])
            hidden_ref[j, t] = hidden
            x_ref[j + 1] += nt_(gelu_parts(hidden)[0].astype(bf16), w_ref[t, :, span(3 * j + 2)])

    final_gain = vec_ref[4 * players : 4 * players + 1]
    final = layer_norm(x_ref[players], final_gain, vec_ref[4 * players + 1 : 4 * players + 2]).astype(bf16)
    f_ref[...] = jnp.concatenate(
        [final[i * length + context : (i + 1) * length] for i in range(share)], 0
    )
    total = jnp.zeros((1, 1), f32)
    grad_f = jnp.zeros(f_ref.shape, f32)
    for t in range(groups):
        out_w = w_ref[t, :, out_cols]
        gap = nn(f_ref[...], out_w) - target_ref[t].astype(f32)
        size = jnp.abs(gap)
        terms = jnp.where(size < 1.0, 0.5 * gap * gap, size - 0.5)
        total += jnp.sum(jnp.sum(terms, 1, keepdims=True), 0, keepdims=True)
        grad_pred = (jnp.clip(gap, -1.0, 1.0) * (1.0 / denominator)).astype(bf16)
        put(grad_ref, t, out_cols, tn(f_ref[...], grad_pred))
        grad_f += nt_(grad_pred, out_w)
    loss_ref[...] = jnp.broadcast_to(total * (1.0 / denominator), loss_ref.shape)
    d_ref[...] = jnp.zeros_like(d_ref)
    tail = length - context
    for i in range(share):
        d_ref[i * length + context : (i + 1) * length] = grad_f[i * tail : (i + 1) * tail]
    grad, gain_g, shift_g = norm_backward(d_ref[...], x_ref[players], final_gain)
    d_ref[...] = grad
    vec_grad_ref[4 * players : 4 * players + 1] = gain_g
    vec_grad_ref[4 * players + 1 : 4 * players + 2] = shift_g

    for j in reversed(range(players)):
        low_ref[...] = d_ref[...].astype(bf16)
        acc_ref[...] = jnp.zeros_like(acc_ref)

        @pl.loop(0, groups)
        def _(t, j=j):
            active, slope = gelu_parts(hidden_ref[j, t])
            low = low_ref[...]
            put(grad_ref, t, span(3 * j + 2), tn(low, active.astype(bf16)))
            grad_hidden = (nn(low, w_ref[t, :, span(3 * j + 2)]) * slope).astype(bf16)
            put(grad_ref, t, span(3 * j + 1), tn(h2_ref[j], grad_hidden))
            acc_ref[...] += nt_(grad_hidden, w_ref[t, :, span(3 * j + 1)])

        grad, gain_g, shift_g = norm_backward(acc_ref[...], mid_ref[j], vec_ref[4 * j + 2 : 4 * j + 3])
        vec_grad_ref[4 * j + 2 : 4 * j + 3] = gain_g
        vec_grad_ref[4 * j + 3 : 4 * j + 4] = shift_g
        grad = d_ref[...] + grad
        d_ref[...] = grad
        low_ref[...] = grad.astype(bf16)
        acc_ref[...] = jnp.zeros_like(acc_ref)

        @pl.loop(0, groups)
        def _(t, j=j):
            low = low_ref[...]
            attn_w = w_ref[t, :, span(3 * j)]
            grad_att = nn(low, attn_w[:, 3 * columns :]).astype(bf16)
            grad_rows = attend_back(rows_ref[j, t], grad_att, head_size, length, None)
            grad_w = jnp.concatenate([tn(h_ref[j], grad_rows), tn(low, att_ref[j, t])], 1)
            put(grad_ref, t, span(3 * j), grad_w)
            acc_ref[...] += nt_(grad_rows, attn_w[:, : 3 * columns])

        grad, gain_g, shift_g = norm_backward(acc_ref[...], x_ref[j], vec_ref[4 * j : 4 * j + 1])
        vec_grad_ref[4 * j : 4 * j + 1] = gain_g
        vec_grad_ref[4 * j + 1 : 4 * j + 2] = shift_g
        d_ref[...] += grad

    mask_grad = jnp.zeros((1, edge), f32)
    for i in range(share):
        mask_grad += jnp.sum(d_ref[i * length + context : (i + 1) * length], 0, keepdims=True)
    vec_grad_ref[4 * players + 2 : 4 * players + 3] = mask_grad
    low = jnp.concatenate(
        [d_ref[i * length : i * length + context] for i in range(share)], 0
    ).astype(bf16)
    back = jnp.zeros((low.shape[0], swap_ref.shape[1]), f32)
    for t in range(groups):
        put(grad_ref, t, in_cols, tn(low, feat_ref[t]))
        back += nt_(nn(low, w_ref[t, :, in_cols]).astype(bf16), swap_ref[t])
    back_ref[...] = back.astype(bf16)


def encoder_feed_back_kernel(
    edge, back_ref, out_ref, mid_ref, normed_ref, hidden_ref, up_ref, down_ref, vec_ref,
    up_grad, down_grad, grad_ref, vec_grad_ref, d_ref, low_ref, acc_ref,
):
    step = pl.program_id(0)
    groups = pl.num_programs(0)
    wide = 2 * edge

    @pl.when(step == 0)
    def _():
        grad, gain_g, shift_g = norm_backward(back_ref[...].astype(f32), out_ref[...], vec_ref[4:5])
        d_ref[...] = grad
        low_ref[...] = grad.astype(bf16)
        acc_ref[...] = jnp.zeros_like(acc_ref)
        vec_grad_ref[...] = jnp.zeros_like(vec_grad_ref)
        vec_grad_ref[4:5] = gain_g
        vec_grad_ref[5:6] = shift_g

    active, slope = gelu_parts(hidden_ref[0])
    active = active.astype(bf16)
    grad_hidden = sum(
        nn(low_ref[:, r * edge : (r + 1) * edge], down_ref[0, :, r * wide : (r + 1) * wide])
        for r in range(2)
    )
    grad_hidden = (grad_hidden * slope).astype(bf16)
    for r in range(2):
        mine = slice(r * edge, (r + 1) * edge)
        columns = slice(r * wide, (r + 1) * wide)
        put(down_grad, 0, columns, tn(low_ref[:, mine], active))
        put(up_grad, 0, columns, tn(normed_ref[:, mine], grad_hidden))
        acc_ref[:, mine] += nt_(grad_hidden, up_ref[0, :, columns])

    @pl.when(step == groups - 1)
    def _():
        grad, gain_g, shift_g = norm_backward(acc_ref[...], mid_ref[...], vec_ref[2:3])
        grad_ref[...] = d_ref[...] + grad
        vec_grad_ref[2:3] = gain_g
        vec_grad_ref[3:4] = shift_g


def encoder_attend_back_kernel(
    edge, unit, context, head_size,
    role_ref, mid_grad_ref, resid_ref, normed_ref, rows_ref, att_ref, w_ref, patch_ref, order_ref,
    vec_ref, grad_ref, vec_grad_ref, low_ref, acc_ref,
):
    step = pl.program_id(0)
    groups = pl.num_programs(0) // 2
    wide = 2 * edge
    columns = wide // 4
    pix = patch_ref.shape[2]

    @pl.when(step == 0)
    def _():
        low_ref[...] = mid_grad_ref[...].astype(bf16)
        acc_ref[...] = jnp.zeros_like(acc_ref)

    @pl.when(step < groups)
    def _():
        grad_att = sum(
            nn(
                low_ref[:, r * edge : (r + 1) * edge],
                w_ref[0, :, r * wide + 3 * columns : (r + 1) * wide],
            )
            for r in range(2)
        ).astype(bf16)
        allowed = same_image(role_ref[0], unit, context)
        grad_rows = attend_back(rows_ref[0], grad_att, head_size, unit, allowed)
        for r in range(2):
            mine = slice(r * edge, (r + 1) * edge)
            grad_w = jnp.concatenate(
                [tn(normed_ref[:, mine], grad_rows), tn(low_ref[:, mine], att_ref[0])], 1
            )
            put(grad_ref, step, slice(r * wide, (r + 1) * wide), grad_w)
            acc_ref[:, mine] += nt_(grad_rows, w_ref[0, :, r * wide : r * wide + 3 * columns])

    @pl.when(step == groups - 1)
    def _():
        grad, gain_g, shift_g = norm_backward(acc_ref[...], resid_ref[...], vec_ref[0:1])
        grad = mid_grad_ref[...] + grad
        low_ref[...] = nn(grad.astype(bf16), order_ref[...]).astype(bf16)
        vec_grad_ref[...] = jnp.zeros_like(vec_grad_ref)
        vec_grad_ref[0:1] = gain_g
        vec_grad_ref[1:2] = shift_g
        vec_grad_ref[6:7] = jnp.sum(grad, 0, keepdims=True)

    @pl.when(step >= groups)
    def _():
        grad_w = jnp.concatenate(
            [tn(low_ref[:, r * edge : (r + 1) * edge], patch_ref[0]) for r in range(2)], 1
        )
        put(grad_ref, step - groups, slice(2 * wide, 2 * wide + 2 * pix), grad_w)


def shampoo_kernel(
    grad_ref, weight_ref, left_ref, right_ref, root_left_ref, root_right_ref, teacher_ref,
    grad_out, weight_out, left_out, right_out, teacher_out,
):
    low = grad_ref[0]
    grad_out[0, 0] = low.astype(f32)
    left_out[0, 0] = 0.95 * left_ref[0, 0] + 0.05 * nt_(low, low)
    right_out[0, 0] = 0.95 * right_ref[0, 0] + 0.05 * tn(low, low)
    high, rest = split(root_left_ref[0, 0])
    side = nn(high, low) + nn(rest, low)
    high, rest = split(side)
    root_high, root_rest = split(root_right_ref[0, 0])
    step = nn(high, root_high) + nn(high, root_rest) + nn(rest, root_high)
    mean = jnp.mean(jnp.mean(step * step, 1, keepdims=True), 0, keepdims=True)
    step = step * lax.rsqrt(mean + 1e-06)
    weight = weight_ref[0, 0]
    new = weight - 0.05 * (step + 0.05 * weight)
    weight_out[0, 0] = new
    teacher_out[0, 0] = 0.7 * teacher_ref[0, 0] + 0.3 * new


MESH = pl.DeviceIdType.MESH


def flip(place, bits):
    bit = 1
    while bit <= bits:
        if bits & bit:
            place = place + bit * (1 - 2 * lax.rem(lax.div(place, bit), 2))
        bit *= 2
    return place


def remote(source, target, send_sem, recv_sem, device):
    return pltpu.make_async_remote_copy(
        src_ref=source, dst_ref=target, send_sem=send_sem, recv_sem=recv_sem,
        device_id=device, device_id_type=MESH,
    )


def greet(routes, d, z):
    barrier = pltpu.get_barrier_semaphore()
    peers = [(d, flip(z, r)) for r in range(1, routes.nt)]
    peers += [routes.partner(s, d, z) for s in range(routes.stages + 1)]
    for peer in peers:
        pl.semaphore_signal(barrier, inc=1, device_id=peer, device_id_type=MESH)
    pl.semaphore_wait(barrier, len(peers))


def guarded(condition, body):
    if condition is None:
        body()
    else:
        pl.when(condition)(body)


class Gather:
    ahead = 2

    def __init__(self, routes, widths, few_rows, sources, mats, sems):
        self.routes, self.widths, self.few_rows = routes, widths, few_rows
        self.own, self.other, self.pred, self.patch_in, self.rows = sources
        self.mats = mats
        self.sems = sems
        self.d, self.z = lax.axis_index("dp"), lax.axis_index("tensor")
        self.role = lax.rem(self.z, 2)
        self.last = len(widths) - 1
        self.items = [(m, r) for m in range(len(widths)) for r in range(routes.nt)]
        self.span = len(self.items) + self.ahead * routes.stages

    def peer(self, r):
        return self.d, flip(self.z, r)

    def peer_role(self, r):
        return lax.rem(flip(self.z, r), 2)

    def source(self, m, r):
        if m == self.last:
            return self.pred
        ref = self.own if r % 2 == 0 else self.other
        return ref.at[:, pl.ds(sum(self.widths[:m]), self.widths[m])]

    def across(self, m, r):
        send, recv = self.sems[0], self.sems[1]
        return remote(
            self.source(m, r), self.mats[m].at[r, 0], send.at[m, r], recv.at[m, r], self.peer(r)
        )

    def local(self, m):
        return pltpu.make_async_copy(self.source(m, 0), self.mats[m].at[0, 0], self.sems[2].at[m])

    def patch(self, r, rows):
        return remote(
            self.patch_in.at[r, pl.ds(0, rows)], self.rows.at[r, pl.ds(0, rows)],
            self.sems[3].at[r], self.sems[4].at[r], self.peer(r),
        )

    def own_patch(self):
        return pltpu.make_async_copy(
            self.patch_in.at[0], self.rows.at[0], self.sems[2].at[self.last + 1]
        )

    def stage(self, m, r, s):
        size = 1 << s
        return remote(
            self.mats[m].at[r, pl.ds(0, size)], self.mats[m].at[r, pl.ds(size, size)],
            self.sems[5].at[m, r, s], self.sems[6].at[m, r, s],
            self.routes.partner(s, self.d, self.z),
        )

    def mine(self, m):
        return self.role == 1 if m == self.last else None

    def theirs(self, m, r):
        return self.peer_role(r) == 1 if m == self.last else None

    def start(self):
        greet(self.routes, self.d, self.z)
        for m in range(len(self.widths)):
            guarded(self.mine(m), lambda m=m: self.local(m).start())
            for r in range(1, self.routes.nt):
                guarded(self.theirs(m, r), lambda m=m, r=r: self.across(m, r).start())
            if m == 0:
                self.own_patch().start()
                for r in range(1, self.routes.nt):
                    for role, rows in ((0, self.few_rows), (1, self.patch_in.shape[1])):
                        pl.when(self.peer_role(r) == role)(
                            lambda r=r, rows=rows: self.patch(r, rows).start()
                        )

    def advance(self, m, r, s):
        if s:
            self.stage(m, r, s - 1).wait_recv()
        elif r:
            self.across(m, r).wait_recv()
        else:
            self.local(m).wait()
        self.stage(m, r, s).start()

    def step(self, n):
        for s in reversed(range(self.routes.stages + 1)):
            if 0 <= n - self.ahead * s < len(self.items):
                m, r = self.items[n - self.ahead * s]
                guarded(self.mine(m), lambda m=m, r=r, s=s: self.advance(m, r, s))

    def arrive(self, m, r):
        self.stage(m, r, self.routes.stages).wait_recv()

    def wait_patches(self):
        self.own_patch().wait()
        for r in range(1, self.routes.nt):
            for role, rows in ((0, self.few_rows), (1, self.patch_in.shape[1])):
                pl.when(self.role == role)(lambda r=r, rows=rows: self.patch(r, rows).wait_recv())

    def finish(self):
        for r in range(1, self.routes.nt):
            for role, rows in ((0, self.few_rows), (1, self.patch_in.shape[1])):
                pl.when(self.peer_role(r) == role)(
                    lambda r=r, rows=rows: self.patch(r, rows).wait_send()
                )
        for m, r in self.items:

            def sent(m=m, r=r):
                for s in range(self.routes.stages + 1):
                    self.stage(m, r, s).wait_send()

            guarded(self.mine(m), sent)
            if r:
                guarded(self.theirs(m, r), lambda m=m, r=r: self.across(m, r).wait_send())


def gather_kernel(
    routes, widths, few_rows, own_ref, other_ref, pred_ref, patch_ref,
    attn_ref, up_ref, down_ref, players_ref, rows_ref, *sems,
):
    gather = Gather(
        routes, widths, few_rows, (own_ref, other_ref, pred_ref, patch_ref, rows_ref),
        (attn_ref, up_ref, down_ref, players_ref), sems,
    )
    gather.start()
    for n in range(gather.span):
        gather.step(n)
    for m, r in gather.items:
        guarded(gather.mine(m), lambda m=m, r=r: gather.arrive(m, r))
    gather.wait_patches()
    gather.finish()


def forward_kernel(
    routes, widths, unit, context, head_size,
    own_ref, other_ref, pred_ref, patch_ref, base_ref, order_ref, vec_ref, pick_ref, swap_ref,
    attn_out, up_out, down_out, players_out, rows_out, mid_out, resid_out, normed_out, qkv_out,
    att_out, out_out, normed2_out, hidden_out, feat_out, target_out,
    attn_ref, up_ref, down_ref, players_ref, rows_ref, x_ref, h_ref, sent_ref, feat_ref,
    back_sem, feat_send, feat_recv, *sems,
):
    nt, nd = routes.nt, routes.nd
    mats = (attn_ref, up_ref, down_ref, players_ref)
    outs = (attn_out, up_out, down_out, players_out)
    kept = resid_out.shape[0]
    gather = Gather(
        routes, widths, kept, (own_ref, other_ref, pred_ref, patch_ref, rows_ref), mats, sems
    )
    role = gather.role
    edge = nd * attn_ref.shape[2]
    side = 2
    wide = side * edge
    pix = rows_ref.shape[2]
    columns = wide // 4

    def matrix(ref, t, first, width):
        return ref[t, :, :, first : first + width].reshape(edge, width)

    def to_hbm(m, r):
        return pltpu.make_async_copy(mats[m].at[r], outs[m].at[r], back_sem.at[m, r])

    def feat_copy():
        return remote(sent_ref, feat_ref, feat_send, feat_recv, gather.peer(1))

    def embed():
        gather.wait_patches()
        x_ref[...] = base_ref[...]

        @pl.loop(0, nt)
        def _(t):
            ordered = sum(
                nn(
                    order_ref[:, m * edge : (m + 1) * edge],
                    matrix(attn_ref, t, side * wide + m * pix, pix),
                )
                for m in range(side)
            ).astype(bf16)
            x_ref[...] += nt_(rows_ref[t], ordered)

        values = x_ref[...]
        resid_out[...] = values[:kept]
        low = layer_norm(values, vec_ref[0:1], vec_ref[1:2]).astype(bf16)
        h_ref[...] = low
        normed_out[...] = low[:kept]

    def attention(t):
        rows = sum(
            nn(h_ref[:, r * edge : (r + 1) * edge], matrix(attn_ref, t, r * wide, 3 * columns))
            for r in range(side)
        ).astype(bf16)
        qkv_out[t] = rows[:kept]
        att = attend(rows, head_size, unit, same_image(role, unit, context))
        att_out[t] = att[:kept]
        for r in range(side):
            x_ref[:, r * edge : (r + 1) * edge] += nt_(
                att, matrix(attn_ref, t, r * wide + 3 * columns, columns)
            )

    def middle():
        values = x_ref[...]
        mid_out[...] = values[:kept]
        low = layer_norm(values, vec_ref[2:3], vec_ref[3:4]).astype(bf16)
        h_ref[...] = low
        normed2_out[...] = low[:kept]

    def feed(t):
        hidden = sum(
            nn(h_ref[:, r * edge : (r + 1) * edge], matrix(up_ref, t, r * wide, wide))
            for r in range(side)
        )
        hidden_out[t] = hidden[:kept]
        active = gelu_parts(hidden)[0].astype(bf16)
        for r in range(side):
            x_ref[:, r * edge : (r + 1) * edge] += nt_(
                active, matrix(down_ref, t, r * wide, wide)
            )

    def last():
        values = x_ref[...]
        out_out[...] = values[:kept]
        final = layer_norm(values, vec_ref[4:5], vec_ref[5:6])

        @pl.when(role == 0)
        def _():
            encoded = final[:kept].astype(bf16)
            for t in range(nt):
                sent_ref[t] = nn(encoded, swap_ref[t]).astype(bf16)
            feat_copy().start()

        @pl.when(role == 1)
        def _():
            target = norm_parts(final)[0].astype(bf16)
            picked = nn(pick_ref[...], target).astype(bf16)
            for t in range(nt):
                target_out[t] = nn(picked, swap_ref[t]).astype(bf16)

        @pl.when(role == 0)
        def _():
            target_out[...] = jnp.zeros_like(target_out)

    lag = gather.ahead * (routes.stages + 1)
    attn_at = nt - 1 + lag
    feed_at = 3 * nt - 1 + lag
    steps = len(gather.items) + lag
    gather.start()

    @pl.loop(0, steps)
    def _(n):
        for k in range(steps):

            @pl.when(n == k)
            def _(k=k):
                gather.step(k)
                if k >= lag:
                    m, r = gather.items[k - lag]

                    def here(m=m, r=r):
                        gather.arrive(m, r)
                        to_hbm(m, r).start()

                    guarded(gather.mine(m), here)

        pl.when(n == attn_at)(embed)

        @pl.when((n > attn_at) & (n <= attn_at + nt))
        def _():
            attention(n - attn_at - 1)

        pl.when(n == feed_at)(middle)

        @pl.when((n >= feed_at) & (n < feed_at + nt))
        def _():
            feed(n - feed_at)

        pl.when(n == feed_at + nt - 1)(last)

    rows_out[...] = rows_ref[:, :kept]

    @pl.when(role == 0)
    def _():
        feat_copy().wait_send()
        feat_out[...] = jnp.zeros_like(feat_out)

    @pl.when(role == 1)
    def _():
        feat_copy().wait_recv()
        feat_out[...] = feat_ref[...]

    gather.finish()
    for m, r in gather.items:
        guarded(gather.mine(m), lambda m=m, r=r: to_hbm(m, r).wait())


def reduce_kernel(
    routes, attn_cols, down_ref, up_ref, attn_ref, pred_ref, block_ref, emb_ref,
    core0, core1, core2, later0, later1, later2, enc_in, pred_in, load,
    load_sem, core_send, core_recv, stage_send, stage_recv, z_send, z_recv,
):
    d, z = lax.axis_index("dp"), lax.axis_index("tensor")
    nt, stages = routes.nt, routes.stages
    middle = routes.nd // 2
    role = lax.rem(z, 2)
    cores = [core0, core1, core2]
    laters = [later0, later1, later2]
    greet(routes, d, z)

    def run(kind, sources, incoming, starts):
        items = [(j, r) for j in range(len(sources)) for r in reversed(range(nt))]

        def part(j, r, first):
            ref, start, width = sources[j]
            return ref.at[r, pl.ds(first, middle), :, pl.ds(start, width)]

        def to_core(j, r):
            return remote(
                part(j, r, middle), cores[j].at[r, :, :, pl.ds(0, sources[j][2])],
                core_send.at[j, r], core_recv.at[j, r], routes.partner(stages, d, z),
            )

        def own(i):
            j, r = items[i]
            return pltpu.make_async_copy(
                part(j, r, 0), load.at[i % 2, :, :, pl.ds(0, sources[j][2])], load_sem.at[i % 2]
            )

        def stage(j, r, s):
            size = 1 << s
            return remote(
                cores[j].at[r, pl.ds(size, size), :, pl.ds(0, sources[j][2])],
                laters[j].at[r, pl.ds(size - 1, size), :, pl.ds(0, sources[j][2])],
                stage_send.at[j, r, s], stage_recv.at[j, r, s], routes.partner(s, d, z),
            )

        def across(j, r):
            return remote(
                cores[j].at[r, 0, :, pl.ds(0, sources[j][2])],
                incoming.at[r, :, pl.ds(starts[j], sources[j][2])],
                z_send.at[kind, j, r], z_recv.at[kind, j, r], (d, flip(z, r)),
            )

        def add(i, q):
            j, r = items[i]
            width = sources[j][2]
            if q == 0:
                own(i).wait()
                to_core(j, r).wait_recv()

                @pl.loop(0, middle)
                def _(k):
                    total = cores[j][r, k, :, 0:width].astype(f32)
                    total += load[i % 2, k, :, 0:width].astype(f32)
                    cores[j][r, k, :, 0:width] = total.astype(bf16)

                if i + 2 < len(items):
                    own(i + 2).start()
            else:
                s = stages - q
                stage(j, r, s).wait_recv()

                @pl.loop(0, 1 << s)
                def _(k):
                    total = cores[j][r, k, :, 0:width].astype(f32)
                    total += laters[j][r, k + ((1 << s) - 1), :, 0:width].astype(f32)
                    cores[j][r, k, :, 0:width] = total.astype(bf16)

            if q < stages:
                stage(j, r, stages - q - 1).start()
            elif r:
                across(j, r).start()

        for i in range(min(2, len(items))):
            own(i).start()
        for j, r in items:
            to_core(j, r).start()
        for n in range(len(items) + stages):
            for q in reversed(range(stages + 1)):
                if 0 <= n - q < len(items):
                    add(n - q, q)
        for j, r in items:
            to_core(j, r).wait_send()
            for s in range(stages):
                stage(j, r, s).wait_send()
            if r:
                across(j, r).wait_send()

    wide = down_ref.shape[3]
    all_cols = attn_ref.shape[3]
    pred_cols = pred_ref.shape[3]
    encoder = [(down_ref, 0, wide), (up_ref, 0, wide), (attn_ref, 0, all_cols)]
    encoder_at = [0, wide, 2 * wide]
    players = [(pred_ref, 0, wide), (pred_ref, wide, pred_cols - wide)]
    players_at = [0, wide]

    @pl.when(role == 0)
    def _():
        run(0, encoder, enc_in, encoder_at)

    @pl.when(role == 1)
    def _():
        run(1, players, pred_in, players_at)

    def collect(kind, sources, incoming, starts, put):
        for j, (_, _, width) in enumerate(sources):
            place = incoming.at[:, :, pl.ds(starts[j], width)]

            def arrive(r, j=j, width=width):
                pltpu.make_async_remote_copy(
                    src_ref=cores[j].at[r, 0, :, pl.ds(0, width)],
                    dst_ref=incoming.at[r, :, pl.ds(starts[j], width)],
                    send_sem=z_send.at[kind, j, r], recv_sem=z_recv.at[kind, j, r],
                    device_id=(d, flip(z, r)), device_id_type=MESH,
                ).wait_recv()

            del place

            @pl.when(role == kind)
            def _(j=j, width=width, arrive=arrive):
                total = cores[j][0, 0, :, 0:width].astype(f32)
                for r in range(2, nt, 2):
                    arrive(r)
                    total += incoming[r, :, starts[j] : starts[j] + width].astype(f32)
                put(j, total)

            @pl.when(role != kind)
            def _(j=j, width=width, arrive=arrive):
                total = None
                for r in range(1, nt, 2):
                    arrive(r)
                    got = incoming[r, :, starts[j] : starts[j] + width].astype(f32)
                    total = got if total is None else total + got
                put(j, total)

    def put_encoder(j, total):
        if j == 2:
            block_ref[:, 0:attn_cols] = total[:, :attn_cols].astype(bf16)
            emb_ref[...] = total[:, attn_cols:]
        else:
            first = attn_cols + (1 - j) * wide
            block_ref[:, first : first + wide] = total.astype(bf16)

    def put_players(j, total):
        first = attn_cols + 2 * wide + players_at[j]
        block_ref[:, first : first + total.shape[1]] = total.astype(bf16)

    collect(1, players, pred_in, players_at, put_players)
    collect(0, encoder, enc_in, encoder_at, put_encoder)
    end = attn_cols + 2 * wide + pred_cols
    block_ref[:, end:] = jnp.zeros((block_ref.shape[0], block_ref.shape[1] - end), bf16)


def split(values):
    high = values.astype(bf16)
    return high, (values - high.astype(f32)).astype(bf16)


def exact_order(values, hot):
    high, rest = split(values)
    low = (values - high.astype(f32) - rest.astype(f32)).astype(bf16)
    return nn(high, hot) + nn(rest, hot) + nn(low, hot)


def backward_kernel(
    routes, context, head_size,
    players_ref, back_in, attn_hbm, up_hbm, down_hbm,
    out_ref, mid_ref, resid_ref, normed2_ref, normed_ref, hidden_ref, qkv_ref, att_ref, rows_ref,
    vec_ref, order_ref, hot_ref, hot_p_ref, pred_vec_ref, loss_ref,
    block_ref, emb_ref, vec_out,
    g0, g1, g2, g3, core0, core1, core2, core3, later0, later1, later2, later3, enc_in, pred_in,
    attn_w, up_w, down_w, back_ref, d_ref, low_ref, acc_ref, vec_grad_ref, vec_send, vec_recv,
    weight_sem, back_send, back_recv, load_sem, core_send, core_recv, stage_send, stage_recv,
    z_send, z_recv, vec_send_sem, vec_recv_sem,
):
    d, z = lax.axis_index("dp"), lax.axis_index("tensor")
    nt, nd, stages = routes.nt, routes.nd, routes.stages
    role = lax.rem(z, 2)
    half = nd // 2
    grads, cores = (g0, g1, g2, g3), (core0, core1, core2, core3)
    laters = (later0, later1, later2, later3)
    rows = g0.shape[2]
    edge = nd * rows
    wide = 2 * edge
    columns = wide // 4
    pix = rows_ref.shape[2]
    unit = resid_ref.shape[0]
    mat = g0.shape[3]
    ahead = 2

    encoder = [(j, r) for r in range(nt) for j in (0, 1)] + [(2, r) for r in range(nt)]
    encoder += [(3, r) for r in range(nt)]
    pred_cols = players_ref.shape[3]
    pred_width = (mat, pred_cols - mat)
    players = [(j, r) for r in reversed(range(nt)) for j in (0, 1)]
    enc_width = (mat, mat, mat, 2 * pix)
    enc_at = (0, mat, 2 * mat, 3 * mat)

    def weight(t, i):
        slot = lax.rem(t, 2)
        source = (up_hbm, down_hbm, attn_hbm)[i].at[t, :, pl.ds(0, mat)]
        target = (up_w, down_w, attn_w)[i].at[slot]
        return pltpu.make_async_copy(source, target, weight_sem.at[i, slot])

    def back_copy():
        return remote(back_in, back_ref, back_send, back_recv, (d, flip(z, 1)))

    class Sums:
        def __init__(self, kind, items, width, incoming, at):
            self.kind, self.items, self.width = kind, items, width
            self.incoming, self.at = incoming, at

        def cut(self, j):
            return pl.ds(0, self.width[j])

        def to_core(self, j, r):
            if self.kind:
                source = players_ref.at[r, pl.ds(half, half), :, pl.ds(self.at[j], self.width[j])]
            else:
                source = grads[j].at[r, pl.ds(half, half)]
            return remote(
                source, cores[j].at[r, :, :, self.cut(j)],
                core_send.at[j, r], core_recv.at[j, r], routes.partner(stages, d, z),
            )

        def load(self, j, r):
            return pltpu.make_async_copy(
                players_ref.at[r, pl.ds(0, half), :, pl.ds(self.at[j], self.width[j])],
                grads[j].at[r, pl.ds(0, half), :, self.cut(j)],
                load_sem.at[j, r],
            )

        def stage(self, j, r, s):
            size = 1 << s
            return remote(
                grads[j].at[r, pl.ds(size, size), :, self.cut(j)],
                laters[j].at[r, pl.ds(size - 1, size), :, self.cut(j)],
                stage_send.at[j, r, s], stage_recv.at[j, r, s], routes.partner(s, d, z),
            )

        def across(self, j, r):
            return remote(
                grads[j].at[r, 0, :, self.cut(j)],
                self.incoming.at[r, :, pl.ds(self.at[j], self.width[j])],
                z_send.at[self.kind, j, r], z_recv.at[self.kind, j, r], (d, flip(z, r)),
            )

        def begin(self, i):
            if i < len(self.items):
                j, r = self.items[i]
                if self.kind:
                    self.load(j, r).start()
                self.to_core(j, r).start()

        def add(self, i, q):
            if not 0 <= i < len(self.items):
                return
            j, r = self.items[i]
            width = self.width[j]
            s = stages - q
            if q == 0:
                if self.kind:
                    self.load(j, r).wait()
                self.to_core(j, r).wait_recv()
            else:
                self.stage(j, r, s).wait_recv()

            @pl.loop(0, 1 << s)
            def _(k):
                total = grads[j][r, k, :, 0:width].astype(f32)
                if q == 0:
                    total += cores[j][r, k, :, 0:width].astype(f32)
                else:
                    total += laters[j][r, k + ((1 << s) - 1), :, 0:width].astype(f32)
                grads[j][r, k, :, 0:width] = total.astype(bf16)

            if q < stages:
                self.stage(j, r, s - 1).start()
            elif r:
                self.across(j, r).start()

        def tick(self, n):
            for q in reversed(range(stages + 1)):
                self.add(n - ahead * (q + 1), q)

        def finish(self):
            for j, r in self.items:
                self.to_core(j, r).wait_send()
                for s in range(stages):
                    self.stage(j, r, s).wait_send()
                if r:
                    self.across(j, r).wait_send()

        def collect(self, j, put):
            columns = slice(self.at[j], self.at[j] + self.width[j])

            @pl.when(role == self.kind)
            def _():
                total = grads[j][0, 0, :, 0 : self.width[j]].astype(f32)
                for r in range(2, nt, 2):
                    self.across(j, r).wait_recv()
                    total += self.incoming[r, :, columns].astype(f32)
                put(total)

            @pl.when(role != self.kind)
            def _():
                total = jnp.zeros((rows, self.width[j]), f32)
                for r in range(1, nt, 2):
                    self.across(j, r).wait_recv()
                    total += self.incoming[r, :, columns].astype(f32)
                put(total)

    enc = Sums(0, encoder, enc_width, enc_in, enc_at)
    play = Sums(1, players, pred_width, pred_in, (0, mat))

    def store(ref, t, first, value):
        ref[t, :, :, first : first + value.shape[1]] = value.astype(bf16).reshape(
            nd, rows, value.shape[1]
        )

    def begin_feed():
        back_copy().wait_recv()
        grad, gain_g, shift_g = norm_backward(back_ref[...].astype(f32), out_ref[...], vec_ref[4:5])
        d_ref[...] = grad
        low_ref[...] = grad.astype(bf16)
        acc_ref[...] = jnp.zeros_like(acc_ref)
        vec_grad_ref[4:5] = gain_g
        vec_grad_ref[5:6] = shift_g

    def feed(t):
        slot = lax.rem(t, 2)
        weight(t, 0).wait()
        weight(t, 1).wait()
        active, slope = gelu_parts(hidden_ref[t])
        active = active.astype(bf16)
        grad_hidden = sum(
            nn(low_ref[:, r * edge : (r + 1) * edge], down_w[slot, :, r * wide : (r + 1) * wide])
            for r in range(2)
        )
        grad_hidden = (grad_hidden * slope).astype(bf16)
        for r in range(2):
            mine = slice(r * edge, (r + 1) * edge)
            store(g0, t, r * wide, tn(low_ref[:, mine], active))
            store(g1, t, r * wide, tn(normed2_ref[:, mine], grad_hidden))
            acc_ref[:, mine] += nt_(grad_hidden, up_w[slot, :, r * wide : (r + 1) * wide])

        @pl.when(t + 2 < nt)
        def _():
            weight(t + 2, 0).start()
            weight(t + 2, 1).start()

    def end_feed():
        grad, gain_g, shift_g = norm_backward(acc_ref[...], mid_ref[...], vec_ref[2:3])
        vec_grad_ref[2:3] = gain_g
        vec_grad_ref[3:4] = shift_g
        grad = d_ref[...] + grad
        d_ref[...] = grad
        low_ref[...] = grad.astype(bf16)
        acc_ref[...] = jnp.zeros_like(acc_ref)

    def attention(t):
        slot = lax.rem(t, 2)
        weight(t, 2).wait()
        grad_att = sum(
            nn(
                low_ref[:, r * edge : (r + 1) * edge],
                attn_w[slot, :, r * wide + 3 * columns : (r + 1) * wide],
            )
            for r in range(2)
        ).astype(bf16)
        allowed = same_image(role, unit, context)
        grad_rows = attend_back(qkv_ref[t], grad_att, head_size, unit, allowed)
        for r in range(2):
            mine = slice(r * edge, (r + 1) * edge)
            grad_w = jnp.concatenate(
                [tn(normed_ref[:, mine], grad_rows), tn(low_ref[:, mine], att_ref[t])], 1
            )
            store(g2, t, r * wide, grad_w)
            acc_ref[:, mine] += nt_(grad_rows, attn_w[slot, :, r * wide : r * wide + 3 * columns])

        @pl.when(t + 2 < nt)
        def _():
            weight(t + 2, 2).start()

    def end_attention():
        grad, gain_g, shift_g = norm_backward(acc_ref[...], resid_ref[...], vec_ref[0:1])
        grad = d_ref[...] + grad
        vec_grad_ref[0:1] = gain_g
        vec_grad_ref[1:2] = shift_g
        vec_grad_ref[6:7] = jnp.sum(grad, 0, keepdims=True)
        low_ref[...] = nn(grad.astype(bf16), order_ref[...]).astype(bf16)

        @pl.loop(0, nt)
        def _(t):
            for m in range(2):
                store(g3, t, m * pix, tn(low_ref[:, m * edge : (m + 1) * edge], rows_ref[t]))

    bits = [("d", 1)] + [("d", b) for b in routes.low_bits]
    bits += [("z", 1 << s) for s in range(nt.bit_length() - 1)]

    def vec_copy(s):
        axis, bit = bits[s]
        peer = (flip(d, bit), z) if axis == "d" else (d, flip(z, bit))
        return remote(
            vec_send.at[s], vec_recv.at[s], vec_send_sem.at[s], vec_recv_sem.at[s], peer
        )

    def vec_pack():
        @pl.when(role == 0)
        def _():
            whole_rows = exact_order(vec_grad_ref[...], hot_ref[...])
            vec_send[0, 0:8] = whole_rows[:, :edge]
            vec_send[0, 8:16] = whole_rows[:, edge:]
            vec_send[0, 16:32] = jnp.zeros((16, edge), f32)

        @pl.when(role == 1)
        def _():
            vec_send[0, 0:16] = jnp.zeros((16, edge), f32)
            vec_send[0, 16:32] = exact_order(pred_vec_ref[...], hot_p_ref[...])
            vec_send[0, 28:29] = jnp.broadcast_to(loss_ref[0:1, 0:1], (1, edge))

        vec_copy(0).start()

    def vec_step(s):
        vec_copy(s).wait_recv()
        total = vec_send[s] + vec_recv[s]
        if s + 1 < len(bits):
            vec_send[s + 1] = total
            vec_copy(s + 1).start()
        else:
            vec_out[...] = total

    ticks = len(encoder) + ahead * (stages + 1)
    first_attention = 2 * nt
    last_attention = 3 * nt

    @pl.when(role == 0)
    def _():
        vec_grad_ref[...] = jnp.zeros_like(vec_grad_ref)
        for t in range(2):
            for i in range(3):
                weight(t, i).start()

    greet(routes, d, z)

    @pl.when(role == 1)
    def _():
        back_copy().start()

    @pl.loop(0, ticks)
    def _(n):
        @pl.when(role == 0)
        def _():
            pl.when(n == 0)(begin_feed)

            @pl.when((n < first_attention) & (lax.rem(n, 2) == 0))
            def _():
                feed(lax.div(n, 2))

            pl.when(n == first_attention)(end_feed)

            @pl.when((n >= first_attention) & (n < last_attention))
            def _():
                attention(n - first_attention)

            pl.when(n == last_attention)(end_attention)

        for k in range(ticks):

            @pl.when(n == k)
            def _(k=k):
                if k == last_attention:
                    vec_pack()
                if k > last_attention and k - last_attention - 1 < len(bits):
                    vec_step(k - last_attention - 1)

                @pl.when(role == 0)
                def _():
                    enc.begin(k)
                    enc.tick(k)

                @pl.when(role == 1)
                def _():
                    play.begin(k)
                    play.tick(k)

    for s in range(max(0, ticks - last_attention - 1), len(bits)):
        vec_step(s)

    def put_block(first):
        def put(total):
            block_ref[:, first : first + total.shape[1]] = total.astype(bf16)

        return put

    def put_embed(total):
        emb_ref[...] = total

    for j in range(2):
        play.collect(j, put_block(3 * mat + j * mat))
    for j, first in ((0, 2 * mat), (1, mat), (2, 0)):
        enc.collect(j, put_block(first))
    enc.collect(3, put_embed)
    end = 3 * mat + pred_cols
    block_ref[:, end:] = jnp.zeros((rows, block_ref.shape[1] - end), bf16)

    @pl.when(role == 0)
    def _():
        enc.finish()

    @pl.when(role == 1)
    def _():
        play.finish()
        back_copy().wait_send()

    for s in range(len(bits)):
        vec_copy(s).wait_send()


def whole(shape):
    return pl.BlockSpec(shape, lambda *_: (0,) * len(shape))


def by_group(shape):
    return pl.BlockSpec((1,) + shape, lambda t: (t, 0, 0))


def compiled():
    return pltpu.CompilerParams(
        dimension_semantics=("arbitrary",), vmem_limit_bytes=KERNEL_BYTES
    )


def cost(flops, moved):
    return pl.CostEstimate(flops=int(flops), bytes_accessed=int(moved), transcendentals=0)


def sincos(cell_index, columns):
    quarter = columns // 4
    frequency = 1.0 / 10000.0 ** (jnp.arange(quarter).astype(f32) / quarter)
    col_angle = (cell_index % SIDE).astype(f32)[..., None] * frequency
    row_angle = (cell_index // SIDE).astype(f32)[..., None] * frequency
    return jnp.concatenate(
        [jnp.sin(col_angle), jnp.cos(col_angle), jnp.sin(row_angle), jnp.cos(row_angle)], -1
    )


def adamw(master, moment, second, gradient, step_rate, weight_decay):
    moment = 0.9 * moment + 0.1 * gradient
    second = 0.999 * second + 0.001 * gradient * gradient
    unbiased_first = moment / (1.0 - 0.9**STEP)
    unbiased_second = second / (1.0 - 0.999**STEP)
    return (
        master
        - step_rate
        * (unbiased_first / (jnp.sqrt(unbiased_second) + 1e-08) + weight_decay * master),
        moment,
        second,
    )


class Routes:
    def __init__(self, nd, nt):
        self.nd, self.nt = nd, nt
        self.low_bits = [1 << s for s in range(1, nd.bit_length() - 1)]
        self.stages = len(self.low_bits)

    def order(self, core):
        return self.low_bits if core == 0 else self.low_bits[::-1]

    def pairs(self, target, keep):
        found = []
        for d in range(self.nd):
            for z in range(self.nt):
                if keep(d, z):
                    d2, z2 = target(d, z)
                    found.append((d * self.nt + z, d2 * self.nt + z2))
        return found

    def partner(self, number, d, z):
        if number == self.stages:
            return flip(d, 1), z
        core = lax.rem(d, 2)
        ends = flip(d, self.order(0)[number]), flip(d, self.order(1)[number])
        return ends[0] + core * (ends[1] - ends[0]), z

    def across(self, r, values, from_role=None):
        def keep(d, z):
            return from_role is None or z % 2 == from_role

        return lax.ppermute(values, AXES, self.pairs(lambda d, z: (d, z ^ r), keep))

    def holders(self, d):
        place = jnp.arange(self.nd, dtype=jnp.int32)
        held = d ^ (place >> self.stages)
        core = held & 1
        for s in range(self.stages):
            bit = (place >> s) & 1
            held = held ^ (bit * jnp.where(core == 0, self.order(0)[s], self.order(1)[s]))
        return held

    def total(self, values):
        for bit in [1] + self.low_bits:
            values = values + lax.ppermute(
                values, AXES, self.pairs(lambda d, z, b=bit: (d ^ b, z), lambda d, z: True)
            )
        r = 1
        while r < self.nt:
            values = values + self.across(r, values)
            r *= 2
        return values


def shards(
    patches,
    ctx_idx,
    tgt_idx,
    owner,
    weights,
    stats_left,
    stats_right,
    root_left,
    root_right,
    teacher_slot_blocks,
    embed,
    embed_m,
    embed_v,
    teacher_embed,
    enc_vectors,
    enc_m,
    enc_v,
    pred_vectors,
    pred_m,
    pred_v,
    teacher_vectors,
):
    nt = lax.axis_size("tensor")
    nd = lax.axis_size("dp")
    routes = Routes(nd, nt)
    half = nt // 2
    d = lax.axis_index("dp")
    z = lax.axis_index("tensor")
    role = z % 2
    student_role = role == 0
    images, npatches, pix_part = patches.shape
    slots = weights.shape[1]
    edge = weights.shape[-1]
    slot_count = slots * nd
    block_count = owner.shape[0]
    width = enc_vectors.shape[1]
    narrow = pred_vectors.shape[1]
    players = (pred_vectors.shape[0] - 3) // 4
    side = width // edge
    teach_count = 3 * side * side
    quarter = width // nt
    context_len = ctx_idx.shape[1]
    target_len = tgt_idx.shape[1]
    seq_len = context_len + target_len
    share = images // half
    rows_part = edge // nd

    both = jnp.stack([weights[0], teacher_slot_blocks[0]]).astype(bf16)
    both = both.reshape(2, slots, nd, rows_part, edge)
    both = lax.all_to_all(both, "dp", split_axis=2, concat_axis=0, tiled=False)
    by_slot = both.transpose(1, 0, 2, 3, 4).reshape(2, slot_count, rows_part, edge)
    mine = by_slot[0][owner].transpose(1, 0, 2).reshape(rows_part, -1)
    teach = by_slot[1][owner[:teach_count]].transpose(1, 0, 2).reshape(rows_part, -1)

    mat = side * width

    def embed_rows(values):
        turned = values.astype(bf16).T.reshape(side, rows_part, pix_part)
        return turned.transpose(1, 0, 2).reshape(rows_part, -1)

    of_student = jnp.concatenate(
        [mine[:, :mat], embed_rows(embed), mine[:, mat : 3 * mat]], 1
    )
    of_teacher = jnp.concatenate([teach[:, :mat], embed_rows(teacher_embed), teach[:, mat:]], 1)
    own = jnp.where(student_role, of_student, of_teacher)
    other = jnp.where(student_role, of_teacher, of_student)
    pred_own = mine[:, 3 * mat :]

    holder = routes.holders(d)
    inside = jnp.arange(rows_part, dtype=jnp.int32)
    feat_p = (holder[:, None] * rows_part + inside[None, :]).reshape(-1)
    feat = jnp.concatenate([r * edge + feat_p for r in range(side)])
    one_hot = (feat[:, None] == jnp.arange(width)[None, :]).astype(f32)
    one_hot_p = (feat_p[:, None] == jnp.arange(narrow)[None, :]).astype(f32)

    def to_local(rows, hot):
        return jnp.einsum("nf,lf->nl", rows, hot, precision=exact, preferred_element_type=f32)

    def to_global(rows, hot):
        return jnp.einsum("nl,lf->nf", rows, hot, precision=exact, preferred_element_type=f32)

    vec = to_local(jnp.where(student_role, enc_vectors, teacher_vectors), one_hot)
    vec = jnp.pad(vec, ((0, 1), (0, 0)))
    pvec = to_local(pred_vectors, one_hot_p)
    pvec = jnp.pad(pvec, ((0, 16 - pvec.shape[0]), (0, 0)))
    pred_z = z - role + 1
    group_feat = (pred_z ^ jnp.arange(nt, dtype=jnp.int32))[:, None] * quarter + jnp.arange(
        quarter, dtype=jnp.int32
    )
    emb_feat = jnp.concatenate(
        [holder[:, None] * 2 * rows_part + m * rows_part + inside[None, :] for m in range(2)]
    ).reshape(-1)
    order = (feat[:, None] == emb_feat[None, :]).astype(bf16)
    swap = (feat[None, :, None] == group_feat[:, None, :]).astype(bf16)

    part = z // 2
    hot = (ctx_idx[:, :, None] == jnp.arange(npatches)[None, None, :]).astype(bf16)
    picked = jnp.einsum("gcn,gnp->gcp", hot, patches, preferred_element_type=f32).astype(bf16)

    def rows_for(target_z):
        where = (target_z // 2) * share
        ctx = lax.dynamic_slice_in_dim(picked, where, share, 0).reshape(-1, pix_part)
        every = lax.dynamic_slice_in_dim(patches, where, share, 0).reshape(-1, pix_part)
        padded = jnp.pad(ctx, ((0, every.shape[0] - ctx.shape[0]), (0, 0)))
        return jnp.where(target_z % 2 == 0, padded, every)

    patch_out = jnp.stack([rows_for(z ^ r) for r in range(nt)])
    my_ctx = lax.dynamic_slice_in_dim(ctx_idx, part * share, share, 0)
    my_tgt = lax.dynamic_slice_in_dim(tgt_idx, part * share, share, 0)
    full_rows = share * npatches
    ctx_rows = share * context_len
    tgt_rows = share * target_len
    ctx_places = jnp.pad(my_ctx.reshape(-1), (0, full_rows - ctx_rows))
    places = jnp.where(student_role, ctx_places, jnp.arange(full_rows) % npatches)
    table = to_local(sincos(jnp.arange(npatches), width), one_hot)
    table_p = to_local(sincos(jnp.arange(npatches), narrow), one_hot_p)
    base = table[places] + vec[6]
    tgt_places = (my_tgt + npatches * jnp.arange(share, dtype=jnp.int32)[:, None]).reshape(-1)
    pick = (tgt_places[:, None] == jnp.arange(full_rows)[None, :]).astype(bf16)
    widths = [mat + side * pix_part, mat, mat, mine.shape[1] - 3 * mat]
    any_space = pl.BlockSpec(memory_space=pl.ANY)
    dma = pltpu.SemaphoreType.DMA
    attn_cols = side * width
    columns = width // nt
    mat_shapes = [jax.ShapeDtypeStruct((nt, nd, rows_part, c), bf16) for c in widths]
    gather_sems = [
        dma((4, nt)),
        dma((4, nt)),
        dma((5,)),
        dma((nt,)),
        dma((nt,)),
        dma((4, nt, routes.stages + 1)),
        dma((4, nt, routes.stages + 1)),
    ]
    in_vmem = pl.BlockSpec(memory_space=VMEM)
    role_word = role.astype(jnp.int32).reshape(1)
    if rows_part % 16 == 0:
        results = pl.pallas_call(
            functools.partial(forward_kernel, routes, widths, npatches, context_len, HD),
            in_specs=[any_space] * 4 + [in_vmem] * 5,
            out_specs=[any_space] * 4 + [in_vmem] * 11,
            out_shape=mat_shapes
            + [
                jax.ShapeDtypeStruct((nt, ctx_rows, pix_part), bf16),
                jax.ShapeDtypeStruct((ctx_rows, width), f32),
                jax.ShapeDtypeStruct((ctx_rows, width), f32),
                jax.ShapeDtypeStruct((ctx_rows, width), bf16),
                jax.ShapeDtypeStruct((nt, ctx_rows, 3 * columns), bf16),
                jax.ShapeDtypeStruct((nt, ctx_rows, columns), bf16),
                jax.ShapeDtypeStruct((ctx_rows, width), f32),
                jax.ShapeDtypeStruct((ctx_rows, width), bf16),
                jax.ShapeDtypeStruct((nt, ctx_rows, width), f32),
                jax.ShapeDtypeStruct((nt, ctx_rows, quarter), bf16),
                jax.ShapeDtypeStruct((nt, tgt_rows, quarter), bf16),
            ],
            scratch_shapes=[VMEM(shape.shape, bf16) for shape in mat_shapes]
            + [
                VMEM((nt, full_rows, pix_part), bf16),
                VMEM((full_rows, width), f32),
                VMEM((full_rows, width), bf16),
                VMEM((nt, ctx_rows, quarter), bf16),
                VMEM((nt, ctx_rows, quarter), bf16),
                dma((4, nt)),
                dma(()),
                dma(()),
            ]
            + gather_sems,
            compiler_params=pltpu.CompilerParams(
                collective_id=0, has_side_effects=True, vmem_limit_bytes=KERNEL_BYTES
            ),
            cost_estimate=cost(14e9, 60e6),
            name="gather_and_encode",
        )(own, other, pred_own, patch_out, base, order, vec, pick, swap)
        gathered, results = results[:4], results[4:]
        patch_rows, middle, resid, normed_a, rows_a, att_a = results[:6]
        output, normed_f, hidden, feat_in, target = results[6:]
        attn_emb, up_w, down_t, pred_all = (g.reshape(nt, edge, -1) for g in gathered)
    else:
        attn_emb, up_w, down_t, pred_all, patch_rows = pl.pallas_call(
            functools.partial(gather_kernel, routes, widths, ctx_rows),
            in_specs=[any_space] * 4,
            out_specs=[any_space] * 5,
            out_shape=mat_shapes
            + [jax.ShapeDtypeStruct((nt, full_rows, pix_part), bf16)],
            scratch_shapes=gather_sems,
            compiler_params=pltpu.CompilerParams(collective_id=0, has_side_effects=True),
            cost_estimate=cost(0, 50e6),
            name="gather_weights",
        )(own, other, pred_own, patch_out)
        attn_emb, up_w, down_t, pred_all = (
            value.reshape(nt, edge, -1) for value in (attn_emb, up_w, down_t, pred_all)
        )
        middle, resid, normed_a, rows_a, att_a = pl.pallas_call(
            functools.partial(encoder_attend_kernel, edge, npatches, context_len, HD, ctx_rows),
            grid=(2 * nt,),
            in_specs=[
                pl.BlockSpec(memory_space=pltpu.SMEM),
                pl.BlockSpec((1, full_rows, pix_part), lambda i: (jnp.minimum(i, nt - 1), 0, 0)),
                whole((full_rows, width)),
                pl.BlockSpec(
                    (1, edge, side * pix_part),
                    lambda i: (jnp.minimum(i, nt - 1), 0, attn_cols // (side * pix_part)),
                ),
                whole((width, width)),
                pl.BlockSpec((1, edge, attn_cols), lambda i: (jnp.maximum(i - nt, 0), 0, 0)),
                whole((8, width)),
            ],
            out_specs=[
                whole((full_rows, width)),
                whole((ctx_rows, width)),
                whole((ctx_rows, width)),
                pl.BlockSpec((1, ctx_rows, 3 * columns), lambda i: (jnp.maximum(i - nt, 0), 0, 0)),
                pl.BlockSpec((1, ctx_rows, columns), lambda i: (jnp.maximum(i - nt, 0), 0, 0)),
            ],
            out_shape=[
                jax.ShapeDtypeStruct((full_rows, width), f32),
                jax.ShapeDtypeStruct((ctx_rows, width), f32),
                jax.ShapeDtypeStruct((ctx_rows, width), bf16),
                jax.ShapeDtypeStruct((nt, ctx_rows, 3 * columns), bf16),
                jax.ShapeDtypeStruct((nt, ctx_rows, columns), bf16),
            ],
            scratch_shapes=[VMEM((full_rows, width), f32), VMEM((full_rows, width), bf16)],
            compiler_params=compiled(),
            cost_estimate=cost(6e9, 12e6),
            name="encoder_attend",
        )(role_word, patch_rows, base, attn_emb, order, attn_emb, vec)
        output, normed_f, hidden, enc_feat, target = pl.pallas_call(
            functools.partial(encoder_feed_kernel, edge, ctx_rows),
            grid=(nt,),
            in_specs=[
                whole((full_rows, width)),
                by_group((edge, mat)),
                by_group((edge, mat)),
                whole((8, width)),
                whole((tgt_rows, full_rows)),
                whole((nt, width, quarter)),
            ],
            out_specs=[
                whole((ctx_rows, width)),
                whole((ctx_rows, width)),
                by_group((ctx_rows, width)),
                whole((nt, ctx_rows, quarter)),
                whole((nt, tgt_rows, quarter)),
            ],
            out_shape=[
                jax.ShapeDtypeStruct((ctx_rows, width), f32),
                jax.ShapeDtypeStruct((ctx_rows, width), bf16),
                jax.ShapeDtypeStruct((nt, ctx_rows, width), f32),
                jax.ShapeDtypeStruct((nt, ctx_rows, quarter), bf16),
                jax.ShapeDtypeStruct((nt, tgt_rows, quarter), bf16),
            ],
            scratch_shapes=[VMEM((full_rows, width), f32), VMEM((full_rows, width), bf16)],
            compiler_params=compiled(),
            cost_estimate=cost(8e9, 14e6),
            name="encoder_feed",
        )(middle, up_w, down_t, vec, pick, swap)

        feat_in = routes.across(1, enc_feat, from_role=0)

    tokens_at = table_p[jnp.concatenate([my_ctx, my_tgt], 1)]
    mask_rows = jnp.arange(seq_len)[None, :, None] >= context_len
    tokens_at = jnp.where(mask_rows, tokens_at + pvec[4 * players + 2], tokens_at)
    tokens_at = tokens_at.reshape(-1, narrow)
    token_rows = share * seq_len
    pred_cols = (3 * players + 1) * edge
    denominator = images * nd * target_len * width
    pred_columns = narrow // nt
    pred_grads, pred_vec_g, loss_tile, back = pl.pallas_call(
        functools.partial(predictor_kernel, share, context_len, players, PHD, denominator),
        in_specs=[in_vmem] * 6,
        out_specs=[in_vmem] * 4,
        out_shape=[
            jax.ShapeDtypeStruct((nt, edge, pred_cols), bf16),
            jax.ShapeDtypeStruct((16, narrow), f32),
            jax.ShapeDtypeStruct((8, 128), f32),
            jax.ShapeDtypeStruct((ctx_rows, width), bf16),
        ],
        scratch_shapes=[
            VMEM((players + 1, token_rows, narrow), f32),
            VMEM((players, token_rows, narrow), f32),
            VMEM((players, token_rows, narrow), bf16),
            VMEM((players, token_rows, narrow), bf16),
            VMEM((players, nt, token_rows, 3 * pred_columns), bf16),
            VMEM((players, nt, token_rows, pred_columns), bf16),
            VMEM((players, nt, token_rows, edge), f32),
            VMEM((token_rows, narrow), f32),
            VMEM((token_rows, narrow), f32),
            VMEM((token_rows, narrow), bf16),
            VMEM((tgt_rows, narrow), bf16),
        ],
        compiler_params=pltpu.CompilerParams(vmem_limit_bytes=KERNEL_BYTES),
        cost_estimate=cost(16e9, 30e6),
        name="predictor",
    )(feat_in, target, tokens_at, pred_all, pvec, swap)
    all_cols = attn_cols + side * pix_part
    middle_size = nd // 2
    block_shape = [
        jax.ShapeDtypeStruct((rows_part, (block_count + 1) * edge), bf16),
        jax.ShapeDtypeStruct((rows_part, side * pix_part), f32),
    ]
    if rows_part % 16 == 0:
        widths_g = (mat, mat, mat, side * pix_part)
        vec_steps = nd.bit_length() + nt.bit_length() - 2
        by_block, emb_sum, vec_sum = pl.pallas_call(
            functools.partial(backward_kernel, routes, context_len, HD),
            in_specs=[any_space] * 5 + [in_vmem] * 15,
            out_specs=[in_vmem] * 3,
            out_shape=block_shape + [jax.ShapeDtypeStruct((32, edge), f32)],
            scratch_shapes=[VMEM((nt, nd, rows_part, c), bf16) for c in widths_g]
            + [VMEM((nt, middle_size, rows_part, c), bf16) for c in widths_g]
            + [VMEM((nt, middle_size - 1, rows_part, c), bf16) for c in widths_g]
            + [
                VMEM((nt, rows_part, sum(widths_g)), bf16),
                VMEM((nt, rows_part, pred_cols), bf16),
                VMEM((2, edge, mat), bf16),
                VMEM((2, edge, mat), bf16),
                VMEM((2, edge, mat), bf16),
                VMEM((ctx_rows, width), bf16),
                VMEM((ctx_rows, width), f32),
                VMEM((ctx_rows, width), bf16),
                VMEM((ctx_rows, width), f32),
                VMEM((8, width), f32),
                VMEM((vec_steps, 32, edge), f32),
                VMEM((vec_steps, 32, edge), f32),
                dma((3, 2)),
                dma(()),
                dma(()),
                dma((4, nt)),
                dma((4, nt)),
                dma((4, nt)),
                dma((4, nt, routes.stages)),
                dma((4, nt, routes.stages)),
                dma((2, 4, nt)),
                dma((2, 4, nt)),
                dma((vec_steps,)),
                dma((vec_steps,)),
            ],
            compiler_params=pltpu.CompilerParams(
                collective_id=1, has_side_effects=True, vmem_limit_bytes=KERNEL_BYTES
            ),
            cost_estimate=cost(14e9, 60e6),
            name="encode_back_and_reduce",
        )(
            pred_grads.reshape(nt, nd, rows_part, -1), back, attn_emb, up_w, down_t,
            output, middle, resid, normed_f, normed_a, hidden, rows_a, att_a, patch_rows,
            vec, order, one_hot.astype(bf16), one_hot_p.astype(bf16), pred_vec_g, loss_tile,
        )
        enc_total = jnp.concatenate([vec_sum[:7], vec_sum[8:15]], 1)
        pred_total = vec_sum[16 : 16 + 4 * players + 3]
        loss_total = vec_sum[28, 0]
    else:
        back = routes.across(1, back, from_role=1)

        grad_shape = jax.ShapeDtypeStruct((nt, edge, mat), bf16)
        up_g, down_g, grad_mid, vec_g1 = pl.pallas_call(
            functools.partial(encoder_feed_back_kernel, edge),
            grid=(nt,),
            in_specs=[
                whole((ctx_rows, width)),
                whole((ctx_rows, width)),
                whole((ctx_rows, width)),
                whole((ctx_rows, width)),
                by_group((ctx_rows, width)),
                by_group((edge, mat)),
                by_group((edge, mat)),
                whole((8, width)),
            ],
            out_specs=[by_group((edge, mat))] * 2 + [whole((ctx_rows, width)), whole((8, width))],
            out_shape=[grad_shape] * 2
            + [
                jax.ShapeDtypeStruct((ctx_rows, width), f32),
                jax.ShapeDtypeStruct((8, width), f32),
            ],
            scratch_shapes=[
                VMEM((ctx_rows, width), f32),
                VMEM((ctx_rows, width), bf16),
                VMEM((ctx_rows, width), f32),
            ],
            compiler_params=compiled(),
            cost_estimate=cost(8e9, 25e6),
            name="encoder_feed_back",
        )(back, output, middle, normed_f, hidden, up_w, down_t, vec)
        attn_g, vec_g2 = pl.pallas_call(
            functools.partial(encoder_attend_back_kernel, edge, npatches, context_len, HD),
            grid=(2 * nt,),
            in_specs=[
                pl.BlockSpec(memory_space=pltpu.SMEM),
                whole((ctx_rows, width)),
                whole((ctx_rows, width)),
                whole((ctx_rows, width)),
                pl.BlockSpec((1, ctx_rows, 3 * columns), lambda i: (jnp.minimum(i, nt - 1), 0, 0)),
                pl.BlockSpec((1, ctx_rows, columns), lambda i: (jnp.minimum(i, nt - 1), 0, 0)),
                pl.BlockSpec((1, edge, attn_cols), lambda i: (jnp.minimum(i, nt - 1), 0, 0)),
                pl.BlockSpec((1, ctx_rows, pix_part), lambda i: (jnp.maximum(i - nt, 0), 0, 0)),
                whole((width, width)),
                whole((8, width)),
            ],
            out_specs=[
                whole((nt, edge, all_cols)),
                whole((8, width)),
            ],
            out_shape=[
                jax.ShapeDtypeStruct((nt, edge, all_cols), bf16),
                jax.ShapeDtypeStruct((8, width), f32),
            ],
            scratch_shapes=[VMEM((ctx_rows, width), bf16), VMEM((ctx_rows, width), f32)],
            compiler_params=compiled(),
            cost_estimate=cost(6e9, 20e6),
            name="encoder_attend_back",
        )(role_word, grad_mid, resid, normed_a, rows_a, att_a, attn_emb, patch_rows, order, vec)

        places = [g.reshape(nt, nd, rows_part, -1) for g in (down_g, up_g, attn_g, pred_grads)]
        by_block, emb_sum = pl.pallas_call(
            functools.partial(reduce_kernel, routes, attn_cols),
            in_specs=[any_space] * 4,
            out_specs=[in_vmem] * 2,
            out_shape=block_shape,
            scratch_shapes=[
                VMEM((nt, middle_size, rows_part, mat), bf16),
                VMEM((nt, middle_size, rows_part, mat), bf16),
                VMEM((nt, middle_size, rows_part, all_cols), bf16),
                VMEM((nt, middle_size - 1, rows_part, mat), bf16),
                VMEM((nt, middle_size - 1, rows_part, mat), bf16),
                VMEM((nt, middle_size - 1, rows_part, all_cols), bf16),
                VMEM((nt, rows_part, 2 * mat + all_cols), bf16),
                VMEM((nt, rows_part, pred_cols), bf16),
                VMEM((2, middle_size, rows_part, all_cols), bf16),
                dma((2,)),
                dma((3, nt)),
                dma((3, nt)),
                dma((3, nt, routes.stages)),
                dma((3, nt, routes.stages)),
                dma((2, 3, nt)),
                dma((2, 3, nt)),
            ],
            compiler_params=pltpu.CompilerParams(
                collective_id=1, has_side_effects=True, vmem_limit_bytes=KERNEL_BYTES
            ),
            cost_estimate=cost(0, 60e6),
            name="reduce_gradients",
        )(*places)

        enc_rows = to_global(vec_g1[:7] + vec_g2[:7], one_hot)
        pred_rows = to_global(pred_vec_g[: 4 * players + 3], one_hot_p)
        enc_rows = jnp.where(student_role, enc_rows, 0.0)
        pred_rows = jnp.where(role == 1, pred_rows, 0.0)
        loss_row = jnp.where(role == 1, loss_tile[0, 0], 0.0)
        packed = jnp.concatenate([enc_rows.reshape(-1), pred_rows.reshape(-1), loss_row[None]])
        packed = jnp.pad(packed, (0, -packed.shape[0] % 1024)).reshape(-1, 128)
        packed = routes.total(packed).reshape(-1)
        enc_total = packed[: enc_rows.size].reshape(enc_rows.shape)
        pred_total = packed[enc_rows.size : enc_rows.size + pred_rows.size].reshape(pred_rows.shape)
        loss_total = packed[enc_rows.size + pred_rows.size]

    by_block = by_block.reshape(rows_part, block_count + 1, edge).transpose(1, 0, 2)
    slot_of = (
        jnp.full((slot_count,), block_count, jnp.int32)
        .at[owner]
        .set(jnp.arange(block_count, dtype=jnp.int32))
    )
    slot_rows = by_block[slot_of].reshape(nd, slots, rows_part, edge)
    slot_rows = lax.all_to_all(slot_rows, "dp", split_axis=0, concat_axis=1, tiled=False)
    low_grads = slot_rows.reshape(slots, edge, edge)

    embed_grad = emb_sum.reshape(rows_part, side, pix_part).transpose(1, 0, 2)
    embed_grad = embed_grad.reshape(-1, pix_part).T

    slot_spec = pl.BlockSpec((1, 1, edge, edge), lambda s: (0, s, 0, 0))
    slot_shape = jax.ShapeDtypeStruct(weights.shape, f32)
    slot_grads, new_weights, new_left, new_right, new_teacher_blocks = pl.pallas_call(
        shampoo_kernel,
        grid=(slots,),
        in_specs=[pl.BlockSpec((1, edge, edge), lambda s: (s, 0, 0))] + [slot_spec] * 6,
        out_specs=[slot_spec] * 5,
        out_shape=[slot_shape] * 5,
        compiler_params=compiled(),
        cost_estimate=cost(3e9, 22e6),
        name="shampoo",
    )(low_grads, weights, stats_left, stats_right, root_left, root_right, teacher_slot_blocks)
    new_embed, new_embed_m, new_embed_v = adamw(embed, embed_m, embed_v, embed_grad, 0.05, 0.05)
    new_enc, new_enc_m, new_enc_v = adamw(enc_vectors, enc_m, enc_v, enc_total, 0.5, 0.0)
    new_pred, new_pred_m, new_pred_v = adamw(pred_vectors, pred_m, pred_v, pred_total, 0.5, 0.0)
    new_teacher_embed = 0.7 * teacher_embed + 0.3 * new_embed
    new_teacher_vectors = 0.7 * teacher_vectors + 0.3 * new_enc
    return (
        loss_total,
        slot_grads,
        new_weights,
        new_left,
        new_right,
        new_teacher_blocks,
        new_embed,
        new_embed_m,
        new_embed_v,
        new_teacher_embed,
        new_enc,
        new_enc_m,
        new_enc_v,
        new_pred,
        new_pred_m,
        new_pred_v,
        new_teacher_vectors,
    )


def solution(mesh):
    blocks = P("tensor", "dp", None, None)
    table = P("tensor", "dp")
    in_specs = (
        (P("dp", None, "tensor"), P("dp", None), P("dp", None), P())
        + (blocks,) * 6
        + (table,) * 4
        + (P(),) * 7
    )
    out_specs = (P(),) + (blocks,) * 5 + (table,) * 4 + (P(),) * 7
    return jax.shard_map(shards, mesh=mesh, in_specs=in_specs, out_specs=out_specs, check_vma=False)
```

```python
import functools
import math

import jax
import jax.numpy as jnp
import numpy as np
from jax import lax
from jax.experimental import pallas as pl
from jax.experimental.pallas import tpu as pltpu
from jax.sharding import PartitionSpec as P

HD = 64
PHD = 32
SIDE = 16
STEP = 10
KERNEL_BYTES = 60 * 1024 * 1024

AXES = ("dp", "tensor")
exact = lax.Precision.HIGHEST
f32 = jnp.float32
bf16 = jnp.bfloat16
VMEM = pltpu.VMEM


def nn(first, second):
    return lax.dot_general(first, second, (((1,), (0,)), ((), ())), preferred_element_type=f32)


def nt_(first, second):
    return lax.dot_general(first, second, (((1,), (1,)), ((), ())), preferred_element_type=f32)


def tn(first, second):
    return lax.dot_general(first, second, (((0,), (0,)), ((), ())), preferred_element_type=f32)


def norm_parts(values):
    centre = values - jnp.mean(values, -1, keepdims=True)
    scale = lax.rsqrt(jnp.mean(centre * centre, -1, keepdims=True) + 1e-06)
    return centre * scale, scale


def layer_norm(values, gain_row, shift_row):
    return norm_parts(values)[0] * gain_row + shift_row


def norm_backward(grad, values, gain_row):
    unit, scale = norm_parts(values)
    weighted = grad * gain_row
    inner = (
        weighted
        - jnp.mean(weighted, -1, keepdims=True)
        - unit * jnp.mean(weighted * unit, -1, keepdims=True)
    )
    return (
        inner * scale,
        jnp.sum(grad * unit, 0, keepdims=True),
        jnp.sum(grad, 0, keepdims=True),
    )


def gelu_parts(values):
    below = 0.5 * (1.0 + lax.erf(values * math.sqrt(0.5)))
    density = jnp.exp(-0.5 * values * values) * (1.0 / math.sqrt(2.0 * math.pi))
    return values * below, below + values * density


def softened_t(queries, keys, head_size, allowed):
    scores = nt_(keys, queries) * (1.0 / math.sqrt(head_size))
    if allowed is not None:
        scores = jnp.where(allowed, scores, -1e30)
    expo = jnp.exp(scores - jnp.max(scores, 0, keepdims=True))
    return expo * (1.0 / jnp.sum(expo, 0, keepdims=True))


def attend(rows, head_size, length, allowed):
    columns = rows.shape[1] // 3
    images = []
    for at in range(0, rows.shape[0], length):
        outs = []
        for h in range(0, columns, head_size):
            q, k, v = (
                rows[at : at + length, j * columns + h : j * columns + h + head_size]
                for j in range(3)
            )
            soft = softened_t(q, k, head_size, allowed).astype(bf16)
            outs.append(tn(v, soft).astype(bf16))
        images.append(jnp.concatenate(outs, 0))
    joined = jnp.concatenate(images, 1) if len(images) > 1 else images[0]
    return joined.T


def attend_back(rows, grad, head_size, length, allowed):
    columns = rows.shape[1] // 3
    factor = 1.0 / math.sqrt(head_size)
    images = []
    for at in range(0, rows.shape[0], length):
        outs = [[], [], []]
        for h in range(0, columns, head_size):
            q, k, v = (
                rows[at : at + length, j * columns + h : j * columns + h + head_size]
                for j in range(3)
            )
            g = grad[at : at + length, h : h + head_size]
            soft = softened_t(q, k, head_size, allowed)
            outs[2].append(nn(soft.astype(bf16), g).astype(bf16))
            ds = nt_(v, g)
            ds = (soft * (ds - jnp.sum(ds * soft, 0, keepdims=True))).astype(bf16)
            outs[0].append((tn(k, ds) * factor).astype(bf16))
            outs[1].append((nn(ds, q) * factor).astype(bf16))
        queries = jnp.concatenate(outs[0], 0).T
        images.append(jnp.concatenate([queries] + outs[1] + outs[2], 1))
    return jnp.concatenate(images, 0) if len(images) > 1 else images[0]


def same_image(role, length, context):
    row = lax.broadcasted_iota(jnp.int32, (length, length), 0) // context
    column = lax.broadcasted_iota(jnp.int32, (length, length), 1) // context
    return (row == column) | (role != 0)


def encoder_attend_kernel(
    edge, unit, context, head_size, kept,
    role_ref, patch_ref, base_ref, emb_ref, order_ref, w_ref, vec_ref,
    mid_ref, resid_ref, normed_ref, rows_ref, att_ref, x_ref, h_ref,
):
    step = pl.program_id(0)
    groups = pl.num_programs(0) // 2
    side = 2
    wide = side * edge
    pix = patch_ref.shape[2]
    columns = wide // 4

    @pl.when(step == 0)
    def _():
        x_ref[...] = base_ref[...]

    @pl.when(step < groups)
    def _():
        ordered = sum(
            nn(order_ref[:, m * edge : (m + 1) * edge], emb_ref[0, :, m * pix : (m + 1) * pix])
            for m in range(side)
        ).astype(bf16)
        x_ref[...] += nt_(patch_ref[0], ordered)

    @pl.when(step == groups - 1)
    def _():
        values = x_ref[...]
        resid_ref[...] = values[:kept]
        low = layer_norm(values, vec_ref[0:1], vec_ref[1:2]).astype(bf16)
        h_ref[...] = low
        normed_ref[...] = low[:kept]

    @pl.when(step >= groups)
    def _():
        rows = sum(
            nn(h_ref[:, r * edge : (r + 1) * edge], w_ref[0, :, r * wide : r * wide + 3 * columns])
            for r in range(side)
        ).astype(bf16)
        rows_ref[0] = rows[:kept]
        att = attend(rows, head_size, unit, same_image(role_ref[0], unit, context))
        att_ref[0] = att[:kept]
        for r in range(side):
            x_ref[:, r * edge : (r + 1) * edge] += nt_(
                att, w_ref[0, :, r * wide + 3 * columns : (r + 1) * wide]
            )

    @pl.when(step == 2 * groups - 1)
    def _():
        mid_ref[...] = x_ref[...]


def encoder_feed_kernel(
    edge, kept, mid_ref, up_ref, down_ref, vec_ref, pick_ref, swap_ref,
    out_ref, normed_ref, hidden_ref, feat_ref, target_ref, x_ref, h_ref,
):
    step = pl.program_id(0)
    groups = pl.num_programs(0)
    side = 2
    wide = side * edge

    @pl.when(step == 0)
    def _():
        values = mid_ref[...]
        x_ref[...] = values
        low = layer_norm(values, vec_ref[2:3], vec_ref[3:4]).astype(bf16)
        h_ref[...] = low
        normed_ref[...] = low[:kept]

    hidden = sum(
        nn(h_ref[:, r * edge : (r + 1) * edge], up_ref[0, :, r * wide : (r + 1) * wide])
        for r in range(side)
    )
    hidden_ref[0] = hidden[:kept]
    active = gelu_parts(hidden)[0].astype(bf16)
    for r in range(side):
        x_ref[:, r * edge : (r + 1) * edge] += nt_(
            active, down_ref[0, :, r * wide : (r + 1) * wide]
        )

    @pl.when(step == groups - 1)
    def _():
        values = x_ref[...]
        out_ref[...] = values[:kept]
        final = layer_norm(values, vec_ref[4:5], vec_ref[5:6])
        encoded = final[:kept].astype(bf16)
        target = norm_parts(final)[0].astype(bf16)
        picked = nn(pick_ref[...], target).astype(bf16)
        for t in range(swap_ref.shape[0]):
            feat_ref[t] = nn(encoded, swap_ref[t]).astype(bf16)
            target_ref[t] = nn(picked, swap_ref[t]).astype(bf16)


def put(grad_ref, t, columns, value):
    grad_ref[t, :, columns] = value.astype(bf16)


def predictor_kernel(
    share, context, players, head_size, denominator,
    feat_ref, target_ref, base_ref, w_hbm, vec_ref, hot_ref,
    grad_hbm, vec_grad_ref, loss_ref, back_ref,
    w_ref, grad_ref, w_sem, grad_sem, x_ref, mid_ref, h_ref, h2_ref, rows_ref, att_ref, hidden_ref, acc_ref, d_ref, low_ref, f_ref,
):
    groups = w_ref.shape[0]
    edge = w_ref.shape[1]
    length = base_ref.shape[0] // share
    quarter = feat_ref.shape[2]
    columns = edge // 4
    last = 3 * players * edge
    in_cols = slice(last, last + quarter)
    out_cols = slice(last + quarter, last + 2 * quarter)

    def span(number):
        return slice(number * edge, (number + 1) * edge)

    def copy_in(number):
        columns = pl.ds(number * edge, edge)
        return pltpu.make_async_copy(
            w_hbm.at[:, :, columns], w_ref.at[:, :, columns], w_sem.at[number]
        )

    def copy_out(number):
        columns = pl.ds(number * edge, edge)
        return pltpu.make_async_copy(
            grad_ref.at[:, :, columns], grad_hbm.at[:, :, columns], grad_sem.at[number]
        )

    def pair(p, number):
        return jnp.concatenate([w_ref[2 * p + i, :, span(number)] for i in range(2)], 1)

    def put_pair(p, number, value):
        for i in range(2):
            put(grad_ref, 2 * p + i, span(number), value[:, i * edge : (i + 1) * edge])

    for number in [3 * players] + list(range(3 * players)):
        copy_in(number).start()
    vec_grad_ref[...] = jnp.zeros_like(vec_grad_ref)
    copy_in(3 * players).wait()
    projected = sum(nt_(feat_ref[t], w_ref[t, :, in_cols]) for t in range(groups))
    x_ref[0] = base_ref[...]
    for i in range(share):
        x_ref[0, i * length : i * length + context] += projected[i * context : (i + 1) * context]

    for j in range(players):
        values = x_ref[j]
        h_ref[j] = layer_norm(values, vec_ref[4 * j : 4 * j + 1], vec_ref[4 * j + 1 : 4 * j + 2]).astype(bf16)
        mid_ref[j] = values
        copy_in(3 * j).wait()

        @pl.loop(0, groups)
        def _(t, j=j):
            rows = nn(h_ref[j], w_ref[t, :, 3 * j * edge : 3 * j * edge + 3 * columns]).astype(bf16)
            rows_ref[j, t] = rows
            att = attend(rows, head_size, length, None)
            att_ref[j, t] = att
            mid_ref[j] += nt_(att, w_ref[t, :, 3 * j * edge + 3 * columns : (3 * j + 1) * edge])

        values = mid_ref[j]
        h2_ref[j] = layer_norm(values, vec_ref[4 * j + 2 : 4 * j + 3], vec_ref[4 * j + 3 : 4 * j + 4]).astype(bf16)
        x_ref[j + 1] = values
        copy_in(3 * j + 1).wait()
        copy_in(3 * j + 2).wait()

        @pl.loop(0, groups // 2)
        def _(p, j=j):
            hidden = nn(h2_ref[j], pair(p, 3 * j + 1))
            hidden_ref[j, p] = hidden
            x_ref[j + 1] += nt_(gelu_parts(hidden)[0].astype(bf16), pair(p, 3 * j + 2))

    final_gain = vec_ref[4 * players : 4 * players + 1]
    final = layer_norm(x_ref[players], final_gain, vec_ref[4 * players + 1 : 4 * players + 2]).astype(bf16)
    f_ref[...] = jnp.concatenate(
        [final[i * length + context : (i + 1) * length] for i in range(share)], 0
    )
    total = jnp.zeros((1, 1), f32)
    grad_f = jnp.zeros(f_ref.shape, f32)
    for t in range(groups):
        out_w = w_ref[t, :, out_cols]
        gap = nn(f_ref[...], out_w) - target_ref[t].astype(f32)
        size = jnp.abs(gap)
        terms = jnp.where(size < 1.0, 0.5 * gap * gap, size - 0.5)
        total += jnp.sum(jnp.sum(terms, 1, keepdims=True), 0, keepdims=True)
        grad_pred = (jnp.clip(gap, -1.0, 1.0) * (1.0 / denominator)).astype(bf16)
        put(grad_ref, t, out_cols, tn(f_ref[...], grad_pred))
        grad_f += nt_(grad_pred, out_w)
    loss_ref[...] = jnp.broadcast_to(total * (1.0 / denominator), loss_ref.shape)
    d_ref[...] = jnp.zeros_like(d_ref)
    tail = length - context
    for i in range(share):
        d_ref[i * length + context : (i + 1) * length] = grad_f[i * tail : (i + 1) * tail]
    grad, gain_g, shift_g = norm_backward(d_ref[...], x_ref[players], final_gain)
    d_ref[...] = grad
    vec_grad_ref[4 * players : 4 * players + 1] = gain_g
    vec_grad_ref[4 * players + 1 : 4 * players + 2] = shift_g

    for j in reversed(range(players)):
        low_ref[...] = d_ref[...].astype(bf16)
        acc_ref[...] = jnp.zeros_like(acc_ref)

        @pl.loop(0, groups // 2)
        def _(p, j=j):
            active, slope = gelu_parts(hidden_ref[j, p])
            low = low_ref[...]
            put_pair(p, 3 * j + 2, tn(low, active.astype(bf16)))
            grad_hidden = (nn(low, pair(p, 3 * j + 2)) * slope).astype(bf16)
            put_pair(p, 3 * j + 1, tn(h2_ref[j], grad_hidden))
            acc_ref[...] += nt_(grad_hidden, pair(p, 3 * j + 1))

        copy_out(3 * j + 2).start()
        copy_out(3 * j + 1).start()
        grad, gain_g, shift_g = norm_backward(
            acc_ref[...], mid_ref[j], vec_ref[4 * j + 2 : 4 * j + 3]
        )
        vec_grad_ref[4 * j + 2 : 4 * j + 3] = gain_g
        vec_grad_ref[4 * j + 3 : 4 * j + 4] = shift_g
        grad = d_ref[...] + grad
        d_ref[...] = grad
        low_ref[...] = grad.astype(bf16)
        acc_ref[...] = jnp.zeros_like(acc_ref)

        @pl.loop(0, groups)
        def _(t, j=j):
            low = low_ref[...]
            attn_w = w_ref[t, :, span(3 * j)]
            grad_att = nn(low, attn_w[:, 3 * columns :]).astype(bf16)
            grad_rows = attend_back(rows_ref[j, t], grad_att, head_size, length, None)
            grad_w = jnp.concatenate([tn(h_ref[j], grad_rows), tn(low, att_ref[j, t])], 1)
            put(grad_ref, t, span(3 * j), grad_w)
            acc_ref[...] += nt_(grad_rows, attn_w[:, : 3 * columns])

        copy_out(3 * j).start()
        grad, gain_g, shift_g = norm_backward(acc_ref[...], x_ref[j], vec_ref[4 * j : 4 * j + 1])
        vec_grad_ref[4 * j : 4 * j + 1] = gain_g
        vec_grad_ref[4 * j + 1 : 4 * j + 2] = shift_g
        d_ref[...] += grad

    mask_grad = jnp.zeros((1, edge), f32)
    for i in range(share):
        mask_grad += jnp.sum(d_ref[i * length + context : (i + 1) * length], 0, keepdims=True)
    vec_grad_ref[4 * players + 2 : 4 * players + 3] = mask_grad
    low = jnp.concatenate(
        [d_ref[i * length : i * length + context] for i in range(share)], 0
    ).astype(bf16)
    back = jnp.zeros((low.shape[0], hot_ref.shape[1]), f32)
    z = lax.axis_index("tensor")
    z = z - lax.rem(z, 2) + 1
    for t in range(groups):
        put(grad_ref, t, in_cols, tn(low, feat_ref[t]))
        first = pl.multiple_of(flip(z, t) * quarter, 16)
        back += nn(nn(low, w_ref[t, :, in_cols]).astype(bf16), hot_ref[pl.ds(first, quarter), :])
    copy_out(3 * players).start()
    back_ref[...] = back.astype(bf16)
    for number in range(3 * players + 1):
        copy_out(number).wait()


def encoder_feed_back_kernel(
    edge, back_ref, out_ref, mid_ref, normed_ref, hidden_ref, up_ref, down_ref, vec_ref,
    up_grad, down_grad, grad_ref, vec_grad_ref, d_ref, low_ref, acc_ref,
):
    step = pl.program_id(0)
    groups = pl.num_programs(0)
    wide = 2 * edge

    @pl.when(step == 0)
    def _():
        grad, gain_g, shift_g = norm_backward(back_ref[...].astype(f32), out_ref[...], vec_ref[4:5])
        d_ref[...] = grad
        low_ref[...] = grad.astype(bf16)
        acc_ref[...] = jnp.zeros_like(acc_ref)
        vec_grad_ref[...] = jnp.zeros_like(vec_grad_ref)
        vec_grad_ref[4:5] = gain_g
        vec_grad_ref[5:6] = shift_g

    active, slope = gelu_parts(hidden_ref[0])
    active = active.astype(bf16)
    grad_hidden = sum(
        nn(low_ref[:, r * edge : (r + 1) * edge], down_ref[0, :, r * wide : (r + 1) * wide])
        for r in range(2)
    )
    grad_hidden = (grad_hidden * slope).astype(bf16)
    for r in range(2):
        mine = slice(r * edge, (r + 1) * edge)
        columns = slice(r * wide, (r + 1) * wide)
        put(down_grad, 0, columns, tn(low_ref[:, mine], active))
        put(up_grad, 0, columns, tn(normed_ref[:, mine], grad_hidden))
        acc_ref[:, mine] += nt_(grad_hidden, up_ref[0, :, columns])

    @pl.when(step == groups - 1)
    def _():
        grad, gain_g, shift_g = norm_backward(acc_ref[...], mid_ref[...], vec_ref[2:3])
        grad_ref[...] = d_ref[...] + grad
        vec_grad_ref[2:3] = gain_g
        vec_grad_ref[3:4] = shift_g


def encoder_attend_back_kernel(
    edge, unit, context, head_size,
    role_ref, mid_grad_ref, resid_ref, normed_ref, rows_ref, att_ref, w_ref, patch_ref, order_ref,
    vec_ref, grad_ref, vec_grad_ref, low_ref, acc_ref,
):
    step = pl.program_id(0)
    groups = pl.num_programs(0) // 2
    wide = 2 * edge
    columns = wide // 4
    pix = patch_ref.shape[2]

    @pl.when(step == 0)
    def _():
        low_ref[...] = mid_grad_ref[...].astype(bf16)
        acc_ref[...] = jnp.zeros_like(acc_ref)

    @pl.when(step < groups)
    def _():
        grad_att = sum(
            nn(
                low_ref[:, r * edge : (r + 1) * edge],
                w_ref[0, :, r * wide + 3 * columns : (r + 1) * wide],
            )
            for r in range(2)
        ).astype(bf16)
        allowed = same_image(role_ref[0], unit, context)
        grad_rows = attend_back(rows_ref[0], grad_att, head_size, unit, allowed)
        for r in range(2):
            mine = slice(r * edge, (r + 1) * edge)
            grad_w = jnp.concatenate(
                [tn(normed_ref[:, mine], grad_rows), tn(low_ref[:, mine], att_ref[0])], 1
            )
            put(grad_ref, step, slice(r * wide, (r + 1) * wide), grad_w)
            acc_ref[:, mine] += nt_(grad_rows, w_ref[0, :, r * wide : r * wide + 3 * columns])

    @pl.when(step == groups - 1)
    def _():
        grad, gain_g, shift_g = norm_backward(acc_ref[...], resid_ref[...], vec_ref[0:1])
        grad = mid_grad_ref[...] + grad
        low_ref[...] = nn(grad.astype(bf16), order_ref[...]).astype(bf16)
        vec_grad_ref[...] = jnp.zeros_like(vec_grad_ref)
        vec_grad_ref[0:1] = gain_g
        vec_grad_ref[1:2] = shift_g
        vec_grad_ref[6:7] = jnp.sum(grad, 0, keepdims=True)

    @pl.when(step >= groups)
    def _():
        grad_w = jnp.concatenate(
            [tn(low_ref[:, r * edge : (r + 1) * edge], patch_ref[0]) for r in range(2)], 1
        )
        put(grad_ref, step - groups, slice(2 * wide, 2 * wide + 2 * pix), grad_w)


def shampoo_kernel(
    grad_ref, weight_ref, left_ref, right_ref, root_left_ref, root_right_ref, teacher_ref,
    grad_out, weight_out, left_out, right_out, teacher_out,
):
    low = grad_ref[0]
    grad_out[0, 0] = low.astype(f32)
    left_out[0, 0] = 0.95 * left_ref[0, 0] + 0.05 * nt_(low, low)
    right_out[0, 0] = 0.95 * right_ref[0, 0] + 0.05 * tn(low, low)
    high, rest = split(root_left_ref[0, 0])
    side = nn(high, low) + nn(rest, low)
    high, rest = split(side)
    root_high, root_rest = split(root_right_ref[0, 0])
    step = nn(high, root_high) + nn(high, root_rest) + nn(rest, root_high)
    mean = jnp.mean(jnp.mean(step * step, 1, keepdims=True), 0, keepdims=True)
    step = step * lax.rsqrt(mean + 1e-06)
    weight = weight_ref[0, 0]
    new = weight - 0.05 * (step + 0.05 * weight)
    weight_out[0, 0] = new
    teacher_out[0, 0] = 0.7 * teacher_ref[0, 0] + 0.3 * new


MESH = pl.DeviceIdType.MESH


def flip(place, bits):
    bit = 1
    while bit <= bits:
        if bits & bit:
            place = place + bit * (1 - 2 * lax.rem(lax.div(place, bit), 2))
        bit *= 2
    return place


def remote(source, target, send_sem, recv_sem, device):
    return pltpu.make_async_remote_copy(
        src_ref=source, dst_ref=target, send_sem=send_sem, recv_sem=recv_sem,
        device_id=device, device_id_type=MESH,
    )


def greet(routes, d, z, everyone=False):
    barrier = pltpu.get_barrier_semaphore()
    peers = [(d, flip(z, r)) for r in range(1, routes.nt)]
    if everyone:
        peers += [(routes.later(d, j), z) for j in range(1, routes.nd)]
    else:
        peers += [routes.partner(s, d, z) for s in range(routes.stages + 1)]
    for peer in peers:
        pl.semaphore_signal(barrier, inc=1, device_id=peer, device_id_type=MESH)
    pl.semaphore_wait(barrier, len(peers))


def sincos_table(columns):
    quarter = columns // 4
    frequency = 1.0 / np.float32(10000.0) ** (np.arange(quarter, dtype=np.float32) / quarter)
    angle = np.arange(SIDE, dtype=np.float32)[:, None] * frequency.astype(np.float32)
    parts = np.concatenate([np.sin(angle), np.cos(angle)], 1).astype(np.float32)
    none = np.zeros_like(parts)
    return np.concatenate(
        [np.concatenate([parts, none], 1), np.concatenate([none, parts], 1)], 0
    )


def guarded(condition, body):
    if condition is None:
        body()
    else:
        pl.when(condition)(body)


class Gather:
    ahead = 2

    def __init__(self, routes, widths, few_rows, sources, mats, sems):
        self.routes, self.widths, self.few_rows = routes, widths, few_rows
        self.own, self.other, self.pred, self.few, self.every, self.rows = sources
        self.mats = mats
        self.sems = sems
        self.d, self.z = lax.axis_index("dp"), lax.axis_index("tensor")
        self.role = lax.rem(self.z, 2)
        self.last = len(widths) - 1
        self.items = [(m, r) for m in range(len(widths)) for r in range(routes.nt)]
        self.span = len(self.items) + self.ahead * routes.stages

    def peer(self, r):
        return self.d, flip(self.z, r)

    def peer_role(self, r):
        return lax.rem(flip(self.z, r), 2)

    def source(self, m, r):
        if m == self.last:
            return self.pred
        ref = self.own if r % 2 == 0 else self.other
        return ref.at[:, pl.ds(sum(self.widths[:m]), self.widths[m])]

    def across(self, m, r):
        send, recv = self.sems[0], self.sems[1]
        return remote(
            self.source(m, r), self.mats[m].at[r, 0], send.at[m, r], recv.at[m, r], self.peer(r)
        )

    def local(self, m):
        return pltpu.make_async_copy(self.source(m, 0), self.mats[m].at[0, 0], self.sems[2].at[m])

    def patch_source(self, r, role):
        place = flip(lax.div(self.z, 2), r // 2)
        ref = self.every if role else self.few
        rows = self.rows.shape[1] if role else self.few_rows
        if len(ref.shape) == 3:
            return ref.at[r, pl.ds(0, rows)], rows
        return ref.at[pl.ds(place * rows, rows)], rows

    def patch(self, r, role):
        source, rows = self.patch_source(r, role)
        return remote(
            source, self.rows.at[r, pl.ds(0, rows)], self.sems[3].at[r], self.sems[4].at[r],
            self.peer(r),
        )

    def own_patch(self, role):
        source, rows = self.patch_source(0, role)
        return pltpu.make_async_copy(
            source, self.rows.at[0, pl.ds(0, rows)], self.sems[2].at[self.last + 1]
        )

    def send_patches(self):
        for role in range(2):
            pl.when(self.role == role)(lambda role=role: self.own_patch(role).start())
            for r in range(1, self.routes.nt):
                pl.when(self.peer_role(r) == role)(
                    lambda r=r, role=role: self.patch(r, role).start()
                )

    def stage(self, m, r, s):
        size = 1 << s
        return remote(
            self.mats[m].at[r, pl.ds(0, size)], self.mats[m].at[r, pl.ds(size, size)],
            self.sems[5].at[m, r, s], self.sems[6].at[m, r, s],
            self.routes.partner(s, self.d, self.z),
        )

    def mine(self, m):
        return self.role == 1 if m == self.last else None

    def theirs(self, m, r):
        return self.peer_role(r) == 1 if m == self.last else None

    def start(self):
        for m in range(len(self.widths)):
            guarded(self.mine(m), lambda m=m: self.local(m).start())
            for r in range(1, self.routes.nt):
                guarded(self.theirs(m, r), lambda m=m, r=r: self.across(m, r).start())

    def advance(self, m, r, s):
        if s:
            self.stage(m, r, s - 1).wait_recv()
        elif r:
            self.across(m, r).wait_recv()
        else:
            self.local(m).wait()
        self.stage(m, r, s).start()

    def step(self, n):
        for s in reversed(range(self.routes.stages + 1)):
            if 0 <= n - self.ahead * s < len(self.items):
                m, r = self.items[n - self.ahead * s]
                guarded(self.mine(m), lambda m=m, r=r, s=s: self.advance(m, r, s))

    def arrive(self, m, r):
        self.stage(m, r, self.routes.stages).wait_recv()

    def wait_patches(self):
        for role in range(2):
            pl.when(self.role == role)(lambda role=role: self.own_patch(role).wait())
            for r in range(1, self.routes.nt):
                pl.when(self.role == role)(lambda r=r, role=role: self.patch(r, role).wait_recv())

    def finish(self):
        for r in range(1, self.routes.nt):
            for role in range(2):
                pl.when(self.peer_role(r) == role)(
                    lambda r=r, role=role: self.patch(r, role).wait_send()
                )
        for m, r in self.items:

            def sent(m=m, r=r):
                for s in range(self.routes.stages + 1):
                    self.stage(m, r, s).wait_send()

            guarded(self.mine(m), sent)
            if r:
                guarded(self.theirs(m, r), lambda m=m, r=r: self.across(m, r).wait_send())


def gather_kernel(
    routes, widths, few_rows, own_ref, other_ref, pred_ref, patch_ref,
    attn_ref, up_ref, down_ref, players_ref, rows_ref, *sems,
):
    gather = Gather(
        routes, widths, few_rows, (own_ref, other_ref, pred_ref, patch_ref, patch_ref, rows_ref),
        (attn_ref, up_ref, down_ref, players_ref), sems,
    )
    greet(routes, gather.d, gather.z)
    gather.start()
    gather.send_patches()
    for n in range(gather.span):
        gather.step(n)
    for m, r in gather.items:
        guarded(gather.mine(m), lambda m=m, r=r: gather.arrive(m, r))
    gather.wait_patches()
    gather.finish()


def split(values):
    high = values.astype(bf16)
    return high, (values - high.astype(f32)).astype(bf16)


def exactly(product, first, second, turn=False):
    values = second if turn else first
    high, rest = split(values)
    low = (values - high.astype(f32) - rest.astype(f32)).astype(bf16)
    if turn:
        return product(first, high) + product(first, rest) + product(first, low)
    return product(high, second) + product(rest, second) + product(low, second)


def forward_kernel(
    routes, widths, unit, context, head_size,
    owner_ref, weight_ref, teach_ref, patch_ref, ctx_ref, tgt_ref, embed_ref, temb_ref,
    evec_ref, tvec_ref, pvec_in, table_in, table_p_in,
    attn_out, up_out, down_out, players_out, rows_out, mid_out, resid_out, normed_out, qkv_out,
    att_out, out_out, normed2_out, hidden_out, feat_out, target_out,
    hot_ref, order_ref, hot_p_ref, vec_ref, pvec_ref, tokens_ref,
    attn_ref, up_ref, down_ref, players_ref, rows_ref, x_ref, h_ref, sent_ref, feat_ref,
    slots_out, slots_ref, own_ref, other_ref, pred_ref, picked_ref,
    back_sem, feat_send, feat_recv, slot_send, slot_recv, slot_sem, *sems,
):
    nt, nd = routes.nt, routes.nd
    mats = (attn_ref, up_ref, down_ref, players_ref)
    outs = (attn_out, up_out, down_out, players_out)
    kept = resid_out.shape[0]
    gather = Gather(
        routes, widths, kept,
        (own_ref, other_ref, pred_ref, picked_ref, patch_ref, rows_ref), mats, sems,
    )
    role = gather.role
    edge = nd * attn_ref.shape[2]
    side = 2
    wide = side * edge
    pix = rows_ref.shape[2]
    columns = wide // 4

    def matrix(ref, t, first, width):
        return ref[t, :, :, first : first + width].reshape(edge, width)

    def to_hbm(m, r):
        return pltpu.make_async_copy(mats[m].at[r], outs[m].at[r], back_sem.at[m, r])

    def feat_copy():
        return remote(sent_ref, feat_ref, feat_send, feat_recv, gather.peer(1))

    d, z = gather.d, gather.z
    rows_part = attn_ref.shape[2]
    slots = weight_ref.shape[0]
    span = x_ref.shape[0]
    images = ctx_ref.shape[0]
    share = span // unit
    part = lax.div(z, 2)

    def slot_copy(j):
        peer = routes.later(d, j)
        return remote(
            slots_out.at[:, :, peer], slots_ref.at[:, pl.ds(d * slots, slots)],
            slot_send.at[j], slot_recv.at[j], (peer, z),
        )

    def own_slots():
        return pltpu.make_async_copy(
            slots_out.at[:, :, d], slots_ref.at[:, pl.ds(d * slots, slots)], slot_sem
        )

    def send_slots():
        for kind, ref in enumerate((weight_ref, teach_ref)):
            for s in range(slots):
                slots_out[kind, s] = ref[s].astype(bf16).reshape(nd, rows_part, edge)
        own_slots().start()
        for j in range(1, nd):
            slot_copy(j).start()

    def by_rows(values):
        turned = values.T.astype(bf16)
        return jnp.concatenate([turned[:rows_part], turned[rows_part:]], 1)

    def take_slots():
        own_slots().wait()
        for j in range(1, nd):
            slot_copy(j).wait_recv()
        blocks = sum(widths[:3]) // edge - 1
        for b in range(blocks):
            first = b * edge if b < 4 else widths[0] + (b - 4) * edge
            own_ref[:, first : first + edge] = slots_ref[role, owner_ref[b]]
            other_ref[:, first : first + edge] = slots_ref[1 - role, owner_ref[b]]
        student, teacher = by_rows(embed_ref[...]), by_rows(temb_ref[...])
        first = widths[0] - student.shape[1]
        own_ref[:, first : widths[0]] = jnp.where(role == 0, student, teacher)
        other_ref[:, first : widths[0]] = jnp.where(role == 0, teacher, student)
        for b in range(blocks, owner_ref.shape[0]):
            first = (b - blocks) * edge
            pred_ref[:, first : first + edge] = slots_ref[0, owner_ref[b]]

    def local_order(step, shift):
        lane = lax.broadcasted_iota(jnp.int32, (1, edge), 1)
        row = lane
        for k in range(nd):
            here = (lane >= k * rows_part) & (lane < (k + 1) * rows_part)
            row = jnp.where(here, lane + (routes.holder(k, d) * step + shift - k * rows_part), row)
        return row

    def one_hot(rows, row):
        return (lax.broadcasted_iota(jnp.int32, (rows, row.shape[1]), 0) == row).astype(bf16)

    def send_patches():
        for g in range(images):
            hot = one_hot(unit, ctx_ref[g : g + 1])
            patches = patch_ref[g * unit : (g + 1) * unit]
            picked_ref[g * context : (g + 1) * context] = tn(hot, patches).astype(bf16)
        gather.send_patches()

    def positions(table, hot, row):
        both = jnp.concatenate(
            [one_hot(unit // 16, lax.rem(row, 16)), one_hot(unit // 16, lax.div(row, 16))], 0
        )
        return exactly(tn, both, exactly(nn, table, hot), turn=True)

    def prepare():
        places = local_order(rows_part, 0)
        feat = jnp.concatenate([places, places + edge], 1)
        hot_ref[...] = one_hot(wide, feat)
        hot_p_ref[...] = one_hot(edge, places)
        emb = [local_order(2 * rows_part, m * rows_part) for m in range(2)]
        order_ref[...] = tn(hot_ref[...], one_hot(wide, jnp.concatenate(emb, 1))).astype(bf16)
        vec_ref[...] = jnp.zeros_like(vec_ref)
        pvec_ref[...] = jnp.zeros_like(pvec_ref)
        count = evec_ref.shape[0]
        vectors = jnp.where(role == 0, evec_ref[...], tvec_ref[...])
        vec_ref[0:count] = exactly(nn, vectors, hot_ref[...])
        count = pvec_in.shape[0]
        pvec_ref[0:count] = exactly(nn, pvec_in[...], hot_p_ref[...])

    def prepare_rows():
        ctx = [ctx_ref[pl.ds(part * share + i, 1), :] for i in range(share)]
        tgt = [tgt_ref[pl.ds(part * share + i, 1), :] for i in range(share)]
        rest = jnp.zeros((1, span - kept), jnp.int32)
        row = jnp.where(
            role == 0,
            jnp.concatenate(ctx + [rest], 1),
            lax.rem(lax.broadcasted_iota(jnp.int32, (1, span), 1), unit),
        )
        x_ref[...] = positions(table_in[...], hot_ref[...], row) + vec_ref[6:7]
        row = jnp.concatenate([v for pair in zip(ctx, tgt) for v in pair], 1)
        tokens = positions(table_p_in[...], hot_p_ref[...], row)
        length = row.shape[1] // share
        number = lax.broadcasted_iota(jnp.int32, tokens.shape, 0)
        is_target = lax.rem(number, length) >= context
        mask_at = pvec_in.shape[0] - 1
        tokens_ref[...] = jnp.where(is_target, tokens + pvec_ref[mask_at : mask_at + 1], tokens)

    def group_rows(t):
        quarter = target_out.shape[2]
        first = flip(z - lax.rem(z, 2) + 1, t) * quarter
        return hot_ref[pl.ds(pl.multiple_of(first, 16), quarter), :]

    def embed():
        gather.wait_patches()

        @pl.loop(0, nt)
        def _(t):
            ordered = sum(
                nn(
                    order_ref[:, m * edge : (m + 1) * edge],
                    matrix(attn_ref, t, side * wide + m * pix, pix),
                )
                for m in range(side)
            ).astype(bf16)
            x_ref[...] += nt_(rows_ref[t], ordered)

        values = x_ref[...]
        resid_out[...] = values[:kept]
        low = layer_norm(values, vec_ref[0:1], vec_ref[1:2]).astype(bf16)
        h_ref[...] = low
        normed_out[...] = low[:kept]

    def attention(t):
        rows = sum(
            nn(h_ref[:, r * edge : (r + 1) * edge], matrix(attn_ref, t, r * wide, 3 * columns))
            for r in range(side)
        ).astype(bf16)
        qkv_out[t] = rows[:kept]
        att = attend(rows, head_size, unit, same_image(role, unit, context))
        att_out[t] = att[:kept]
        for r in range(side):
            x_ref[:, r * edge : (r + 1) * edge] += nt_(
                att, matrix(attn_ref, t, r * wide + 3 * columns, columns)
            )

    def middle():
        values = x_ref[...]
        mid_out[...] = values[:kept]
        low = layer_norm(values, vec_ref[2:3], vec_ref[3:4]).astype(bf16)
        h_ref[...] = low
        normed2_out[...] = low[:kept]

    def feed(t):
        hidden = sum(
            nn(h_ref[:, r * edge : (r + 1) * edge], matrix(up_ref, t, r * wide, wide))
            for r in range(side)
        )
        hidden_out[t] = hidden[:kept]
        active = gelu_parts(hidden)[0].astype(bf16)
        for r in range(side):
            x_ref[:, r * edge : (r + 1) * edge] += nt_(
                active, matrix(down_ref, t, r * wide, wide)
            )

    def last():
        values = x_ref[...]
        out_out[...] = values[:kept]
        final = layer_norm(values, vec_ref[4:5], vec_ref[5:6])

        @pl.when(role == 0)
        def _():
            encoded = final[:kept].astype(bf16)
            for t in range(nt):
                sent_ref[t] = nt_(encoded, group_rows(t)).astype(bf16)
            feat_copy().start()

        @pl.when(role == 1)
        def _():
            target = norm_parts(final)[0].astype(bf16)
            tgt = [tgt_ref[pl.ds(part * share + i, 1), :] + i * unit for i in range(share)]
            picked = tn(one_hot(span, jnp.concatenate(tgt, 1)), target).astype(bf16)
            for t in range(nt):
                target_out[t] = nt_(picked, group_rows(t)).astype(bf16)

        @pl.when(role == 0)
        def _():
            target_out[...] = jnp.zeros_like(target_out)

    lag = gather.ahead * (routes.stages + 1)
    attn_at = nt - 1 + lag
    feed_at = 3 * nt - 1 + lag
    steps = len(gather.items) + lag
    greet(routes, d, z, everyone=True)
    send_slots()
    send_patches()
    prepare()
    take_slots()
    gather.start()
    prepare_rows()

    @pl.loop(0, steps)
    def _(n):
        for k in range(steps):

            @pl.when(n == k)
            def _(k=k):
                gather.step(k)
                if k >= lag:
                    m, r = gather.items[k - lag]

                    def here(m=m, r=r):
                        gather.arrive(m, r)
                        to_hbm(m, r).start()

                    guarded(gather.mine(m), here)

        pl.when(n == attn_at)(embed)

        @pl.when((n > attn_at) & (n <= attn_at + nt))
        def _():
            attention(n - attn_at - 1)

        pl.when(n == feed_at)(middle)

        @pl.when((n >= feed_at) & (n < feed_at + nt))
        def _():
            feed(n - feed_at)

        pl.when(n == feed_at + nt - 1)(last)

    rows_out[...] = rows_ref[:, :kept]

    @pl.when(role == 0)
    def _():
        feat_copy().wait_send()
        feat_out[...] = jnp.zeros_like(feat_out)

    @pl.when(role == 1)
    def _():
        feat_copy().wait_recv()
        feat_out[...] = feat_ref[...]

    gather.finish()
    for j in range(1, nd):
        slot_copy(j).wait_send()
    for m, r in gather.items:
        guarded(gather.mine(m), lambda m=m, r=r: to_hbm(m, r).wait())


def reduce_kernel(
    routes, attn_cols, down_ref, up_ref, attn_ref, pred_ref, block_ref, emb_ref,
    core0, core1, core2, later0, later1, later2, enc_in, pred_in, load,
    load_sem, core_send, core_recv, stage_send, stage_recv, z_send, z_recv,
):
    d, z = lax.axis_index("dp"), lax.axis_index("tensor")
    nt, stages = routes.nt, routes.stages
    middle = routes.nd // 2
    role = lax.rem(z, 2)
    cores = [core0, core1, core2]
    laters = [later0, later1, later2]
    greet(routes, d, z)

    def run(kind, sources, incoming, starts):
        items = [(j, r) for j in range(len(sources)) for r in reversed(range(nt))]

        def part(j, r, first):
            ref, start, width = sources[j]
            return ref.at[r, pl.ds(first, middle), :, pl.ds(start, width)]

        def to_core(j, r):
            return remote(
                part(j, r, middle), cores[j].at[r, :, :, pl.ds(0, sources[j][2])],
                core_send.at[j, r], core_recv.at[j, r], routes.partner(stages, d, z),
            )

        def own(i):
            j, r = items[i]
            return pltpu.make_async_copy(
                part(j, r, 0), load.at[i % 2, :, :, pl.ds(0, sources[j][2])], load_sem.at[i % 2]
            )

        def stage(j, r, s):
            size = 1 << s
            return remote(
                cores[j].at[r, pl.ds(size, size), :, pl.ds(0, sources[j][2])],
                laters[j].at[r, pl.ds(size - 1, size), :, pl.ds(0, sources[j][2])],
                stage_send.at[j, r, s], stage_recv.at[j, r, s], routes.partner(s, d, z),
            )

        def across(j, r):
            return remote(
                cores[j].at[r, 0, :, pl.ds(0, sources[j][2])],
                incoming.at[r, :, pl.ds(starts[j], sources[j][2])],
                z_send.at[kind, j, r], z_recv.at[kind, j, r], (d, flip(z, r)),
            )

        def add(i, q):
            j, r = items[i]
            width = sources[j][2]
            if q == 0:
                own(i).wait()
                to_core(j, r).wait_recv()

                @pl.loop(0, middle)
                def _(k):
                    total = cores[j][r, k, :, 0:width].astype(f32)
                    total += load[i % 2, k, :, 0:width].astype(f32)
                    cores[j][r, k, :, 0:width] = total.astype(bf16)

                if i + 2 < len(items):
                    own(i + 2).start()
            else:
                s = stages - q
                stage(j, r, s).wait_recv()

                @pl.loop(0, 1 << s)
                def _(k):
                    total = cores[j][r, k, :, 0:width].astype(f32)
                    total += laters[j][r, k + ((1 << s) - 1), :, 0:width].astype(f32)
                    cores[j][r, k, :, 0:width] = total.astype(bf16)

            if q < stages:
                stage(j, r, stages - q - 1).start()
            elif r:
                across(j, r).start()

        for i in range(min(2, len(items))):
            own(i).start()
        for j, r in items:
            to_core(j, r).start()
        for n in range(len(items) + stages):
            for q in reversed(range(stages + 1)):
                if 0 <= n - q < len(items):
                    add(n - q, q)
        for j, r in items:
            to_core(j, r).wait_send()
            for s in range(stages):
                stage(j, r, s).wait_send()
            if r:
                across(j, r).wait_send()

    wide = down_ref.shape[3]
    all_cols = attn_ref.shape[3]
    pred_cols = pred_ref.shape[3]
    encoder = [(down_ref, 0, wide), (up_ref, 0, wide), (attn_ref, 0, all_cols)]
    encoder_at = [0, wide, 2 * wide]
    players = [(pred_ref, 0, wide), (pred_ref, wide, pred_cols - wide)]
    players_at = [0, wide]

    @pl.when(role == 0)
    def _():
        run(0, encoder, enc_in, encoder_at)

    @pl.when(role == 1)
    def _():
        run(1, players, pred_in, players_at)

    def collect(kind, sources, incoming, starts, put):
        for j, (_, _, width) in enumerate(sources):
            place = incoming.at[:, :, pl.ds(starts[j], width)]

            def arrive(r, j=j, width=width):
                pltpu.make_async_remote_copy(
                    src_ref=cores[j].at[r, 0, :, pl.ds(0, width)],
                    dst_ref=incoming.at[r, :, pl.ds(starts[j], width)],
                    send_sem=z_send.at[kind, j, r], recv_sem=z_recv.at[kind, j, r],
                    device_id=(d, flip(z, r)), device_id_type=MESH,
                ).wait_recv()

            del place

            @pl.when(role == kind)
            def _(j=j, width=width, arrive=arrive):
                total = cores[j][0, 0, :, 0:width].astype(f32)
                for r in range(2, nt, 2):
                    arrive(r)
                    total += incoming[r, :, starts[j] : starts[j] + width].astype(f32)
                put(j, total)

            @pl.when(role != kind)
            def _(j=j, width=width, arrive=arrive):
                total = None
                for r in range(1, nt, 2):
                    arrive(r)
                    got = incoming[r, :, starts[j] : starts[j] + width].astype(f32)
                    total = got if total is None else total + got
                put(j, total)

    def put_encoder(j, total):
        if j == 2:
            block_ref[:, 0:attn_cols] = total[:, :attn_cols].astype(bf16)
            emb_ref[...] = total[:, attn_cols:]
        else:
            first = attn_cols + (1 - j) * wide
            block_ref[:, first : first + wide] = total.astype(bf16)

    def put_players(j, total):
        first = attn_cols + 2 * wide + players_at[j]
        block_ref[:, first : first + total.shape[1]] = total.astype(bf16)

    collect(1, players, pred_in, players_at, put_players)
    collect(0, encoder, enc_in, encoder_at, put_encoder)
    end = attn_cols + 2 * wide + pred_cols
    block_ref[:, end:] = jnp.zeros((block_ref.shape[0], block_ref.shape[1] - end), bf16)


def backward_kernel(
    routes, context, head_size,
    slot_of_ref, players_ref, back_in, attn_hbm, up_hbm, down_hbm,
    out_ref, mid_ref, resid_ref, normed2_ref, normed_ref, hidden_ref, qkv_ref, att_ref, rows_ref,
    vec_ref, order_ref, hot_ref, hot_p_ref, pred_vec_ref, loss_ref,
    low_out, emb_ref, vec_out,
    block_ref, slots_ref, g0, g1, g2, g3, core0, core1, core2, core3, later0, later1, later2, later3, enc_in, pred_in,
    attn_w, up_w, down_w, back_ref, d_ref, low_ref, acc_ref, vec_grad_ref, vec_send, vec_recv,
    weight_sem, back_send, back_recv, load_sem, core_send, core_recv, stage_send, stage_recv,
    z_send, z_recv, vec_send_sem, vec_recv_sem, slot_send, slot_recv, slot_sem,
):
    d, z = lax.axis_index("dp"), lax.axis_index("tensor")
    nt, nd, stages = routes.nt, routes.nd, routes.stages
    role = lax.rem(z, 2)
    half = nd // 2
    grads, cores = (g0, g1, g2, g3), (core0, core1, core2, core3)
    laters = (later0, later1, later2, later3)
    rows = g0.shape[2]
    edge = nd * rows
    wide = 2 * edge
    columns = wide // 4
    pix = rows_ref.shape[2]
    unit = resid_ref.shape[0]
    mat = g0.shape[3]
    ahead = 2

    encoder = [(j, r) for r in range(nt) for j in (0, 1)] + [(2, r) for r in range(nt)]
    encoder += [(3, r) for r in range(nt)]
    pred_cols = players_ref.shape[3]
    pred_width = (mat, pred_cols - mat)
    players = [(j, r) for r in reversed(range(nt)) for j in (0, 1)]
    enc_width = (mat, mat, mat, 2 * pix)
    enc_at = (0, mat, 2 * mat, 3 * mat)

    def weight(t, i):
        slot = lax.rem(t, 2)
        source = (up_hbm, down_hbm, attn_hbm)[i].at[t, :, pl.ds(0, mat)]
        target = (up_w, down_w, attn_w)[i].at[slot]
        return pltpu.make_async_copy(source, target, weight_sem.at[i, slot])

    def back_copy():
        return remote(back_in, back_ref, back_send, back_recv, (d, flip(z, 1)))

    class Sums:
        def __init__(self, kind, items, width, incoming, at):
            self.kind, self.items, self.width = kind, items, width
            self.incoming, self.at = incoming, at

        def cut(self, j):
            return pl.ds(0, self.width[j])

        def to_core(self, j, r):
            if self.kind:
                source = players_ref.at[r, pl.ds(half, half), :, pl.ds(self.at[j], self.width[j])]
            else:
                source = grads[j].at[r, pl.ds(half, half)]
            return remote(
                source, cores[j].at[r, :, :, self.cut(j)],
                core_send.at[j, r], core_recv.at[j, r], routes.partner(stages, d, z),
            )

        def load(self, j, r):
            return pltpu.make_async_copy(
                players_ref.at[r, pl.ds(0, half), :, pl.ds(self.at[j], self.width[j])],
                grads[j].at[r, pl.ds(0, half), :, self.cut(j)],
                load_sem.at[j, r],
            )

        def stage(self, j, r, s):
            size = 1 << s
            return remote(
                grads[j].at[r, pl.ds(size, size), :, self.cut(j)],
                laters[j].at[r, pl.ds(size - 1, size), :, self.cut(j)],
                stage_send.at[j, r, s], stage_recv.at[j, r, s], routes.partner(s, d, z),
            )

        def across(self, j, r):
            return remote(
                grads[j].at[r, 0, :, self.cut(j)],
                self.incoming.at[r, :, pl.ds(self.at[j], self.width[j])],
                z_send.at[self.kind, j, r], z_recv.at[self.kind, j, r], (d, flip(z, r)),
            )

        def begin(self, i):
            if i < len(self.items):
                j, r = self.items[i]
                if self.kind:
                    self.load(j, r).start()
                self.to_core(j, r).start()

        def add(self, i, q):
            if not 0 <= i < len(self.items):
                return
            j, r = self.items[i]
            width = self.width[j]
            s = stages - q
            if q == 0:
                if self.kind:
                    self.load(j, r).wait()
                self.to_core(j, r).wait_recv()
            else:
                self.stage(j, r, s).wait_recv()

            @pl.loop(0, 1 << s)
            def _(k):
                total = grads[j][r, k, :, 0:width].astype(f32)
                if q == 0:
                    total += cores[j][r, k, :, 0:width].astype(f32)
                else:
                    total += laters[j][r, k + ((1 << s) - 1), :, 0:width].astype(f32)
                grads[j][r, k, :, 0:width] = total.astype(bf16)

            if q < stages:
                self.stage(j, r, s - 1).start()
            elif r:
                self.across(j, r).start()

        def tick(self, n):
            for q in reversed(range(stages + 1)):
                self.add(n - ahead * (q + 1), q)

        def finish(self):
            for j, r in self.items:
                self.to_core(j, r).wait_send()
                for s in range(stages):
                    self.stage(j, r, s).wait_send()
                if r:
                    self.across(j, r).wait_send()

        def collect(self, j, put):
            columns = slice(self.at[j], self.at[j] + self.width[j])

            @pl.when(role == self.kind)
            def _():
                total = grads[j][0, 0, :, 0 : self.width[j]].astype(f32)
                for r in range(2, nt, 2):
                    self.across(j, r).wait_recv()
                    total += self.incoming[r, :, columns].astype(f32)
                put(total)

            @pl.when(role != self.kind)
            def _():
                total = jnp.zeros((rows, self.width[j]), f32)
                for r in range(1, nt, 2):
                    self.across(j, r).wait_recv()
                    total += self.incoming[r, :, columns].astype(f32)
                put(total)

    enc = Sums(0, encoder, enc_width, enc_in, enc_at)
    play = Sums(1, players, pred_width, pred_in, (0, mat))

    def store(ref, t, first, value):
        ref[t, :, :, first : first + value.shape[1]] = value.astype(bf16).reshape(
            nd, rows, value.shape[1]
        )

    def begin_feed():
        back_copy().wait_recv()
        grad, gain_g, shift_g = norm_backward(back_ref[...].astype(f32), out_ref[...], vec_ref[4:5])
        d_ref[...] = grad
        low_ref[...] = grad.astype(bf16)
        acc_ref[...] = jnp.zeros_like(acc_ref)
        vec_grad_ref[4:5] = gain_g
        vec_grad_ref[5:6] = shift_g

    def feed(t):
        slot = lax.rem(t, 2)
        weight(t, 0).wait()
        weight(t, 1).wait()
        active, slope = gelu_parts(hidden_ref[t])
        active = active.astype(bf16)
        grad_hidden = sum(
            nn(low_ref[:, r * edge : (r + 1) * edge], down_w[slot, :, r * wide : (r + 1) * wide])
            for r in range(2)
        )
        grad_hidden = (grad_hidden * slope).astype(bf16)
        for r in range(2):
            mine = slice(r * edge, (r + 1) * edge)
            store(g0, t, r * wide, tn(low_ref[:, mine], active))
            store(g1, t, r * wide, tn(normed2_ref[:, mine], grad_hidden))
            acc_ref[:, mine] += nt_(grad_hidden, up_w[slot, :, r * wide : (r + 1) * wide])

        @pl.when(t + 2 < nt)
        def _():
            weight(t + 2, 0).start()
            weight(t + 2, 1).start()

    def end_feed():
        grad, gain_g, shift_g = norm_backward(acc_ref[...], mid_ref[...], vec_ref[2:3])
        vec_grad_ref[2:3] = gain_g
        vec_grad_ref[3:4] = shift_g
        grad = d_ref[...] + grad
        d_ref[...] = grad
        low_ref[...] = grad.astype(bf16)
        acc_ref[...] = jnp.zeros_like(acc_ref)

    def attention(t):
        slot = lax.rem(t, 2)
        weight(t, 2).wait()
        grad_att = sum(
            nn(
                low_ref[:, r * edge : (r + 1) * edge],
                attn_w[slot, :, r * wide + 3 * columns : (r + 1) * wide],
            )
            for r in range(2)
        ).astype(bf16)
        allowed = same_image(role, unit, context)
        grad_rows = attend_back(qkv_ref[t], grad_att, head_size, unit, allowed)
        for r in range(2):
            mine = slice(r * edge, (r + 1) * edge)
            grad_w = jnp.concatenate(
                [tn(normed_ref[:, mine], grad_rows), tn(low_ref[:, mine], att_ref[t])], 1
            )
            store(g2, t, r * wide, grad_w)
            acc_ref[:, mine] += nt_(grad_rows, attn_w[slot, :, r * wide : r * wide + 3 * columns])

        @pl.when(t + 2 < nt)
        def _():
            weight(t + 2, 2).start()

    def end_attention():
        grad, gain_g, shift_g = norm_backward(acc_ref[...], resid_ref[...], vec_ref[0:1])
        grad = d_ref[...] + grad
        vec_grad_ref[0:1] = gain_g
        vec_grad_ref[1:2] = shift_g
        vec_grad_ref[6:7] = jnp.sum(grad, 0, keepdims=True)
        low_ref[...] = nn(grad.astype(bf16), order_ref[...]).astype(bf16)

        @pl.loop(0, nt)
        def _(t):
            for m in range(2):
                store(g3, t, m * pix, tn(low_ref[:, m * edge : (m + 1) * edge], rows_ref[t]))

    bits = [("d", 1)] + [("d", b) for b in routes.low_bits]
    bits += [("z", 1 << s) for s in range(nt.bit_length() - 1)]

    def vec_copy(s):
        axis, bit = bits[s]
        peer = (flip(d, bit), z) if axis == "d" else (d, flip(z, bit))
        return remote(
            vec_send.at[s], vec_recv.at[s], vec_send_sem.at[s], vec_recv_sem.at[s], peer
        )

    def vec_pack():
        @pl.when(role == 0)
        def _():
            whole_rows = exactly(nt_, vec_grad_ref[...], hot_ref[...])
            vec_send[0, 0:8] = whole_rows[:, :edge]
            vec_send[0, 8:16] = whole_rows[:, edge:]
            vec_send[0, 16:32] = jnp.zeros((16, edge), f32)

        @pl.when(role == 1)
        def _():
            vec_send[0, 0:16] = jnp.zeros((16, edge), f32)
            vec_send[0, 16:32] = exactly(nt_, pred_vec_ref[...], hot_p_ref[...])
            vec_send[0, 28:29] = jnp.broadcast_to(loss_ref[0:1, 0:1], (1, edge))

        vec_copy(0).start()

    def vec_step(s):
        vec_copy(s).wait_recv()
        total = vec_send[s] + vec_recv[s]
        if s + 1 < len(bits):
            vec_send[s + 1] = total
            vec_copy(s + 1).start()
        else:
            vec_out[...] = total

    ticks = len(encoder) + ahead * (stages + 1)
    first_attention = 2 * nt
    last_attention = 3 * nt

    @pl.when(role == 0)
    def _():
        vec_grad_ref[...] = jnp.zeros_like(vec_grad_ref)
        for t in range(2):
            for i in range(3):
                weight(t, i).start()

    greet(routes, d, z, everyone=True)

    @pl.when(role == 1)
    def _():
        back_copy().start()

    @pl.loop(0, ticks)
    def _(n):
        @pl.when(role == 0)
        def _():
            pl.when(n == 0)(begin_feed)

            @pl.when((n < first_attention) & (lax.rem(n, 2) == 0))
            def _():
                feed(lax.div(n, 2))

            pl.when(n == first_attention)(end_feed)

            @pl.when((n >= first_attention) & (n < last_attention))
            def _():
                attention(n - first_attention)

            pl.when(n == last_attention)(end_attention)

        for k in range(ticks):

            @pl.when(n == k)
            def _(k=k):
                if k == last_attention:
                    vec_pack()
                if k > last_attention and k - last_attention - 1 < len(bits):
                    vec_step(k - last_attention - 1)

                @pl.when(role == 0)
                def _():
                    enc.begin(k)
                    enc.tick(k)

                @pl.when(role == 1)
                def _():
                    play.begin(k)
                    play.tick(k)

    for s in range(max(0, ticks - last_attention - 1), len(bits)):
        vec_step(s)

    def put_block(first):
        def put(total):
            low = total.astype(bf16)
            for i in range(low.shape[1] // edge):
                block_ref[first + i] = low[:, i * edge : (i + 1) * edge]

        return put

    def put_embed(total):
        emb_ref[...] = total

    per_mat = mat // edge
    for j in range(2):
        play.collect(j, put_block((3 + j) * per_mat))
    for j, first in ((0, 2 * per_mat), (1, per_mat), (2, 0)):
        enc.collect(j, put_block(first))
    block_ref[block_ref.shape[0] - 1] = jnp.zeros(block_ref.shape[1:], bf16)
    slots = slots_ref.shape[1]

    def slot_copy(j):
        peer = routes.later(d, j)
        return remote(
            slots_ref.at[peer], low_out.at[:, d], slot_send.at[j], slot_recv.at[j], (peer, z)
        )

    def own_slots():
        return pltpu.make_async_copy(slots_ref.at[d], low_out.at[:, d], slot_sem)

    for s in range(nd * slots):
        slots_ref[s // slots, s % slots] = block_ref[slot_of_ref[s]]
    for j in range(1, nd):
        slot_copy(j).start()
    own_slots().start()
    enc.collect(3, put_embed)

    @pl.when(role == 0)
    def _():
        enc.finish()

    @pl.when(role == 1)
    def _():
        play.finish()
        back_copy().wait_send()

    for s in range(len(bits)):
        vec_copy(s).wait_send()
    own_slots().wait()
    for j in range(1, nd):
        slot_copy(j).wait()


def whole(shape):
    return pl.BlockSpec(shape, lambda *_: (0,) * len(shape))


def by_group(shape):
    return pl.BlockSpec((1,) + shape, lambda t: (t, 0, 0))


def compiled():
    return pltpu.CompilerParams(
        dimension_semantics=("arbitrary",), vmem_limit_bytes=KERNEL_BYTES
    )


def cost(flops, moved):
    return pl.CostEstimate(flops=int(flops), bytes_accessed=int(moved), transcendentals=0)


def sincos(cell_index, columns):
    quarter = columns // 4
    frequency = 1.0 / 10000.0 ** (jnp.arange(quarter).astype(f32) / quarter)
    col_angle = (cell_index % SIDE).astype(f32)[..., None] * frequency
    row_angle = (cell_index // SIDE).astype(f32)[..., None] * frequency
    return jnp.concatenate(
        [jnp.sin(col_angle), jnp.cos(col_angle), jnp.sin(row_angle), jnp.cos(row_angle)], -1
    )


def adamw(master, moment, second, gradient, step_rate, weight_decay):
    moment = 0.9 * moment + 0.1 * gradient
    second = 0.999 * second + 0.001 * gradient * gradient
    unbiased_first = moment / (1.0 - 0.9**STEP)
    unbiased_second = second / (1.0 - 0.999**STEP)
    return (
        master
        - step_rate
        * (unbiased_first / (jnp.sqrt(unbiased_second) + 1e-08) + weight_decay * master),
        moment,
        second,
    )


class Routes:
    def __init__(self, nd, nt):
        self.nd, self.nt = nd, nt
        self.low_bits = [1 << s for s in range(1, nd.bit_length() - 1)]
        self.stages = len(self.low_bits)

    def order(self, core):
        return self.low_bits if core == 0 else self.low_bits[::-1]

    def pairs(self, target, keep):
        found = []
        for d in range(self.nd):
            for z in range(self.nt):
                if keep(d, z):
                    d2, z2 = target(d, z)
                    found.append((d * self.nt + z, d2 * self.nt + z2))
        return found

    def later(self, d, j):
        return lax.rem(d + j, self.nd)

    def holder(self, k, d):
        held = flip(d, k >> self.stages)
        core = lax.rem(held, 2)
        for s in range(self.stages):
            if (k >> s) & 1:
                ends = flip(held, self.order(0)[s]), flip(held, self.order(1)[s])
                held = ends[0] + core * (ends[1] - ends[0])
        return held

    def partner(self, number, d, z):
        if number == self.stages:
            return flip(d, 1), z
        core = lax.rem(d, 2)
        ends = flip(d, self.order(0)[number]), flip(d, self.order(1)[number])
        return ends[0] + core * (ends[1] - ends[0]), z

    def across(self, r, values, from_role=None):
        def keep(d, z):
            return from_role is None or z % 2 == from_role

        return lax.ppermute(values, AXES, self.pairs(lambda d, z: (d, z ^ r), keep))

    def holders(self, d):
        place = jnp.arange(self.nd, dtype=jnp.int32)
        held = d ^ (place >> self.stages)
        core = held & 1
        for s in range(self.stages):
            bit = (place >> s) & 1
            held = held ^ (bit * jnp.where(core == 0, self.order(0)[s], self.order(1)[s]))
        return held

    def total(self, values):
        for bit in [1] + self.low_bits:
            values = values + lax.ppermute(
                values, AXES, self.pairs(lambda d, z, b=bit: (d ^ b, z), lambda d, z: True)
            )
        r = 1
        while r < self.nt:
            values = values + self.across(r, values)
            r *= 2
        return values


def shards(
    patches,
    ctx_idx,
    tgt_idx,
    owner,
    weights,
    stats_left,
    stats_right,
    root_left,
    root_right,
    teacher_slot_blocks,
    embed,
    embed_m,
    embed_v,
    teacher_embed,
    enc_vectors,
    enc_m,
    enc_v,
    pred_vectors,
    pred_m,
    pred_v,
    teacher_vectors,
):
    nt = lax.axis_size("tensor")
    nd = lax.axis_size("dp")
    routes = Routes(nd, nt)
    half = nt // 2
    d = lax.axis_index("dp")
    z = lax.axis_index("tensor")
    role = z % 2
    student_role = role == 0
    images, npatches, pix_part = patches.shape
    slots = weights.shape[1]
    edge = weights.shape[-1]
    slot_count = slots * nd
    block_count = owner.shape[0]
    width = enc_vectors.shape[1]
    narrow = pred_vectors.shape[1]
    players = (pred_vectors.shape[0] - 3) // 4
    side = width // edge
    teach_count = 3 * side * side
    quarter = width // nt
    context_len = ctx_idx.shape[1]
    target_len = tgt_idx.shape[1]
    seq_len = context_len + target_len
    share = images // half
    rows_part = edge // nd

    both = jnp.stack([weights[0], teacher_slot_blocks[0]]).astype(bf16)
    both = both.reshape(2, slots, nd, rows_part, edge)
    both = lax.all_to_all(both, "dp", split_axis=2, concat_axis=0, tiled=False)
    by_slot = both.transpose(1, 0, 2, 3, 4).reshape(2, slot_count, rows_part, edge)
    mine = by_slot[0][owner].transpose(1, 0, 2).reshape(rows_part, -1)
    teach = by_slot[1][owner[:teach_count]].transpose(1, 0, 2).reshape(rows_part, -1)

    mat = side * width

    def embed_rows(values):
        turned = values.astype(bf16).T.reshape(side, rows_part, pix_part)
        return turned.transpose(1, 0, 2).reshape(rows_part, -1)

    of_student = jnp.concatenate(
        [mine[:, :mat], embed_rows(embed), mine[:, mat : 3 * mat]], 1
    )
    of_teacher = jnp.concatenate([teach[:, :mat], embed_rows(teacher_embed), teach[:, mat:]], 1)
    own = jnp.where(student_role, of_student, of_teacher)
    other = jnp.where(student_role, of_teacher, of_student)
    pred_own = mine[:, 3 * mat :]

    holder = routes.holders(d)
    inside = jnp.arange(rows_part, dtype=jnp.int32)
    feat_p = (holder[:, None] * rows_part + inside[None, :]).reshape(-1)
    feat = jnp.concatenate([r * edge + feat_p for r in range(side)])
    one_hot = (feat[:, None] == jnp.arange(width)[None, :]).astype(f32)
    one_hot_p = (feat_p[:, None] == jnp.arange(narrow)[None, :]).astype(f32)

    def to_local(rows, hot):
        return jnp.einsum("nf,lf->nl", rows, hot, precision=exact, preferred_element_type=f32)

    def to_global(rows, hot):
        return jnp.einsum("nl,lf->nf", rows, hot, precision=exact, preferred_element_type=f32)

    vec = to_local(jnp.where(student_role, enc_vectors, teacher_vectors), one_hot)
    vec = jnp.pad(vec, ((0, 1), (0, 0)))
    pvec = to_local(pred_vectors, one_hot_p)
    pvec = jnp.pad(pvec, ((0, 16 - pvec.shape[0]), (0, 0)))
    pred_z = z - role + 1
    group_feat = (pred_z ^ jnp.arange(nt, dtype=jnp.int32))[:, None] * quarter + jnp.arange(
        quarter, dtype=jnp.int32
    )
    emb_feat = jnp.concatenate(
        [holder[:, None] * 2 * rows_part + m * rows_part + inside[None, :] for m in range(2)]
    ).reshape(-1)
    order = (feat[:, None] == emb_feat[None, :]).astype(bf16)
    swap = (feat[None, :, None] == group_feat[:, None, :]).astype(bf16)

    part = z // 2
    hot = (ctx_idx[:, :, None] == jnp.arange(npatches)[None, None, :]).astype(bf16)
    picked = jnp.einsum("gcn,gnp->gcp", hot, patches, preferred_element_type=f32).astype(bf16)

    def rows_for(target_z):
        where = (target_z // 2) * share
        ctx = lax.dynamic_slice_in_dim(picked, where, share, 0).reshape(-1, pix_part)
        every = lax.dynamic_slice_in_dim(patches, where, share, 0).reshape(-1, pix_part)
        padded = jnp.pad(ctx, ((0, every.shape[0] - ctx.shape[0]), (0, 0)))
        return jnp.where(target_z % 2 == 0, padded, every)

    patch_out = jnp.stack([rows_for(z ^ r) for r in range(nt)])
    my_ctx = lax.dynamic_slice_in_dim(ctx_idx, part * share, share, 0)
    my_tgt = lax.dynamic_slice_in_dim(tgt_idx, part * share, share, 0)
    full_rows = share * npatches
    ctx_rows = share * context_len
    tgt_rows = share * target_len
    ctx_places = jnp.pad(my_ctx.reshape(-1), (0, full_rows - ctx_rows))
    places = jnp.where(student_role, ctx_places, jnp.arange(full_rows) % npatches)
    table = to_local(sincos(jnp.arange(npatches), width), one_hot)
    table_p = to_local(sincos(jnp.arange(npatches), narrow), one_hot_p)
    base = table[places] + vec[6]
    tgt_places = (my_tgt + npatches * jnp.arange(share, dtype=jnp.int32)[:, None]).reshape(-1)
    pick = (tgt_places[:, None] == jnp.arange(full_rows)[None, :]).astype(bf16)
    widths = [mat + side * pix_part, mat, mat, mine.shape[1] - 3 * mat]
    any_space = pl.BlockSpec(memory_space=pl.ANY)
    dma = pltpu.SemaphoreType.DMA
    attn_cols = side * width
    columns = width // nt
    mat_shapes = [jax.ShapeDtypeStruct((nt, nd, rows_part, c), bf16) for c in widths]
    gather_sems = [
        dma((4, nt)),
        dma((4, nt)),
        dma((5,)),
        dma((nt,)),
        dma((nt,)),
        dma((4, nt, routes.stages + 1)),
        dma((4, nt, routes.stages + 1)),
    ]
    in_vmem = pl.BlockSpec(memory_space=VMEM)
    role_word = role.astype(jnp.int32).reshape(1)
    if rows_part % 16 == 0:
        results = pl.pallas_call(
            functools.partial(forward_kernel, routes, widths, npatches, context_len, HD),
            in_specs=[pl.BlockSpec(memory_space=pltpu.SMEM)] + [in_vmem] * 12,
            out_specs=[any_space] * 4 + [in_vmem] * 17,
            out_shape=mat_shapes
            + [
                jax.ShapeDtypeStruct((nt, ctx_rows, pix_part), bf16),
                jax.ShapeDtypeStruct((ctx_rows, width), f32),
                jax.ShapeDtypeStruct((ctx_rows, width), f32),
                jax.ShapeDtypeStruct((ctx_rows, width), bf16),
                jax.ShapeDtypeStruct((nt, ctx_rows, 3 * columns), bf16),
                jax.ShapeDtypeStruct((nt, ctx_rows, columns), bf16),
                jax.ShapeDtypeStruct((ctx_rows, width), f32),
                jax.ShapeDtypeStruct((ctx_rows, width), bf16),
                jax.ShapeDtypeStruct((nt, ctx_rows, width), f32),
                jax.ShapeDtypeStruct((nt, ctx_rows, quarter), bf16),
                jax.ShapeDtypeStruct((nt, tgt_rows, quarter), bf16),
                jax.ShapeDtypeStruct((width, width), bf16),
                jax.ShapeDtypeStruct((width, width), bf16),
                jax.ShapeDtypeStruct((narrow, narrow), bf16),
                jax.ShapeDtypeStruct((8, width), f32),
                jax.ShapeDtypeStruct((16, narrow), f32),
                jax.ShapeDtypeStruct((share * seq_len, narrow), f32),
            ],
            scratch_shapes=[VMEM(shape.shape, bf16) for shape in mat_shapes]
            + [
                VMEM((nt, full_rows, pix_part), bf16),
                VMEM((full_rows, width), f32),
                VMEM((full_rows, width), bf16),
                VMEM((nt, ctx_rows, quarter), bf16),
                VMEM((nt, ctx_rows, quarter), bf16),
                VMEM((2, slots, nd, rows_part, edge), bf16),
                VMEM((2, slot_count, rows_part, edge), bf16),
                VMEM((rows_part, sum(widths[:3])), bf16),
                VMEM((rows_part, sum(widths[:3])), bf16),
                VMEM((rows_part, widths[3]), bf16),
                VMEM((images * context_len, pix_part), bf16),
                dma((4, nt)),
                dma(()),
                dma(()),
                dma((nd,)),
                dma((nd,)),
                dma(()),
            ]
            + gather_sems,
            compiler_params=pltpu.CompilerParams(
                collective_id=0, has_side_effects=True, vmem_limit_bytes=KERNEL_BYTES
            ),
            cost_estimate=cost(14e9, 60e6),
            name="gather_and_encode",
        )(
            owner, weights[0], teacher_slot_blocks[0], patches.reshape(-1, pix_part),
            ctx_idx, tgt_idx, embed, teacher_embed, enc_vectors, teacher_vectors, pred_vectors,
            jnp.asarray(sincos_table(width)), jnp.asarray(sincos_table(narrow)),
        )
        gathered, results = results[:4], results[4:]
        patch_rows, middle, resid, normed_a, rows_a, att_a = results[:6]
        output, normed_f, hidden, feat_in, target = results[6:11]
        hot, order, hot_p, vec, pvec, tokens_at = results[11:]
        attn_emb, up_w, down_t, pred_all = (g.reshape(nt, edge, -1) for g in gathered)
    else:
        attn_emb, up_w, down_t, pred_all, patch_rows = pl.pallas_call(
            functools.partial(gather_kernel, routes, widths, ctx_rows),
            in_specs=[any_space] * 4,
            out_specs=[any_space] * 5,
            out_shape=mat_shapes
            + [jax.ShapeDtypeStruct((nt, full_rows, pix_part), bf16)],
            scratch_shapes=gather_sems,
            compiler_params=pltpu.CompilerParams(collective_id=0, has_side_effects=True),
            cost_estimate=cost(0, 50e6),
            name="gather_weights",
        )(own, other, pred_own, patch_out)
        attn_emb, up_w, down_t, pred_all = (
            value.reshape(nt, edge, -1) for value in (attn_emb, up_w, down_t, pred_all)
        )
        middle, resid, normed_a, rows_a, att_a = pl.pallas_call(
            functools.partial(encoder_attend_kernel, edge, npatches, context_len, HD, ctx_rows),
            grid=(2 * nt,),
            in_specs=[
                pl.BlockSpec(memory_space=pltpu.SMEM),
                pl.BlockSpec((1, full_rows, pix_part), lambda i: (jnp.minimum(i, nt - 1), 0, 0)),
                whole((full_rows, width)),
                pl.BlockSpec(
                    (1, edge, side * pix_part),
                    lambda i: (jnp.minimum(i, nt - 1), 0, attn_cols // (side * pix_part)),
                ),
                whole((width, width)),
                pl.BlockSpec((1, edge, attn_cols), lambda i: (jnp.maximum(i - nt, 0), 0, 0)),
                whole((8, width)),
            ],
            out_specs=[
                whole((full_rows, width)),
                whole((ctx_rows, width)),
                whole((ctx_rows, width)),
                pl.BlockSpec((1, ctx_rows, 3 * columns), lambda i: (jnp.maximum(i - nt, 0), 0, 0)),
                pl.BlockSpec((1, ctx_rows, columns), lambda i: (jnp.maximum(i - nt, 0), 0, 0)),
            ],
            out_shape=[
                jax.ShapeDtypeStruct((full_rows, width), f32),
                jax.ShapeDtypeStruct((ctx_rows, width), f32),
                jax.ShapeDtypeStruct((ctx_rows, width), bf16),
                jax.ShapeDtypeStruct((nt, ctx_rows, 3 * columns), bf16),
                jax.ShapeDtypeStruct((nt, ctx_rows, columns), bf16),
            ],
            scratch_shapes=[VMEM((full_rows, width), f32), VMEM((full_rows, width), bf16)],
            compiler_params=compiled(),
            cost_estimate=cost(6e9, 12e6),
            name="encoder_attend",
        )(role_word, patch_rows, base, attn_emb, order, attn_emb, vec)
        output, normed_f, hidden, enc_feat, target = pl.pallas_call(
            functools.partial(encoder_feed_kernel, edge, ctx_rows),
            grid=(nt,),
            in_specs=[
                whole((full_rows, width)),
                by_group((edge, mat)),
                by_group((edge, mat)),
                whole((8, width)),
                whole((tgt_rows, full_rows)),
                whole((nt, width, quarter)),
            ],
            out_specs=[
                whole((ctx_rows, width)),
                whole((ctx_rows, width)),
                by_group((ctx_rows, width)),
                whole((nt, ctx_rows, quarter)),
                whole((nt, tgt_rows, quarter)),
            ],
            out_shape=[
                jax.ShapeDtypeStruct((ctx_rows, width), f32),
                jax.ShapeDtypeStruct((ctx_rows, width), bf16),
                jax.ShapeDtypeStruct((nt, ctx_rows, width), f32),
                jax.ShapeDtypeStruct((nt, ctx_rows, quarter), bf16),
                jax.ShapeDtypeStruct((nt, tgt_rows, quarter), bf16),
            ],
            scratch_shapes=[VMEM((full_rows, width), f32), VMEM((full_rows, width), bf16)],
            compiler_params=compiled(),
            cost_estimate=cost(8e9, 14e6),
            name="encoder_feed",
        )(middle, up_w, down_t, vec, pick, swap)

        feat_in = routes.across(1, enc_feat, from_role=0)
        tokens_at = table_p[jnp.concatenate([my_ctx, my_tgt], 1)]
        mask_rows = jnp.arange(seq_len)[None, :, None] >= context_len
        tokens_at = jnp.where(mask_rows, tokens_at + pvec[4 * players + 2], tokens_at)
        tokens_at = tokens_at.reshape(-1, narrow)
        hot = one_hot.T.astype(bf16)

    token_rows = share * seq_len
    pred_cols = (3 * players + 1) * edge
    denominator = images * nd * target_len * width
    pred_columns = narrow // nt
    pred_grads, pred_vec_g, loss_tile, back = pl.pallas_call(
        functools.partial(predictor_kernel, share, context_len, players, PHD, denominator),
        in_specs=[in_vmem] * 3 + [any_space] + [in_vmem] * 2,
        out_specs=[any_space] + [in_vmem] * 3,
        out_shape=[
            jax.ShapeDtypeStruct((nt, edge, pred_cols), bf16),
            jax.ShapeDtypeStruct((16, narrow), f32),
            jax.ShapeDtypeStruct((8, 128), f32),
            jax.ShapeDtypeStruct((ctx_rows, width), bf16),
        ],
        scratch_shapes=[
            VMEM((nt, edge, pred_cols), bf16),
            VMEM((nt, edge, pred_cols), bf16),
            dma((3 * players + 1,)),
            dma((3 * players + 1,)),
            VMEM((players + 1, token_rows, narrow), f32),
            VMEM((players, token_rows, narrow), f32),
            VMEM((players, token_rows, narrow), bf16),
            VMEM((players, token_rows, narrow), bf16),
            VMEM((players, nt, token_rows, 3 * pred_columns), bf16),
            VMEM((players, nt, token_rows, pred_columns), bf16),
            VMEM((players, nt // 2, token_rows, 2 * edge), f32),
            VMEM((token_rows, narrow), f32),
            VMEM((token_rows, narrow), f32),
            VMEM((token_rows, narrow), bf16),
            VMEM((tgt_rows, narrow), bf16),
        ],
        compiler_params=pltpu.CompilerParams(vmem_limit_bytes=KERNEL_BYTES),
        cost_estimate=cost(16e9, 30e6),
        name="predictor",
    )(feat_in, target, tokens_at, pred_all, pvec, hot)
    all_cols = attn_cols + side * pix_part
    middle_size = nd // 2
    block_shape = [
        jax.ShapeDtypeStruct((rows_part, (block_count + 1) * edge), bf16),
        jax.ShapeDtypeStruct((rows_part, side * pix_part), f32),
    ]
    if rows_part % 16 == 0:
        widths_g = (mat, mat, mat, side * pix_part)
        vec_steps = nd.bit_length() + nt.bit_length() - 2
        slot_numbers = jnp.arange(slot_count, dtype=jnp.int32)
        holds = (owner[None, :] == slot_numbers[:, None]).astype(jnp.int32)
        order_of = jnp.arange(block_count, dtype=jnp.int32) - block_count
        slot_of = block_count + jnp.sum(holds * order_of[None, :], 1)
        low_grads, emb_sum, vec_sum = pl.pallas_call(
            functools.partial(backward_kernel, routes, context_len, HD),
            in_specs=[pl.BlockSpec(memory_space=pltpu.SMEM)]
            + [any_space] * 5
            + [in_vmem] * 15,
            out_specs=[any_space] + [in_vmem] * 2,
            out_shape=[
                jax.ShapeDtypeStruct((slots, nd, rows_part, edge), bf16),
                block_shape[1],
            ]
            + [jax.ShapeDtypeStruct((32, edge), f32)],
            scratch_shapes=[
                VMEM((block_count + 1, rows_part, edge), bf16),
                VMEM((nd, slots, rows_part, edge), bf16),
            ]
            + [VMEM((nt, nd, rows_part, c), bf16) for c in widths_g]
            + [VMEM((nt, middle_size, rows_part, c), bf16) for c in widths_g]
            + [VMEM((nt, middle_size - 1, rows_part, c), bf16) for c in widths_g]
            + [
                VMEM((nt, rows_part, sum(widths_g)), bf16),
                VMEM((nt, rows_part, pred_cols), bf16),
                VMEM((2, edge, mat), bf16),
                VMEM((2, edge, mat), bf16),
                VMEM((2, edge, mat), bf16),
                VMEM((ctx_rows, width), bf16),
                VMEM((ctx_rows, width), f32),
                VMEM((ctx_rows, width), bf16),
                VMEM((ctx_rows, width), f32),
                VMEM((8, width), f32),
                VMEM((vec_steps, 32, edge), f32),
                VMEM((vec_steps, 32, edge), f32),
                dma((3, 2)),
                dma(()),
                dma(()),
                dma((4, nt)),
                dma((4, nt)),
                dma((4, nt)),
                dma((4, nt, routes.stages)),
                dma((4, nt, routes.stages)),
                dma((2, 4, nt)),
                dma((2, 4, nt)),
                dma((vec_steps,)),
                dma((vec_steps,)),
                dma((nd,)),
                dma((nd,)),
                dma(()),
            ],
            compiler_params=pltpu.CompilerParams(
                collective_id=1, has_side_effects=True, vmem_limit_bytes=KERNEL_BYTES
            ),
            cost_estimate=cost(14e9, 60e6),
            name="encode_back_and_reduce",
        )(
            slot_of, pred_grads.reshape(nt, nd, rows_part, -1), back, attn_emb, up_w, down_t,
            output, middle, resid, normed_f, normed_a, hidden, rows_a, att_a, patch_rows,
            vec, order, hot, hot_p, pred_vec_g, loss_tile,
        )
        enc_total = jnp.concatenate([vec_sum[:7], vec_sum[8:15]], 1)
        pred_total = vec_sum[16 : 16 + 4 * players + 3]
        loss_total = vec_sum[28, 0]
        low_grads = low_grads.reshape(slots, edge, edge)
    else:
        back = routes.across(1, back, from_role=1)

        grad_shape = jax.ShapeDtypeStruct((nt, edge, mat), bf16)
        up_g, down_g, grad_mid, vec_g1 = pl.pallas_call(
            functools.partial(encoder_feed_back_kernel, edge),
            grid=(nt,),
            in_specs=[
                whole((ctx_rows, width)),
                whole((ctx_rows, width)),
                whole((ctx_rows, width)),
                whole((ctx_rows, width)),
                by_group((ctx_rows, width)),
                by_group((edge, mat)),
                by_group((edge, mat)),
                whole((8, width)),
            ],
            out_specs=[by_group((edge, mat))] * 2 + [whole((ctx_rows, width)), whole((8, width))],
            out_shape=[grad_shape] * 2
            + [
                jax.ShapeDtypeStruct((ctx_rows, width), f32),
                jax.ShapeDtypeStruct((8, width), f32),
            ],
            scratch_shapes=[
                VMEM((ctx_rows, width), f32),
                VMEM((ctx_rows, width), bf16),
                VMEM((ctx_rows, width), f32),
            ],
            compiler_params=compiled(),
            cost_estimate=cost(8e9, 25e6),
            name="encoder_feed_back",
        )(back, output, middle, normed_f, hidden, up_w, down_t, vec)
        attn_g, vec_g2 = pl.pallas_call(
            functools.partial(encoder_attend_back_kernel, edge, npatches, context_len, HD),
            grid=(2 * nt,),
            in_specs=[
                pl.BlockSpec(memory_space=pltpu.SMEM),
                whole((ctx_rows, width)),
                whole((ctx_rows, width)),
                whole((ctx_rows, width)),
                pl.BlockSpec((1, ctx_rows, 3 * columns), lambda i: (jnp.minimum(i, nt - 1), 0, 0)),
                pl.BlockSpec((1, ctx_rows, columns), lambda i: (jnp.minimum(i, nt - 1), 0, 0)),
                pl.BlockSpec((1, edge, attn_cols), lambda i: (jnp.minimum(i, nt - 1), 0, 0)),
                pl.BlockSpec((1, ctx_rows, pix_part), lambda i: (jnp.maximum(i - nt, 0), 0, 0)),
                whole((width, width)),
                whole((8, width)),
            ],
            out_specs=[
                whole((nt, edge, all_cols)),
                whole((8, width)),
            ],
            out_shape=[
                jax.ShapeDtypeStruct((nt, edge, all_cols), bf16),
                jax.ShapeDtypeStruct((8, width), f32),
            ],
            scratch_shapes=[VMEM((ctx_rows, width), bf16), VMEM((ctx_rows, width), f32)],
            compiler_params=compiled(),
            cost_estimate=cost(6e9, 20e6),
            name="encoder_attend_back",
        )(role_word, grad_mid, resid, normed_a, rows_a, att_a, attn_emb, patch_rows, order, vec)

        places = [g.reshape(nt, nd, rows_part, -1) for g in (down_g, up_g, attn_g, pred_grads)]
        by_block, emb_sum = pl.pallas_call(
            functools.partial(reduce_kernel, routes, attn_cols),
            in_specs=[any_space] * 4,
            out_specs=[in_vmem] * 2,
            out_shape=block_shape,
            scratch_shapes=[
                VMEM((nt, middle_size, rows_part, mat), bf16),
                VMEM((nt, middle_size, rows_part, mat), bf16),
                VMEM((nt, middle_size, rows_part, all_cols), bf16),
                VMEM((nt, middle_size - 1, rows_part, mat), bf16),
                VMEM((nt, middle_size - 1, rows_part, mat), bf16),
                VMEM((nt, middle_size - 1, rows_part, all_cols), bf16),
                VMEM((nt, rows_part, 2 * mat + all_cols), bf16),
                VMEM((nt, rows_part, pred_cols), bf16),
                VMEM((2, middle_size, rows_part, all_cols), bf16),
                dma((2,)),
                dma((3, nt)),
                dma((3, nt)),
                dma((3, nt, routes.stages)),
                dma((3, nt, routes.stages)),
                dma((2, 3, nt)),
                dma((2, 3, nt)),
            ],
            compiler_params=pltpu.CompilerParams(
                collective_id=1, has_side_effects=True, vmem_limit_bytes=KERNEL_BYTES
            ),
            cost_estimate=cost(0, 60e6),
            name="reduce_gradients",
        )(*places)

        enc_rows = to_global(vec_g1[:7] + vec_g2[:7], one_hot)
        pred_rows = to_global(pred_vec_g[: 4 * players + 3], one_hot_p)
        enc_rows = jnp.where(student_role, enc_rows, 0.0)
        pred_rows = jnp.where(role == 1, pred_rows, 0.0)
        loss_row = jnp.where(role == 1, loss_tile[0, 0], 0.0)
        packed = jnp.concatenate([enc_rows.reshape(-1), pred_rows.reshape(-1), loss_row[None]])
        packed = jnp.pad(packed, (0, -packed.shape[0] % 1024)).reshape(-1, 128)
        packed = routes.total(packed).reshape(-1)
        enc_total = packed[: enc_rows.size].reshape(enc_rows.shape)
        pred_total = packed[enc_rows.size : enc_rows.size + pred_rows.size].reshape(pred_rows.shape)
        loss_total = packed[enc_rows.size + pred_rows.size]
        by_block = by_block.reshape(rows_part, block_count + 1, edge).transpose(1, 0, 2)
        slot_of = (
            jnp.full((slot_count,), block_count, jnp.int32)
            .at[owner]
            .set(jnp.arange(block_count, dtype=jnp.int32))
        )
        slot_rows = by_block[slot_of].reshape(nd, slots, rows_part, edge)
        slot_rows = lax.all_to_all(slot_rows, "dp", split_axis=0, concat_axis=1, tiled=False)
        low_grads = slot_rows.reshape(slots, edge, edge)

    embed_grad = emb_sum.reshape(rows_part, side, pix_part).transpose(1, 0, 2)
    embed_grad = embed_grad.reshape(-1, pix_part).T

    slot_spec = pl.BlockSpec((1, 1, edge, edge), lambda s: (0, s, 0, 0))
    slot_shape = jax.ShapeDtypeStruct(weights.shape, f32)
    slot_grads, new_weights, new_left, new_right, new_teacher_blocks = pl.pallas_call(
        shampoo_kernel,
        grid=(slots,),
        in_specs=[pl.BlockSpec((1, edge, edge), lambda s: (s, 0, 0))] + [slot_spec] * 6,
        out_specs=[slot_spec] * 5,
        out_shape=[slot_shape] * 5,
        compiler_params=compiled(),
        cost_estimate=cost(3e9, 22e6),
        name="shampoo",
    )(low_grads, weights, stats_left, stats_right, root_left, root_right, teacher_slot_blocks)
    new_embed, new_embed_m, new_embed_v = adamw(embed, embed_m, embed_v, embed_grad, 0.05, 0.05)
    new_enc, new_enc_m, new_enc_v = adamw(enc_vectors, enc_m, enc_v, enc_total, 0.5, 0.0)
    new_pred, new_pred_m, new_pred_v = adamw(pred_vectors, pred_m, pred_v, pred_total, 0.5, 0.0)
    new_teacher_embed = 0.7 * teacher_embed + 0.3 * new_embed
    new_teacher_vectors = 0.7 * teacher_vectors + 0.3 * new_enc
    return (
        loss_total,
        slot_grads,
        new_weights,
        new_left,
        new_right,
        new_teacher_blocks,
        new_embed,
        new_embed_m,
        new_embed_v,
        new_teacher_embed,
        new_enc,
        new_enc_m,
        new_enc_v,
        new_pred,
        new_pred_m,
        new_pred_v,
        new_teacher_vectors,
    )


def solution(mesh):
    blocks = P("tensor", "dp", None, None)
    table = P("tensor", "dp")
    in_specs = (
        (P("dp", None, "tensor"), P("dp", None), P("dp", None), P())
        + (blocks,) * 6
        + (table,) * 4
        + (P(),) * 7
    )
    out_specs = (P(),) + (blocks,) * 5 + (table,) * 4 + (P(),) * 7
    return jax.shard_map(shards, mesh=mesh, in_specs=in_specs, out_specs=out_specs, check_vma=False)
```

```python
import functools
import math

import jax
import jax.numpy as jnp
import numpy as np
from jax import lax
from jax.experimental import pallas as pl
from jax.experimental.pallas import tpu as pltpu
from jax.sharding import PartitionSpec as P

HD = 64
PHD = 32
SIDE = 16
STEP = 10
KERNEL_BYTES = 60 * 1024 * 1024

AXES = ("dp", "tensor")
exact = lax.Precision.HIGHEST
f32 = jnp.float32
bf16 = jnp.bfloat16
VMEM = pltpu.VMEM


def nn(first, second):
    return lax.dot_general(first, second, (((1,), (0,)), ((), ())), preferred_element_type=f32)


def nt_(first, second):
    return lax.dot_general(first, second, (((1,), (1,)), ((), ())), preferred_element_type=f32)


def tn(first, second):
    return lax.dot_general(first, second, (((0,), (0,)), ((), ())), preferred_element_type=f32)


def norm_parts(values):
    centre = values - jnp.mean(values, -1, keepdims=True)
    scale = lax.rsqrt(jnp.mean(centre * centre, -1, keepdims=True) + 1e-06)
    return centre * scale, scale


def layer_norm(values, gain_row, shift_row):
    return norm_parts(values)[0] * gain_row + shift_row


def norm_backward(grad, values, gain_row):
    unit, scale = norm_parts(values)
    weighted = grad * gain_row
    inner = (
        weighted
        - jnp.mean(weighted, -1, keepdims=True)
        - unit * jnp.mean(weighted * unit, -1, keepdims=True)
    )
    return (
        inner * scale,
        jnp.sum(grad * unit, 0, keepdims=True),
        jnp.sum(grad, 0, keepdims=True),
    )


def gelu_parts(values):
    below = 0.5 * (1.0 + lax.erf(values * math.sqrt(0.5)))
    density = jnp.exp(-0.5 * values * values) * (1.0 / math.sqrt(2.0 * math.pi))
    return values * below, below + values * density


def softened_t(queries, keys, head_size, allowed):
    scores = nt_(keys, queries) * (1.0 / math.sqrt(head_size))
    if allowed is not None:
        scores = jnp.where(allowed, scores, -1e30)
    expo = jnp.exp(scores - jnp.max(scores, 0, keepdims=True))
    return expo * (1.0 / jnp.sum(expo, 0, keepdims=True))


def attend(rows, head_size, length, allowed):
    columns = rows.shape[1] // 3
    images = []
    for at in range(0, rows.shape[0], length):
        outs = []
        for h in range(0, columns, head_size):
            q, k, v = (
                rows[at : at + length, j * columns + h : j * columns + h + head_size]
                for j in range(3)
            )
            soft = softened_t(q, k, head_size, allowed).astype(bf16)
            outs.append(tn(v, soft).astype(bf16))
        images.append(jnp.concatenate(outs, 0))
    joined = jnp.concatenate(images, 1) if len(images) > 1 else images[0]
    return joined.T


def attend_back(rows, grad, head_size, length, allowed):
    columns = rows.shape[1] // 3
    factor = 1.0 / math.sqrt(head_size)
    images = []
    for at in range(0, rows.shape[0], length):
        outs = [[], [], []]
        for h in range(0, columns, head_size):
            q, k, v = (
                rows[at : at + length, j * columns + h : j * columns + h + head_size]
                for j in range(3)
            )
            g = grad[at : at + length, h : h + head_size]
            soft = softened_t(q, k, head_size, allowed)
            outs[2].append(nn(soft.astype(bf16), g).astype(bf16))
            ds = nt_(v, g)
            ds = (soft * (ds - jnp.sum(ds * soft, 0, keepdims=True))).astype(bf16)
            outs[0].append((tn(k, ds) * factor).astype(bf16))
            outs[1].append((nn(ds, q) * factor).astype(bf16))
        queries = jnp.concatenate(outs[0], 0).T
        images.append(jnp.concatenate([queries] + outs[1] + outs[2], 1))
    return jnp.concatenate(images, 0) if len(images) > 1 else images[0]


def same_image(role, length, context):
    row = lax.broadcasted_iota(jnp.int32, (length, length), 0) // context
    column = lax.broadcasted_iota(jnp.int32, (length, length), 1) // context
    return (row == column) | (role != 0)


def encoder_attend_kernel(
    edge, unit, context, head_size, kept,
    role_ref, patch_ref, base_ref, emb_ref, order_ref, w_ref, vec_ref,
    mid_ref, resid_ref, normed_ref, rows_ref, att_ref, x_ref, h_ref,
):
    step = pl.program_id(0)
    groups = pl.num_programs(0) // 2
    side = 2
    wide = side * edge
    pix = patch_ref.shape[2]
    columns = wide // 4

    @pl.when(step == 0)
    def _():
        x_ref[...] = base_ref[...]

    @pl.when(step < groups)
    def _():
        ordered = sum(
            nn(order_ref[:, m * edge : (m + 1) * edge], emb_ref[0, :, m * pix : (m + 1) * pix])
            for m in range(side)
        ).astype(bf16)
        x_ref[...] += nt_(patch_ref[0], ordered)

    @pl.when(step == groups - 1)
    def _():
        values = x_ref[...]
        resid_ref[...] = values[:kept]
        low = layer_norm(values, vec_ref[0:1], vec_ref[1:2]).astype(bf16)
        h_ref[...] = low
        normed_ref[...] = low[:kept]

    @pl.when(step >= groups)
    def _():
        rows = sum(
            nn(h_ref[:, r * edge : (r + 1) * edge], w_ref[0, :, r * wide : r * wide + 3 * columns])
            for r in range(side)
        ).astype(bf16)
        rows_ref[0] = rows[:kept]
        att = attend(rows, head_size, unit, same_image(role_ref[0], unit, context))
        att_ref[0] = att[:kept]
        for r in range(side):
            x_ref[:, r * edge : (r + 1) * edge] += nt_(
                att, w_ref[0, :, r * wide + 3 * columns : (r + 1) * wide]
            )

    @pl.when(step == 2 * groups - 1)
    def _():
        mid_ref[...] = x_ref[...]


def encoder_feed_kernel(
    edge, kept, mid_ref, up_ref, down_ref, vec_ref, pick_ref, swap_ref,
    out_ref, normed_ref, hidden_ref, feat_ref, target_ref, x_ref, h_ref,
):
    step = pl.program_id(0)
    groups = pl.num_programs(0)
    side = 2
    wide = side * edge

    @pl.when(step == 0)
    def _():
        values = mid_ref[...]
        x_ref[...] = values
        low = layer_norm(values, vec_ref[2:3], vec_ref[3:4]).astype(bf16)
        h_ref[...] = low
        normed_ref[...] = low[:kept]

    hidden = sum(
        nn(h_ref[:, r * edge : (r + 1) * edge], up_ref[0, :, r * wide : (r + 1) * wide])
        for r in range(side)
    )
    hidden_ref[0] = hidden[:kept]
    active = gelu_parts(hidden)[0].astype(bf16)
    for r in range(side):
        x_ref[:, r * edge : (r + 1) * edge] += nt_(
            active, down_ref[0, :, r * wide : (r + 1) * wide]
        )

    @pl.when(step == groups - 1)
    def _():
        values = x_ref[...]
        out_ref[...] = values[:kept]
        final = layer_norm(values, vec_ref[4:5], vec_ref[5:6])
        encoded = final[:kept].astype(bf16)
        target = norm_parts(final)[0].astype(bf16)
        picked = nn(pick_ref[...], target).astype(bf16)
        for t in range(swap_ref.shape[0]):
            feat_ref[t] = nn(encoded, swap_ref[t]).astype(bf16)
            target_ref[t] = nn(picked, swap_ref[t]).astype(bf16)


def put(grad_ref, t, columns, value):
    grad_ref[t, :, columns] = value.astype(bf16)


def predictor_kernel(
    share, context, players, head_size, denominator,
    feat_ref, target_ref, base_ref, first_hbm, second_hbm, vec_ref, hot_ref,
    grad_hbm, vec_grad_ref, loss_ref, back_ref,
    w_ref, grad_ref, w_sem, grad_sem, x_ref, mid_ref, h_ref, h2_ref, rows_ref, att_ref, hidden_ref, acc_ref, d_ref, low_ref, f_ref,
):
    groups = w_ref.shape[0]
    edge = w_ref.shape[1]
    length = base_ref.shape[0] // share
    quarter = feat_ref.shape[2]
    columns = edge // 4
    last = 3 * players * edge
    in_cols = slice(last, last + quarter)
    out_cols = slice(last + quarter, last + 2 * quarter)

    def span(number):
        return slice(number * edge, (number + 1) * edge)

    def copy_in(number):
        ref, place = first_hbm, (number + 1) % (3 * players + 1)
        if place * edge >= first_hbm.shape[2]:
            ref, place = second_hbm, place - first_hbm.shape[2] // edge
        return pltpu.make_async_copy(
            ref.at[:, :, pl.ds(place * edge, edge)],
            w_ref.at[:, :, pl.ds(number * edge, edge)],
            w_sem.at[number],
        )

    def copy_out(number):
        columns = pl.ds(number * edge, edge)
        return pltpu.make_async_copy(
            grad_ref.at[:, :, columns], grad_hbm.at[:, :, columns], grad_sem.at[number]
        )

    def pair(p, number):
        return jnp.concatenate([w_ref[2 * p + i, :, span(number)] for i in range(2)], 1)

    def put_pair(p, number, value):
        for i in range(2):
            put(grad_ref, 2 * p + i, span(number), value[:, i * edge : (i + 1) * edge])

    for number in [3 * players] + list(range(3 * players)):
        copy_in(number).start()
    vec_grad_ref[...] = jnp.zeros_like(vec_grad_ref)
    copy_in(3 * players).wait()
    projected = sum(nt_(feat_ref[t], w_ref[t, :, in_cols]) for t in range(groups))
    x_ref[0] = base_ref[...]
    for i in range(share):
        x_ref[0, i * length : i * length + context] += projected[i * context : (i + 1) * context]

    for j in range(players):
        values = x_ref[j]
        h_ref[j] = layer_norm(values, vec_ref[4 * j : 4 * j + 1], vec_ref[4 * j + 1 : 4 * j + 2]).astype(bf16)
        mid_ref[j] = values
        copy_in(3 * j).wait()

        @pl.loop(0, groups // 2)
        def _(p, j=j):
            both = nn(h_ref[j], pair(p, 3 * j)).astype(bf16)
            mixed = None
            for i in range(2):
                t = 2 * p + i
                rows = both[:, i * edge : i * edge + 3 * columns]
                rows_ref[j, t] = rows
                att = attend(rows, head_size, length, None)
                att_ref[j, t] = att
                out = nt_(att, w_ref[t, :, 3 * j * edge + 3 * columns : (3 * j + 1) * edge])
                mixed = out if mixed is None else mixed + out
            mid_ref[j] += mixed

        values = mid_ref[j]
        h2_ref[j] = layer_norm(values, vec_ref[4 * j + 2 : 4 * j + 3], vec_ref[4 * j + 3 : 4 * j + 4]).astype(bf16)
        x_ref[j + 1] = values
        copy_in(3 * j + 1).wait()
        copy_in(3 * j + 2).wait()

        @pl.loop(0, groups // 2)
        def _(p, j=j):
            hidden = nn(h2_ref[j], pair(p, 3 * j + 1))
            hidden_ref[j, p] = hidden
            x_ref[j + 1] += nt_(gelu_parts(hidden)[0].astype(bf16), pair(p, 3 * j + 2))

    final_gain = vec_ref[4 * players : 4 * players + 1]
    final = layer_norm(x_ref[players], final_gain, vec_ref[4 * players + 1 : 4 * players + 2]).astype(bf16)
    f_ref[...] = jnp.concatenate(
        [final[i * length + context : (i + 1) * length] for i in range(share)], 0
    )
    total = jnp.zeros((1, 1), f32)
    grad_f = jnp.zeros(f_ref.shape, f32)
    for t in range(groups):
        out_w = w_ref[t, :, out_cols]
        gap = nn(f_ref[...], out_w) - target_ref[t].astype(f32)
        size = jnp.abs(gap)
        terms = jnp.where(size < 1.0, 0.5 * gap * gap, size - 0.5)
        total += jnp.sum(jnp.sum(terms, 1, keepdims=True), 0, keepdims=True)
        grad_pred = (jnp.clip(gap, -1.0, 1.0) * (1.0 / denominator)).astype(bf16)
        put(grad_ref, t, out_cols, tn(f_ref[...], grad_pred))
        grad_f += nt_(grad_pred, out_w)
    loss_ref[...] = jnp.broadcast_to(total * (1.0 / denominator), loss_ref.shape)
    d_ref[...] = jnp.zeros_like(d_ref)
    tail = length - context
    for i in range(share):
        d_ref[i * length + context : (i + 1) * length] = grad_f[i * tail : (i + 1) * tail]
    grad, gain_g, shift_g = norm_backward(d_ref[...], x_ref[players], final_gain)
    d_ref[...] = grad
    vec_grad_ref[4 * players : 4 * players + 1] = gain_g
    vec_grad_ref[4 * players + 1 : 4 * players + 2] = shift_g

    for j in reversed(range(players)):
        low_ref[...] = d_ref[...].astype(bf16)
        acc_ref[...] = jnp.zeros_like(acc_ref)

        @pl.loop(0, groups // 2)
        def _(p, j=j):
            active, slope = gelu_parts(hidden_ref[j, p])
            low = low_ref[...]
            put_pair(p, 3 * j + 2, tn(low, active.astype(bf16)))
            grad_hidden = (nn(low, pair(p, 3 * j + 2)) * slope).astype(bf16)
            put_pair(p, 3 * j + 1, tn(h2_ref[j], grad_hidden))
            acc_ref[...] += nt_(grad_hidden, pair(p, 3 * j + 1))

        copy_out(3 * j + 2).start()
        copy_out(3 * j + 1).start()
        grad, gain_g, shift_g = norm_backward(
            acc_ref[...], mid_ref[j], vec_ref[4 * j + 2 : 4 * j + 3]
        )
        vec_grad_ref[4 * j + 2 : 4 * j + 3] = gain_g
        vec_grad_ref[4 * j + 3 : 4 * j + 4] = shift_g
        grad = d_ref[...] + grad
        d_ref[...] = grad
        low_ref[...] = grad.astype(bf16)
        acc_ref[...] = jnp.zeros_like(acc_ref)

        @pl.loop(0, groups // 2)
        def _(p, j=j):
            low = low_ref[...]
            total = None
            for i in range(2):
                t = 2 * p + i
                attn_w = w_ref[t, :, span(3 * j)]
                grad_att = nn(low, attn_w[:, 3 * columns :]).astype(bf16)
                grad_rows = attend_back(rows_ref[j, t], grad_att, head_size, length, None)
                grad_w = jnp.concatenate([tn(h_ref[j], grad_rows), tn(low, att_ref[j, t])], 1)
                put(grad_ref, t, span(3 * j), grad_w)
                out = nt_(grad_rows, attn_w[:, : 3 * columns])
                total = out if total is None else total + out
            acc_ref[...] += total

        copy_out(3 * j).start()
        grad, gain_g, shift_g = norm_backward(acc_ref[...], x_ref[j], vec_ref[4 * j : 4 * j + 1])
        vec_grad_ref[4 * j : 4 * j + 1] = gain_g
        vec_grad_ref[4 * j + 1 : 4 * j + 2] = shift_g
        d_ref[...] += grad

    mask_grad = jnp.zeros((1, edge), f32)
    for i in range(share):
        mask_grad += jnp.sum(d_ref[i * length + context : (i + 1) * length], 0, keepdims=True)
    vec_grad_ref[4 * players + 2 : 4 * players + 3] = mask_grad
    low = jnp.concatenate(
        [d_ref[i * length : i * length + context] for i in range(share)], 0
    ).astype(bf16)
    back = jnp.zeros((low.shape[0], hot_ref.shape[1]), f32)
    z = lax.axis_index("tensor")
    z = z - lax.rem(z, 2) + 1
    for t in range(groups):
        put(grad_ref, t, in_cols, tn(low, feat_ref[t]))
        first = pl.multiple_of(flip(z, t) * quarter, 16)
        back += nn(nn(low, w_ref[t, :, in_cols]).astype(bf16), hot_ref[pl.ds(first, quarter), :])
    copy_out(3 * players).start()
    back_ref[...] = back.astype(bf16)
    for number in range(3 * players + 1):
        copy_out(number).wait()


def encoder_feed_back_kernel(
    edge, back_ref, out_ref, mid_ref, normed_ref, hidden_ref, up_ref, down_ref, vec_ref,
    up_grad, down_grad, grad_ref, vec_grad_ref, d_ref, low_ref, acc_ref,
):
    step = pl.program_id(0)
    groups = pl.num_programs(0)
    wide = 2 * edge

    @pl.when(step == 0)
    def _():
        grad, gain_g, shift_g = norm_backward(back_ref[...].astype(f32), out_ref[...], vec_ref[4:5])
        d_ref[...] = grad
        low_ref[...] = grad.astype(bf16)
        acc_ref[...] = jnp.zeros_like(acc_ref)
        vec_grad_ref[...] = jnp.zeros_like(vec_grad_ref)
        vec_grad_ref[4:5] = gain_g
        vec_grad_ref[5:6] = shift_g

    active, slope = gelu_parts(hidden_ref[0])
    active = active.astype(bf16)
    grad_hidden = sum(
        nn(low_ref[:, r * edge : (r + 1) * edge], down_ref[0, :, r * wide : (r + 1) * wide])
        for r in range(2)
    )
    grad_hidden = (grad_hidden * slope).astype(bf16)
    for r in range(2):
        mine = slice(r * edge, (r + 1) * edge)
        columns = slice(r * wide, (r + 1) * wide)
        put(down_grad, 0, columns, tn(low_ref[:, mine], active))
        put(up_grad, 0, columns, tn(normed_ref[:, mine], grad_hidden))
        acc_ref[:, mine] += nt_(grad_hidden, up_ref[0, :, columns])

    @pl.when(step == groups - 1)
    def _():
        grad, gain_g, shift_g = norm_backward(acc_ref[...], mid_ref[...], vec_ref[2:3])
        grad_ref[...] = d_ref[...] + grad
        vec_grad_ref[2:3] = gain_g
        vec_grad_ref[3:4] = shift_g


def encoder_attend_back_kernel(
    edge, unit, context, head_size,
    role_ref, mid_grad_ref, resid_ref, normed_ref, rows_ref, att_ref, w_ref, patch_ref, order_ref,
    vec_ref, grad_ref, vec_grad_ref, low_ref, acc_ref,
):
    step = pl.program_id(0)
    groups = pl.num_programs(0) // 2
    wide = 2 * edge
    columns = wide // 4
    pix = patch_ref.shape[2]

    @pl.when(step == 0)
    def _():
        low_ref[...] = mid_grad_ref[...].astype(bf16)
        acc_ref[...] = jnp.zeros_like(acc_ref)

    @pl.when(step < groups)
    def _():
        grad_att = sum(
            nn(
                low_ref[:, r * edge : (r + 1) * edge],
                w_ref[0, :, r * wide + 3 * columns : (r + 1) * wide],
            )
            for r in range(2)
        ).astype(bf16)
        allowed = same_image(role_ref[0], unit, context)
        grad_rows = attend_back(rows_ref[0], grad_att, head_size, unit, allowed)
        for r in range(2):
            mine = slice(r * edge, (r + 1) * edge)
            grad_w = jnp.concatenate(
                [tn(normed_ref[:, mine], grad_rows), tn(low_ref[:, mine], att_ref[0])], 1
            )
            put(grad_ref, step, slice(r * wide, (r + 1) * wide), grad_w)
            acc_ref[:, mine] += nt_(grad_rows, w_ref[0, :, r * wide : r * wide + 3 * columns])

    @pl.when(step == groups - 1)
    def _():
        grad, gain_g, shift_g = norm_backward(acc_ref[...], resid_ref[...], vec_ref[0:1])
        grad = mid_grad_ref[...] + grad
        low_ref[...] = nn(grad.astype(bf16), order_ref[...]).astype(bf16)
        vec_grad_ref[...] = jnp.zeros_like(vec_grad_ref)
        vec_grad_ref[0:1] = gain_g
        vec_grad_ref[1:2] = shift_g
        vec_grad_ref[6:7] = jnp.sum(grad, 0, keepdims=True)

    @pl.when(step >= groups)
    def _():
        grad_w = jnp.concatenate(
            [tn(low_ref[:, r * edge : (r + 1) * edge], patch_ref[0]) for r in range(2)], 1
        )
        put(grad_ref, step - groups, slice(2 * wide, 2 * wide + 2 * pix), grad_w)


def shampoo_kernel(
    grad_ref, weight_ref, left_ref, right_ref, root_left_ref, root_right_ref, teacher_ref,
    grad_out, weight_out, left_out, right_out, teacher_out,
):
    low = grad_ref[0]
    grad_out[0, 0] = low.astype(f32)
    left_out[0, 0] = 0.95 * left_ref[0, 0] + 0.05 * nt_(low, low)
    right_out[0, 0] = 0.95 * right_ref[0, 0] + 0.05 * tn(low, low)
    high, rest = split(root_left_ref[0, 0])
    side = nn(high, low) + nn(rest, low)
    high, rest = split(side)
    root_high, root_rest = split(root_right_ref[0, 0])
    step = nn(high, root_high) + nn(high, root_rest) + nn(rest, root_high)
    mean = jnp.mean(jnp.mean(step * step, 1, keepdims=True), 0, keepdims=True)
    step = step * lax.rsqrt(mean + 1e-06)
    weight = weight_ref[0, 0]
    new = weight - 0.05 * (step + 0.05 * weight)
    weight_out[0, 0] = new
    teacher_out[0, 0] = 0.7 * teacher_ref[0, 0] + 0.3 * new


MESH = pl.DeviceIdType.MESH


def flip(place, bits):
    bit = 1
    while bit <= bits:
        if bits & bit:
            place = place + bit * (1 - 2 * lax.rem(lax.div(place, bit), 2))
        bit *= 2
    return place


def remote(source, target, send_sem, recv_sem, device):
    return pltpu.make_async_remote_copy(
        src_ref=source, dst_ref=target, send_sem=send_sem, recv_sem=recv_sem,
        device_id=device, device_id_type=MESH,
    )


def greet(routes, d, z, everyone=False):
    barrier = pltpu.get_barrier_semaphore()
    peers = [(d, flip(z, r)) for r in range(1, routes.nt)]
    if everyone:
        peers += [(routes.later(d, j), z) for j in range(1, routes.nd)]
    else:
        peers += [routes.partner(s, d, z) for s in range(routes.stages + 1)]
    for peer in peers:
        pl.semaphore_signal(barrier, inc=1, device_id=peer, device_id_type=MESH)
    pl.semaphore_wait(barrier, len(peers))


def sincos_table(columns):
    quarter = columns // 4
    frequency = 1.0 / np.float32(10000.0) ** (np.arange(quarter, dtype=np.float32) / quarter)
    angle = np.arange(SIDE, dtype=np.float32)[:, None] * frequency.astype(np.float32)
    parts = np.concatenate([np.sin(angle), np.cos(angle)], 1).astype(np.float32)
    none = np.zeros_like(parts)
    return np.concatenate(
        [np.concatenate([parts, none], 1), np.concatenate([none, parts], 1)], 0
    )


def guarded(condition, body):
    if condition is None:
        body()
    else:
        pl.when(condition)(body)


class Gather:
    ahead = 2
    players = 3

    def __init__(self, routes, widths, pre, few_rows, sources, mats, sems):
        self.routes, self.widths, self.pre, self.few_rows = routes, widths, pre, few_rows
        self.own, self.other, self.pred, self.few, self.every, self.rows = sources
        self.mats = mats
        self.sems = sems
        self.d, self.z = lax.axis_index("dp"), lax.axis_index("tensor")
        self.role = lax.rem(self.z, 2)
        self.last = len(widths) - 1
        self.items = [(m, r) for m in range(len(widths)) for r in range(routes.nt)]
        self.events = {}
        self.there = {}
        self.plan()

    def plan(self):
        for i, (m, r) in enumerate(self.items):
            pre = self.pre[m]
            if pre and r == 0:
                first = m - self.players
                for s in range(pre):
                    self.at(first + s * (self.ahead + first), s, self.alone, m, s)
                self.at(self.send_at[first], pre, self.share, m)
            for s in range(pre, self.routes.stages + 1):
                self.at(i + self.ahead * (s - pre), s, self.advance, m, r, s)
            self.there[m, r] = i + self.ahead * (self.routes.stages + 1 - pre)

    send_at = (6, 12)

    def at(self, step, order, action, m, *rest):
        def run():
            condition = None if action in (self.alone, self.share) else self.mine(m)
            guarded(condition, lambda: action(m, *rest))

        self.events.setdefault(step, []).append((-order, run))

    def peer(self, r):
        return self.d, flip(self.z, r)

    def peer_role(self, r):
        return lax.rem(flip(self.z, r), 2)

    def source(self, m, r):
        if m >= self.players:
            first = sum(self.widths[self.players : m])
            return self.pred.at[:, pl.ds(first, self.widths[m])]
        ref = self.own if r % 2 == 0 else self.other
        return ref.at[:, pl.ds(sum(self.widths[:m]), self.widths[m])]

    def across(self, m, r):
        source, target = self.source(m, r), self.mats[m].at[r, 0]
        if self.pre[m]:
            pieces = pl.ds(0, 1 << self.pre[m])
            source, target = self.mats[m].at[0, pieces], self.mats[m].at[r, pieces]
        return remote(source, target, self.sems[0].at[m, r], self.sems[1].at[m, r], self.peer(r))

    def local(self, m):
        return pltpu.make_async_copy(self.source(m, 0), self.mats[m].at[0, 0], self.sems[2].at[m])

    def patch_source(self, r, role):
        place = flip(lax.div(self.z, 2), r // 2)
        ref = self.every if role else self.few
        rows = self.rows.shape[1] if role else self.few_rows
        if len(ref.shape) == 3:
            return ref.at[r, pl.ds(0, rows)], rows
        return ref.at[pl.ds(place * rows, rows)], rows

    def patch(self, r, role):
        source, rows = self.patch_source(r, role)
        return remote(
            source, self.rows.at[r, pl.ds(0, rows)], self.sems[3].at[r], self.sems[4].at[r],
            self.peer(r),
        )

    def own_patch(self, role):
        source, rows = self.patch_source(0, role)
        return pltpu.make_async_copy(
            source, self.rows.at[0, pl.ds(0, rows)], self.sems[2].at[self.last + 1]
        )

    def send_patches(self):
        for role in range(2):
            pl.when(self.role == role)(lambda role=role: self.own_patch(role).start())
            for r in range(1, self.routes.nt):
                pl.when(self.peer_role(r) == role)(
                    lambda r=r, role=role: self.patch(r, role).start()
                )

    def stage(self, m, r, s):
        size = 1 << s
        return remote(
            self.mats[m].at[r, pl.ds(0, size)], self.mats[m].at[r, pl.ds(size, size)],
            self.sems[5].at[m, r, s], self.sems[6].at[m, r, s],
            self.routes.partner(s, self.d, self.z),
        )

    def mine(self, m):
        return self.role == 1 if m >= self.players else None

    def theirs(self, m, r):
        return self.peer_role(r) == 1 if m >= self.players else None

    def send(self, m):
        for r in range(1, self.routes.nt):
            guarded(self.theirs(m, r), lambda r=r: self.across(m, r).start())

    def start(self):
        for m in range(len(self.widths)):
            guarded(None if self.pre[m] else self.mine(m), lambda m=m: self.local(m).start())
            if not self.pre[m]:
                self.send(m)

    def alone(self, m, s):
        if s:
            self.stage(m, 0, s - 1).wait_recv()
        else:
            self.local(m).wait()
        self.stage(m, 0, s).start()

    def share(self, m):
        self.stage(m, 0, self.pre[m] - 1).wait_recv()
        self.send(m)

    def advance(self, m, r, s):
        if s > self.pre[m]:
            self.stage(m, r, s - 1).wait_recv()
        elif r:
            self.across(m, r).wait_recv()
        elif not s:
            self.local(m).wait()
        self.stage(m, r, s).start()

    def step(self, n):
        for _, run in sorted(self.events.get(n, []), key=lambda event: event[0]):
            run()

    def span(self):
        return max(self.there.values()) + 1

    def arrive(self, m, r):
        self.stage(m, r, self.routes.stages).wait_recv()

    def wait_patches(self):
        for role in range(2):
            pl.when(self.role == role)(lambda role=role: self.own_patch(role).wait())
            for r in range(1, self.routes.nt):
                pl.when(self.role == role)(lambda r=r, role=role: self.patch(r, role).wait_recv())

    def finish(self):
        for r in range(1, self.routes.nt):
            for role in range(2):
                pl.when(self.peer_role(r) == role)(
                    lambda r=r, role=role: self.patch(r, role).wait_send()
                )
        for m, r in self.items:
            pre = self.pre[m]

            def sent(m=m, r=r, pre=pre):
                for s in range(pre, self.routes.stages + 1):
                    self.stage(m, r, s).wait_send()

            guarded(self.mine(m), sent)
            if r:
                guarded(self.theirs(m, r), lambda m=m, r=r: self.across(m, r).wait_send())
            else:
                for s in range(pre):
                    self.stage(m, 0, s).wait_send()


def gather_kernel(
    routes, widths, few_rows, own_ref, other_ref, pred_ref, patch_ref,
    attn_ref, up_ref, down_ref, first_ref, second_ref, rows_ref, *sems,
):
    gather = Gather(
        routes, widths, (0,) * 5, few_rows,
        (own_ref, other_ref, pred_ref, patch_ref, patch_ref, rows_ref),
        (attn_ref, up_ref, down_ref, first_ref, second_ref), sems,
    )
    greet(routes, gather.d, gather.z)
    gather.start()
    gather.send_patches()
    for n in range(gather.span()):
        gather.step(n)
    for m, r in gather.items:
        guarded(gather.mine(m), lambda m=m, r=r: gather.arrive(m, r))
    gather.wait_patches()
    gather.finish()


def split(values):
    high = values.astype(bf16)
    return high, (values - high.astype(f32)).astype(bf16)


def exactly(product, first, second, turn=False):
    values = second if turn else first
    high, rest = split(values)
    low = (values - high.astype(f32) - rest.astype(f32)).astype(bf16)
    if turn:
        return product(first, high) + product(first, rest) + product(first, low)
    return product(high, second) + product(rest, second) + product(low, second)


def forward_kernel(
    routes, widths, unit, context, head_size,
    owner_ref, weight_ref, teach_ref, patch_ref, ctx_ref, tgt_ref, embed_ref, temb_ref,
    evec_ref, tvec_ref, pvec_in, table_in, table_p_in,
    attn_out, up_out, down_out, first_out, second_out, rows_out, mid_out, resid_out, normed_out, qkv_out,
    att_out, out_out, normed2_out, hidden_out, feat_out, target_out,
    hot_ref, order_ref, hot_p_ref, vec_ref, pvec_ref, tokens_ref,
    attn_ref, up_ref, down_ref, first_ref, second_ref, rows_ref, x_ref, h_ref, sent_ref, feat_ref,
    slots_out, slots_ref, own_ref, other_ref, pred_ref, picked_ref,
    back_sem, feat_send, feat_recv, slot_send, slot_recv, slot_sem, *sems,
):
    nt, nd = routes.nt, routes.nd
    mats = (attn_ref, up_ref, down_ref, first_ref, second_ref)
    outs = (attn_out, up_out, down_out, first_out, second_out)
    kept = resid_out.shape[0]
    gather = Gather(
        routes, widths, (0, 0, 0, 1, 1), kept,
        (own_ref, other_ref, pred_ref, picked_ref, patch_ref, rows_ref), mats, sems,
    )
    role = gather.role
    edge = nd * attn_ref.shape[2]
    side = 2
    wide = side * edge
    pix = rows_ref.shape[2]
    columns = wide // 4

    def matrix(ref, t, first, width):
        return ref[t, :, :, first : first + width].reshape(edge, width)

    def to_hbm(m, r):
        return pltpu.make_async_copy(mats[m].at[r], outs[m].at[r], back_sem.at[m, r])

    def feat_copy():
        return remote(sent_ref, feat_ref, feat_send, feat_recv, gather.peer(1))

    d, z = gather.d, gather.z
    rows_part = attn_ref.shape[2]
    slots = weight_ref.shape[0]
    span = x_ref.shape[0]
    images = ctx_ref.shape[0]
    share = span // unit
    part = lax.div(z, 2)

    def slot_copy(j):
        peer = routes.later(d, j)
        return remote(
            slots_out.at[:, :, peer], slots_ref.at[:, pl.ds(d * slots, slots)],
            slot_send.at[j], slot_recv.at[j], (peer, z),
        )

    def own_slots():
        return pltpu.make_async_copy(
            slots_out.at[:, :, d], slots_ref.at[:, pl.ds(d * slots, slots)], slot_sem
        )

    def send_slots():
        for kind, ref in enumerate((weight_ref, teach_ref)):
            for s in range(slots):
                slots_out[kind, s] = ref[s].astype(bf16).reshape(nd, rows_part, edge)
        own_slots().start()
        for j in range(1, nd):
            slot_copy(j).start()

    def by_rows(values):
        turned = values.T.astype(bf16)
        return jnp.concatenate([turned[:rows_part], turned[rows_part:]], 1)

    def take_slots():
        own_slots().wait()
        for j in range(1, nd):
            slot_copy(j).wait_recv()
        blocks = sum(widths[:3]) // edge - 1
        for b in range(blocks):
            first = b * edge if b < 4 else widths[0] + (b - 4) * edge
            own_ref[:, first : first + edge] = slots_ref[role, owner_ref[b]]
            other_ref[:, first : first + edge] = slots_ref[1 - role, owner_ref[b]]
        student, teacher = by_rows(embed_ref[...]), by_rows(temb_ref[...])
        first = widths[0] - student.shape[1]
        own_ref[:, first : widths[0]] = jnp.where(role == 0, student, teacher)
        other_ref[:, first : widths[0]] = jnp.where(role == 0, teacher, student)
        count = owner_ref.shape[0]
        for b in range(blocks, count):
            first = (b - blocks + 1) * edge if b < count - 1 else 0
            pred_ref[:, first : first + edge] = slots_ref[0, owner_ref[b]]

    def local_order(step, shift):
        lane = lax.broadcasted_iota(jnp.int32, (1, edge), 1)
        row = lane
        for k in range(nd):
            here = (lane >= k * rows_part) & (lane < (k + 1) * rows_part)
            row = jnp.where(here, lane + (routes.holder(k, d) * step + shift - k * rows_part), row)
        return row

    def one_hot(rows, row):
        return (lax.broadcasted_iota(jnp.int32, (rows, row.shape[1]), 0) == row).astype(bf16)

    def send_patches():
        for g in range(images):
            hot = one_hot(unit, ctx_ref[g : g + 1])
            patches = patch_ref[g * unit : (g + 1) * unit]
            picked_ref[g * context : (g + 1) * context] = tn(hot, patches).astype(bf16)
        gather.send_patches()

    def positions(table, hot, row):
        both = jnp.concatenate(
            [one_hot(unit // 16, lax.rem(row, 16)), one_hot(unit // 16, lax.div(row, 16))], 0
        )
        return exactly(tn, both, exactly(nn, table, hot), turn=True)

    def prepare():
        places = local_order(rows_part, 0)
        feat = jnp.concatenate([places, places + edge], 1)
        hot_ref[...] = one_hot(wide, feat)
        hot_p_ref[...] = one_hot(edge, places)
        emb = [local_order(2 * rows_part, m * rows_part) for m in range(2)]
        order_ref[...] = tn(hot_ref[...], one_hot(wide, jnp.concatenate(emb, 1))).astype(bf16)
        vec_ref[...] = jnp.zeros_like(vec_ref)
        pvec_ref[...] = jnp.zeros_like(pvec_ref)
        count = evec_ref.shape[0]
        vectors = jnp.where(role == 0, evec_ref[...], tvec_ref[...])
        vec_ref[0:count] = exactly(nn, vectors, hot_ref[...])
        count = pvec_in.shape[0]
        pvec_ref[0:count] = exactly(nn, pvec_in[...], hot_p_ref[...])

    def prepare_rows():
        ctx = [ctx_ref[pl.ds(part * share + i, 1), :] for i in range(share)]
        tgt = [tgt_ref[pl.ds(part * share + i, 1), :] for i in range(share)]
        rest = jnp.zeros((1, span - kept), jnp.int32)
        row = jnp.where(
            role == 0,
            jnp.concatenate(ctx + [rest], 1),
            lax.rem(lax.broadcasted_iota(jnp.int32, (1, span), 1), unit),
        )
        x_ref[...] = positions(table_in[...], hot_ref[...], row) + vec_ref[6:7]
        row = jnp.concatenate([v for pair in zip(ctx, tgt) for v in pair], 1)
        tokens = positions(table_p_in[...], hot_p_ref[...], row)
        length = row.shape[1] // share
        number = lax.broadcasted_iota(jnp.int32, tokens.shape, 0)
        is_target = lax.rem(number, length) >= context
        mask_at = pvec_in.shape[0] - 1
        tokens_ref[...] = jnp.where(is_target, tokens + pvec_ref[mask_at : mask_at + 1], tokens)

    def group_rows(t):
        quarter = target_out.shape[2]
        first = flip(z - lax.rem(z, 2) + 1, t) * quarter
        return hot_ref[pl.ds(pl.multiple_of(first, 16), quarter), :]

    def embed():
        gather.wait_patches()

        @pl.loop(0, nt)
        def _(t):
            ordered = sum(
                nn(
                    order_ref[:, m * edge : (m + 1) * edge],
                    matrix(attn_ref, t, side * wide + m * pix, pix),
                )
                for m in range(side)
            ).astype(bf16)
            x_ref[...] += nt_(rows_ref[t], ordered)

        values = x_ref[...]
        resid_out[...] = values[:kept]
        low = layer_norm(values, vec_ref[0:1], vec_ref[1:2]).astype(bf16)
        h_ref[...] = low
        normed_out[...] = low[:kept]

    def attention(t):
        rows = sum(
            nn(h_ref[:, r * edge : (r + 1) * edge], matrix(attn_ref, t, r * wide, 3 * columns))
            for r in range(side)
        ).astype(bf16)
        qkv_out[t] = rows[:kept]
        att = attend(rows, head_size, unit, same_image(role, unit, context))
        att_out[t] = att[:kept]
        for r in range(side):
            x_ref[:, r * edge : (r + 1) * edge] += nt_(
                att, matrix(attn_ref, t, r * wide + 3 * columns, columns)
            )

    def middle():
        values = x_ref[...]
        mid_out[...] = values[:kept]
        low = layer_norm(values, vec_ref[2:3], vec_ref[3:4]).astype(bf16)
        h_ref[...] = low
        normed2_out[...] = low[:kept]

    def feed(t):
        hidden = sum(
            nn(h_ref[:, r * edge : (r + 1) * edge], matrix(up_ref, t, r * wide, wide))
            for r in range(side)
        )
        hidden_out[t] = hidden[:kept]
        active = gelu_parts(hidden)[0].astype(bf16)
        for r in range(side):
            x_ref[:, r * edge : (r + 1) * edge] += nt_(
                active, matrix(down_ref, t, r * wide, wide)
            )

    def last():
        values = x_ref[...]
        out_out[...] = values[:kept]
        final = layer_norm(values, vec_ref[4:5], vec_ref[5:6])

        @pl.when(role == 0)
        def _():
            encoded = final[:kept].astype(bf16)
            for t in range(nt):
                sent_ref[t] = nt_(encoded, group_rows(t)).astype(bf16)
            feat_copy().start()

        @pl.when(role == 1)
        def _():
            target = norm_parts(final)[0].astype(bf16)
            tgt = [tgt_ref[pl.ds(part * share + i, 1), :] + i * unit for i in range(share)]
            picked = tn(one_hot(span, jnp.concatenate(tgt, 1)), target).astype(bf16)
            for t in range(nt):
                target_out[t] = nt_(picked, group_rows(t)).astype(bf16)

        @pl.when(role == 0)
        def _():
            target_out[...] = jnp.zeros_like(target_out)

    attn_at = max(gather.there[0, r] for r in range(nt))
    feed_at = max([attn_at + nt + 1] + [gather.there[2, r] - r for r in range(nt)])
    steps = max(gather.span(), feed_at + nt)
    greet(routes, d, z, everyone=True)
    send_slots()
    send_patches()
    prepare()
    take_slots()
    gather.start()
    prepare_rows()

    @pl.loop(0, steps)
    def _(n):
        for k in range(steps):

            @pl.when(n == k)
            def _(k=k):
                gather.step(k)
                for m, r in gather.items:
                    if gather.there[m, r] != k:
                        continue

                    def here(m=m, r=r):
                        gather.arrive(m, r)
                        to_hbm(m, r).start()

                    guarded(gather.mine(m), here)

        pl.when(n == attn_at)(embed)

        @pl.when((n > attn_at) & (n <= attn_at + nt))
        def _():
            attention(n - attn_at - 1)

        pl.when(n == feed_at)(middle)

        @pl.when((n >= feed_at) & (n < feed_at + nt))
        def _():
            feed(n - feed_at)

        pl.when(n == feed_at + nt - 1)(last)

    rows_out[...] = rows_ref[:, :kept]

    @pl.when(role == 0)
    def _():
        feat_copy().wait_send()
        feat_out[...] = jnp.zeros_like(feat_out)

    @pl.when(role == 1)
    def _():
        feat_copy().wait_recv()
        feat_out[...] = feat_ref[...]

    gather.finish()
    for j in range(1, nd):
        slot_copy(j).wait_send()
    for m, r in gather.items:
        guarded(gather.mine(m), lambda m=m, r=r: to_hbm(m, r).wait())


def reduce_kernel(
    routes, attn_cols, down_ref, up_ref, attn_ref, pred_ref, block_ref, emb_ref,
    core0, core1, core2, later0, later1, later2, enc_in, pred_in, load,
    load_sem, core_send, core_recv, stage_send, stage_recv, z_send, z_recv,
):
    d, z = lax.axis_index("dp"), lax.axis_index("tensor")
    nt, stages = routes.nt, routes.stages
    middle = routes.nd // 2
    role = lax.rem(z, 2)
    cores = [core0, core1, core2]
    laters = [later0, later1, later2]
    greet(routes, d, z)

    def run(kind, sources, incoming, starts):
        items = [(j, r) for j in range(len(sources)) for r in reversed(range(nt))]

        def part(j, r, first):
            ref, start, width = sources[j]
            return ref.at[r, pl.ds(first, middle), :, pl.ds(start, width)]

        def to_core(j, r):
            return remote(
                part(j, r, middle), cores[j].at[r, :, :, pl.ds(0, sources[j][2])],
                core_send.at[j, r], core_recv.at[j, r], routes.partner(stages, d, z),
            )

        def own(i):
            j, r = items[i]
            return pltpu.make_async_copy(
                part(j, r, 0), load.at[i % 2, :, :, pl.ds(0, sources[j][2])], load_sem.at[i % 2]
            )

        def stage(j, r, s):
            size = 1 << s
            return remote(
                cores[j].at[r, pl.ds(size, size), :, pl.ds(0, sources[j][2])],
                laters[j].at[r, pl.ds(size - 1, size), :, pl.ds(0, sources[j][2])],
                stage_send.at[j, r, s], stage_recv.at[j, r, s], routes.partner(s, d, z),
            )

        def across(j, r):
            return remote(
                cores[j].at[r, 0, :, pl.ds(0, sources[j][2])],
                incoming.at[r, :, pl.ds(starts[j], sources[j][2])],
                z_send.at[kind, j, r], z_recv.at[kind, j, r], (d, flip(z, r)),
            )

        def add(i, q):
            j, r = items[i]
            width = sources[j][2]
            if q == 0:
                own(i).wait()
                to_core(j, r).wait_recv()

                @pl.loop(0, middle)
                def _(k):
                    total = cores[j][r, k, :, 0:width].astype(f32)
                    total += load[i % 2, k, :, 0:width].astype(f32)
                    cores[j][r, k, :, 0:width] = total.astype(bf16)

                if i + 2 < len(items):
                    own(i + 2).start()
            else:
                s = stages - q
                stage(j, r, s).wait_recv()

                @pl.loop(0, 1 << s)
                def _(k):
                    total = cores[j][r, k, :, 0:width].astype(f32)
                    total += laters[j][r, k + ((1 << s) - 1), :, 0:width].astype(f32)
                    cores[j][r, k, :, 0:width] = total.astype(bf16)

            if q < stages:
                stage(j, r, stages - q - 1).start()
            elif r:
                across(j, r).start()

        for i in range(min(2, len(items))):
            own(i).start()
        for j, r in items:
            to_core(j, r).start()
        for n in range(len(items) + stages):
            for q in reversed(range(stages + 1)):
                if 0 <= n - q < len(items):
                    add(n - q, q)
        for j, r in items:
            to_core(j, r).wait_send()
            for s in range(stages):
                stage(j, r, s).wait_send()
            if r:
                across(j, r).wait_send()

    wide = down_ref.shape[3]
    all_cols = attn_ref.shape[3]
    pred_cols = pred_ref.shape[3]
    encoder = [(down_ref, 0, wide), (up_ref, 0, wide), (attn_ref, 0, all_cols)]
    encoder_at = [0, wide, 2 * wide]
    players = [(pred_ref, 0, wide), (pred_ref, wide, pred_cols - wide)]
    players_at = [0, wide]

    @pl.when(role == 0)
    def _():
        run(0, encoder, enc_in, encoder_at)

    @pl.when(role == 1)
    def _():
        run(1, players, pred_in, players_at)

    def collect(kind, sources, incoming, starts, put):
        for j, (_, _, width) in enumerate(sources):
            place = incoming.at[:, :, pl.ds(starts[j], width)]

            def arrive(r, j=j, width=width):
                pltpu.make_async_remote_copy(
                    src_ref=cores[j].at[r, 0, :, pl.ds(0, width)],
                    dst_ref=incoming.at[r, :, pl.ds(starts[j], width)],
                    send_sem=z_send.at[kind, j, r], recv_sem=z_recv.at[kind, j, r],
                    device_id=(d, flip(z, r)), device_id_type=MESH,
                ).wait_recv()

            del place

            @pl.when(role == kind)
            def _(j=j, width=width, arrive=arrive):
                total = cores[j][0, 0, :, 0:width].astype(f32)
                for r in range(2, nt, 2):
                    arrive(r)
                    total += incoming[r, :, starts[j] : starts[j] + width].astype(f32)
                put(j, total)

            @pl.when(role != kind)
            def _(j=j, width=width, arrive=arrive):
                total = None
                for r in range(1, nt, 2):
                    arrive(r)
                    got = incoming[r, :, starts[j] : starts[j] + width].astype(f32)
                    total = got if total is None else total + got
                put(j, total)

    def put_encoder(j, total):
        if j == 2:
            block_ref[:, 0:attn_cols] = total[:, :attn_cols].astype(bf16)
            emb_ref[...] = total[:, attn_cols:]
        else:
            first = attn_cols + (1 - j) * wide
            block_ref[:, first : first + wide] = total.astype(bf16)

    def put_players(j, total):
        first = attn_cols + 2 * wide + players_at[j]
        block_ref[:, first : first + total.shape[1]] = total.astype(bf16)

    collect(1, players, pred_in, players_at, put_players)
    collect(0, encoder, enc_in, encoder_at, put_encoder)
    end = attn_cols + 2 * wide + pred_cols
    block_ref[:, end:] = jnp.zeros((block_ref.shape[0], block_ref.shape[1] - end), bf16)


def backward_kernel(
    routes, context, head_size,
    slot_of_ref, players_ref, back_in, attn_hbm, up_hbm, down_hbm,
    out_ref, mid_ref, resid_ref, normed2_ref, normed_ref, hidden_ref, qkv_ref, att_ref, rows_ref,
    vec_ref, order_ref, hot_ref, hot_p_ref, pred_vec_ref, loss_ref,
    low_out, emb_ref, vec_out,
    block_ref, slots_ref, g0, g1, g2, g3, core0, core1, core2, core3, later0, later1, later2, later3, enc_in, pred_in,
    attn_w, up_w, down_w, back_ref, d_ref, low_ref, acc_ref, vec_grad_ref, vec_send, vec_recv,
    weight_sem, back_send, back_recv, load_sem, core_send, core_recv, stage_send, stage_recv,
    z_send, z_recv, vec_send_sem, vec_recv_sem, slot_send, slot_recv, slot_sem,
):
    d, z = lax.axis_index("dp"), lax.axis_index("tensor")
    nt, nd, stages = routes.nt, routes.nd, routes.stages
    role = lax.rem(z, 2)
    half = nd // 2
    grads, cores = (g0, g1, g2, g3), (core0, core1, core2, core3)
    laters = (later0, later1, later2, later3)
    rows = g0.shape[2]
    edge = nd * rows
    wide = 2 * edge
    columns = wide // 4
    pix = rows_ref.shape[2]
    unit = resid_ref.shape[0]
    mat = g0.shape[3]
    ahead = 2

    every = pl.ds(0, nt)
    encoder = [(j, r) for r in range(nt) for j in (0, 1)] + [(2, r) for r in range(nt)]
    encoder += [(3, every)]
    pred_cols = players_ref.shape[3]
    pred_width = (mat, pred_cols - mat)
    players = [(j, r) for r in reversed(range(nt)) for j in (0, 1)]
    enc_width = (mat, mat, mat, 2 * pix)
    enc_at = (0, mat, 2 * mat, 3 * mat)

    def weight(t, i):
        slot = lax.rem(t, 2)
        source = (up_hbm, down_hbm, attn_hbm)[i].at[t, :, pl.ds(0, mat)]
        target = (up_w, down_w, attn_w)[i].at[slot]
        return pltpu.make_async_copy(source, target, weight_sem.at[i, slot])

    def back_copy():
        return remote(back_in, back_ref, back_send, back_recv, (d, flip(z, 1)))

    def groups_of(r):
        return range(nt) if r is every else [r]

    def number(r):
        return 0 if r is every else r

    class Sums:
        def __init__(self, kind, items, width, incoming, at):
            self.kind, self.items, self.width = kind, items, width
            self.incoming, self.at = incoming, at

        def cut(self, j):
            return pl.ds(0, self.width[j])

        def to_core(self, j, r):
            if self.kind:
                source = players_ref.at[r, pl.ds(half, half), :, pl.ds(self.at[j], self.width[j])]
            else:
                source = grads[j].at[r, pl.ds(half, half)]
            return remote(
                source, cores[j].at[r, :, :, self.cut(j)],
                core_send.at[j, number(r)], core_recv.at[j, number(r)],
                routes.partner(stages, d, z),
            )

        def load(self, j, r):
            return pltpu.make_async_copy(
                players_ref.at[r, pl.ds(0, half), :, pl.ds(self.at[j], self.width[j])],
                grads[j].at[r, pl.ds(0, half), :, self.cut(j)],
                load_sem.at[j, r],
            )

        def stage(self, j, r, s):
            size = 1 << s
            return remote(
                grads[j].at[r, pl.ds(size, size), :, self.cut(j)],
                laters[j].at[r, pl.ds(size - 1, size), :, self.cut(j)],
                stage_send.at[j, number(r), s], stage_recv.at[j, number(r), s],
                routes.partner(s, d, z),
            )

        def across(self, j, r):
            return remote(
                grads[j].at[r, 0, :, self.cut(j)],
                self.incoming.at[r, :, pl.ds(self.at[j], self.width[j])],
                z_send.at[self.kind, j, r], z_recv.at[self.kind, j, r], (d, flip(z, r)),
            )

        def begin(self, i):
            if i < len(self.items):
                j, r = self.items[i]
                if self.kind:
                    self.load(j, r).start()
                self.to_core(j, r).start()

        def add(self, i, q):
            if not 0 <= i < len(self.items):
                return
            j, r = self.items[i]
            width = self.width[j]
            s = stages - q
            if q == 0:
                if self.kind:
                    self.load(j, r).wait()
                self.to_core(j, r).wait_recv()
            else:
                self.stage(j, r, s).wait_recv()

            @pl.loop(0, 1 << s)
            def _(k):
                for g in groups_of(r):
                    total = grads[j][g, k, :, 0:width].astype(f32)
                    if q == 0:
                        total += cores[j][g, k, :, 0:width].astype(f32)
                    else:
                        total += laters[j][g, k + ((1 << s) - 1), :, 0:width].astype(f32)
                    grads[j][g, k, :, 0:width] = total.astype(bf16)

            if q < stages:
                self.stage(j, r, s - 1).start()
            else:
                for g in groups_of(r):
                    if g:
                        self.across(j, g).start()

        def tick(self, n):
            for q in reversed(range(stages + 1)):
                self.add(n - ahead * (q + 1), q)

        def finish(self):
            for j, r in self.items:
                self.to_core(j, r).wait_send()
                for s in range(stages):
                    self.stage(j, r, s).wait_send()
                for g in groups_of(r):
                    if g:
                        self.across(j, g).wait_send()

        def collect(self, j, put):
            columns = slice(self.at[j], self.at[j] + self.width[j])

            @pl.when(role == self.kind)
            def _():
                total = grads[j][0, 0, :, 0 : self.width[j]].astype(f32)
                for r in range(2, nt, 2):
                    self.across(j, r).wait_recv()
                    total += self.incoming[r, :, columns].astype(f32)
                put(total)

            @pl.when(role != self.kind)
            def _():
                total = jnp.zeros((rows, self.width[j]), f32)
                for r in range(1, nt, 2):
                    self.across(j, r).wait_recv()
                    total += self.incoming[r, :, columns].astype(f32)
                put(total)

    enc = Sums(0, encoder, enc_width, enc_in, enc_at)
    play = Sums(1, players, pred_width, pred_in, (0, mat))

    def store(ref, t, first, value):
        ref[t, :, :, first : first + value.shape[1]] = value.astype(bf16).reshape(
            nd, rows, value.shape[1]
        )

    def begin_feed():
        back_copy().wait_recv()
        grad, gain_g, shift_g = norm_backward(back_ref[...].astype(f32), out_ref[...], vec_ref[4:5])
        d_ref[...] = grad
        low_ref[...] = grad.astype(bf16)
        acc_ref[...] = jnp.zeros_like(acc_ref)
        vec_grad_ref[4:5] = gain_g
        vec_grad_ref[5:6] = shift_g

    def feed(t):
        slot = lax.rem(t, 2)
        weight(t, 0).wait()
        weight(t, 1).wait()
        active, slope = gelu_parts(hidden_ref[t])
        active = active.astype(bf16)
        grad_hidden = sum(
            nn(low_ref[:, r * edge : (r + 1) * edge], down_w[slot, :, r * wide : (r + 1) * wide])
            for r in range(2)
        )
        grad_hidden = (grad_hidden * slope).astype(bf16)
        for r in range(2):
            mine = slice(r * edge, (r + 1) * edge)
            store(g0, t, r * wide, tn(low_ref[:, mine], active))
            store(g1, t, r * wide, tn(normed2_ref[:, mine], grad_hidden))
            acc_ref[:, mine] += nt_(grad_hidden, up_w[slot, :, r * wide : (r + 1) * wide])

        @pl.when(t + 2 < nt)
        def _():
            weight(t + 2, 0).start()
            weight(t + 2, 1).start()

    def end_feed():
        grad, gain_g, shift_g = norm_backward(acc_ref[...], mid_ref[...], vec_ref[2:3])
        vec_grad_ref[2:3] = gain_g
        vec_grad_ref[3:4] = shift_g
        grad = d_ref[...] + grad
        d_ref[...] = grad
        low_ref[...] = grad.astype(bf16)
        acc_ref[...] = jnp.zeros_like(acc_ref)

    def attention(t):
        slot = lax.rem(t, 2)
        weight(t, 2).wait()
        grad_att = sum(
            nn(
                low_ref[:, r * edge : (r + 1) * edge],
                attn_w[slot, :, r * wide + 3 * columns : (r + 1) * wide],
            )
            for r in range(2)
        ).astype(bf16)
        allowed = same_image(role, unit, context)
        grad_rows = attend_back(qkv_ref[t], grad_att, head_size, unit, allowed)
        for r in range(2):
            mine = slice(r * edge, (r + 1) * edge)
            grad_w = jnp.concatenate(
                [tn(normed_ref[:, mine], grad_rows), tn(low_ref[:, mine], att_ref[t])], 1
            )
            store(g2, t, r * wide, grad_w)
            acc_ref[:, mine] += nt_(grad_rows, attn_w[slot, :, r * wide : r * wide + 3 * columns])

        @pl.when(t + 2 < nt)
        def _():
            weight(t + 2, 2).start()

    def end_attention():
        grad, gain_g, shift_g = norm_backward(acc_ref[...], resid_ref[...], vec_ref[0:1])
        grad = d_ref[...] + grad
        vec_grad_ref[0:1] = gain_g
        vec_grad_ref[1:2] = shift_g
        vec_grad_ref[6:7] = jnp.sum(grad, 0, keepdims=True)
        low_ref[...] = nn(grad.astype(bf16), order_ref[...]).astype(bf16)

        @pl.loop(0, nt)
        def _(t):
            for m in range(2):
                store(g3, t, m * pix, tn(low_ref[:, m * edge : (m + 1) * edge], rows_ref[t]))

    bits = [("d", 1)] + [("d", b) for b in routes.low_bits]
    bits += [("z", 1 << s) for s in range(nt.bit_length() - 1)]

    def vec_copy(s):
        axis, bit = bits[s]
        peer = (flip(d, bit), z) if axis == "d" else (d, flip(z, bit))
        return remote(
            vec_send.at[s], vec_recv.at[s], vec_send_sem.at[s], vec_recv_sem.at[s], peer
        )

    def vec_pack():
        @pl.when(role == 0)
        def _():
            whole_rows = exactly(nt_, vec_grad_ref[...], hot_ref[...])
            vec_send[0, 0:8] = whole_rows[:, :edge]
            vec_send[0, 8:16] = whole_rows[:, edge:]
            vec_send[0, 16:32] = jnp.zeros((16, edge), f32)

        @pl.when(role == 1)
        def _():
            vec_send[0, 0:16] = jnp.zeros((16, edge), f32)
            vec_send[0, 16:32] = exactly(nt_, pred_vec_ref[...], hot_p_ref[...])
            vec_send[0, 28:29] = jnp.broadcast_to(loss_ref[0:1, 0:1], (1, edge))

        vec_copy(0).start()

    def vec_step(s):
        vec_copy(s).wait_recv()
        total = vec_send[s] + vec_recv[s]
        if s + 1 < len(bits):
            vec_send[s + 1] = total
            vec_copy(s + 1).start()
        else:
            vec_out[...] = total

    ticks = len(encoder) + ahead * (stages + 1)
    first_attention = 2 * nt
    last_attention = 3 * nt

    @pl.when(role == 0)
    def _():
        vec_grad_ref[...] = jnp.zeros_like(vec_grad_ref)
        for t in range(2):
            for i in range(3):
                weight(t, i).start()

    greet(routes, d, z, everyone=True)

    @pl.when(role == 1)
    def _():
        back_copy().start()

    @pl.loop(0, ticks)
    def _(n):
        @pl.when(role == 0)
        def _():
            pl.when(n == 0)(begin_feed)

            @pl.when((n < first_attention) & (lax.rem(n, 2) == 0))
            def _():
                feed(lax.div(n, 2))

            pl.when(n == first_attention)(end_feed)

            @pl.when((n >= first_attention) & (n < last_attention))
            def _():
                attention(n - first_attention)

            pl.when(n == last_attention)(end_attention)

        for k in range(ticks):

            @pl.when(n == k)
            def _(k=k):
                if k == last_attention:
                    vec_pack()
                if k > last_attention and k - last_attention - 1 < len(bits):
                    vec_step(k - last_attention - 1)

                @pl.when(role == 0)
                def _():
                    enc.begin(k)
                    enc.tick(k)

                @pl.when(role == 1)
                def _():
                    play.begin(k)
                    play.tick(k)

    for s in range(max(0, ticks - last_attention - 1), len(bits)):
        vec_step(s)

    def put_block(first):
        def put(total):
            low = total.astype(bf16)
            for i in range(low.shape[1] // edge):
                block_ref[first + i] = low[:, i * edge : (i + 1) * edge]

        return put

    def put_embed(total):
        emb_ref[...] = total

    per_mat = mat // edge
    for j in range(2):
        play.collect(j, put_block((3 + j) * per_mat))
    for j, first in ((0, 2 * per_mat), (1, per_mat), (2, 0)):
        enc.collect(j, put_block(first))
    block_ref[block_ref.shape[0] - 1] = jnp.zeros(block_ref.shape[1:], bf16)
    slots = slots_ref.shape[1]

    def slot_copy(j):
        peer = routes.later(d, j)
        return remote(
            slots_ref.at[peer], low_out.at[:, d], slot_send.at[j], slot_recv.at[j], (peer, z)
        )

    def own_slots():
        return pltpu.make_async_copy(slots_ref.at[d], low_out.at[:, d], slot_sem)

    for s in range(nd * slots):
        slots_ref[s // slots, s % slots] = block_ref[slot_of_ref[s]]
    for j in range(1, nd):
        slot_copy(j).start()
    own_slots().start()
    enc.collect(3, put_embed)

    @pl.when(role == 0)
    def _():
        enc.finish()

    @pl.when(role == 1)
    def _():
        play.finish()
        back_copy().wait_send()

    for s in range(len(bits)):
        vec_copy(s).wait_send()
    own_slots().wait()
    for j in range(1, nd):
        slot_copy(j).wait()


def whole(shape):
    return pl.BlockSpec(shape, lambda *_: (0,) * len(shape))


def by_group(shape):
    return pl.BlockSpec((1,) + shape, lambda t: (t, 0, 0))


def compiled():
    return pltpu.CompilerParams(
        dimension_semantics=("arbitrary",), vmem_limit_bytes=KERNEL_BYTES
    )


def cost(flops, moved):
    return pl.CostEstimate(flops=int(flops), bytes_accessed=int(moved), transcendentals=0)


def sincos(cell_index, columns):
    quarter = columns // 4
    frequency = 1.0 / 10000.0 ** (jnp.arange(quarter).astype(f32) / quarter)
    col_angle = (cell_index % SIDE).astype(f32)[..., None] * frequency
    row_angle = (cell_index // SIDE).astype(f32)[..., None] * frequency
    return jnp.concatenate(
        [jnp.sin(col_angle), jnp.cos(col_angle), jnp.sin(row_angle), jnp.cos(row_angle)], -1
    )


def adamw(master, moment, second, gradient, step_rate, weight_decay):
    moment = 0.9 * moment + 0.1 * gradient
    second = 0.999 * second + 0.001 * gradient * gradient
    unbiased_first = moment / (1.0 - 0.9**STEP)
    unbiased_second = second / (1.0 - 0.999**STEP)
    return (
        master
        - step_rate
        * (unbiased_first / (jnp.sqrt(unbiased_second) + 1e-08) + weight_decay * master),
        moment,
        second,
    )


class Routes:
    def __init__(self, nd, nt):
        self.nd, self.nt = nd, nt
        self.low_bits = [1 << s for s in range(1, nd.bit_length() - 1)]
        self.stages = len(self.low_bits)

    def order(self, core):
        return self.low_bits if core == 0 else self.low_bits[::-1]

    def pairs(self, target, keep):
        found = []
        for d in range(self.nd):
            for z in range(self.nt):
                if keep(d, z):
                    d2, z2 = target(d, z)
                    found.append((d * self.nt + z, d2 * self.nt + z2))
        return found

    def later(self, d, j):
        return lax.rem(d + j, self.nd)

    def holder(self, k, d):
        held = flip(d, k >> self.stages)
        core = lax.rem(held, 2)
        for s in range(self.stages):
            if (k >> s) & 1:
                ends = flip(held, self.order(0)[s]), flip(held, self.order(1)[s])
                held = ends[0] + core * (ends[1] - ends[0])
        return held

    def partner(self, number, d, z):
        if number == self.stages:
            return flip(d, 1), z
        core = lax.rem(d, 2)
        ends = flip(d, self.order(0)[number]), flip(d, self.order(1)[number])
        return ends[0] + core * (ends[1] - ends[0]), z

    def across(self, r, values, from_role=None):
        def keep(d, z):
            return from_role is None or z % 2 == from_role

        return lax.ppermute(values, AXES, self.pairs(lambda d, z: (d, z ^ r), keep))

    def holders(self, d):
        place = jnp.arange(self.nd, dtype=jnp.int32)
        held = d ^ (place >> self.stages)
        core = held & 1
        for s in range(self.stages):
            bit = (place >> s) & 1
            held = held ^ (bit * jnp.where(core == 0, self.order(0)[s], self.order(1)[s]))
        return held

    def total(self, values):
        for bit in [1] + self.low_bits:
            values = values + lax.ppermute(
                values, AXES, self.pairs(lambda d, z, b=bit: (d ^ b, z), lambda d, z: True)
            )
        r = 1
        while r < self.nt:
            values = values + self.across(r, values)
            r *= 2
        return values


def shards(
    patches,
    ctx_idx,
    tgt_idx,
    owner,
    weights,
    stats_left,
    stats_right,
    root_left,
    root_right,
    teacher_slot_blocks,
    embed,
    embed_m,
    embed_v,
    teacher_embed,
    enc_vectors,
    enc_m,
    enc_v,
    pred_vectors,
    pred_m,
    pred_v,
    teacher_vectors,
):
    nt = lax.axis_size("tensor")
    nd = lax.axis_size("dp")
    routes = Routes(nd, nt)
    half = nt // 2
    d = lax.axis_index("dp")
    z = lax.axis_index("tensor")
    role = z % 2
    student_role = role == 0
    images, npatches, pix_part = patches.shape
    slots = weights.shape[1]
    edge = weights.shape[-1]
    slot_count = slots * nd
    block_count = owner.shape[0]
    width = enc_vectors.shape[1]
    narrow = pred_vectors.shape[1]
    players = (pred_vectors.shape[0] - 3) // 4
    side = width // edge
    teach_count = 3 * side * side
    quarter = width // nt
    context_len = ctx_idx.shape[1]
    target_len = tgt_idx.shape[1]
    seq_len = context_len + target_len
    share = images // half
    rows_part = edge // nd

    both = jnp.stack([weights[0], teacher_slot_blocks[0]]).astype(bf16)
    both = both.reshape(2, slots, nd, rows_part, edge)
    both = lax.all_to_all(both, "dp", split_axis=2, concat_axis=0, tiled=False)
    by_slot = both.transpose(1, 0, 2, 3, 4).reshape(2, slot_count, rows_part, edge)
    mine = by_slot[0][owner].transpose(1, 0, 2).reshape(rows_part, -1)
    teach = by_slot[1][owner[:teach_count]].transpose(1, 0, 2).reshape(rows_part, -1)

    mat = side * width

    def embed_rows(values):
        turned = values.astype(bf16).T.reshape(side, rows_part, pix_part)
        return turned.transpose(1, 0, 2).reshape(rows_part, -1)

    of_student = jnp.concatenate(
        [mine[:, :mat], embed_rows(embed), mine[:, mat : 3 * mat]], 1
    )
    of_teacher = jnp.concatenate([teach[:, :mat], embed_rows(teacher_embed), teach[:, mat:]], 1)
    own = jnp.where(student_role, of_student, of_teacher)
    other = jnp.where(student_role, of_teacher, of_student)
    maps = 3 * mat + 3 * players * edge
    pred_own = jnp.concatenate([mine[:, maps:], mine[:, 3 * mat : maps]], 1)

    holder = routes.holders(d)
    inside = jnp.arange(rows_part, dtype=jnp.int32)
    feat_p = (holder[:, None] * rows_part + inside[None, :]).reshape(-1)
    feat = jnp.concatenate([r * edge + feat_p for r in range(side)])
    one_hot = (feat[:, None] == jnp.arange(width)[None, :]).astype(f32)
    one_hot_p = (feat_p[:, None] == jnp.arange(narrow)[None, :]).astype(f32)

    def to_local(rows, hot):
        return jnp.einsum("nf,lf->nl", rows, hot, precision=exact, preferred_element_type=f32)

    def to_global(rows, hot):
        return jnp.einsum("nl,lf->nf", rows, hot, precision=exact, preferred_element_type=f32)

    vec = to_local(jnp.where(student_role, enc_vectors, teacher_vectors), one_hot)
    vec = jnp.pad(vec, ((0, 1), (0, 0)))
    pvec = to_local(pred_vectors, one_hot_p)
    pvec = jnp.pad(pvec, ((0, 16 - pvec.shape[0]), (0, 0)))
    pred_z = z - role + 1
    group_feat = (pred_z ^ jnp.arange(nt, dtype=jnp.int32))[:, None] * quarter + jnp.arange(
        quarter, dtype=jnp.int32
    )
    emb_feat = jnp.concatenate(
        [holder[:, None] * 2 * rows_part + m * rows_part + inside[None, :] for m in range(2)]
    ).reshape(-1)
    order = (feat[:, None] == emb_feat[None, :]).astype(bf16)
    swap = (feat[None, :, None] == group_feat[:, None, :]).astype(bf16)

    part = z // 2
    hot = (ctx_idx[:, :, None] == jnp.arange(npatches)[None, None, :]).astype(bf16)
    picked = jnp.einsum("gcn,gnp->gcp", hot, patches, preferred_element_type=f32).astype(bf16)

    def rows_for(target_z):
        where = (target_z // 2) * share
        ctx = lax.dynamic_slice_in_dim(picked, where, share, 0).reshape(-1, pix_part)
        every = lax.dynamic_slice_in_dim(patches, where, share, 0).reshape(-1, pix_part)
        padded = jnp.pad(ctx, ((0, every.shape[0] - ctx.shape[0]), (0, 0)))
        return jnp.where(target_z % 2 == 0, padded, every)

    patch_out = jnp.stack([rows_for(z ^ r) for r in range(nt)])
    my_ctx = lax.dynamic_slice_in_dim(ctx_idx, part * share, share, 0)
    my_tgt = lax.dynamic_slice_in_dim(tgt_idx, part * share, share, 0)
    full_rows = share * npatches
    ctx_rows = share * context_len
    tgt_rows = share * target_len
    ctx_places = jnp.pad(my_ctx.reshape(-1), (0, full_rows - ctx_rows))
    places = jnp.where(student_role, ctx_places, jnp.arange(full_rows) % npatches)
    table = to_local(sincos(jnp.arange(npatches), width), one_hot)
    table_p = to_local(sincos(jnp.arange(npatches), narrow), one_hot_p)
    base = table[places] + vec[6]
    tgt_places = (my_tgt + npatches * jnp.arange(share, dtype=jnp.int32)[:, None]).reshape(-1)
    pick = (tgt_places[:, None] == jnp.arange(full_rows)[None, :]).astype(bf16)
    widths = [mat + side * pix_part, mat, mat, 4 * edge, 3 * (players - 1) * edge]
    any_space = pl.BlockSpec(memory_space=pl.ANY)
    dma = pltpu.SemaphoreType.DMA
    attn_cols = side * width
    columns = width // nt
    mat_shapes = [jax.ShapeDtypeStruct((nt, nd, rows_part, c), bf16) for c in widths]
    gather_sems = [
        dma((5, nt)),
        dma((5, nt)),
        dma((6,)),
        dma((nt,)),
        dma((nt,)),
        dma((5, nt, routes.stages + 1)),
        dma((5, nt, routes.stages + 1)),
    ]
    in_vmem = pl.BlockSpec(memory_space=VMEM)
    role_word = role.astype(jnp.int32).reshape(1)
    if rows_part % 16 == 0:
        results = pl.pallas_call(
            functools.partial(forward_kernel, routes, widths, npatches, context_len, HD),
            in_specs=[pl.BlockSpec(memory_space=pltpu.SMEM)] + [in_vmem] * 12,
            out_specs=[any_space] * 5 + [in_vmem] * 17,
            out_shape=mat_shapes
            + [
                jax.ShapeDtypeStruct((nt, ctx_rows, pix_part), bf16),
                jax.ShapeDtypeStruct((ctx_rows, width), f32),
                jax.ShapeDtypeStruct((ctx_rows, width), f32),
                jax.ShapeDtypeStruct((ctx_rows, width), bf16),
                jax.ShapeDtypeStruct((nt, ctx_rows, 3 * columns), bf16),
                jax.ShapeDtypeStruct((nt, ctx_rows, columns), bf16),
                jax.ShapeDtypeStruct((ctx_rows, width), f32),
                jax.ShapeDtypeStruct((ctx_rows, width), bf16),
                jax.ShapeDtypeStruct((nt, ctx_rows, width), f32),
                jax.ShapeDtypeStruct((nt, ctx_rows, quarter), bf16),
                jax.ShapeDtypeStruct((nt, tgt_rows, quarter), bf16),
                jax.ShapeDtypeStruct((width, width), bf16),
                jax.ShapeDtypeStruct((width, width), bf16),
                jax.ShapeDtypeStruct((narrow, narrow), bf16),
                jax.ShapeDtypeStruct((8, width), f32),
                jax.ShapeDtypeStruct((16, narrow), f32),
                jax.ShapeDtypeStruct((share * seq_len, narrow), f32),
            ],
            scratch_shapes=[VMEM(shape.shape, bf16) for shape in mat_shapes]
            + [
                VMEM((nt, full_rows, pix_part), bf16),
                VMEM((full_rows, width), f32),
                VMEM((full_rows, width), bf16),
                VMEM((nt, ctx_rows, quarter), bf16),
                VMEM((nt, ctx_rows, quarter), bf16),
                VMEM((2, slots, nd, rows_part, edge), bf16),
                VMEM((2, slot_count, rows_part, edge), bf16),
                VMEM((rows_part, sum(widths[:3])), bf16),
                VMEM((rows_part, sum(widths[:3])), bf16),
                VMEM((rows_part, sum(widths[3:])), bf16),
                VMEM((images * context_len, pix_part), bf16),
                dma((5, nt)),
                dma(()),
                dma(()),
                dma((nd,)),
                dma((nd,)),
                dma(()),
            ]
            + gather_sems,
            compiler_params=pltpu.CompilerParams(
                collective_id=0, has_side_effects=True, vmem_limit_bytes=KERNEL_BYTES
            ),
            cost_estimate=cost(14e9, 60e6),
            name="gather_and_encode",
        )(
            owner, weights[0], teacher_slot_blocks[0], patches.reshape(-1, pix_part),
            ctx_idx, tgt_idx, embed, teacher_embed, enc_vectors, teacher_vectors, pred_vectors,
            jnp.asarray(sincos_table(width)), jnp.asarray(sincos_table(narrow)),
        )
        gathered, results = results[:5], results[5:]
        patch_rows, middle, resid, normed_a, rows_a, att_a = results[:6]
        output, normed_f, hidden, feat_in, target = results[6:11]
        hot, order, hot_p, vec, pvec, tokens_at = results[11:]
        attn_emb, up_w, down_t, pred_first, pred_second = (
            g.reshape(nt, edge, -1) for g in gathered
        )
    else:
        attn_emb, up_w, down_t, pred_first, pred_second, patch_rows = pl.pallas_call(
            functools.partial(gather_kernel, routes, widths, ctx_rows),
            in_specs=[any_space] * 4,
            out_specs=[any_space] * 6,
            out_shape=mat_shapes
            + [jax.ShapeDtypeStruct((nt, full_rows, pix_part), bf16)],
            scratch_shapes=gather_sems,
            compiler_params=pltpu.CompilerParams(collective_id=0, has_side_effects=True),
            cost_estimate=cost(0, 50e6),
            name="gather_weights",
        )(own, other, pred_own, patch_out)
        attn_emb, up_w, down_t, pred_first, pred_second = (
            value.reshape(nt, edge, -1)
            for value in (attn_emb, up_w, down_t, pred_first, pred_second)
        )
        middle, resid, normed_a, rows_a, att_a = pl.pallas_call(
            functools.partial(encoder_attend_kernel, edge, npatches, context_len, HD, ctx_rows),
            grid=(2 * nt,),
            in_specs=[
                pl.BlockSpec(memory_space=pltpu.SMEM),
                pl.BlockSpec((1, full_rows, pix_part), lambda i: (jnp.minimum(i, nt - 1), 0, 0)),
                whole((full_rows, width)),
                pl.BlockSpec(
                    (1, edge, side * pix_part),
                    lambda i: (jnp.minimum(i, nt - 1), 0, attn_cols // (side * pix_part)),
                ),
                whole((width, width)),
                pl.BlockSpec((1, edge, attn_cols), lambda i: (jnp.maximum(i - nt, 0), 0, 0)),
                whole((8, width)),
            ],
            out_specs=[
                whole((full_rows, width)),
                whole((ctx_rows, width)),
                whole((ctx_rows, width)),
                pl.BlockSpec((1, ctx_rows, 3 * columns), lambda i: (jnp.maximum(i - nt, 0), 0, 0)),
                pl.BlockSpec((1, ctx_rows, columns), lambda i: (jnp.maximum(i - nt, 0), 0, 0)),
            ],
            out_shape=[
                jax.ShapeDtypeStruct((full_rows, width), f32),
                jax.ShapeDtypeStruct((ctx_rows, width), f32),
                jax.ShapeDtypeStruct((ctx_rows, width), bf16),
                jax.ShapeDtypeStruct((nt, ctx_rows, 3 * columns), bf16),
                jax.ShapeDtypeStruct((nt, ctx_rows, columns), bf16),
            ],
            scratch_shapes=[VMEM((full_rows, width), f32), VMEM((full_rows, width), bf16)],
            compiler_params=compiled(),
            cost_estimate=cost(6e9, 12e6),
            name="encoder_attend",
        )(role_word, patch_rows, base, attn_emb, order, attn_emb, vec)
        output, normed_f, hidden, enc_feat, target = pl.pallas_call(
            functools.partial(encoder_feed_kernel, edge, ctx_rows),
            grid=(nt,),
            in_specs=[
                whole((full_rows, width)),
                by_group((edge, mat)),
                by_group((edge, mat)),
                whole((8, width)),
                whole((tgt_rows, full_rows)),
                whole((nt, width, quarter)),
            ],
            out_specs=[
                whole((ctx_rows, width)),
                whole((ctx_rows, width)),
                by_group((ctx_rows, width)),
                whole((nt, ctx_rows, quarter)),
                whole((nt, tgt_rows, quarter)),
            ],
            out_shape=[
                jax.ShapeDtypeStruct((ctx_rows, width), f32),
                jax.ShapeDtypeStruct((ctx_rows, width), bf16),
                jax.ShapeDtypeStruct((nt, ctx_rows, width), f32),
                jax.ShapeDtypeStruct((nt, ctx_rows, quarter), bf16),
                jax.ShapeDtypeStruct((nt, tgt_rows, quarter), bf16),
            ],
            scratch_shapes=[VMEM((full_rows, width), f32), VMEM((full_rows, width), bf16)],
            compiler_params=compiled(),
            cost_estimate=cost(8e9, 14e6),
            name="encoder_feed",
        )(middle, up_w, down_t, vec, pick, swap)

        feat_in = routes.across(1, enc_feat, from_role=0)
        tokens_at = table_p[jnp.concatenate([my_ctx, my_tgt], 1)]
        mask_rows = jnp.arange(seq_len)[None, :, None] >= context_len
        tokens_at = jnp.where(mask_rows, tokens_at + pvec[4 * players + 2], tokens_at)
        tokens_at = tokens_at.reshape(-1, narrow)
        hot = one_hot.T.astype(bf16)

    token_rows = share * seq_len
    pred_cols = (3 * players + 1) * edge
    denominator = images * nd * target_len * width
    pred_columns = narrow // nt
    pred_grads, pred_vec_g, loss_tile, back = pl.pallas_call(
        functools.partial(predictor_kernel, share, context_len, players, PHD, denominator),
        in_specs=[in_vmem] * 3 + [any_space] * 2 + [in_vmem] * 2,
        out_specs=[any_space] + [in_vmem] * 3,
        out_shape=[
            jax.ShapeDtypeStruct((nt, edge, pred_cols), bf16),
            jax.ShapeDtypeStruct((16, narrow), f32),
            jax.ShapeDtypeStruct((8, 128), f32),
            jax.ShapeDtypeStruct((ctx_rows, width), bf16),
        ],
        scratch_shapes=[
            VMEM((nt, edge, pred_cols), bf16),
            VMEM((nt, edge, pred_cols), bf16),
            dma((3 * players + 1,)),
            dma((3 * players + 1,)),
            VMEM((players + 1, token_rows, narrow), f32),
            VMEM((players, token_rows, narrow), f32),
            VMEM((players, token_rows, narrow), bf16),
            VMEM((players, token_rows, narrow), bf16),
            VMEM((players, nt, token_rows, 3 * pred_columns), bf16),
            VMEM((players, nt, token_rows, pred_columns), bf16),
            VMEM((players, nt // 2, token_rows, 2 * edge), f32),
            VMEM((token_rows, narrow), f32),
            VMEM((token_rows, narrow), f32),
            VMEM((token_rows, narrow), bf16),
            VMEM((tgt_rows, narrow), bf16),
        ],
        compiler_params=pltpu.CompilerParams(vmem_limit_bytes=KERNEL_BYTES),
        cost_estimate=cost(16e9, 30e6),
        name="predictor",
    )(feat_in, target, tokens_at, pred_first, pred_second, pvec, hot)
    all_cols = attn_cols + side * pix_part
    middle_size = nd // 2
    block_shape = [
        jax.ShapeDtypeStruct((rows_part, (block_count + 1) * edge), bf16),
        jax.ShapeDtypeStruct((rows_part, side * pix_part), f32),
    ]
    if rows_part % 16 == 0:
        widths_g = (mat, mat, mat, side * pix_part)
        vec_steps = nd.bit_length() + nt.bit_length() - 2
        slot_numbers = jnp.arange(slot_count, dtype=jnp.int32)
        holds = (owner[None, :] == slot_numbers[:, None]).astype(jnp.int32)
        order_of = jnp.arange(block_count, dtype=jnp.int32) - block_count
        slot_of = block_count + jnp.sum(holds * order_of[None, :], 1)
        low_grads, emb_sum, vec_sum = pl.pallas_call(
            functools.partial(backward_kernel, routes, context_len, HD),
            in_specs=[pl.BlockSpec(memory_space=pltpu.SMEM)]
            + [any_space] * 5
            + [in_vmem] * 15,
            out_specs=[any_space] + [in_vmem] * 2,
            out_shape=[
                jax.ShapeDtypeStruct((slots, nd, rows_part, edge), bf16),
                block_shape[1],
            ]
            + [jax.ShapeDtypeStruct((32, edge), f32)],
            scratch_shapes=[
                VMEM((block_count + 1, rows_part, edge), bf16),
                VMEM((nd, slots, rows_part, edge), bf16),
            ]
            + [VMEM((nt, nd, rows_part, c), bf16) for c in widths_g]
            + [VMEM((nt, middle_size, rows_part, c), bf16) for c in widths_g]
            + [VMEM((nt, middle_size - 1, rows_part, c), bf16) for c in widths_g]
            + [
                VMEM((nt, rows_part, sum(widths_g)), bf16),
                VMEM((nt, rows_part, pred_cols), bf16),
                VMEM((2, edge, mat), bf16),
                VMEM((2, edge, mat), bf16),
                VMEM((2, edge, mat), bf16),
                VMEM((ctx_rows, width), bf16),
                VMEM((ctx_rows, width), f32),
                VMEM((ctx_rows, width), bf16),
                VMEM((ctx_rows, width), f32),
                VMEM((8, width), f32),
                VMEM((vec_steps, 32, edge), f32),
                VMEM((vec_steps, 32, edge), f32),
                dma((3, 2)),
                dma(()),
                dma(()),
                dma((4, nt)),
                dma((4, nt)),
                dma((4, nt)),
                dma((4, nt, routes.stages)),
                dma((4, nt, routes.stages)),
                dma((2, 4, nt)),
                dma((2, 4, nt)),
                dma((vec_steps,)),
                dma((vec_steps,)),
                dma((nd,)),
                dma((nd,)),
                dma(()),
            ],
            compiler_params=pltpu.CompilerParams(
                collective_id=1, has_side_effects=True, vmem_limit_bytes=KERNEL_BYTES
            ),
            cost_estimate=cost(14e9, 60e6),
            name="encode_back_and_reduce",
        )(
            slot_of, pred_grads.reshape(nt, nd, rows_part, -1), back, attn_emb, up_w, down_t,
            output, middle, resid, normed_f, normed_a, hidden, rows_a, att_a, patch_rows,
            vec, order, hot, hot_p, pred_vec_g, loss_tile,
        )
        enc_total = jnp.concatenate([vec_sum[:7], vec_sum[8:15]], 1)
        pred_total = vec_sum[16 : 16 + 4 * players + 3]
        loss_total = vec_sum[28, 0]
        low_grads = low_grads.reshape(slots, edge, edge)
    else:
        back = routes.across(1, back, from_role=1)

        grad_shape = jax.ShapeDtypeStruct((nt, edge, mat), bf16)
        up_g, down_g, grad_mid, vec_g1 = pl.pallas_call(
            functools.partial(encoder_feed_back_kernel, edge),
            grid=(nt,),
            in_specs=[
                whole((ctx_rows, width)),
                whole((ctx_rows, width)),
                whole((ctx_rows, width)),
                whole((ctx_rows, width)),
                by_group((ctx_rows, width)),
                by_group((edge, mat)),
                by_group((edge, mat)),
                whole((8, width)),
            ],
            out_specs=[by_group((edge, mat))] * 2 + [whole((ctx_rows, width)), whole((8, width))],
            out_shape=[grad_shape] * 2
            + [
                jax.ShapeDtypeStruct((ctx_rows, width), f32),
                jax.ShapeDtypeStruct((8, width), f32),
            ],
            scratch_shapes=[
                VMEM((ctx_rows, width), f32),
                VMEM((ctx_rows, width), bf16),
                VMEM((ctx_rows, width), f32),
            ],
            compiler_params=compiled(),
            cost_estimate=cost(8e9, 25e6),
            name="encoder_feed_back",
        )(back, output, middle, normed_f, hidden, up_w, down_t, vec)
        attn_g, vec_g2 = pl.pallas_call(
            functools.partial(encoder_attend_back_kernel, edge, npatches, context_len, HD),
            grid=(2 * nt,),
            in_specs=[
                pl.BlockSpec(memory_space=pltpu.SMEM),
                whole((ctx_rows, width)),
                whole((ctx_rows, width)),
                whole((ctx_rows, width)),
                pl.BlockSpec((1, ctx_rows, 3 * columns), lambda i: (jnp.minimum(i, nt - 1), 0, 0)),
                pl.BlockSpec((1, ctx_rows, columns), lambda i: (jnp.minimum(i, nt - 1), 0, 0)),
                pl.BlockSpec((1, edge, attn_cols), lambda i: (jnp.minimum(i, nt - 1), 0, 0)),
                pl.BlockSpec((1, ctx_rows, pix_part), lambda i: (jnp.maximum(i - nt, 0), 0, 0)),
                whole((width, width)),
                whole((8, width)),
            ],
            out_specs=[
                whole((nt, edge, all_cols)),
                whole((8, width)),
            ],
            out_shape=[
                jax.ShapeDtypeStruct((nt, edge, all_cols), bf16),
                jax.ShapeDtypeStruct((8, width), f32),
            ],
            scratch_shapes=[VMEM((ctx_rows, width), bf16), VMEM((ctx_rows, width), f32)],
            compiler_params=compiled(),
            cost_estimate=cost(6e9, 20e6),
            name="encoder_attend_back",
        )(role_word, grad_mid, resid, normed_a, rows_a, att_a, attn_emb, patch_rows, order, vec)

        places = [g.reshape(nt, nd, rows_part, -1) for g in (down_g, up_g, attn_g, pred_grads)]
        by_block, emb_sum = pl.pallas_call(
            functools.partial(reduce_kernel, routes, attn_cols),
            in_specs=[any_space] * 4,
            out_specs=[in_vmem] * 2,
            out_shape=block_shape,
            scratch_shapes=[
                VMEM((nt, middle_size, rows_part, mat), bf16),
                VMEM((nt, middle_size, rows_part, mat), bf16),
                VMEM((nt, middle_size, rows_part, all_cols), bf16),
                VMEM((nt, middle_size - 1, rows_part, mat), bf16),
                VMEM((nt, middle_size - 1, rows_part, mat), bf16),
                VMEM((nt, middle_size - 1, rows_part, all_cols), bf16),
                VMEM((nt, rows_part, 2 * mat + all_cols), bf16),
                VMEM((nt, rows_part, pred_cols), bf16),
                VMEM((2, middle_size, rows_part, all_cols), bf16),
                dma((2,)),
                dma((3, nt)),
                dma((3, nt)),
                dma((3, nt, routes.stages)),
                dma((3, nt, routes.stages)),
                dma((2, 3, nt)),
                dma((2, 3, nt)),
            ],
            compiler_params=pltpu.CompilerParams(
                collective_id=1, has_side_effects=True, vmem_limit_bytes=KERNEL_BYTES
            ),
            cost_estimate=cost(0, 60e6),
            name="reduce_gradients",
        )(*places)

        enc_rows = to_global(vec_g1[:7] + vec_g2[:7], one_hot)
        pred_rows = to_global(pred_vec_g[: 4 * players + 3], one_hot_p)
        enc_rows = jnp.where(student_role, enc_rows, 0.0)
        pred_rows = jnp.where(role == 1, pred_rows, 0.0)
        loss_row = jnp.where(role == 1, loss_tile[0, 0], 0.0)
        packed = jnp.concatenate([enc_rows.reshape(-1), pred_rows.reshape(-1), loss_row[None]])
        packed = jnp.pad(packed, (0, -packed.shape[0] % 1024)).reshape(-1, 128)
        packed = routes.total(packed).reshape(-1)
        enc_total = packed[: enc_rows.size].reshape(enc_rows.shape)
        pred_total = packed[enc_rows.size : enc_rows.size + pred_rows.size].reshape(pred_rows.shape)
        loss_total = packed[enc_rows.size + pred_rows.size]
        by_block = by_block.reshape(rows_part, block_count + 1, edge).transpose(1, 0, 2)
        slot_of = (
            jnp.full((slot_count,), block_count, jnp.int32)
            .at[owner]
            .set(jnp.arange(block_count, dtype=jnp.int32))
        )
        slot_rows = by_block[slot_of].reshape(nd, slots, rows_part, edge)
        slot_rows = lax.all_to_all(slot_rows, "dp", split_axis=0, concat_axis=1, tiled=False)
        low_grads = slot_rows.reshape(slots, edge, edge)

    embed_grad = emb_sum.reshape(rows_part, side, pix_part).transpose(1, 0, 2)
    embed_grad = embed_grad.reshape(-1, pix_part).T

    slot_spec = pl.BlockSpec((1, 1, edge, edge), lambda s: (0, s, 0, 0))
    slot_shape = jax.ShapeDtypeStruct(weights.shape, f32)
    slot_grads, new_weights, new_left, new_right, new_teacher_blocks = pl.pallas_call(
        shampoo_kernel,
        grid=(slots,),
        in_specs=[pl.BlockSpec((1, edge, edge), lambda s: (s, 0, 0))] + [slot_spec] * 6,
        out_specs=[slot_spec] * 5,
        out_shape=[slot_shape] * 5,
        compiler_params=compiled(),
        cost_estimate=cost(3e9, 22e6),
        name="shampoo",
    )(low_grads, weights, stats_left, stats_right, root_left, root_right, teacher_slot_blocks)
    new_embed, new_embed_m, new_embed_v = adamw(embed, embed_m, embed_v, embed_grad, 0.05, 0.05)
    new_enc, new_enc_m, new_enc_v = adamw(enc_vectors, enc_m, enc_v, enc_total, 0.5, 0.0)
    new_pred, new_pred_m, new_pred_v = adamw(pred_vectors, pred_m, pred_v, pred_total, 0.5, 0.0)
    new_teacher_embed = 0.7 * teacher_embed + 0.3 * new_embed
    new_teacher_vectors = 0.7 * teacher_vectors + 0.3 * new_enc
    return (
        loss_total,
        slot_grads,
        new_weights,
        new_left,
        new_right,
        new_teacher_blocks,
        new_embed,
        new_embed_m,
        new_embed_v,
        new_teacher_embed,
        new_enc,
        new_enc_m,
        new_enc_v,
        new_pred,
        new_pred_m,
        new_pred_v,
        new_teacher_vectors,
    )


def solution(mesh):
    blocks = P("tensor", "dp", None, None)
    table = P("tensor", "dp")
    in_specs = (
        (P("dp", None, "tensor"), P("dp", None), P("dp", None), P())
        + (blocks,) * 6
        + (table,) * 4
        + (P(),) * 7
    )
    out_specs = (P(),) + (blocks,) * 5 + (table,) * 4 + (P(),) * 7
    return jax.shard_map(shards, mesh=mesh, in_specs=in_specs, out_specs=out_specs, check_vma=False)
```

```python
import functools
import math

import jax
import jax.numpy as jnp
import numpy as np
from jax import lax
from jax.experimental import pallas as pl
from jax.experimental.pallas import tpu as pltpu
from jax.sharding import PartitionSpec as P

HD = 64
PHD = 32
SIDE = 16
STEP = 10
KERNEL_BYTES = 60 * 1024 * 1024

AXES = ("dp", "tensor")
exact = lax.Precision.HIGHEST
f32 = jnp.float32
bf16 = jnp.bfloat16
VMEM = pltpu.VMEM


def nn(first, second):
    return lax.dot_general(first, second, (((1,), (0,)), ((), ())), preferred_element_type=f32)


def nt_(first, second):
    return lax.dot_general(first, second, (((1,), (1,)), ((), ())), preferred_element_type=f32)


def tn(first, second):
    return lax.dot_general(first, second, (((0,), (0,)), ((), ())), preferred_element_type=f32)


def norm_parts(values):
    centre = values - jnp.mean(values, -1, keepdims=True)
    scale = lax.rsqrt(jnp.mean(centre * centre, -1, keepdims=True) + 1e-06)
    return centre * scale, scale


def layer_norm(values, gain_row, shift_row):
    return norm_parts(values)[0] * gain_row + shift_row


def norm_backward(grad, values, gain_row):
    unit, scale = norm_parts(values)
    weighted = grad * gain_row
    inner = (
        weighted
        - jnp.mean(weighted, -1, keepdims=True)
        - unit * jnp.mean(weighted * unit, -1, keepdims=True)
    )
    return (
        inner * scale,
        jnp.sum(grad * unit, 0, keepdims=True),
        jnp.sum(grad, 0, keepdims=True),
    )


def gelu_parts(values):
    below = 0.5 * (1.0 + lax.erf(values * math.sqrt(0.5)))
    density = jnp.exp(-0.5 * values * values) * (1.0 / math.sqrt(2.0 * math.pi))
    return values * below, below + values * density


def softened_t(queries, keys, head_size, allowed):
    scores = nt_(keys, queries) * (1.0 / math.sqrt(head_size))
    if allowed is not None:
        scores = jnp.where(allowed, scores, -1e30)
    expo = jnp.exp(scores - jnp.max(scores, 0, keepdims=True))
    return expo * (1.0 / jnp.sum(expo, 0, keepdims=True))


def attend(rows, head_size, length, allowed):
    columns = rows.shape[1] // 3
    images = []
    for at in range(0, rows.shape[0], length):
        outs = []
        for h in range(0, columns, head_size):
            q, k, v = (
                rows[at : at + length, j * columns + h : j * columns + h + head_size]
                for j in range(3)
            )
            soft = softened_t(q, k, head_size, allowed).astype(bf16)
            outs.append(tn(v, soft).astype(bf16))
        images.append(jnp.concatenate(outs, 0))
    joined = jnp.concatenate(images, 1) if len(images) > 1 else images[0]
    return joined.T


def attend_back(rows, grad, head_size, length, allowed):
    columns = rows.shape[1] // 3
    factor = 1.0 / math.sqrt(head_size)
    images = []
    for at in range(0, rows.shape[0], length):
        outs = [[], [], []]
        for h in range(0, columns, head_size):
            q, k, v = (
                rows[at : at + length, j * columns + h : j * columns + h + head_size]
                for j in range(3)
            )
            g = grad[at : at + length, h : h + head_size]
            soft = softened_t(q, k, head_size, allowed)
            outs[2].append(nn(soft.astype(bf16), g).astype(bf16))
            ds = nt_(v, g)
            ds = (soft * (ds - jnp.sum(ds * soft, 0, keepdims=True))).astype(bf16)
            outs[0].append((tn(k, ds) * factor).astype(bf16))
            outs[1].append((nn(ds, q) * factor).astype(bf16))
        queries = jnp.concatenate(outs[0], 0).T
        images.append(jnp.concatenate([queries] + outs[1] + outs[2], 1))
    return jnp.concatenate(images, 0) if len(images) > 1 else images[0]


def same_image(role, length, context):
    row = lax.broadcasted_iota(jnp.int32, (length, length), 0) // context
    column = lax.broadcasted_iota(jnp.int32, (length, length), 1) // context
    return (row == column) | (role != 0)


def encoder_attend_kernel(
    edge, unit, context, head_size, kept,
    role_ref, patch_ref, base_ref, emb_ref, order_ref, w_ref, vec_ref,
    mid_ref, resid_ref, normed_ref, rows_ref, att_ref, x_ref, h_ref,
):
    step = pl.program_id(0)
    groups = pl.num_programs(0) // 2
    side = 2
    wide = side * edge
    pix = patch_ref.shape[2]
    columns = wide // 4

    @pl.when(step == 0)
    def _():
        x_ref[...] = base_ref[...]

    @pl.when(step < groups)
    def _():
        ordered = sum(
            nn(order_ref[:, m * edge : (m + 1) * edge], emb_ref[0, :, m * pix : (m + 1) * pix])
            for m in range(side)
        ).astype(bf16)
        x_ref[...] += nt_(patch_ref[0], ordered)

    @pl.when(step == groups - 1)
    def _():
        values = x_ref[...]
        resid_ref[...] = values[:kept]
        low = layer_norm(values, vec_ref[0:1], vec_ref[1:2]).astype(bf16)
        h_ref[...] = low
        normed_ref[...] = low[:kept]

    @pl.when(step >= groups)
    def _():
        rows = sum(
            nn(h_ref[:, r * edge : (r + 1) * edge], w_ref[0, :, r * wide : r * wide + 3 * columns])
            for r in range(side)
        ).astype(bf16)
        rows_ref[0] = rows[:kept]
        att = attend(rows, head_size, unit, same_image(role_ref[0], unit, context))
        att_ref[0] = att[:kept]
        for r in range(side):
            x_ref[:, r * edge : (r + 1) * edge] += nt_(
                att, w_ref[0, :, r * wide + 3 * columns : (r + 1) * wide]
            )

    @pl.when(step == 2 * groups - 1)
    def _():
        mid_ref[...] = x_ref[...]


def encoder_feed_kernel(
    edge, kept, mid_ref, up_ref, down_ref, vec_ref, pick_ref, swap_ref,
    out_ref, normed_ref, hidden_ref, feat_ref, target_ref, x_ref, h_ref,
):
    step = pl.program_id(0)
    groups = pl.num_programs(0)
    side = 2
    wide = side * edge

    @pl.when(step == 0)
    def _():
        values = mid_ref[...]
        x_ref[...] = values
        low = layer_norm(values, vec_ref[2:3], vec_ref[3:4]).astype(bf16)
        h_ref[...] = low
        normed_ref[...] = low[:kept]

    hidden = sum(
        nn(h_ref[:, r * edge : (r + 1) * edge], up_ref[0, :, r * wide : (r + 1) * wide])
        for r in range(side)
    )
    hidden_ref[0] = hidden[:kept]
    active = gelu_parts(hidden)[0].astype(bf16)
    for r in range(side):
        x_ref[:, r * edge : (r + 1) * edge] += nt_(
            active, down_ref[0, :, r * wide : (r + 1) * wide]
        )

    @pl.when(step == groups - 1)
    def _():
        values = x_ref[...]
        out_ref[...] = values[:kept]
        final = layer_norm(values, vec_ref[4:5], vec_ref[5:6])
        encoded = final[:kept].astype(bf16)
        target = norm_parts(final)[0].astype(bf16)
        picked = nn(pick_ref[...], target).astype(bf16)
        for t in range(swap_ref.shape[0]):
            feat_ref[t] = nn(encoded, swap_ref[t]).astype(bf16)
            target_ref[t] = nn(picked, swap_ref[t]).astype(bf16)


def put(grad_ref, t, columns, value):
    grad_ref[t, :, columns] = value.astype(bf16)


def predictor_kernel(
    share, context, players, head_size, denominator,
    feat_ref, target_ref, base_ref, first_hbm, second_hbm, vec_ref, hot_ref,
    grad_hbm, vec_grad_ref, loss_ref, back_ref,
    w_ref, grad_ref, w_sem, grad_sem, x_ref, mid_ref, h_ref, h2_ref, rows_ref, att_ref, hidden_ref, acc_ref, d_ref, low_ref, f_ref,
):
    groups = w_ref.shape[0]
    edge = w_ref.shape[1]
    length = base_ref.shape[0] // share
    quarter = feat_ref.shape[2]
    columns = edge // 4
    last = 3 * players * edge
    in_cols = slice(last, last + quarter)
    out_cols = slice(last + quarter, last + 2 * quarter)

    def span(number):
        return slice(number * edge, (number + 1) * edge)

    def copy_in(number):
        ref, place = first_hbm, (number + 1) % (3 * players + 1)
        if place * edge >= first_hbm.shape[2]:
            ref, place = second_hbm, place - first_hbm.shape[2] // edge
        return pltpu.make_async_copy(
            ref.at[:, :, pl.ds(place * edge, edge)],
            w_ref.at[:, :, pl.ds(number * edge, edge)],
            w_sem.at[number],
        )

    def copy_out(number):
        columns = pl.ds(number * edge, edge)
        return pltpu.make_async_copy(
            grad_ref.at[:, :, columns], grad_hbm.at[:, :, columns], grad_sem.at[number]
        )

    def pair(p, number):
        return jnp.concatenate([w_ref[2 * p + i, :, span(number)] for i in range(2)], 1)

    def put_pair(p, number, value):
        for i in range(2):
            put(grad_ref, 2 * p + i, span(number), value[:, i * edge : (i + 1) * edge])

    for number in [3 * players] + list(range(3 * players)):
        copy_in(number).start()
    vec_grad_ref[...] = jnp.zeros_like(vec_grad_ref)
    copy_in(3 * players).wait()
    projected = sum(nt_(feat_ref[t], w_ref[t, :, in_cols]) for t in range(groups))
    x_ref[0] = base_ref[...]
    for i in range(share):
        x_ref[0, i * length : i * length + context] += projected[i * context : (i + 1) * context]

    for j in range(players):
        values = x_ref[j]
        h_ref[j] = layer_norm(values, vec_ref[4 * j : 4 * j + 1], vec_ref[4 * j + 1 : 4 * j + 2]).astype(bf16)
        mid_ref[j] = values
        copy_in(3 * j).wait()

        @pl.loop(0, groups // 2)
        def _(p, j=j):
            both = nn(h_ref[j], pair(p, 3 * j)).astype(bf16)
            mixed = None
            for i in range(2):
                t = 2 * p + i
                rows = both[:, i * edge : i * edge + 3 * columns]
                rows_ref[j, t] = rows
                att = attend(rows, head_size, length, None)
                att_ref[j, t] = att
                out = nt_(att, w_ref[t, :, 3 * j * edge + 3 * columns : (3 * j + 1) * edge])
                mixed = out if mixed is None else mixed + out
            mid_ref[j] += mixed

        values = mid_ref[j]
        h2_ref[j] = layer_norm(values, vec_ref[4 * j + 2 : 4 * j + 3], vec_ref[4 * j + 3 : 4 * j + 4]).astype(bf16)
        x_ref[j + 1] = values
        copy_in(3 * j + 1).wait()
        copy_in(3 * j + 2).wait()

        @pl.loop(0, groups // 2)
        def _(p, j=j):
            hidden = nn(h2_ref[j], pair(p, 3 * j + 1))
            hidden_ref[j, p] = hidden
            x_ref[j + 1] += nt_(gelu_parts(hidden)[0].astype(bf16), pair(p, 3 * j + 2))

    final_gain = vec_ref[4 * players : 4 * players + 1]
    final = layer_norm(x_ref[players], final_gain, vec_ref[4 * players + 1 : 4 * players + 2]).astype(bf16)
    f_ref[...] = jnp.concatenate(
        [final[i * length + context : (i + 1) * length] for i in range(share)], 0
    )
    total = jnp.zeros((1, 1), f32)
    grad_f = jnp.zeros(f_ref.shape, f32)
    for t in range(groups):
        out_w = w_ref[t, :, out_cols]
        gap = nn(f_ref[...], out_w) - target_ref[t].astype(f32)
        size = jnp.abs(gap)
        terms = jnp.where(size < 1.0, 0.5 * gap * gap, size - 0.5)
        total += jnp.sum(jnp.sum(terms, 1, keepdims=True), 0, keepdims=True)
        grad_pred = (jnp.clip(gap, -1.0, 1.0) * (1.0 / denominator)).astype(bf16)
        put(grad_ref, t, out_cols, tn(f_ref[...], grad_pred))
        grad_f += nt_(grad_pred, out_w)
    loss_ref[...] = jnp.broadcast_to(total * (1.0 / denominator), loss_ref.shape)
    d_ref[...] = jnp.zeros_like(d_ref)
    tail = length - context
    for i in range(share):
        d_ref[i * length + context : (i + 1) * length] = grad_f[i * tail : (i + 1) * tail]
    grad, gain_g, shift_g = norm_backward(d_ref[...], x_ref[players], final_gain)
    d_ref[...] = grad
    vec_grad_ref[4 * players : 4 * players + 1] = gain_g
    vec_grad_ref[4 * players + 1 : 4 * players + 2] = shift_g

    for j in reversed(range(players)):
        low_ref[...] = d_ref[...].astype(bf16)
        acc_ref[...] = jnp.zeros_like(acc_ref)

        @pl.loop(0, groups // 2)
        def _(p, j=j):
            active, slope = gelu_parts(hidden_ref[j, p])
            low = low_ref[...]
            put_pair(p, 3 * j + 2, tn(low, active.astype(bf16)))
            grad_hidden = (nn(low, pair(p, 3 * j + 2)) * slope).astype(bf16)
            put_pair(p, 3 * j + 1, tn(h2_ref[j], grad_hidden))
            acc_ref[...] += nt_(grad_hidden, pair(p, 3 * j + 1))

        copy_out(3 * j + 2).start()
        copy_out(3 * j + 1).start()
        grad, gain_g, shift_g = norm_backward(
            acc_ref[...], mid_ref[j], vec_ref[4 * j + 2 : 4 * j + 3]
        )
        vec_grad_ref[4 * j + 2 : 4 * j + 3] = gain_g
        vec_grad_ref[4 * j + 3 : 4 * j + 4] = shift_g
        grad = d_ref[...] + grad
        d_ref[...] = grad
        low_ref[...] = grad.astype(bf16)
        acc_ref[...] = jnp.zeros_like(acc_ref)

        @pl.loop(0, groups // 2)
        def _(p, j=j):
            low = low_ref[...]
            total = None
            for i in range(2):
                t = 2 * p + i
                attn_w = w_ref[t, :, span(3 * j)]
                grad_att = nn(low, attn_w[:, 3 * columns :]).astype(bf16)
                grad_rows = attend_back(rows_ref[j, t], grad_att, head_size, length, None)
                grad_w = jnp.concatenate([tn(h_ref[j], grad_rows), tn(low, att_ref[j, t])], 1)
                put(grad_ref, t, span(3 * j), grad_w)
                out = nt_(grad_rows, attn_w[:, : 3 * columns])
                total = out if total is None else total + out
            acc_ref[...] += total

        copy_out(3 * j).start()
        grad, gain_g, shift_g = norm_backward(acc_ref[...], x_ref[j], vec_ref[4 * j : 4 * j + 1])
        vec_grad_ref[4 * j : 4 * j + 1] = gain_g
        vec_grad_ref[4 * j + 1 : 4 * j + 2] = shift_g
        d_ref[...] += grad

    mask_grad = jnp.zeros((1, edge), f32)
    for i in range(share):
        mask_grad += jnp.sum(d_ref[i * length + context : (i + 1) * length], 0, keepdims=True)
    vec_grad_ref[4 * players + 2 : 4 * players + 3] = mask_grad
    low = jnp.concatenate(
        [d_ref[i * length : i * length + context] for i in range(share)], 0
    ).astype(bf16)
    back = jnp.zeros((low.shape[0], hot_ref.shape[1]), f32)
    z = lax.axis_index("tensor")
    z = z - lax.rem(z, 2) + 1
    for t in range(groups):
        put(grad_ref, t, in_cols, tn(low, feat_ref[t]))
        first = pl.multiple_of(flip(z, t) * quarter, 16)
        back += nn(nn(low, w_ref[t, :, in_cols]).astype(bf16), hot_ref[pl.ds(first, quarter), :])
    copy_out(3 * players).start()
    back_ref[...] = back.astype(bf16)
    for number in range(3 * players + 1):
        copy_out(number).wait()


def encoder_feed_back_kernel(
    edge, back_ref, out_ref, mid_ref, normed_ref, hidden_ref, up_ref, down_ref, vec_ref,
    up_grad, down_grad, grad_ref, vec_grad_ref, d_ref, low_ref, acc_ref,
):
    step = pl.program_id(0)
    groups = pl.num_programs(0)
    wide = 2 * edge

    @pl.when(step == 0)
    def _():
        grad, gain_g, shift_g = norm_backward(back_ref[...].astype(f32), out_ref[...], vec_ref[4:5])
        d_ref[...] = grad
        low_ref[...] = grad.astype(bf16)
        acc_ref[...] = jnp.zeros_like(acc_ref)
        vec_grad_ref[...] = jnp.zeros_like(vec_grad_ref)
        vec_grad_ref[4:5] = gain_g
        vec_grad_ref[5:6] = shift_g

    active, slope = gelu_parts(hidden_ref[0])
    active = active.astype(bf16)
    grad_hidden = sum(
        nn(low_ref[:, r * edge : (r + 1) * edge], down_ref[0, :, r * wide : (r + 1) * wide])
        for r in range(2)
    )
    grad_hidden = (grad_hidden * slope).astype(bf16)
    for r in range(2):
        mine = slice(r * edge, (r + 1) * edge)
        columns = slice(r * wide, (r + 1) * wide)
        put(down_grad, 0, columns, tn(low_ref[:, mine], active))
        put(up_grad, 0, columns, tn(normed_ref[:, mine], grad_hidden))
        acc_ref[:, mine] += nt_(grad_hidden, up_ref[0, :, columns])

    @pl.when(step == groups - 1)
    def _():
        grad, gain_g, shift_g = norm_backward(acc_ref[...], mid_ref[...], vec_ref[2:3])
        grad_ref[...] = d_ref[...] + grad
        vec_grad_ref[2:3] = gain_g
        vec_grad_ref[3:4] = shift_g


def encoder_attend_back_kernel(
    edge, unit, context, head_size,
    role_ref, mid_grad_ref, resid_ref, normed_ref, rows_ref, att_ref, w_ref, patch_ref, order_ref,
    vec_ref, grad_ref, vec_grad_ref, low_ref, acc_ref,
):
    step = pl.program_id(0)
    groups = pl.num_programs(0) // 2
    wide = 2 * edge
    columns = wide // 4
    pix = patch_ref.shape[2]

    @pl.when(step == 0)
    def _():
        low_ref[...] = mid_grad_ref[...].astype(bf16)
        acc_ref[...] = jnp.zeros_like(acc_ref)

    @pl.when(step < groups)
    def _():
        grad_att = sum(
            nn(
                low_ref[:, r * edge : (r + 1) * edge],
                w_ref[0, :, r * wide + 3 * columns : (r + 1) * wide],
            )
            for r in range(2)
        ).astype(bf16)
        allowed = same_image(role_ref[0], unit, context)
        grad_rows = attend_back(rows_ref[0], grad_att, head_size, unit, allowed)
        for r in range(2):
            mine = slice(r * edge, (r + 1) * edge)
            grad_w = jnp.concatenate(
                [tn(normed_ref[:, mine], grad_rows), tn(low_ref[:, mine], att_ref[0])], 1
            )
            put(grad_ref, step, slice(r * wide, (r + 1) * wide), grad_w)
            acc_ref[:, mine] += nt_(grad_rows, w_ref[0, :, r * wide : r * wide + 3 * columns])

    @pl.when(step == groups - 1)
    def _():
        grad, gain_g, shift_g = norm_backward(acc_ref[...], resid_ref[...], vec_ref[0:1])
        grad = mid_grad_ref[...] + grad
        low_ref[...] = nn(grad.astype(bf16), order_ref[...]).astype(bf16)
        vec_grad_ref[...] = jnp.zeros_like(vec_grad_ref)
        vec_grad_ref[0:1] = gain_g
        vec_grad_ref[1:2] = shift_g
        vec_grad_ref[6:7] = jnp.sum(grad, 0, keepdims=True)

    @pl.when(step >= groups)
    def _():
        grad_w = jnp.concatenate(
            [tn(low_ref[:, r * edge : (r + 1) * edge], patch_ref[0]) for r in range(2)], 1
        )
        put(grad_ref, step - groups, slice(2 * wide, 2 * wide + 2 * pix), grad_w)


def adamw(master, moment, second, gradient, step_rate, weight_decay):
    moment = 0.9 * moment + 0.1 * gradient
    second = 0.999 * second + 0.001 * gradient * gradient
    unbiased_first = moment / (1.0 - 0.9**STEP)
    unbiased_second = second / (1.0 - 0.999**STEP)
    return (
        master
        - step_rate
        * (unbiased_first / (jnp.sqrt(unbiased_second) + 1e-08) + weight_decay * master),
        moment,
        second,
    )


def update_kernel(
    grad_ref, weight_ref, left_ref, right_ref, root_left_ref, root_right_ref, teacher_ref,
    emb_grad, emb, emb_m, emb_v, temb, enc_grad, enc, enc_m, enc_v,
    pred_grad, pred, pred_m, pred_v, tvec,
    grad_out, weight_out, left_out, right_out, teacher_out,
    emb_out, emb_m_out, emb_v_out, temb_out, enc_out, enc_m_out, enc_v_out,
    pred_out, pred_m_out, pred_v_out, tvec_out, loss_out,
):
    low = grad_ref[0]
    grad_out[0, 0] = low.astype(f32)
    left_out[0, 0] = 0.95 * left_ref[0, 0] + 0.05 * nt_(low, low)
    right_out[0, 0] = 0.95 * right_ref[0, 0] + 0.05 * tn(low, low)
    high, rest = split(root_left_ref[0, 0])
    side = nn(high, low) + nn(rest, low)
    high, rest = split(side)
    root_high, root_rest = split(root_right_ref[0, 0])
    step = nn(high, root_high) + nn(high, root_rest) + nn(rest, root_high)
    mean = jnp.mean(jnp.mean(step * step, 1, keepdims=True), 0, keepdims=True)
    step = step * lax.rsqrt(mean + 1e-06)
    weight = weight_ref[0, 0]
    new = weight - 0.05 * (step + 0.05 * weight)
    weight_out[0, 0] = new
    teacher_out[0, 0] = 0.7 * teacher_ref[0, 0] + 0.3 * new

    @pl.when(pl.program_id(0) == 0)
    def _():
        new, m, v = adamw(emb[...], emb_m[...], emb_v[...], emb_grad[...], 0.05, 0.05)
        emb_out[...], emb_m_out[...], emb_v_out[...] = new, m, v
        temb_out[...] = 0.7 * temb[...] + 0.3 * new
        rows = enc.shape[0]
        new, m, v = adamw(enc[...], enc_m[...], enc_v[...], enc_grad[0:rows], 0.5, 0.0)
        enc_out[...], enc_m_out[...], enc_v_out[...] = new, m, v
        tvec_out[...] = 0.7 * tvec[...] + 0.3 * new
        rows = pred.shape[0]
        new, m, v = adamw(pred[...], pred_m[...], pred_v[...], pred_grad[0:rows], 0.5, 0.0)
        pred_out[...], pred_m_out[...], pred_v_out[...] = new, m, v
        loss_out[...] = pred_grad[12:13, 0:1]


MESH = pl.DeviceIdType.MESH


def flip(place, bits):
    bit = 1
    while bit <= bits:
        if bits & bit:
            place = place + bit * (1 - 2 * lax.rem(lax.div(place, bit), 2))
        bit *= 2
    return place


def remote(source, target, send_sem, recv_sem, device):
    return pltpu.make_async_remote_copy(
        src_ref=source, dst_ref=target, send_sem=send_sem, recv_sem=recv_sem,
        device_id=device, device_id_type=MESH,
    )


def greet(routes, d, z, everyone=False):
    barrier = pltpu.get_barrier_semaphore()
    peers = [(d, flip(z, r)) for r in range(1, routes.nt)]
    if everyone:
        peers += [(routes.later(d, j), z) for j in range(1, routes.nd)]
    else:
        peers += [routes.partner(s, d, z) for s in range(routes.stages + 1)]
    for peer in peers:
        pl.semaphore_signal(barrier, inc=1, device_id=peer, device_id_type=MESH)
    pl.semaphore_wait(barrier, len(peers))


def sincos_table(columns):
    quarter = columns // 4
    frequency = 1.0 / np.float32(10000.0) ** (np.arange(quarter, dtype=np.float32) / quarter)
    angle = np.arange(SIDE, dtype=np.float32)[:, None] * frequency.astype(np.float32)
    parts = np.concatenate([np.sin(angle), np.cos(angle)], 1).astype(np.float32)
    none = np.zeros_like(parts)
    return np.concatenate(
        [np.concatenate([parts, none], 1), np.concatenate([none, parts], 1)], 0
    )


def guarded(condition, body):
    if condition is None:
        body()
    else:
        pl.when(condition)(body)


class Gather:
    ahead = 2
    players = 3

    def __init__(self, routes, widths, pre, few_rows, sources, mats, sems):
        self.routes, self.widths, self.pre, self.few_rows = routes, widths, pre, few_rows
        self.own, self.other, self.pred, self.few, self.every, self.rows = sources
        self.mats = mats
        self.sems = sems
        self.d, self.z = lax.axis_index("dp"), lax.axis_index("tensor")
        self.role = lax.rem(self.z, 2)
        self.last = len(widths) - 1
        self.items = [(m, r) for m in range(len(widths)) for r in range(routes.nt)]
        self.events = {}
        self.there = {}
        self.plan()

    def plan(self):
        for i, (m, r) in enumerate(self.items):
            pre = self.pre[m]
            if pre and r == 0:
                first = m - self.players
                for s in range(pre):
                    self.at(first + s * (self.ahead + first), s, self.alone, m, s)
                self.at(self.send_at[first], pre, self.share, m)
            for s in range(pre, self.routes.stages + 1):
                self.at(i + self.ahead * (s - pre), s, self.advance, m, r, s)
            self.there[m, r] = i + self.ahead * (self.routes.stages + 1 - pre)

    send_at = (6, 12)

    def at(self, step, order, action, m, *rest):
        def run():
            condition = None if action in (self.alone, self.share) else self.mine(m)
            guarded(condition, lambda: action(m, *rest))

        self.events.setdefault(step, []).append((-order, run))

    def peer(self, r):
        return self.d, flip(self.z, r)

    def peer_role(self, r):
        return lax.rem(flip(self.z, r), 2)

    def source(self, m, r):
        if m >= self.players:
            first = sum(self.widths[self.players : m])
            return self.pred.at[:, pl.ds(first, self.widths[m])]
        ref = self.own if r % 2 == 0 else self.other
        return ref.at[:, pl.ds(sum(self.widths[:m]), self.widths[m])]

    def across(self, m, r):
        source, target = self.source(m, r), self.mats[m].at[r, 0]
        if self.pre[m]:
            pieces = pl.ds(0, 1 << self.pre[m])
            source, target = self.mats[m].at[0, pieces], self.mats[m].at[r, pieces]
        return remote(source, target, self.sems[0].at[m, r], self.sems[1].at[m, r], self.peer(r))

    def local(self, m):
        return pltpu.make_async_copy(self.source(m, 0), self.mats[m].at[0, 0], self.sems[2].at[m])

    def patch_source(self, r, role):
        place = flip(lax.div(self.z, 2), r // 2)
        ref = self.every if role else self.few
        rows = self.rows.shape[1] if role else self.few_rows
        if len(ref.shape) == 3:
            return ref.at[r, pl.ds(0, rows)], rows
        return ref.at[pl.ds(place * rows, rows)], rows

    def patch(self, r, role):
        source, rows = self.patch_source(r, role)
        return remote(
            source, self.rows.at[r, pl.ds(0, rows)], self.sems[3].at[r], self.sems[4].at[r],
            self.peer(r),
        )

    def own_patch(self, role):
        source, rows = self.patch_source(0, role)
        return pltpu.make_async_copy(
            source, self.rows.at[0, pl.ds(0, rows)], self.sems[2].at[self.last + 1]
        )

    def send_patches(self):
        for role in range(2):
            pl.when(self.role == role)(lambda role=role: self.own_patch(role).start())
            for r in range(1, self.routes.nt):
                pl.when(self.peer_role(r) == role)(
                    lambda r=r, role=role: self.patch(r, role).start()
                )

    def stage(self, m, r, s):
        size = 1 << s
        return remote(
            self.mats[m].at[r, pl.ds(0, size)], self.mats[m].at[r, pl.ds(size, size)],
            self.sems[5].at[m, r, s], self.sems[6].at[m, r, s],
            self.routes.partner(s, self.d, self.z),
        )

    def mine(self, m):
        return self.role == 1 if m >= self.players else None

    def theirs(self, m, r):
        return self.peer_role(r) == 1 if m >= self.players else None

    def send(self, m):
        for r in range(1, self.routes.nt):
            guarded(self.theirs(m, r), lambda r=r: self.across(m, r).start())

    def start(self):
        for m in range(len(self.widths)):
            guarded(None if self.pre[m] else self.mine(m), lambda m=m: self.local(m).start())
            if not self.pre[m]:
                self.send(m)

    def alone(self, m, s):
        if s:
            self.stage(m, 0, s - 1).wait_recv()
        else:
            self.local(m).wait()
        self.stage(m, 0, s).start()

    def share(self, m):
        self.stage(m, 0, self.pre[m] - 1).wait_recv()
        self.send(m)

    def advance(self, m, r, s):
        if s > self.pre[m]:
            self.stage(m, r, s - 1).wait_recv()
        elif r:
            self.across(m, r).wait_recv()
        elif not s:
            self.local(m).wait()
        self.stage(m, r, s).start()

    def step(self, n):
        for _, run in sorted(self.events.get(n, []), key=lambda event: event[0]):
            run()

    def span(self):
        return max(self.there.values()) + 1

    def arrive(self, m, r):
        self.stage(m, r, self.routes.stages).wait_recv()

    def wait_patches(self):
        for role in range(2):
            pl.when(self.role == role)(lambda role=role: self.own_patch(role).wait())
            for r in range(1, self.routes.nt):
                pl.when(self.role == role)(lambda r=r, role=role: self.patch(r, role).wait_recv())

    def finish(self):
        for r in range(1, self.routes.nt):
            for role in range(2):
                pl.when(self.peer_role(r) == role)(
                    lambda r=r, role=role: self.patch(r, role).wait_send()
                )
        for m, r in self.items:
            pre = self.pre[m]

            def sent(m=m, r=r, pre=pre):
                for s in range(pre, self.routes.stages + 1):
                    self.stage(m, r, s).wait_send()

            guarded(self.mine(m), sent)
            if r:
                guarded(self.theirs(m, r), lambda m=m, r=r: self.across(m, r).wait_send())
            else:
                for s in range(pre):
                    self.stage(m, 0, s).wait_send()


def gather_kernel(
    routes, widths, few_rows, own_ref, other_ref, pred_ref, patch_ref,
    attn_ref, up_ref, down_ref, first_ref, second_ref, rows_ref, *sems,
):
    gather = Gather(
        routes, widths, (0,) * 5, few_rows,
        (own_ref, other_ref, pred_ref, patch_ref, patch_ref, rows_ref),
        (attn_ref, up_ref, down_ref, first_ref, second_ref), sems,
    )
    greet(routes, gather.d, gather.z)
    gather.start()
    gather.send_patches()
    for n in range(gather.span()):
        gather.step(n)
    for m, r in gather.items:
        guarded(gather.mine(m), lambda m=m, r=r: gather.arrive(m, r))
    gather.wait_patches()
    gather.finish()


def split(values):
    high = values.astype(bf16)
    return high, (values - high.astype(f32)).astype(bf16)


def exactly(product, first, second, turn=False):
    values = second if turn else first
    high, rest = split(values)
    low = (values - high.astype(f32) - rest.astype(f32)).astype(bf16)
    if turn:
        return product(first, high) + product(first, rest) + product(first, low)
    return product(high, second) + product(rest, second) + product(low, second)


def forward_kernel(
    routes, widths, unit, context, head_size,
    owner_ref, weight_ref, teach_ref, turned_ref, ctx_ref, tgt_ref, embed_ref, temb_ref,
    evec_ref, tvec_ref, pvec_in, table_in, table_p_in,
    attn_out, up_out, down_out, first_out, second_out, rows_out, mid_out, resid_out, normed_out, qkv_out,
    att_out, out_out, normed2_out, hidden_out, feat_out, target_out,
    hot_ref, order_ref, hot_p_ref, vec_ref, pvec_ref, tokens_ref,
    attn_ref, up_ref, down_ref, first_ref, second_ref, rows_ref, x_ref, h_ref, sent_ref, feat_ref,
    slots_out, slots_ref, own_ref, other_ref, pred_ref, picked_ref, patch_ref,
    back_sem, feat_send, feat_recv, slot_send, slot_recv, slot_sem, *sems,
):
    nt, nd = routes.nt, routes.nd
    mats = (attn_ref, up_ref, down_ref, first_ref, second_ref)
    outs = (attn_out, up_out, down_out, first_out, second_out)
    kept = resid_out.shape[0]
    gather = Gather(
        routes, widths, (0, 0, 0, 1, 1), kept,
        (own_ref, other_ref, pred_ref, picked_ref, patch_ref, rows_ref), mats, sems,
    )
    role = gather.role
    edge = nd * attn_ref.shape[2]
    side = 2
    wide = side * edge
    pix = rows_ref.shape[2]
    columns = wide // 4

    def matrix(ref, t, first, width):
        return ref[t, :, :, first : first + width].reshape(edge, width)

    def to_hbm(m, r):
        return pltpu.make_async_copy(mats[m].at[r], outs[m].at[r], back_sem.at[m, r])

    def feat_copy():
        return remote(sent_ref, feat_ref, feat_send, feat_recv, gather.peer(1))

    d, z = gather.d, gather.z
    rows_part = attn_ref.shape[2]
    slots = weight_ref.shape[0]
    span = x_ref.shape[0]
    images = ctx_ref.shape[0]
    share = span // unit
    part = lax.div(z, 2)

    def slot_copy(j):
        peer = routes.later(d, j)
        return remote(
            slots_out.at[:, :, peer], slots_ref.at[:, pl.ds(d * slots, slots)],
            slot_send.at[j], slot_recv.at[j], (peer, z),
        )

    def own_slots():
        return pltpu.make_async_copy(
            slots_out.at[:, :, d], slots_ref.at[:, pl.ds(d * slots, slots)], slot_sem
        )

    def send_slots():
        for kind, ref in enumerate((weight_ref, teach_ref)):
            for s in range(slots):
                slots_out[kind, s] = ref[s].astype(bf16).reshape(nd, rows_part, edge)
        own_slots().start()
        for j in range(1, nd):
            slot_copy(j).start()

    def by_rows(values):
        turned = values.T.astype(bf16)
        return jnp.concatenate([turned[:rows_part], turned[rows_part:]], 1)

    def take_slots():
        own_slots().wait()
        for j in range(1, nd):
            slot_copy(j).wait_recv()
        blocks = sum(widths[:3]) // edge - 1
        for b in range(blocks):
            first = b * edge if b < 4 else widths[0] + (b - 4) * edge
            own_ref[:, first : first + edge] = slots_ref[role, owner_ref[b]]
            other_ref[:, first : first + edge] = slots_ref[1 - role, owner_ref[b]]
        student, teacher = by_rows(embed_ref[...]), by_rows(temb_ref[...])
        first = widths[0] - student.shape[1]
        own_ref[:, first : widths[0]] = jnp.where(role == 0, student, teacher)
        other_ref[:, first : widths[0]] = jnp.where(role == 0, teacher, student)
        count = owner_ref.shape[0]
        for b in range(blocks, count):
            first = (b - blocks + 1) * edge if b < count - 1 else 0
            pred_ref[:, first : first + edge] = slots_ref[0, owner_ref[b]]

    def local_order(step, shift):
        lane = lax.broadcasted_iota(jnp.int32, (1, edge), 1)
        row = lane
        for k in range(nd):
            here = (lane >= k * rows_part) & (lane < (k + 1) * rows_part)
            row = jnp.where(here, lane + (routes.holder(k, d) * step + shift - k * rows_part), row)
        return row

    def one_hot(rows, row):
        return (lax.broadcasted_iota(jnp.int32, (rows, row.shape[1]), 0) == row).astype(bf16)

    def send_patches():
        for g in range(images):
            hot = one_hot(unit, ctx_ref[g : g + 1])
            patches = turned_ref[g].T
            patch_ref[g * unit : (g + 1) * unit] = patches
            picked_ref[g * context : (g + 1) * context] = tn(hot, patches).astype(bf16)
        gather.send_patches()

    def positions(table, hot, row):
        both = jnp.concatenate(
            [one_hot(unit // 16, lax.rem(row, 16)), one_hot(unit // 16, lax.div(row, 16))], 0
        )
        return exactly(tn, both, exactly(nn, table, hot), turn=True)

    def prepare():
        places = local_order(rows_part, 0)
        feat = jnp.concatenate([places, places + edge], 1)
        hot_ref[...] = one_hot(wide, feat)
        hot_p_ref[...] = one_hot(edge, places)
        emb = [local_order(2 * rows_part, m * rows_part) for m in range(2)]
        order_ref[...] = tn(hot_ref[...], one_hot(wide, jnp.concatenate(emb, 1))).astype(bf16)
        vec_ref[...] = jnp.zeros_like(vec_ref)
        pvec_ref[...] = jnp.zeros_like(pvec_ref)
        count = evec_ref.shape[0]
        vectors = jnp.where(role == 0, evec_ref[...], tvec_ref[...])
        vec_ref[0:count] = exactly(nn, vectors, hot_ref[...])
        count = pvec_in.shape[0]
        pvec_ref[0:count] = exactly(nn, pvec_in[...], hot_p_ref[...])

    def prepare_rows():
        ctx = [ctx_ref[pl.ds(part * share + i, 1), :] for i in range(share)]
        tgt = [tgt_ref[pl.ds(part * share + i, 1), :] for i in range(share)]
        rest = jnp.zeros((1, span - kept), jnp.int32)
        row = jnp.where(
            role == 0,
            jnp.concatenate(ctx + [rest], 1),
            lax.rem(lax.broadcasted_iota(jnp.int32, (1, span), 1), unit),
        )
        x_ref[...] = positions(table_in[...], hot_ref[...], row) + vec_ref[6:7]
        row = jnp.concatenate([v for pair in zip(ctx, tgt) for v in pair], 1)
        tokens = positions(table_p_in[...], hot_p_ref[...], row)
        length = row.shape[1] // share
        number = lax.broadcasted_iota(jnp.int32, tokens.shape, 0)
        is_target = lax.rem(number, length) >= context
        mask_at = pvec_in.shape[0] - 1
        tokens_ref[...] = jnp.where(is_target, tokens + pvec_ref[mask_at : mask_at + 1], tokens)

    def group_rows(t):
        quarter = target_out.shape[2]
        first = flip(z - lax.rem(z, 2) + 1, t) * quarter
        return hot_ref[pl.ds(pl.multiple_of(first, 16), quarter), :]

    def embed():
        gather.wait_patches()

        @pl.loop(0, nt)
        def _(t):
            ordered = sum(
                nn(
                    order_ref[:, m * edge : (m + 1) * edge],
                    matrix(attn_ref, t, side * wide + m * pix, pix),
                )
                for m in range(side)
            ).astype(bf16)
            x_ref[...] += nt_(rows_ref[t], ordered)

        values = x_ref[...]
        resid_out[...] = values[:kept]
        low = layer_norm(values, vec_ref[0:1], vec_ref[1:2]).astype(bf16)
        h_ref[...] = low
        normed_out[...] = low[:kept]

    def attention(t):
        rows = sum(
            nn(h_ref[:, r * edge : (r + 1) * edge], matrix(attn_ref, t, r * wide, 3 * columns))
            for r in range(side)
        ).astype(bf16)
        qkv_out[t] = rows[:kept]
        att = attend(rows, head_size, unit, same_image(role, unit, context))
        att_out[t] = att[:kept]
        for r in range(side):
            x_ref[:, r * edge : (r + 1) * edge] += nt_(
                att, matrix(attn_ref, t, r * wide + 3 * columns, columns)
            )

    def middle():
        values = x_ref[...]
        mid_out[...] = values[:kept]
        low = layer_norm(values, vec_ref[2:3], vec_ref[3:4]).astype(bf16)
        h_ref[...] = low
        normed2_out[...] = low[:kept]

    def feed(t):
        hidden = sum(
            nn(h_ref[:, r * edge : (r + 1) * edge], matrix(up_ref, t, r * wide, wide))
            for r in range(side)
        )
        hidden_out[t] = hidden[:kept]
        active = gelu_parts(hidden)[0].astype(bf16)
        for r in range(side):
            x_ref[:, r * edge : (r + 1) * edge] += nt_(
                active, matrix(down_ref, t, r * wide, wide)
            )

    def last():
        values = x_ref[...]
        out_out[...] = values[:kept]
        final = layer_norm(values, vec_ref[4:5], vec_ref[5:6])

        @pl.when(role == 0)
        def _():
            encoded = final[:kept].astype(bf16)
            for t in range(nt):
                sent_ref[t] = nt_(encoded, group_rows(t)).astype(bf16)
            feat_copy().start()

        @pl.when(role == 1)
        def _():
            target = norm_parts(final)[0].astype(bf16)
            tgt = [tgt_ref[pl.ds(part * share + i, 1), :] + i * unit for i in range(share)]
            picked = tn(one_hot(span, jnp.concatenate(tgt, 1)), target).astype(bf16)
            for t in range(nt):
                target_out[t] = nt_(picked, group_rows(t)).astype(bf16)

        @pl.when(role == 0)
        def _():
            target_out[...] = jnp.zeros_like(target_out)

    attn_at = max(gather.there[0, r] for r in range(nt))
    feed_at = max([attn_at + nt + 1] + [gather.there[2, r] - r for r in range(nt)])
    steps = max(gather.span(), feed_at + nt)
    greet(routes, d, z, everyone=True)
    send_slots()
    send_patches()
    prepare()
    take_slots()
    gather.start()
    prepare_rows()

    @pl.loop(0, steps)
    def _(n):
        for k in range(steps):

            @pl.when(n == k)
            def _(k=k):
                gather.step(k)
                for m, r in gather.items:
                    if gather.there[m, r] != k:
                        continue

                    def here(m=m, r=r):
                        gather.arrive(m, r)
                        to_hbm(m, r).start()

                    guarded(gather.mine(m), here)

        pl.when(n == attn_at)(embed)

        @pl.when((n > attn_at) & (n <= attn_at + nt))
        def _():
            attention(n - attn_at - 1)

        pl.when(n == feed_at)(middle)

        @pl.when((n >= feed_at) & (n < feed_at + nt))
        def _():
            feed(n - feed_at)

        pl.when(n == feed_at + nt - 1)(last)

    rows_out[...] = rows_ref[:, :kept]

    @pl.when(role == 0)
    def _():
        feat_copy().wait_send()
        feat_out[...] = jnp.zeros_like(feat_out)

    @pl.when(role == 1)
    def _():
        feat_copy().wait_recv()
        feat_out[...] = feat_ref[...]

    gather.finish()
    for j in range(1, nd):
        slot_copy(j).wait_send()
    for m, r in gather.items:
        guarded(gather.mine(m), lambda m=m, r=r: to_hbm(m, r).wait())


def reduce_kernel(
    routes, attn_cols, down_ref, up_ref, attn_ref, pred_ref, block_ref, emb_ref,
    core0, core1, core2, later0, later1, later2, enc_in, pred_in, load,
    load_sem, core_send, core_recv, stage_send, stage_recv, z_send, z_recv,
):
    d, z = lax.axis_index("dp"), lax.axis_index("tensor")
    nt, stages = routes.nt, routes.stages
    middle = routes.nd // 2
    role = lax.rem(z, 2)
    cores = [core0, core1, core2]
    laters = [later0, later1, later2]
    greet(routes, d, z)

    def run(kind, sources, incoming, starts):
        items = [(j, r) for j in range(len(sources)) for r in reversed(range(nt))]

        def part(j, r, first):
            ref, start, width = sources[j]
            return ref.at[r, pl.ds(first, middle), :, pl.ds(start, width)]

        def to_core(j, r):
            return remote(
                part(j, r, middle), cores[j].at[r, :, :, pl.ds(0, sources[j][2])],
                core_send.at[j, r], core_recv.at[j, r], routes.partner(stages, d, z),
            )

        def own(i):
            j, r = items[i]
            return pltpu.make_async_copy(
                part(j, r, 0), load.at[i % 2, :, :, pl.ds(0, sources[j][2])], load_sem.at[i % 2]
            )

        def stage(j, r, s):
            size = 1 << s
            return remote(
                cores[j].at[r, pl.ds(size, size), :, pl.ds(0, sources[j][2])],
                laters[j].at[r, pl.ds(size - 1, size), :, pl.ds(0, sources[j][2])],
                stage_send.at[j, r, s], stage_recv.at[j, r, s], routes.partner(s, d, z),
            )

        def across(j, r):
            return remote(
                cores[j].at[r, 0, :, pl.ds(0, sources[j][2])],
                incoming.at[r, :, pl.ds(starts[j], sources[j][2])],
                z_send.at[kind, j, r], z_recv.at[kind, j, r], (d, flip(z, r)),
            )

        def add(i, q):
            j, r = items[i]
            width = sources[j][2]
            if q == 0:
                own(i).wait()
                to_core(j, r).wait_recv()

                @pl.loop(0, middle)
                def _(k):
                    total = cores[j][r, k, :, 0:width].astype(f32)
                    total += load[i % 2, k, :, 0:width].astype(f32)
                    cores[j][r, k, :, 0:width] = total.astype(bf16)

                if i + 2 < len(items):
                    own(i + 2).start()
            else:
                s = stages - q
                stage(j, r, s).wait_recv()

                @pl.loop(0, 1 << s)
                def _(k):
                    total = cores[j][r, k, :, 0:width].astype(f32)
                    total += laters[j][r, k + ((1 << s) - 1), :, 0:width].astype(f32)
                    cores[j][r, k, :, 0:width] = total.astype(bf16)

            if q < stages:
                stage(j, r, stages - q - 1).start()
            elif r:
                across(j, r).start()

        for i in range(min(2, len(items))):
            own(i).start()
        for j, r in items:
            to_core(j, r).start()
        for n in range(len(items) + stages):
            for q in reversed(range(stages + 1)):
                if 0 <= n - q < len(items):
                    add(n - q, q)
        for j, r in items:
            to_core(j, r).wait_send()
            for s in range(stages):
                stage(j, r, s).wait_send()
            if r:
                across(j, r).wait_send()

    wide = down_ref.shape[3]
    all_cols = attn_ref.shape[3]
    pred_cols = pred_ref.shape[3]
    encoder = [(down_ref, 0, wide), (up_ref, 0, wide), (attn_ref, 0, all_cols)]
    encoder_at = [0, wide, 2 * wide]
    players = [(pred_ref, 0, wide), (pred_ref, wide, pred_cols - wide)]
    players_at = [0, wide]

    @pl.when(role == 0)
    def _():
        run(0, encoder, enc_in, encoder_at)

    @pl.when(role == 1)
    def _():
        run(1, players, pred_in, players_at)

    def collect(kind, sources, incoming, starts, put):
        for j, (_, _, width) in enumerate(sources):
            place = incoming.at[:, :, pl.ds(starts[j], width)]

            def arrive(r, j=j, width=width):
                pltpu.make_async_remote_copy(
                    src_ref=cores[j].at[r, 0, :, pl.ds(0, width)],
                    dst_ref=incoming.at[r, :, pl.ds(starts[j], width)],
                    send_sem=z_send.at[kind, j, r], recv_sem=z_recv.at[kind, j, r],
                    device_id=(d, flip(z, r)), device_id_type=MESH,
                ).wait_recv()

            del place

            @pl.when(role == kind)
            def _(j=j, width=width, arrive=arrive):
                total = cores[j][0, 0, :, 0:width].astype(f32)
                for r in range(2, nt, 2):
                    arrive(r)
                    total += incoming[r, :, starts[j] : starts[j] + width].astype(f32)
                put(j, total)

            @pl.when(role != kind)
            def _(j=j, width=width, arrive=arrive):
                total = None
                for r in range(1, nt, 2):
                    arrive(r)
                    got = incoming[r, :, starts[j] : starts[j] + width].astype(f32)
                    total = got if total is None else total + got
                put(j, total)

    def put_encoder(j, total):
        if j == 2:
            block_ref[:, 0:attn_cols] = total[:, :attn_cols].astype(bf16)
            emb_ref[...] = total[:, attn_cols:]
        else:
            first = attn_cols + (1 - j) * wide
            block_ref[:, first : first + wide] = total.astype(bf16)

    def put_players(j, total):
        first = attn_cols + 2 * wide + players_at[j]
        block_ref[:, first : first + total.shape[1]] = total.astype(bf16)

    collect(1, players, pred_in, players_at, put_players)
    collect(0, encoder, enc_in, encoder_at, put_encoder)
    end = attn_cols + 2 * wide + pred_cols
    block_ref[:, end:] = jnp.zeros((block_ref.shape[0], block_ref.shape[1] - end), bf16)


def backward_kernel(
    routes, context, head_size,
    slot_of_ref, players_ref, back_in, attn_hbm, up_hbm, down_hbm,
    out_ref, mid_ref, resid_ref, normed2_ref, normed_ref, hidden_ref, qkv_ref, att_ref, rows_ref,
    vec_ref, order_ref, hot_ref, hot_p_ref, pred_vec_ref, loss_ref,
    low_out, emb_ref, enc_out, pred_out,
    block_ref, slots_ref, g0, g1, g2, g3, core0, core1, core2, core3, later0, later1, later2, later3, enc_in, pred_in,
    attn_w, up_w, down_w, back_ref, d_ref, low_ref, acc_ref, vec_grad_ref, vec_send, vec_recv,
    weight_sem, back_send, back_recv, load_sem, core_send, core_recv, stage_send, stage_recv,
    z_send, z_recv, vec_send_sem, vec_recv_sem, slot_send, slot_recv, slot_sem,
):
    d, z = lax.axis_index("dp"), lax.axis_index("tensor")
    nt, nd, stages = routes.nt, routes.nd, routes.stages
    role = lax.rem(z, 2)
    half = nd // 2
    grads, cores = (g0, g1, g2, g3), (core0, core1, core2, core3)
    laters = (later0, later1, later2, later3)
    rows = g0.shape[2]
    edge = nd * rows
    wide = 2 * edge
    columns = wide // 4
    pix = rows_ref.shape[2]
    unit = resid_ref.shape[0]
    mat = g0.shape[3]
    ahead = 2

    every = pl.ds(0, nt)
    encoder = [(j, r) for r in range(nt) for j in (0, 1)] + [(2, r) for r in range(nt)]
    encoder += [(3, every)]
    pred_cols = players_ref.shape[3]
    pred_width = (mat, pred_cols - mat)
    players = [(j, r) for r in reversed(range(nt)) for j in (0, 1)]
    enc_width = (mat, mat, mat, 2 * pix)
    enc_at = (0, mat, 2 * mat, 3 * mat)

    def weight(t, i):
        slot = lax.rem(t, 2)
        source = (up_hbm, down_hbm, attn_hbm)[i].at[t, :, pl.ds(0, mat)]
        target = (up_w, down_w, attn_w)[i].at[slot]
        return pltpu.make_async_copy(source, target, weight_sem.at[i, slot])

    def back_copy():
        return remote(back_in, back_ref, back_send, back_recv, (d, flip(z, 1)))

    def groups_of(r):
        return range(nt) if r is every else [r]

    def number(r):
        return 0 if r is every else r

    class Sums:
        def __init__(self, kind, items, width, incoming, at):
            self.kind, self.items, self.width = kind, items, width
            self.incoming, self.at = incoming, at

        def cut(self, j):
            return pl.ds(0, self.width[j])

        def to_core(self, j, r):
            if self.kind:
                source = players_ref.at[r, pl.ds(half, half), :, pl.ds(self.at[j], self.width[j])]
            else:
                source = grads[j].at[r, pl.ds(half, half)]
            return remote(
                source, cores[j].at[r, :, :, self.cut(j)],
                core_send.at[j, number(r)], core_recv.at[j, number(r)],
                routes.partner(stages, d, z),
            )

        def load(self, j, r):
            return pltpu.make_async_copy(
                players_ref.at[r, pl.ds(0, half), :, pl.ds(self.at[j], self.width[j])],
                grads[j].at[r, pl.ds(0, half), :, self.cut(j)],
                load_sem.at[j, r],
            )

        def stage(self, j, r, s):
            size = 1 << s
            return remote(
                grads[j].at[r, pl.ds(size, size), :, self.cut(j)],
                laters[j].at[r, pl.ds(size - 1, size), :, self.cut(j)],
                stage_send.at[j, number(r), s], stage_recv.at[j, number(r), s],
                routes.partner(s, d, z),
            )

        def across(self, j, r):
            return remote(
                grads[j].at[r, 0, :, self.cut(j)],
                self.incoming.at[r, :, pl.ds(self.at[j], self.width[j])],
                z_send.at[self.kind, j, r], z_recv.at[self.kind, j, r], (d, flip(z, r)),
            )

        def begin(self, i):
            if i < len(self.items):
                j, r = self.items[i]
                if self.kind:
                    self.load(j, r).start()
                self.to_core(j, r).start()

        def add(self, i, q):
            if not 0 <= i < len(self.items):
                return
            j, r = self.items[i]
            width = self.width[j]
            s = stages - q
            if q == 0:
                if self.kind:
                    self.load(j, r).wait()
                self.to_core(j, r).wait_recv()
            else:
                self.stage(j, r, s).wait_recv()

            @pl.loop(0, 1 << s)
            def _(k):
                for g in groups_of(r):
                    total = grads[j][g, k, :, 0:width].astype(f32)
                    if q == 0:
                        total += cores[j][g, k, :, 0:width].astype(f32)
                    else:
                        total += laters[j][g, k + ((1 << s) - 1), :, 0:width].astype(f32)
                    grads[j][g, k, :, 0:width] = total.astype(bf16)

            if q < stages:
                self.stage(j, r, s - 1).start()
            else:
                for g in groups_of(r):
                    if g:
                        self.across(j, g).start()

        def tick(self, n):
            for q in reversed(range(stages + 1)):
                self.add(n - ahead * (q + 1), q)

        def finish(self):
            for j, r in self.items:
                self.to_core(j, r).wait_send()
                for s in range(stages):
                    self.stage(j, r, s).wait_send()
                for g in groups_of(r):
                    if g:
                        self.across(j, g).wait_send()

        def collect(self, j, put):
            columns = slice(self.at[j], self.at[j] + self.width[j])

            @pl.when(role == self.kind)
            def _():
                total = grads[j][0, 0, :, 0 : self.width[j]].astype(f32)
                for r in range(2, nt, 2):
                    self.across(j, r).wait_recv()
                    total += self.incoming[r, :, columns].astype(f32)
                put(total)

            @pl.when(role != self.kind)
            def _():
                total = jnp.zeros((rows, self.width[j]), f32)
                for r in range(1, nt, 2):
                    self.across(j, r).wait_recv()
                    total += self.incoming[r, :, columns].astype(f32)
                put(total)

    enc = Sums(0, encoder, enc_width, enc_in, enc_at)
    play = Sums(1, players, pred_width, pred_in, (0, mat))

    def store(ref, t, first, value):
        ref[t, :, :, first : first + value.shape[1]] = value.astype(bf16).reshape(
            nd, rows, value.shape[1]
        )

    def begin_feed():
        back_copy().wait_recv()
        grad, gain_g, shift_g = norm_backward(back_ref[...].astype(f32), out_ref[...], vec_ref[4:5])
        d_ref[...] = grad
        low_ref[...] = grad.astype(bf16)
        acc_ref[...] = jnp.zeros_like(acc_ref)
        vec_grad_ref[4:5] = gain_g
        vec_grad_ref[5:6] = shift_g

    def feed(t):
        slot = lax.rem(t, 2)
        weight(t, 0).wait()
        weight(t, 1).wait()
        active, slope = gelu_parts(hidden_ref[t])
        active = active.astype(bf16)
        grad_hidden = sum(
            nn(low_ref[:, r * edge : (r + 1) * edge], down_w[slot, :, r * wide : (r + 1) * wide])
            for r in range(2)
        )
        grad_hidden = (grad_hidden * slope).astype(bf16)
        for r in range(2):
            mine = slice(r * edge, (r + 1) * edge)
            store(g0, t, r * wide, tn(low_ref[:, mine], active))
            store(g1, t, r * wide, tn(normed2_ref[:, mine], grad_hidden))
            acc_ref[:, mine] += nt_(grad_hidden, up_w[slot, :, r * wide : (r + 1) * wide])

        @pl.when(t + 2 < nt)
        def _():
            weight(t + 2, 0).start()
            weight(t + 2, 1).start()

    def end_feed():
        grad, gain_g, shift_g = norm_backward(acc_ref[...], mid_ref[...], vec_ref[2:3])
        vec_grad_ref[2:3] = gain_g
        vec_grad_ref[3:4] = shift_g
        grad = d_ref[...] + grad
        d_ref[...] = grad
        low_ref[...] = grad.astype(bf16)
        acc_ref[...] = jnp.zeros_like(acc_ref)

    def attention(t):
        slot = lax.rem(t, 2)
        weight(t, 2).wait()
        grad_att = sum(
            nn(
                low_ref[:, r * edge : (r + 1) * edge],
                attn_w[slot, :, r * wide + 3 * columns : (r + 1) * wide],
            )
            for r in range(2)
        ).astype(bf16)
        allowed = same_image(role, unit, context)
        grad_rows = attend_back(qkv_ref[t], grad_att, head_size, unit, allowed)
        for r in range(2):
            mine = slice(r * edge, (r + 1) * edge)
            grad_w = jnp.concatenate(
                [tn(normed_ref[:, mine], grad_rows), tn(low_ref[:, mine], att_ref[t])], 1
            )
            store(g2, t, r * wide, grad_w)
            acc_ref[:, mine] += nt_(grad_rows, attn_w[slot, :, r * wide : r * wide + 3 * columns])

        @pl.when(t + 2 < nt)
        def _():
            weight(t + 2, 2).start()

    def end_attention():
        grad, gain_g, shift_g = norm_backward(acc_ref[...], resid_ref[...], vec_ref[0:1])
        grad = d_ref[...] + grad
        vec_grad_ref[0:1] = gain_g
        vec_grad_ref[1:2] = shift_g
        vec_grad_ref[6:7] = jnp.sum(grad, 0, keepdims=True)
        low_ref[...] = nn(grad.astype(bf16), order_ref[...]).astype(bf16)

        @pl.loop(0, nt)
        def _(t):
            for m in range(2):
                store(g3, t, m * pix, tn(low_ref[:, m * edge : (m + 1) * edge], rows_ref[t]))

    bits = [("d", 1)] + [("d", b) for b in routes.low_bits]
    bits += [("z", 1 << s) for s in range(nt.bit_length() - 1)]

    def vec_copy(s):
        axis, bit = bits[s]
        peer = (flip(d, bit), z) if axis == "d" else (d, flip(z, bit))
        return remote(
            vec_send.at[s], vec_recv.at[s], vec_send_sem.at[s], vec_recv_sem.at[s], peer
        )

    def vec_pack():
        @pl.when(role == 0)
        def _():
            whole_rows = exactly(nt_, vec_grad_ref[...], hot_ref[...])
            vec_send[0, 0:8] = whole_rows[:, :edge]
            vec_send[0, 8:16] = whole_rows[:, edge:]
            vec_send[0, 16:32] = jnp.zeros((16, edge), f32)

        @pl.when(role == 1)
        def _():
            vec_send[0, 0:16] = jnp.zeros((16, edge), f32)
            vec_send[0, 16:32] = exactly(nt_, pred_vec_ref[...], hot_p_ref[...])
            vec_send[0, 28:29] = jnp.broadcast_to(loss_ref[0:1, 0:1], (1, edge))

        vec_copy(0).start()

    def vec_step(s):
        vec_copy(s).wait_recv()
        total = vec_send[s] + vec_recv[s]
        if s + 1 < len(bits):
            vec_send[s + 1] = total
            vec_copy(s + 1).start()
        else:
            enc_out[...] = jnp.concatenate([total[0:8], total[8:16]], 1)
            pred_out[...] = total[16:32]

    ticks = len(encoder) + ahead * (stages + 1)
    first_attention = 2 * nt
    last_attention = 3 * nt

    @pl.when(role == 0)
    def _():
        vec_grad_ref[...] = jnp.zeros_like(vec_grad_ref)
        for t in range(2):
            for i in range(3):
                weight(t, i).start()

    greet(routes, d, z, everyone=True)

    @pl.when(role == 1)
    def _():
        back_copy().start()

    @pl.loop(0, ticks)
    def _(n):
        @pl.when(role == 0)
        def _():
            pl.when(n == 0)(begin_feed)

            @pl.when((n < first_attention) & (lax.rem(n, 2) == 0))
            def _():
                feed(lax.div(n, 2))

            pl.when(n == first_attention)(end_feed)

            @pl.when((n >= first_attention) & (n < last_attention))
            def _():
                attention(n - first_attention)

            pl.when(n == last_attention)(end_attention)

        for k in range(ticks):

            @pl.when(n == k)
            def _(k=k):
                if k == last_attention:
                    vec_pack()
                if k > last_attention and k - last_attention - 1 < len(bits):
                    vec_step(k - last_attention - 1)

                @pl.when(role == 0)
                def _():
                    enc.begin(k)
                    enc.tick(k)

                @pl.when(role == 1)
                def _():
                    play.begin(k)
                    play.tick(k)

    for s in range(max(0, ticks - last_attention - 1), len(bits)):
        vec_step(s)

    def put_block(first):
        def put(total):
            low = total.astype(bf16)
            for i in range(low.shape[1] // edge):
                block_ref[first + i] = low[:, i * edge : (i + 1) * edge]

        return put

    def put_embed(total):
        emb_ref[...] = jnp.concatenate([total[:, :pix].T, total[:, pix:].T], 1)

    per_mat = mat // edge
    for j in range(2):
        play.collect(j, put_block((3 + j) * per_mat))
    for j, first in ((0, 2 * per_mat), (1, per_mat), (2, 0)):
        enc.collect(j, put_block(first))
    block_ref[block_ref.shape[0] - 1] = jnp.zeros(block_ref.shape[1:], bf16)
    slots = slots_ref.shape[1]

    def slot_copy(j):
        peer = routes.later(d, j)
        return remote(
            slots_ref.at[peer], low_out.at[:, d], slot_send.at[j], slot_recv.at[j], (peer, z)
        )

    def own_slots():
        return pltpu.make_async_copy(slots_ref.at[d], low_out.at[:, d], slot_sem)

    for s in range(nd * slots):
        slots_ref[s // slots, s % slots] = block_ref[slot_of_ref[s]]
    for j in range(1, nd):
        slot_copy(j).start()
    own_slots().start()
    enc.collect(3, put_embed)

    @pl.when(role == 0)
    def _():
        enc.finish()

    @pl.when(role == 1)
    def _():
        play.finish()
        back_copy().wait_send()

    for s in range(len(bits)):
        vec_copy(s).wait_send()
    own_slots().wait()
    for j in range(1, nd):
        slot_copy(j).wait()


def whole(shape):
    return pl.BlockSpec(shape, lambda *_: (0,) * len(shape))


def by_group(shape):
    return pl.BlockSpec((1,) + shape, lambda t: (t, 0, 0))


def compiled():
    return pltpu.CompilerParams(
        dimension_semantics=("arbitrary",), vmem_limit_bytes=KERNEL_BYTES
    )


def cost(flops, moved):
    return pl.CostEstimate(flops=int(flops), bytes_accessed=int(moved), transcendentals=0)


def sincos(cell_index, columns):
    quarter = columns // 4
    frequency = 1.0 / 10000.0 ** (jnp.arange(quarter).astype(f32) / quarter)
    col_angle = (cell_index % SIDE).astype(f32)[..., None] * frequency
    row_angle = (cell_index // SIDE).astype(f32)[..., None] * frequency
    return jnp.concatenate(
        [jnp.sin(col_angle), jnp.cos(col_angle), jnp.sin(row_angle), jnp.cos(row_angle)], -1
    )


class Routes:
    def __init__(self, nd, nt):
        self.nd, self.nt = nd, nt
        self.low_bits = [1 << s for s in range(1, nd.bit_length() - 1)]
        self.stages = len(self.low_bits)

    def order(self, core):
        return self.low_bits if core == 0 else self.low_bits[::-1]

    def pairs(self, target, keep):
        found = []
        for d in range(self.nd):
            for z in range(self.nt):
                if keep(d, z):
                    d2, z2 = target(d, z)
                    found.append((d * self.nt + z, d2 * self.nt + z2))
        return found

    def later(self, d, j):
        return lax.rem(d + j, self.nd)

    def holder(self, k, d):
        held = flip(d, k >> self.stages)
        core = lax.rem(held, 2)
        for s in range(self.stages):
            if (k >> s) & 1:
                ends = flip(held, self.order(0)[s]), flip(held, self.order(1)[s])
                held = ends[0] + core * (ends[1] - ends[0])
        return held

    def partner(self, number, d, z):
        if number == self.stages:
            return flip(d, 1), z
        core = lax.rem(d, 2)
        ends = flip(d, self.order(0)[number]), flip(d, self.order(1)[number])
        return ends[0] + core * (ends[1] - ends[0]), z

    def across(self, r, values, from_role=None):
        def keep(d, z):
            return from_role is None or z % 2 == from_role

        return lax.ppermute(values, AXES, self.pairs(lambda d, z: (d, z ^ r), keep))

    def holders(self, d):
        place = jnp.arange(self.nd, dtype=jnp.int32)
        held = d ^ (place >> self.stages)
        core = held & 1
        for s in range(self.stages):
            bit = (place >> s) & 1
            held = held ^ (bit * jnp.where(core == 0, self.order(0)[s], self.order(1)[s]))
        return held

    def total(self, values):
        for bit in [1] + self.low_bits:
            values = values + lax.ppermute(
                values, AXES, self.pairs(lambda d, z, b=bit: (d ^ b, z), lambda d, z: True)
            )
        r = 1
        while r < self.nt:
            values = values + self.across(r, values)
            r *= 2
        return values


def shards(
    patches,
    ctx_idx,
    tgt_idx,
    owner,
    weights,
    stats_left,
    stats_right,
    root_left,
    root_right,
    teacher_slot_blocks,
    embed,
    embed_m,
    embed_v,
    teacher_embed,
    enc_vectors,
    enc_m,
    enc_v,
    pred_vectors,
    pred_m,
    pred_v,
    teacher_vectors,
):
    nt = lax.axis_size("tensor")
    nd = lax.axis_size("dp")
    routes = Routes(nd, nt)
    half = nt // 2
    d = lax.axis_index("dp")
    z = lax.axis_index("tensor")
    role = z % 2
    student_role = role == 0
    images, npatches, pix_part = patches.shape
    slots = weights.shape[1]
    edge = weights.shape[-1]
    slot_count = slots * nd
    block_count = owner.shape[0]
    width = enc_vectors.shape[1]
    narrow = pred_vectors.shape[1]
    players = (pred_vectors.shape[0] - 3) // 4
    side = width // edge
    teach_count = 3 * side * side
    quarter = width // nt
    context_len = ctx_idx.shape[1]
    target_len = tgt_idx.shape[1]
    seq_len = context_len + target_len
    share = images // half
    rows_part = edge // nd

    both = jnp.stack([weights[0], teacher_slot_blocks[0]]).astype(bf16)
    both = both.reshape(2, slots, nd, rows_part, edge)
    both = lax.all_to_all(both, "dp", split_axis=2, concat_axis=0, tiled=False)
    by_slot = both.transpose(1, 0, 2, 3, 4).reshape(2, slot_count, rows_part, edge)
    mine = by_slot[0][owner].transpose(1, 0, 2).reshape(rows_part, -1)
    teach = by_slot[1][owner[:teach_count]].transpose(1, 0, 2).reshape(rows_part, -1)

    mat = side * width

    def embed_rows(values):
        turned = values.astype(bf16).T.reshape(side, rows_part, pix_part)
        return turned.transpose(1, 0, 2).reshape(rows_part, -1)

    of_student = jnp.concatenate(
        [mine[:, :mat], embed_rows(embed), mine[:, mat : 3 * mat]], 1
    )
    of_teacher = jnp.concatenate([teach[:, :mat], embed_rows(teacher_embed), teach[:, mat:]], 1)
    own = jnp.where(student_role, of_student, of_teacher)
    other = jnp.where(student_role, of_teacher, of_student)
    maps = 3 * mat + 3 * players * edge
    pred_own = jnp.concatenate([mine[:, maps:], mine[:, 3 * mat : maps]], 1)

    holder = routes.holders(d)
    inside = jnp.arange(rows_part, dtype=jnp.int32)
    feat_p = (holder[:, None] * rows_part + inside[None, :]).reshape(-1)
    feat = jnp.concatenate([r * edge + feat_p for r in range(side)])
    one_hot = (feat[:, None] == jnp.arange(width)[None, :]).astype(f32)
    one_hot_p = (feat_p[:, None] == jnp.arange(narrow)[None, :]).astype(f32)

    def to_local(rows, hot):
        return jnp.einsum("nf,lf->nl", rows, hot, precision=exact, preferred_element_type=f32)

    def to_global(rows, hot):
        return jnp.einsum("nl,lf->nf", rows, hot, precision=exact, preferred_element_type=f32)

    vec = to_local(jnp.where(student_role, enc_vectors, teacher_vectors), one_hot)
    vec = jnp.pad(vec, ((0, 1), (0, 0)))
    pvec = to_local(pred_vectors, one_hot_p)
    pvec = jnp.pad(pvec, ((0, 16 - pvec.shape[0]), (0, 0)))
    pred_z = z - role + 1
    group_feat = (pred_z ^ jnp.arange(nt, dtype=jnp.int32))[:, None] * quarter + jnp.arange(
        quarter, dtype=jnp.int32
    )
    emb_feat = jnp.concatenate(
        [holder[:, None] * 2 * rows_part + m * rows_part + inside[None, :] for m in range(2)]
    ).reshape(-1)
    order = (feat[:, None] == emb_feat[None, :]).astype(bf16)
    swap = (feat[None, :, None] == group_feat[:, None, :]).astype(bf16)

    part = z // 2
    hot = (ctx_idx[:, :, None] == jnp.arange(npatches)[None, None, :]).astype(bf16)
    picked = jnp.einsum("gcn,gnp->gcp", hot, patches, preferred_element_type=f32).astype(bf16)

    def rows_for(target_z):
        where = (target_z // 2) * share
        ctx = lax.dynamic_slice_in_dim(picked, where, share, 0).reshape(-1, pix_part)
        every = lax.dynamic_slice_in_dim(patches, where, share, 0).reshape(-1, pix_part)
        padded = jnp.pad(ctx, ((0, every.shape[0] - ctx.shape[0]), (0, 0)))
        return jnp.where(target_z % 2 == 0, padded, every)

    patch_out = jnp.stack([rows_for(z ^ r) for r in range(nt)])
    my_ctx = lax.dynamic_slice_in_dim(ctx_idx, part * share, share, 0)
    my_tgt = lax.dynamic_slice_in_dim(tgt_idx, part * share, share, 0)
    full_rows = share * npatches
    ctx_rows = share * context_len
    tgt_rows = share * target_len
    ctx_places = jnp.pad(my_ctx.reshape(-1), (0, full_rows - ctx_rows))
    places = jnp.where(student_role, ctx_places, jnp.arange(full_rows) % npatches)
    table = to_local(sincos(jnp.arange(npatches), width), one_hot)
    table_p = to_local(sincos(jnp.arange(npatches), narrow), one_hot_p)
    base = table[places] + vec[6]
    tgt_places = (my_tgt + npatches * jnp.arange(share, dtype=jnp.int32)[:, None]).reshape(-1)
    pick = (tgt_places[:, None] == jnp.arange(full_rows)[None, :]).astype(bf16)
    widths = [mat + side * pix_part, mat, mat, 4 * edge, 3 * (players - 1) * edge]
    any_space = pl.BlockSpec(memory_space=pl.ANY)
    dma = pltpu.SemaphoreType.DMA
    attn_cols = side * width
    columns = width // nt
    mat_shapes = [jax.ShapeDtypeStruct((nt, nd, rows_part, c), bf16) for c in widths]
    gather_sems = [
        dma((5, nt)),
        dma((5, nt)),
        dma((6,)),
        dma((nt,)),
        dma((nt,)),
        dma((5, nt, routes.stages + 1)),
        dma((5, nt, routes.stages + 1)),
    ]
    in_vmem = pl.BlockSpec(memory_space=VMEM)
    role_word = role.astype(jnp.int32).reshape(1)
    if rows_part % 16 == 0:
        results = pl.pallas_call(
            functools.partial(forward_kernel, routes, widths, npatches, context_len, HD),
            in_specs=[pl.BlockSpec(memory_space=pltpu.SMEM)] + [in_vmem] * 12,
            out_specs=[any_space] * 5 + [in_vmem] * 17,
            out_shape=mat_shapes
            + [
                jax.ShapeDtypeStruct((nt, ctx_rows, pix_part), bf16),
                jax.ShapeDtypeStruct((ctx_rows, width), f32),
                jax.ShapeDtypeStruct((ctx_rows, width), f32),
                jax.ShapeDtypeStruct((ctx_rows, width), bf16),
                jax.ShapeDtypeStruct((nt, ctx_rows, 3 * columns), bf16),
                jax.ShapeDtypeStruct((nt, ctx_rows, columns), bf16),
                jax.ShapeDtypeStruct((ctx_rows, width), f32),
                jax.ShapeDtypeStruct((ctx_rows, width), bf16),
                jax.ShapeDtypeStruct((nt, ctx_rows, width), f32),
                jax.ShapeDtypeStruct((nt, ctx_rows, quarter), bf16),
                jax.ShapeDtypeStruct((nt, tgt_rows, quarter), bf16),
                jax.ShapeDtypeStruct((width, width), bf16),
                jax.ShapeDtypeStruct((width, width), bf16),
                jax.ShapeDtypeStruct((narrow, narrow), bf16),
                jax.ShapeDtypeStruct((8, width), f32),
                jax.ShapeDtypeStruct((16, narrow), f32),
                jax.ShapeDtypeStruct((share * seq_len, narrow), f32),
            ],
            scratch_shapes=[VMEM(shape.shape, bf16) for shape in mat_shapes]
            + [
                VMEM((nt, full_rows, pix_part), bf16),
                VMEM((full_rows, width), f32),
                VMEM((full_rows, width), bf16),
                VMEM((nt, ctx_rows, quarter), bf16),
                VMEM((nt, ctx_rows, quarter), bf16),
                VMEM((2, slots, nd, rows_part, edge), bf16),
                VMEM((2, slot_count, rows_part, edge), bf16),
                VMEM((rows_part, sum(widths[:3])), bf16),
                VMEM((rows_part, sum(widths[:3])), bf16),
                VMEM((rows_part, sum(widths[3:])), bf16),
                VMEM((images * context_len, pix_part), bf16),
                VMEM((images * npatches, pix_part), bf16),
                dma((5, nt)),
                dma(()),
                dma(()),
                dma((nd,)),
                dma((nd,)),
                dma(()),
            ]
            + gather_sems,
            compiler_params=pltpu.CompilerParams(
                collective_id=0, has_side_effects=True, vmem_limit_bytes=KERNEL_BYTES
            ),
            cost_estimate=cost(14e9, 60e6),
            name="gather_and_encode",
        )(
            owner, weights[0], teacher_slot_blocks[0], patches.transpose(0, 2, 1),
            ctx_idx, tgt_idx, embed, teacher_embed, enc_vectors, teacher_vectors, pred_vectors,
            jnp.asarray(sincos_table(width)), jnp.asarray(sincos_table(narrow)),
        )
        gathered, results = results[:5], results[5:]
        patch_rows, middle, resid, normed_a, rows_a, att_a = results[:6]
        output, normed_f, hidden, feat_in, target = results[6:11]
        hot, order, hot_p, vec, pvec, tokens_at = results[11:]
        attn_emb, up_w, down_t, pred_first, pred_second = (
            g.reshape(nt, edge, -1) for g in gathered
        )
    else:
        attn_emb, up_w, down_t, pred_first, pred_second, patch_rows = pl.pallas_call(
            functools.partial(gather_kernel, routes, widths, ctx_rows),
            in_specs=[any_space] * 4,
            out_specs=[any_space] * 6,
            out_shape=mat_shapes
            + [jax.ShapeDtypeStruct((nt, full_rows, pix_part), bf16)],
            scratch_shapes=gather_sems,
            compiler_params=pltpu.CompilerParams(collective_id=0, has_side_effects=True),
            cost_estimate=cost(0, 50e6),
            name="gather_weights",
        )(own, other, pred_own, patch_out)
        attn_emb, up_w, down_t, pred_first, pred_second = (
            value.reshape(nt, edge, -1)
            for value in (attn_emb, up_w, down_t, pred_first, pred_second)
        )
        middle, resid, normed_a, rows_a, att_a = pl.pallas_call(
            functools.partial(encoder_attend_kernel, edge, npatches, context_len, HD, ctx_rows),
            grid=(2 * nt,),
            in_specs=[
                pl.BlockSpec(memory_space=pltpu.SMEM),
                pl.BlockSpec((1, full_rows, pix_part), lambda i: (jnp.minimum(i, nt - 1), 0, 0)),
                whole((full_rows, width)),
                pl.BlockSpec(
                    (1, edge, side * pix_part),
                    lambda i: (jnp.minimum(i, nt - 1), 0, attn_cols // (side * pix_part)),
                ),
                whole((width, width)),
                pl.BlockSpec((1, edge, attn_cols), lambda i: (jnp.maximum(i - nt, 0), 0, 0)),
                whole((8, width)),
            ],
            out_specs=[
                whole((full_rows, width)),
                whole((ctx_rows, width)),
                whole((ctx_rows, width)),
                pl.BlockSpec((1, ctx_rows, 3 * columns), lambda i: (jnp.maximum(i - nt, 0), 0, 0)),
                pl.BlockSpec((1, ctx_rows, columns), lambda i: (jnp.maximum(i - nt, 0), 0, 0)),
            ],
            out_shape=[
                jax.ShapeDtypeStruct((full_rows, width), f32),
                jax.ShapeDtypeStruct((ctx_rows, width), f32),
                jax.ShapeDtypeStruct((ctx_rows, width), bf16),
                jax.ShapeDtypeStruct((nt, ctx_rows, 3 * columns), bf16),
                jax.ShapeDtypeStruct((nt, ctx_rows, columns), bf16),
            ],
            scratch_shapes=[VMEM((full_rows, width), f32), VMEM((full_rows, width), bf16)],
            compiler_params=compiled(),
            cost_estimate=cost(6e9, 12e6),
            name="encoder_attend",
        )(role_word, patch_rows, base, attn_emb, order, attn_emb, vec)
        output, normed_f, hidden, enc_feat, target = pl.pallas_call(
            functools.partial(encoder_feed_kernel, edge, ctx_rows),
            grid=(nt,),
            in_specs=[
                whole((full_rows, width)),
                by_group((edge, mat)),
                by_group((edge, mat)),
                whole((8, width)),
                whole((tgt_rows, full_rows)),
                whole((nt, width, quarter)),
            ],
            out_specs=[
                whole((ctx_rows, width)),
                whole((ctx_rows, width)),
                by_group((ctx_rows, width)),
                whole((nt, ctx_rows, quarter)),
                whole((nt, tgt_rows, quarter)),
            ],
            out_shape=[
                jax.ShapeDtypeStruct((ctx_rows, width), f32),
                jax.ShapeDtypeStruct((ctx_rows, width), bf16),
                jax.ShapeDtypeStruct((nt, ctx_rows, width), f32),
                jax.ShapeDtypeStruct((nt, ctx_rows, quarter), bf16),
                jax.ShapeDtypeStruct((nt, tgt_rows, quarter), bf16),
            ],
            scratch_shapes=[VMEM((full_rows, width), f32), VMEM((full_rows, width), bf16)],
            compiler_params=compiled(),
            cost_estimate=cost(8e9, 14e6),
            name="encoder_feed",
        )(middle, up_w, down_t, vec, pick, swap)

        feat_in = routes.across(1, enc_feat, from_role=0)
        tokens_at = table_p[jnp.concatenate([my_ctx, my_tgt], 1)]
        mask_rows = jnp.arange(seq_len)[None, :, None] >= context_len
        tokens_at = jnp.where(mask_rows, tokens_at + pvec[4 * players + 2], tokens_at)
        tokens_at = tokens_at.reshape(-1, narrow)
        hot = one_hot.T.astype(bf16)

    token_rows = share * seq_len
    pred_cols = (3 * players + 1) * edge
    denominator = images * nd * target_len * width
    pred_columns = narrow // nt
    pred_grads, pred_vec_g, loss_tile, back = pl.pallas_call(
        functools.partial(predictor_kernel, share, context_len, players, PHD, denominator),
        in_specs=[in_vmem] * 3 + [any_space] * 2 + [in_vmem] * 2,
        out_specs=[any_space] + [in_vmem] * 3,
        out_shape=[
            jax.ShapeDtypeStruct((nt, edge, pred_cols), bf16),
            jax.ShapeDtypeStruct((16, narrow), f32),
            jax.ShapeDtypeStruct((8, 128), f32),
            jax.ShapeDtypeStruct((ctx_rows, width), bf16),
        ],
        scratch_shapes=[
            VMEM((nt, edge, pred_cols), bf16),
            VMEM((nt, edge, pred_cols), bf16),
            dma((3 * players + 1,)),
            dma((3 * players + 1,)),
            VMEM((players + 1, token_rows, narrow), f32),
            VMEM((players, token_rows, narrow), f32),
            VMEM((players, token_rows, narrow), bf16),
            VMEM((players, token_rows, narrow), bf16),
            VMEM((players, nt, token_rows, 3 * pred_columns), bf16),
            VMEM((players, nt, token_rows, pred_columns), bf16),
            VMEM((players, nt // 2, token_rows, 2 * edge), f32),
            VMEM((token_rows, narrow), f32),
            VMEM((token_rows, narrow), f32),
            VMEM((token_rows, narrow), bf16),
            VMEM((tgt_rows, narrow), bf16),
        ],
        compiler_params=pltpu.CompilerParams(vmem_limit_bytes=KERNEL_BYTES),
        cost_estimate=cost(16e9, 30e6),
        name="predictor",
    )(feat_in, target, tokens_at, pred_first, pred_second, pvec, hot)
    all_cols = attn_cols + side * pix_part
    middle_size = nd // 2
    block_shape = [
        jax.ShapeDtypeStruct((rows_part, (block_count + 1) * edge), bf16),
        jax.ShapeDtypeStruct((rows_part, side * pix_part), f32),
    ]
    if rows_part % 16 == 0:
        widths_g = (mat, mat, mat, side * pix_part)
        vec_steps = nd.bit_length() + nt.bit_length() - 2
        slot_numbers = jnp.arange(slot_count, dtype=jnp.int32)
        holds = (owner[None, :] == slot_numbers[:, None]).astype(jnp.int32)
        order_of = jnp.arange(block_count, dtype=jnp.int32) - block_count
        slot_of = block_count + jnp.sum(holds * order_of[None, :], 1)
        low_grads, embed_grad, enc_total, pred_total = pl.pallas_call(
            functools.partial(backward_kernel, routes, context_len, HD),
            in_specs=[pl.BlockSpec(memory_space=pltpu.SMEM)]
            + [any_space] * 5
            + [in_vmem] * 15,
            out_specs=[any_space] + [in_vmem] * 3,
            out_shape=[
                jax.ShapeDtypeStruct((slots, nd, rows_part, edge), bf16),
                jax.ShapeDtypeStruct((pix_part, side * rows_part), f32),
                jax.ShapeDtypeStruct((8, width), f32),
                jax.ShapeDtypeStruct((16, narrow), f32),
            ],
            scratch_shapes=[
                VMEM((block_count + 1, rows_part, edge), bf16),
                VMEM((nd, slots, rows_part, edge), bf16),
            ]
            + [VMEM((nt, nd, rows_part, c), bf16) for c in widths_g]
            + [VMEM((nt, middle_size, rows_part, c), bf16) for c in widths_g]
            + [VMEM((nt, middle_size - 1, rows_part, c), bf16) for c in widths_g]
            + [
                VMEM((nt, rows_part, sum(widths_g)), bf16),
                VMEM((nt, rows_part, pred_cols), bf16),
                VMEM((2, edge, mat), bf16),
                VMEM((2, edge, mat), bf16),
                VMEM((2, edge, mat), bf16),
                VMEM((ctx_rows, width), bf16),
                VMEM((ctx_rows, width), f32),
                VMEM((ctx_rows, width), bf16),
                VMEM((ctx_rows, width), f32),
                VMEM((8, width), f32),
                VMEM((vec_steps, 32, edge), f32),
                VMEM((vec_steps, 32, edge), f32),
                dma((3, 2)),
                dma(()),
                dma(()),
                dma((4, nt)),
                dma((4, nt)),
                dma((4, nt)),
                dma((4, nt, routes.stages)),
                dma((4, nt, routes.stages)),
                dma((2, 4, nt)),
                dma((2, 4, nt)),
                dma((vec_steps,)),
                dma((vec_steps,)),
                dma((nd,)),
                dma((nd,)),
                dma(()),
            ],
            compiler_params=pltpu.CompilerParams(
                collective_id=1, has_side_effects=True, vmem_limit_bytes=KERNEL_BYTES
            ),
            cost_estimate=cost(14e9, 60e6),
            name="encode_back_and_reduce",
        )(
            slot_of, pred_grads.reshape(nt, nd, rows_part, -1), back, attn_emb, up_w, down_t,
            output, middle, resid, normed_f, normed_a, hidden, rows_a, att_a, patch_rows,
            vec, order, hot, hot_p, pred_vec_g, loss_tile,
        )
        low_grads = low_grads.reshape(slots, edge, edge)
    else:
        back = routes.across(1, back, from_role=1)

        grad_shape = jax.ShapeDtypeStruct((nt, edge, mat), bf16)
        up_g, down_g, grad_mid, vec_g1 = pl.pallas_call(
            functools.partial(encoder_feed_back_kernel, edge),
            grid=(nt,),
            in_specs=[
                whole((ctx_rows, width)),
                whole((ctx_rows, width)),
                whole((ctx_rows, width)),
                whole((ctx_rows, width)),
                by_group((ctx_rows, width)),
                by_group((edge, mat)),
                by_group((edge, mat)),
                whole((8, width)),
            ],
            out_specs=[by_group((edge, mat))] * 2 + [whole((ctx_rows, width)), whole((8, width))],
            out_shape=[grad_shape] * 2
            + [
                jax.ShapeDtypeStruct((ctx_rows, width), f32),
                jax.ShapeDtypeStruct((8, width), f32),
            ],
            scratch_shapes=[
                VMEM((ctx_rows, width), f32),
                VMEM((ctx_rows, width), bf16),
                VMEM((ctx_rows, width), f32),
            ],
            compiler_params=compiled(),
            cost_estimate=cost(8e9, 25e6),
            name="encoder_feed_back",
        )(back, output, middle, normed_f, hidden, up_w, down_t, vec)
        attn_g, vec_g2 = pl.pallas_call(
            functools.partial(encoder_attend_back_kernel, edge, npatches, context_len, HD),
            grid=(2 * nt,),
            in_specs=[
                pl.BlockSpec(memory_space=pltpu.SMEM),
                whole((ctx_rows, width)),
                whole((ctx_rows, width)),
                whole((ctx_rows, width)),
                pl.BlockSpec((1, ctx_rows, 3 * columns), lambda i: (jnp.minimum(i, nt - 1), 0, 0)),
                pl.BlockSpec((1, ctx_rows, columns), lambda i: (jnp.minimum(i, nt - 1), 0, 0)),
                pl.BlockSpec((1, edge, attn_cols), lambda i: (jnp.minimum(i, nt - 1), 0, 0)),
                pl.BlockSpec((1, ctx_rows, pix_part), lambda i: (jnp.maximum(i - nt, 0), 0, 0)),
                whole((width, width)),
                whole((8, width)),
            ],
            out_specs=[
                whole((nt, edge, all_cols)),
                whole((8, width)),
            ],
            out_shape=[
                jax.ShapeDtypeStruct((nt, edge, all_cols), bf16),
                jax.ShapeDtypeStruct((8, width), f32),
            ],
            scratch_shapes=[VMEM((ctx_rows, width), bf16), VMEM((ctx_rows, width), f32)],
            compiler_params=compiled(),
            cost_estimate=cost(6e9, 20e6),
            name="encoder_attend_back",
        )(role_word, grad_mid, resid, normed_a, rows_a, att_a, attn_emb, patch_rows, order, vec)

        places = [g.reshape(nt, nd, rows_part, -1) for g in (down_g, up_g, attn_g, pred_grads)]
        by_block, emb_sum = pl.pallas_call(
            functools.partial(reduce_kernel, routes, attn_cols),
            in_specs=[any_space] * 4,
            out_specs=[in_vmem] * 2,
            out_shape=block_shape,
            scratch_shapes=[
                VMEM((nt, middle_size, rows_part, mat), bf16),
                VMEM((nt, middle_size, rows_part, mat), bf16),
                VMEM((nt, middle_size, rows_part, all_cols), bf16),
                VMEM((nt, middle_size - 1, rows_part, mat), bf16),
                VMEM((nt, middle_size - 1, rows_part, mat), bf16),
                VMEM((nt, middle_size - 1, rows_part, all_cols), bf16),
                VMEM((nt, rows_part, 2 * mat + all_cols), bf16),
                VMEM((nt, rows_part, pred_cols), bf16),
                VMEM((2, middle_size, rows_part, all_cols), bf16),
                dma((2,)),
                dma((3, nt)),
                dma((3, nt)),
                dma((3, nt, routes.stages)),
                dma((3, nt, routes.stages)),
                dma((2, 3, nt)),
                dma((2, 3, nt)),
            ],
            compiler_params=pltpu.CompilerParams(
                collective_id=1, has_side_effects=True, vmem_limit_bytes=KERNEL_BYTES
            ),
            cost_estimate=cost(0, 60e6),
            name="reduce_gradients",
        )(*places)

        enc_rows = to_global(vec_g1[:7] + vec_g2[:7], one_hot)
        pred_rows = to_global(pred_vec_g[: 4 * players + 3], one_hot_p)
        enc_rows = jnp.where(student_role, enc_rows, 0.0)
        pred_rows = jnp.where(role == 1, pred_rows, 0.0)
        loss_row = jnp.where(role == 1, loss_tile[0, 0], 0.0)
        packed = jnp.concatenate([enc_rows.reshape(-1), pred_rows.reshape(-1), loss_row[None]])
        packed = jnp.pad(packed, (0, -packed.shape[0] % 1024)).reshape(-1, 128)
        packed = routes.total(packed).reshape(-1)
        enc_total = packed[: enc_rows.size].reshape(enc_rows.shape)
        pred_total = packed[enc_rows.size : enc_rows.size + pred_rows.size].reshape(pred_rows.shape)
        loss_total = packed[enc_rows.size + pred_rows.size]
        by_block = by_block.reshape(rows_part, block_count + 1, edge).transpose(1, 0, 2)
        slot_of = (
            jnp.full((slot_count,), block_count, jnp.int32)
            .at[owner]
            .set(jnp.arange(block_count, dtype=jnp.int32))
        )
        slot_rows = by_block[slot_of].reshape(nd, slots, rows_part, edge)
        slot_rows = lax.all_to_all(slot_rows, "dp", split_axis=0, concat_axis=1, tiled=False)
        low_grads = slot_rows.reshape(slots, edge, edge)
        embed_grad = emb_sum.reshape(rows_part, side, pix_part).transpose(1, 0, 2)
        embed_grad = embed_grad.reshape(-1, pix_part).T
        enc_total = jnp.pad(enc_total, ((0, 1), (0, 0)))
        pred_total = jnp.pad(pred_total, ((0, 5), (0, 0))).at[12].set(loss_total)

    slot_spec = pl.BlockSpec((1, 1, edge, edge), lambda s: (0, s, 0, 0))
    slot_shape = jax.ShapeDtypeStruct(weights.shape, f32)
    table_shape = jax.ShapeDtypeStruct(embed.shape, f32)
    enc_shape = jax.ShapeDtypeStruct(enc_vectors.shape, f32)
    pred_shape = jax.ShapeDtypeStruct(pred_vectors.shape, f32)
    shapes = [table_shape] * 4 + [enc_shape] * 3 + [pred_shape] * 3 + [enc_shape]
    shapes.append(jax.ShapeDtypeStruct((1, 1), f32))
    small = (
        embed_grad, embed, embed_m, embed_v, teacher_embed, enc_total, enc_vectors, enc_m, enc_v,
        pred_total, pred_vectors, pred_m, pred_v, teacher_vectors,
    )
    results = pl.pallas_call(
        update_kernel,
        grid=(slots,),
        in_specs=[pl.BlockSpec((1, edge, edge), lambda s: (s, 0, 0))]
        + [slot_spec] * 6
        + [whole(value.shape) for value in small],
        out_specs=[slot_spec] * 5 + [whole(shape.shape) for shape in shapes],
        out_shape=[slot_shape] * 5 + shapes,
        compiler_params=compiled(),
        cost_estimate=cost(3e9, 22e6),
        name="update",
    )(low_grads, weights, stats_left, stats_right, root_left, root_right, teacher_slot_blocks, *small)
    return (results[-1][0, 0],) + tuple(results[:-1])


def solution(mesh):
    blocks = P("tensor", "dp", None, None)
    table = P("tensor", "dp")
    in_specs = (
        (P("dp", None, "tensor"), P("dp", None), P("dp", None), P())
        + (blocks,) * 6
        + (table,) * 4
        + (P(),) * 7
    )
    out_specs = (P(),) + (blocks,) * 5 + (table,) * 4 + (P(),) * 7
    return jax.shard_map(shards, mesh=mesh, in_specs=in_specs, out_specs=out_specs, check_vma=False)
```
